32 devices in a mesh: mp: 4 (over y, x), dp: 8 (over z, core).
Axes of the slice: x: 2, y: 2, z: 4, core: 2. Of those that a mesh axis runs over, the one named last changes fastest.
Arguments:
- tokens: bfloat16 [8192, 2048], P('dp', 'mp')
- cotangent: bfloat16 [8192, 2048], P('dp', 'mp'), may hold values from -6 to 6
- seq_lengths: int32 [8, 16], P('dp'), may hold values from 0 to 1024, as said below
- w_qkv: float32 [2048, 3, 2048], P('dp', None, 'mp'), may hold values from -0.125 to 0.125
- qkv_bias_state: float32 [2, 3, 2048], P(None, None, ('mp', 'dp')), as said below
- w_out: float32 [2048, 2048], P('mp', 'dp'), may hold values from -0.5 to 0.5
- out_bias_state: float32 [2, 2, 2048], P(None, None, ('mp', 'dp')), as said below
- w_up: float32 [2048, 8192], P('dp', 'mp'), may hold values from -0.125 to 0.125
- up_bias_state: float32 [2, 8192], P(None, ('mp', 'dp')), as said below
- w_down: float32 [8192, 2048], P('mp', 'dp'), may hold values from -0.0625 to 0.0625
- ln_state: float32 [2, 2, 2048], P(None, None, ('mp', 'dp')), as said below
- qkv_left: float32 [2, 4, 8, 256, 256], P(None, 'mp', 'dp')
- qkv_right: float32 [2, 4, 8, 1536, 1536], P(None, 'mp', 'dp')
- out_left: float32 [2, 4, 8, 512, 512], P(None, 'mp', 'dp')
- out_right: float32 [2, 4, 8, 256, 256], P(None, 'mp', 'dp')
- up_left: float32 [2, 4, 8, 256, 256], P(None, 'mp', 'dp')
- up_right: float32 [2, 4, 8, 2048, 2048], P(None, 'mp', 'dp')
- down_left: float32 [2, 4, 8, 2048, 2048], P(None, 'mp', 'dp')
- down_right: float32 [2, 4, 8, 256, 256], P(None, 'mp', 'dp')
Outputs:
- output: bfloat16 [8192, 2048], P('dp', 'mp')
- input_grad: float32 [8192, 2048], P('dp', 'mp')
- new_w_qkv: float32 [2048, 3, 2048], P('dp', None, 'mp')
- new_w_out: float32 [2048, 2048], P('mp', 'dp')
- new_w_up: float32 [2048, 8192], P('dp', 'mp')
- new_w_down: float32 [8192, 2048], P('mp', 'dp')
- new_vector_params: float32 [7, 2048], P(None, ('mp', 'dp'))
- new_vector_stats: float32 [7, 2048], P(None, ('mp', 'dp'))
- new_up_bias: float32 [8192], P(('mp', 'dp'))
- new_up_stat: float32 [8192], P(('mp', 'dp'))
- qkv_left_new: float32 [4, 8, 256, 256], P('mp', 'dp')
- qkv_right_new: float32 [4, 8, 1536, 1536], P('mp', 'dp')
- out_left_new: float32 [4, 8, 512, 512], P('mp', 'dp')
- out_right_new: float32 [4, 8, 256, 256], P('mp', 'dp')
- up_left_new: float32 [4, 8, 256, 256], P('mp', 'dp')
- up_right_new: float32 [4, 8, 2048, 2048], P('mp', 'dp')
- down_left_new: float32 [4, 8, 2048, 2048], P('mp', 'dp')
- down_right_new: float32 [4, 8, 256, 256], P('mp', 'dp')
The draws below stay inside these ranges and needn't reach their ends.
Inputs may be any that keep to these rules, and one draw needn't show every extreme that they name: `seq_lengths`: row b lists, in order, the lengths of the sequences packed back to back from the first row of block b of 1024 rows; 0 marks an empty slot, every other length is 64 or more; a row sums to at most 1024, the rest of the block is padding; some block holds a sequence of 1024. `ln_state`: index 1 holds positive statistics. `qkv_bias_state`: index 1 holds positive statistics. `out_bias_state`: index 1 holds positive statistics. `up_bias_state`: index 1 holds positive statistics.
All inputs are finite; a program needn't handle non-finite values.
Results may differ from the reference program's by a relative error of at most 0.033.
Values may be sent and summed in bfloat16 or wider, within the bound.
A program may use at most 320 MiB of HBM per device.

```python
import math
import jax
import jax.numpy as jnp
from jax import lax

D = 2048
HEADS = 32
HEAD_DIM = 64
ROT_DIM = 32
FF = 8192
TOK_DEV = 1024
MIN_SEQ = 64
MAXLEN = 1024
SEQS = 16
MPS = 4
DPS = 8
TOKENS = 8192
D_OWN = 256
HEAD_COLS = 512
QKV_COLS = 1536
FF_COLS = 2048


def draw_tokens(key, part):
    subkeys = jax.random.split(jax.random.fold_in(key, 3), 2)
    columns = jnp.arange(D, dtype=jnp.float32)
    rising = 0.4 * jnp.exp(columns / D * math.log(3.0))
    spread = jnp.exp(jax.random.uniform(subkeys[1], (D,), jnp.float32, 0.0, math.log(4.0)))
    values = jnp.clip(jax.random.normal(subkeys[0], (TOKENS, D), jnp.float32), -6.0, 6.0)
    return (values * rising[None, :] * spread[None, :]).astype(jnp.bfloat16)


def draw_seq_lengths(key, part):
    subkeys = jax.random.split(jax.random.fold_in(key, 5), 4)
    levels = max((MAXLEN // MIN_SEQ).bit_length(), 1)
    array_shape = (DPS, SEQS)
    power_one = jax.random.randint(subkeys[0], array_shape, 0, levels)
    power_two = jax.random.randint(subkeys[1], array_shape, 0, levels)
    powers = jnp.minimum(power_one, power_two).astype(jnp.int32)
    base_len = MIN_SEQ * jnp.left_shift(jnp.ones(array_shape, jnp.int32), powers)
    extension = jax.random.randint(subkeys[2], array_shape, 0, 1 << 24) % base_len
    lengths = jnp.minimum(base_len + extension, MAXLEN).astype(jnp.int32)
    chosen = jax.random.randint(subkeys[3], (), 0, DPS)
    row_index = jnp.arange(DPS)[:, None]
    col_index = jnp.arange(SEQS)[None, :]
    lengths = jnp.where((row_index == chosen) & (col_index == 0), MAXLEN, lengths).astype(jnp.int32)

    def placing(running, column):
        fits_in = running + column <= TOK_DEV
        taken = jnp.where(fits_in, column, 0).astype(jnp.int32)
        return (running + taken, taken)
    unused, kept = lax.scan(placing, jnp.zeros((DPS,), jnp.int32), lengths.T)
    return kept.T.astype(jnp.int32)


def positive_stat(key, array_shape, stat_scale):
    return stat_scale * jnp.exp(jax.random.uniform(key, array_shape, jnp.float32, math.log(0.5), math.log(8.0)))


def draw_ln_state(key, part):
    subkeys = jax.random.split(jax.random.fold_in(key, 7), 3)
    columns = jnp.arange(D, dtype=jnp.float32) / D
    low_end = 0.5
    high_end = 2.0
    rising = low_end * jnp.exp(columns * math.log(high_end / low_end))
    gains = rising * (1.0 + 0.1 * jnp.clip(jax.random.normal(subkeys[0], (D,), jnp.float32), -4.0, 4.0))
    shifts = 0.2 * jnp.clip(jax.random.normal(subkeys[1], (D,), jnp.float32), -4.0, 4.0)
    stats = positive_stat(subkeys[2], (2, D), TOKENS * 3.0)
    return jnp.stack([jnp.stack([gains, shifts]), stats])


def draw_qkv_bias_state(key, part):
    subkeys = jax.random.split(jax.random.fold_in(key, 9), 2)
    params = 0.3 * jnp.clip(jax.random.normal(subkeys[0], (3, D), jnp.float32), -4.0, 4.0)
    stats = positive_stat(subkeys[1], (3, D), TOKENS * 1.0)
    return jnp.stack([params, stats])


def draw_out_bias_state(key, part):
    subkeys = jax.random.split(jax.random.fold_in(key, 13), 2)
    params = 0.3 * jnp.clip(jax.random.normal(subkeys[0], (2, D), jnp.float32), -4.0, 4.0)
    stats = positive_stat(subkeys[1], (2, D), TOKENS * 1.0)
    return jnp.stack([params, stats])


def draw_up_bias_state(key, part):
    subkeys = jax.random.split(jax.random.fold_in(key, 17), 2)
    params = 0.3 * jnp.clip(jax.random.normal(subkeys[0], (FF,), jnp.float32), -4.0, 4.0)
    stats = positive_stat(subkeys[1], (FF,), TOKENS * 0.1)
    return jnp.stack([params, stats])


def statistic_pair(key, size, other, grad_square):
    subkeys = jax.random.split(key, 4)
    matrix_shape = (MPS, DPS, size, size)
    base_level = other * grad_square
    identity = jnp.eye(size, dtype=jnp.float32)
    stat_diag = positive_stat(subkeys[0], (MPS, DPS, size), base_level)
    noise_one = jax.random.normal(subkeys[1], matrix_shape, jnp.float32)
    sym_one = (noise_one + jnp.swapaxes(noise_one, -1, -2)) * (0.2 * base_level / math.sqrt(2.0 * size))
    statistic = sym_one * (1.0 - identity) + identity * stat_diag[..., None]
    root_level = base_level ** (-0.25)
    root_diag = root_level * jax.random.uniform(subkeys[2], (MPS, DPS, size), jnp.float32, 0.5, 1.0)
    noise_two = jax.random.normal(subkeys[3], matrix_shape, jnp.float32)
    sym_two = (noise_two + jnp.swapaxes(noise_two, -1, -2)) * (0.2 * root_level / math.sqrt(2.0 * size))
    inverse_root = sym_two * (1.0 - identity) + identity * root_diag[..., None]
    return jnp.stack([statistic, inverse_root])


def draw_qkv_left(key, part):
    return statistic_pair(jax.random.fold_in(key, 21), D_OWN, QKV_COLS, TOKENS * 1.0)


def draw_qkv_right(key, part):
    return statistic_pair(jax.random.fold_in(key, 22), QKV_COLS, D_OWN, TOKENS * 1.0)


def draw_out_left(key, part):
    return statistic_pair(jax.random.fold_in(key, 23), HEAD_COLS, D_OWN, TOKENS * 0.04)


def draw_out_right(key, part):
    return statistic_pair(jax.random.fold_in(key, 24), D_OWN, HEAD_COLS, TOKENS * 0.04)


def draw_up_left(key, part):
    return statistic_pair(jax.random.fold_in(key, 25), D_OWN, FF_COLS, TOKENS * 0.09)


def draw_up_right(key, part):
    return statistic_pair(jax.random.fold_in(key, 26), FF_COLS, D_OWN, TOKENS * 0.09)


def draw_down_left(key, part):
    return statistic_pair(jax.random.fold_in(key, 27), FF_COLS, D_OWN, TOKENS * 0.36)


def draw_down_right(key, part):
    return statistic_pair(jax.random.fold_in(key, 28), D_OWN, FF_COLS, TOKENS * 0.36)


def block_levels(stream_key, extent, shards, least, high):
    def one(axis_at, blocks):
        heights = jax.random.uniform(jax.random.fold_in(jax.random.fold_in(stream_key, 6), axis_at), (blocks,), jnp.float32, least / len(shards), high / len(shards))
        return jnp.repeat(jnp.exp(heights), extent[axis_at] // blocks).reshape((-1,) + (1,) * (len(extent) - axis_at - 1))

    factor_of = one(*shards[0])
    for cut in shards[1:]:
        factor_of = factor_of * one(*cut)
    return factor_of


def normal_values(rng, shape, width, limit, shards=(), kind=jnp.bfloat16):
    array = width * jax.random.normal(rng, shape, jnp.float32)
    if shards:
        array = array * block_levels(rng, shape, shards, -0.22, 0.18)
    return jnp.clip(array, -limit, limit).astype(kind)


def setup_inputs(seed: int = 0) -> dict:
    key_list = jax.random.split(jax.random.key(seed), 20)
    return {
        "tokens": draw_tokens(jax.random.fold_in(key_list[19], 71), 0),
        "cotangent": normal_values(key_list[1], (TOKENS, D), 1.0, 6.0, ((0, 8), (1, 4))),
        "seq_lengths": draw_seq_lengths(jax.random.fold_in(key_list[19], 71), 0),
        "w_qkv": normal_values(key_list[3], (D, 3, D), D ** -0.5, 0.125, ((0, 8), (2, 4)), jnp.float32),
        "qkv_bias_state": draw_qkv_bias_state(jax.random.fold_in(key_list[19], 71), 0),
        "w_out": normal_values(key_list[5], (D, D), (D // 16) ** -0.5, 0.5, ((0, 4), (1, 8)), jnp.float32),
        "out_bias_state": draw_out_bias_state(jax.random.fold_in(key_list[19], 71), 0),
        "w_up": normal_values(key_list[7], (D, FF), D ** -0.5, 0.125, ((0, 8), (1, 4)), jnp.float32),
        "up_bias_state": draw_up_bias_state(jax.random.fold_in(key_list[19], 71), 0),
        "w_down": normal_values(key_list[9], (FF, D), FF ** -0.5, 0.0625, ((0, 4), (1, 8)), jnp.float32),
        "ln_state": draw_ln_state(jax.random.fold_in(key_list[19], 71), 0),
        "qkv_left": draw_qkv_left(jax.random.fold_in(key_list[19], 71), 0),
        "qkv_right": draw_qkv_right(jax.random.fold_in(key_list[19], 71), 0),
        "out_left": draw_out_left(jax.random.fold_in(key_list[19], 71), 0),
        "out_right": draw_out_right(jax.random.fold_in(key_list[19], 71), 0),
        "up_left": draw_up_left(jax.random.fold_in(key_list[19], 71), 0),
        "up_right": draw_up_right(jax.random.fold_in(key_list[19], 71), 0),
        "down_left": draw_down_left(jax.random.fold_in(key_list[19], 71), 0),
        "down_right": draw_down_right(jax.random.fold_in(key_list[19], 71), 0),
    }


norm_eps = 1e-05
matrix_rate = 1.0
vector_rate = 0.4
masked_score = -1e+30
highest = lax.Precision.HIGHEST

@jax.custom_vjp
def low(v):
    return lax.optimization_barrier(v.astype(jnp.bfloat16)).astype(jnp.float32)

@jax.custom_vjp
def low_back(v):
    return v

def low_keep(v):
    return (low(v), None)

def low_pass(kept, grad):
    return (grad,)

def back_keep(v):
    return (v, None)

def back_low(kept, grad):
    return (low(grad),)
low.defvjp(low_keep, low_pass)
low_back.defvjp(back_keep, back_low)

def rounded(values):
    return values.astype(jnp.bfloat16).astype(jnp.float32)

def segment_layout(lengths, row_count):
    positions = jnp.arange(row_count, dtype=jnp.int32)
    seq_ends = jnp.cumsum(lengths).astype(jnp.int32)
    finished = seq_ends[None, :] <= positions[:, None]
    segment = lax.optimization_barrier(jnp.sum(finished.astype(jnp.int32), axis=1)).astype(jnp.int32)
    starting = lax.optimization_barrier(jnp.max(jnp.where(finished, seq_ends[None, :], 0), axis=1)).astype(jnp.int32)
    is_valid = positions < seq_ends[-1]
    segment = jnp.where(is_valid, segment, lengths.shape[0] + positions).astype(jnp.int32)
    offsets = (positions - starting).astype(jnp.float32)
    return (segment, offsets, is_valid.astype(jnp.float32))

def rope_tables(offsets):
    half_rot = ROT_DIM // 2
    freq_index = jnp.arange(half_rot, dtype=jnp.float32)
    inverse = jnp.exp(-(2.0 * freq_index / ROT_DIM) * math.log(10000.0))
    angles = offsets[:, None] * inverse[None, :]
    return (jnp.cos(angles)[:, None, :], jnp.sin(angles)[:, None, :])

def rotate(values, cosine, sine, direction):
    half_rot = ROT_DIM // 2
    first_half = values[..., :half_rot]
    second_half = values[..., half_rot:ROT_DIM]
    untouched = values[..., ROT_DIM:]
    new_first = first_half * cosine - direction * second_half * sine
    new_second = second_half * cosine + direction * first_half * sine
    return jnp.concatenate([new_first, new_second, untouched], axis=-1)

def block_forward(params, inputs, segment, offsets):
    qkv_weight, out_weight, up_weight, down_weight, qkv_bias, up_bias, norm_params, out_bias = params
    row_count = inputs.shape[0]
    row_mean = lax.optimization_barrier(jnp.mean(inputs, axis=-1, keepdims=True))
    row_var = lax.optimization_barrier(jnp.mean(inputs * inputs, axis=-1, keepdims=True)) - row_mean * row_mean
    normalized = (inputs - row_mean) * lax.rsqrt(row_var + norm_eps)
    normed = low(normalized * norm_params[0] + norm_params[1])
    projected = jnp.einsum('td,dcf->tcf', normed, qkv_weight, precision=highest) + qkv_bias[None]
    projected = low_back(projected).reshape(row_count, 3, HEADS, HEAD_DIM)
    cosine, sine = rope_tables(offsets)
    queries = low(rotate(projected[:, 0], cosine, sine, 1.0))
    key_rows = low(rotate(projected[:, 1], cosine, sine, 1.0))
    value_rows = low(projected[:, 2])
    positions = jnp.arange(row_count)
    allowed = (segment[:, None] == segment[None, :]) & (positions[None, :] <= positions[:, None])

    def one_head(operands):
        head_q, head_k, head_v = operands
        scores = low_back(jnp.dot(head_q, head_k.T, precision=highest) * HEAD_DIM ** (-0.5))
        scores = jnp.where(allowed, scores, masked_score)
        peak = lax.optimization_barrier(jnp.max(scores, axis=-1, keepdims=True))
        log_total = peak + jnp.log(lax.optimization_barrier(jnp.sum(jnp.exp(scores - peak), axis=-1, keepdims=True)))
        probability = jnp.exp(scores - log_total)
        return jnp.dot(low(probability), head_v, precision=highest)
    attended = lax.map(jax.checkpoint(one_head), (queries.transpose(1, 0, 2), key_rows.transpose(1, 0, 2), value_rows.transpose(1, 0, 2)))
    attended = attended.transpose(1, 0, 2).reshape(row_count, D)
    attended = low(low_back(attended))
    hidden = low_back(jnp.dot(normed, up_weight, precision=highest) + up_bias)
    activated = low(jax.nn.gelu(hidden, approximate=True))
    attn_branch = jnp.dot(attended, out_weight, precision=highest)
    mlp_branch = jnp.dot(activated, down_weight, precision=highest)
    return inputs + attn_branch + mlp_branch + out_bias[0] + out_bias[1]

def add_grads(running_total, block_grad):
    return running_total + block_grad

def shampoo(weight_blocks, grad_blocks, left, right):
    left_new = 0.5 * left[0] + 0.5 * jnp.einsum('mdij,mdkj->mdik', grad_blocks, grad_blocks, precision=highest)
    right_new = 0.5 * right[0] + 0.5 * jnp.einsum('mdji,mdjk->mdik', grad_blocks, grad_blocks, precision=highest)
    step_one = jnp.einsum('mdij,mdjk->mdik', left[1], grad_blocks, precision=highest)
    step_two = jnp.einsum('mdij,mdjk->mdik', step_one, right[1], precision=highest)
    return (weight_blocks - matrix_rate * step_two, left_new, right_new)

def vector_update(state, grad):
    stat_new = 0.5 * state[1] + 0.5 * grad * grad
    param_new = state[0] - vector_rate * grad * lax.rsqrt(stat_new)
    return (param_new, stat_new)

def reference(tokens, cotangent, seq_lengths, w_qkv, qkv_bias_state, w_out, out_bias_state, w_up, up_bias_state, w_down, ln_state, qkv_left, qkv_right, out_left, out_right, up_left, up_right, down_left, down_right):
    params = (rounded(w_qkv), rounded(w_out), rounded(w_up), rounded(w_down), rounded(qkv_bias_state[0]), rounded(up_bias_state[0]), rounded(ln_state[0]), rounded(out_bias_state[0]))
    inputs = tokens.astype(jnp.float32).reshape(DPS, TOK_DEV, D)
    upstream = cotangent.astype(jnp.float32).reshape(DPS, TOK_DEV, D)

    def per_block(running_grads, pieces):
        block_in, block_up, block_lengths = pieces
        segment, offsets, is_valid = segment_layout(block_lengths, TOK_DEV)

        def forward(weights, values):
            return block_forward(weights, values, segment, offsets)
        result, pullback = jax.vjp(forward, params, block_in)
        grad_params, grad_in = pullback(block_up * is_valid[:, None])
        running_grads = jax.tree.map(add_grads, running_grads, grad_params)
        return (running_grads, (result.astype(jnp.bfloat16), grad_in))
    start_grads = jax.tree.map(jnp.zeros_like, params)
    grads, (out_blocks, grad_blocks) = lax.scan(per_block, start_grads, (inputs, upstream, seq_lengths))
    output = out_blocks.reshape(TOKENS, D)
    input_grad = grad_blocks.reshape(TOKENS, D)
    grad_qkv, grad_out, grad_up, grad_down, grad_bqkv, grad_bup, grad_norm, grad_obias = grads
    qkv_blocks = w_qkv.reshape(DPS, D_OWN, 3, MPS, HEAD_COLS).transpose(3, 0, 1, 2, 4).reshape(MPS, DPS, D_OWN, QKV_COLS)
    qkv_gblocks = grad_qkv.reshape(DPS, D_OWN, 3, MPS, HEAD_COLS).transpose(3, 0, 1, 2, 4).reshape(MPS, DPS, D_OWN, QKV_COLS)
    qkv_new, qkv_left_new, qkv_right_new = shampoo(qkv_blocks, qkv_gblocks, qkv_left, qkv_right)
    new_w_qkv = qkv_new.reshape(MPS, DPS, D_OWN, 3, HEAD_COLS).transpose(1, 2, 3, 0, 4).reshape(D, 3, D)
    out_blocks_w = w_out.reshape(MPS, HEAD_COLS, DPS, D_OWN).transpose(0, 2, 1, 3)
    out_gblocks = grad_out.reshape(MPS, HEAD_COLS, DPS, D_OWN).transpose(0, 2, 1, 3)
    out_new, out_left_new, out_right_new = shampoo(out_blocks_w, out_gblocks, out_left, out_right)
    new_w_out = out_new.transpose(0, 2, 1, 3).reshape(D, D)
    up_blocks = w_up.reshape(DPS, D_OWN, MPS, FF_COLS).transpose(2, 0, 1, 3)
    up_gblocks = grad_up.reshape(DPS, D_OWN, MPS, FF_COLS).transpose(2, 0, 1, 3)
    up_new, up_left_new, up_right_new = shampoo(up_blocks, up_gblocks, up_left, up_right)
    new_w_up = up_new.transpose(1, 2, 0, 3).reshape(D, FF)
    down_blocks = w_down.reshape(MPS, FF_COLS, DPS, D_OWN).transpose(0, 2, 1, 3)
    down_gblocks = grad_down.reshape(MPS, FF_COLS, DPS, D_OWN).transpose(0, 2, 1, 3)
    down_new, down_left_new, down_right_new = shampoo(down_blocks, down_gblocks, down_left, down_right)
    new_w_down = down_new.transpose(0, 2, 1, 3).reshape(FF, D)
    qkv_params, qkv_stats = vector_update(qkv_bias_state, grad_bqkv)
    obias_params, obias_stats = vector_update(out_bias_state, grad_obias)
    norm_new_params, norm_new_stats = vector_update(ln_state, grad_norm)
    new_up_bias, new_up_stat = vector_update(up_bias_state, grad_bup)
    new_vector_params = jnp.concatenate([qkv_params, obias_params, norm_new_params], axis=0)
    new_vector_stats = jnp.concatenate([qkv_stats, obias_stats, norm_new_stats], axis=0)
    return (output, input_grad, new_w_qkv, new_w_out, new_w_up, new_w_down, new_vector_params, new_vector_stats, new_up_bias, new_up_stat, qkv_left_new, qkv_right_new, out_left_new, out_right_new, up_left_new, up_right_new, down_left_new, down_right_new)
```

```python
import functools
import math

import jax
import jax.numpy as jnp
from jax import lax
from jax.experimental import pallas as pl
from jax.experimental.pallas import tpu as pltpu
from jax.sharding import PartitionSpec as P

HEAD_DIM = 64
ROT_DIM = 32
LANES = 128
ROW_TILE = 256


norm_eps = 1e-05
matrix_rate = 1.0
vector_rate = 0.4
masked_score = -1e30


def segment_layout(lengths, row_count):
    positions = jnp.arange(row_count, dtype=jnp.int32)
    seq_ends = jnp.cumsum(lengths)
    finished = seq_ends[None, :] <= positions[:, None]
    segment = jnp.sum(finished.astype(jnp.int32), axis=1)
    starting = jnp.max(jnp.where(finished, seq_ends[None, :], 0), axis=1)
    is_valid = positions < seq_ends[-1]
    segment = jnp.where(is_valid, segment, lengths.shape[0] + positions)
    offsets = (positions - starting).astype(jnp.float32)
    return (segment, offsets, is_valid.astype(jnp.float32))


def rope_tables(offsets):
    half_rot = ROT_DIM // 2
    freq_index = jnp.arange(half_rot, dtype=jnp.float32)
    inverse = jnp.exp(-(2.0 * freq_index / ROT_DIM) * math.log(10000.0))
    angles = offsets[:, None] * inverse[None, :]
    return (jnp.cos(angles), jnp.sin(angles))


def gelu_pair(values):
    square = values * values
    inner = math.sqrt(2.0 / math.pi) * values * (1.0 + 0.044715 * square)
    bent = jnp.tanh(inner)
    half = 0.5 * (1.0 + bent)
    slope = half + 0.5 * values * (1.0 - bent * bent) * math.sqrt(2.0 / math.pi) * (
        1.0 + 3.0 * 0.044715 * square
    )
    return (values * half, slope)


def take(array, index, axis=0):
    return lax.dynamic_index_in_dim(array, index, axis, keepdims=False)


def mp_pairs(bit):
    return [(source, source ^ bit) for source in range(lax.axis_size("mp"))]


def mp_gather(share):
    if lax.axis_size("mp") != 4:
        return lax.all_gather(share, "mp", axis=1, tiled=True)
    place = lax.axis_index("mp")
    rows, width = share.shape
    half = rows // 2
    over_x = lax.ppermute(share, "mp", mp_pairs(1))
    over_y = lax.ppermute(share, "mp", mp_pairs(2))
    top = lax.ppermute(over_y[:half], "mp", mp_pairs(1))
    bottom = lax.ppermute(over_x[half:], "mp", mp_pairs(2))
    whole = jnp.zeros((rows, 4 * width), share.dtype)
    whole = lax.dynamic_update_slice(whole, share, (0, place * width))
    whole = lax.dynamic_update_slice(whole, over_x, (0, (place ^ 1) * width))
    whole = lax.dynamic_update_slice(whole, over_y, (0, (place ^ 2) * width))
    whole = lax.dynamic_update_slice(whole, top, (0, (place ^ 3) * width))
    return lax.dynamic_update_slice(whole, bottom, (half, (place ^ 3) * width))


def summed(*terms):
    total = terms[0].astype(jnp.float32)
    for term in terms[1:]:
        total = total + term.astype(jnp.float32)
    return total


def mp_scatter(partial):
    if lax.axis_size("mp") != 4:
        return lax.psum_scatter(partial, "mp", scatter_dimension=1, tiled=True).astype(jnp.float32)
    place = lax.axis_index("mp")
    rows = partial.shape[0]
    width = partial.shape[1] // 4
    half = rows // 2

    def part(start, bits):
        return lax.dynamic_slice(partial, (start, (place ^ bits) * width), (half, width))

    top_far = lax.ppermute(part(0, 3), "mp", mp_pairs(1))
    bottom_far = lax.ppermute(part(half, 3), "mp", mp_pairs(2))
    top_near = lax.ppermute(part(0, 1), "mp", mp_pairs(1))
    bottom_near = lax.ppermute(part(half, 2), "mp", mp_pairs(2))
    top_send = summed(part(0, 2), top_far).astype(jnp.bfloat16)
    bottom_send = summed(part(half, 1), bottom_far).astype(jnp.bfloat16)
    top_last = lax.ppermute(top_send, "mp", mp_pairs(2))
    bottom_last = lax.ppermute(bottom_send, "mp", mp_pairs(1))
    top = summed(part(0, 0), top_near, top_last)
    bottom = summed(part(half, 0), bottom_near, bottom_last)
    return jnp.concatenate([top, bottom], axis=0)


def parity_columns(rows, parity):
    size = lax.axis_size("dp")
    width = rows.shape[1] // size
    pieces = [
        lax.dynamic_slice_in_dim(rows, (2 * chip + parity) * width, width, 1)
        for chip in range(size // 2)
    ]
    return jnp.concatenate(pieces, axis=1)


def over_rows(left, right):
    return lax.dot_general(left, right, (((0,), (0,)), ((), ())), preferred_element_type=jnp.float32)


def tie(value, *others):
    return lax.optimization_barrier((value,) + others)[0]


class OwnerSum:
    def __init__(self, far_product):
        self.size = lax.axis_size("dp")
        self.count = self.size // 2
        self.spot = lax.axis_index("dp") // 2
        self.step = 0
        self.sent = 0
        self.rising = None
        self.falling = None
        self.from_sibling = lax.ppermute(
            far_product.astype(jnp.bfloat16), "dp", [(at, at ^ 1) for at in range(self.size)]
        )

    def add_near(self, near_product):
        blocks = summed(near_product, self.from_sibling).astype(jnp.bfloat16)
        self.blocks = blocks.reshape(self.count, -1, blocks.shape[1])
        return self.ready()

    def ready(self):
        self.step += 1
        last = self.count - 1
        up_block = take(self.blocks, jnp.clip(self.count + self.spot - self.step, 0, last))
        down_block = take(self.blocks, jnp.clip(self.spot - self.count + self.step, 0, last))
        if self.rising is not None:
            up_block = summed(up_block, self.rising).astype(jnp.bfloat16)
            down_block = summed(down_block, self.falling).astype(jnp.bfloat16)
        self.sends = (up_block, down_block)
        return self.sends

    def send(self):
        up_pairs = [
            (2 * chip + core, 2 * chip + 2 + core)
            for chip in range(self.step)
            for core in range(2)
        ]
        down_pairs = [
            (2 * chip + core, 2 * chip - 2 + core)
            for chip in range(self.count - self.step, self.count)
            for core in range(2)
        ]
        self.sent += 1
        self.rising = lax.ppermute(self.sends[0], "dp", up_pairs)
        self.falling = lax.ppermute(self.sends[1], "dp", down_pairs)

    def advance(self):
        self.send()
        if self.step < self.count - 1:
            return self.ready()
        return (self.rising, self.falling)

    def rest(self):
        while self.sent < self.count - 1:
            self.advance()
        return self

    def total(self):
        return summed(take(self.blocks, self.spot), self.rising, self.falling)


def exchange_kernel(axes, count, same, in_ref, out_ref, send_sems, recv_sems):
    sizes = [lax.axis_size(axis) for axis in axes]
    place = lax.axis_index(axes[0])
    for axis, size in zip(axes[1:], sizes[1:]):
        place = place * size + lax.axis_index(axis)

    def device(peer):
        if len(axes) == 1:
            return {axes[0]: peer}
        return {axes[0]: peer // sizes[1], axes[1]: lax.rem(peer, sizes[1])}

    barrier = pltpu.get_barrier_semaphore()

    def greet(step, carry):
        peer = lax.rem(place + step, count)
        pl.semaphore_signal(
            barrier, inc=1, device_id=device(peer), device_id_type=pl.DeviceIdType.MESH
        )
        return carry

    lax.fori_loop(1, count, greet, 0)
    pl.semaphore_wait(barrier, count - 1)

    def copy_to(step):
        peer = lax.rem(place + step, count)
        source = in_ref.at[0] if same else in_ref.at[peer]
        return pltpu.make_async_remote_copy(
            src_ref=source,
            dst_ref=out_ref.at[place],
            send_sem=send_sems.at[step],
            recv_sem=recv_sems.at[step],
            device_id=device(peer),
            device_id_type=pl.DeviceIdType.MESH,
        )

    def begin(step, carry):
        copy_to(step).start()
        return carry

    def finish(step, carry):
        copy_to(step).wait()
        return carry

    lax.fori_loop(1, count, begin, 0)
    out_ref[place] = in_ref[0] if same else in_ref[place]
    lax.fori_loop(1, count, finish, 0)


def exchange(values, axes, collective_id, same):
    count = 1
    for axis in axes:
        count *= lax.axis_size(axis)
    return pl.pallas_call(
        functools.partial(exchange_kernel, axes, count, same),
        out_shape=jax.ShapeDtypeStruct((count,) + values.shape[1:], values.dtype),
        in_specs=[pl.BlockSpec(memory_space=pltpu.VMEM)],
        out_specs=pl.BlockSpec(memory_space=pltpu.VMEM),
        scratch_shapes=[pltpu.SemaphoreType.DMA((count,)), pltpu.SemaphoreType.DMA((count,))],
        compiler_params=pltpu.CompilerParams(collective_id=collective_id, has_side_effects=True),
        name="exchange",
    )(values)


def contract(left, right, left_axis, right_axis):
    return lax.dot_general(
        left, right, (((left_axis,), (right_axis,)), ((), ())), preferred_element_type=jnp.float32
    )


def attention_kernel(
    head_cols,
    q_ref,
    k_ref,
    v_ref,
    go_ref,
    seg_col_ref,
    seg_row_ref,
    keep_ref,
    ahead_ref,
    behind_ref,
    or_ref,
    grad_ref,
    bias_ref,
    q_low,
    k_low,
    v_low,
    dq_acc,
    dk_acc,
    dv_acc,
):
    rows = q_ref.shape[0]
    tiles = rows // ROW_TILE
    pair = pl.program_id(0)
    scale = HEAD_DIM ** (-0.5)

    @pl.when(pair == 0)
    def _():
        for tile in range(tiles):
            here = pl.ds(tile * ROW_TILE, ROW_TILE)
            shape = (ROW_TILE, rows)
            row_ids = lax.broadcasted_iota(jnp.int32, shape, 0) + tile * ROW_TILE
            key_ids = lax.broadcasted_iota(jnp.int32, shape, 1)
            allowed = (seg_col_ref[here, :] == seg_row_ref[...]) & (key_ids <= row_ids)
            bias_ref[here, :] = jnp.where(allowed, 0.0, masked_score)

    def turned(values, here, direction):
        ahead = pltpu.roll(values, LANES - ROT_DIM // 2, 1)
        behind = pltpu.roll(values, ROT_DIM // 2, 1)
        return values * keep_ref[here, :] + direction * (
            ahead * ahead_ref[here, :] + behind * behind_ref[here, :]
        )

    for tile in range(tiles):
        here = pl.ds(tile * ROW_TILE, ROW_TILE)
        q_low[here, :] = (turned(q_ref[here, :], here, 1.0).astype(jnp.bfloat16)) * scale
        k_low[here, :] = turned(k_ref[here, :], here, 1.0).astype(jnp.bfloat16)
        v_low[here, :] = v_ref[here, :].astype(jnp.bfloat16)
    dk_acc[...] = jnp.zeros_like(dk_acc)
    dv_acc[...] = jnp.zeros_like(dv_acc)

    lane = lax.broadcasted_iota(jnp.int32, (ROW_TILE, LANES), 1)
    for tile in range(tiles):
        here = pl.ds(tile * ROW_TILE, ROW_TILE)
        reach = (tile + 1) * ROW_TILE
        keys = pl.ds(0, reach)
        outs = []
        query_grads = []
        for head in range(LANES // HEAD_DIM):
            mine = (lane >= head * HEAD_DIM) & (lane < (head + 1) * HEAD_DIM)
            none = jnp.zeros((ROW_TILE, LANES), jnp.bfloat16)
            query = jnp.where(mine, q_low[here, :], none)
            grad_out = jnp.where(mine, go_ref[here, :], none)
            scores = contract(query, k_low[keys, :], 1, 1) + bias_ref[here, keys]
            peak = jnp.max(scores, axis=1, keepdims=True)
            weights = jnp.exp(scores - peak)
            share = 1.0 / jnp.sum(weights, axis=1, keepdims=True)
            probs = weights * share
            probs_low = probs.astype(jnp.bfloat16)
            outs.append(contract(probs_low, v_low[keys, :], 1, 0))
            grad_probs = contract(grad_out, v_low[keys, :], 1, 1)
            delta = jnp.sum(probs * grad_probs, axis=1, keepdims=True)
            grad_scores = (probs * (grad_probs - delta)).astype(jnp.bfloat16)
            query_grads.append(contract(grad_scores, k_low[keys, :], 1, 0))
            dk_acc[keys, :] += contract(grad_scores, query, 0, 0)
            dv_acc[keys, :] += contract(probs_low, grad_out, 0, 0)
        first = lane < HEAD_DIM
        or_ref[here, :] = jnp.where(first, outs[0], outs[1]).astype(jnp.bfloat16)
        dq_acc[here, :] = jnp.where(first, query_grads[0], query_grads[1])
    column = pl.multiple_of(pair * LANES, LANES)
    for tile in range(tiles):
        here = pl.ds(tile * ROW_TILE, ROW_TILE)
        query_grad = turned(dq_acc[here, :], here, -1.0) * scale
        grad_ref[here, pl.ds(column, LANES)] = query_grad.astype(jnp.bfloat16)
        key_grad = turned(dk_acc[here, :], here, -1.0)
        grad_ref[here, pl.ds(head_cols + column, LANES)] = key_grad.astype(jnp.bfloat16)
        grad_ref[here, pl.ds(2 * head_cols + column, LANES)] = dv_acc[here, :].astype(jnp.bfloat16)


def attention(projected, grad_attended, segment, cosine, sine):
    rows, columns = projected.shape
    head_cols = columns // 3
    pairs = head_cols // LANES
    still = jnp.ones((rows, HEAD_DIM - ROT_DIM), jnp.float32)
    zero = jnp.zeros((rows, ROT_DIM // 2), jnp.float32)
    repeat = (1, LANES // HEAD_DIM)
    keep = jnp.tile(jnp.concatenate([cosine, cosine, still], axis=1), repeat)
    ahead = jnp.tile(jnp.concatenate([-sine, zero, 0.0 * still], axis=1), repeat)
    behind = jnp.tile(jnp.concatenate([zero, sine, 0.0 * still], axis=1), repeat)
    whole = lambda pair: (0, 0)
    table = pl.BlockSpec((rows, LANES), whole)
    flops = 12 * rows * rows * LANES * 2 * pairs
    return pl.pallas_call(
        functools.partial(attention_kernel, head_cols),
        grid=(pairs,),
        in_specs=[
            pl.BlockSpec((rows, LANES), lambda pair: (0, pair)),
            pl.BlockSpec((rows, LANES), lambda pair: (0, pairs + pair)),
            pl.BlockSpec((rows, LANES), lambda pair: (0, 2 * pairs + pair)),
            pl.BlockSpec((rows, LANES), lambda pair: (0, pair)),
            pl.BlockSpec((rows, 1), whole),
            pl.BlockSpec((1, rows), whole),
            table,
            table,
            table,
        ],
        out_specs=[
            pl.BlockSpec((rows, LANES), lambda pair: (0, pair)),
            pl.BlockSpec((rows, columns), whole),
        ],
        out_shape=[
            jax.ShapeDtypeStruct((rows, head_cols), jnp.bfloat16),
            jax.ShapeDtypeStruct((rows, columns), jnp.bfloat16),
        ],
        scratch_shapes=[
            pltpu.VMEM((rows, rows), jnp.float32),
            pltpu.VMEM((rows, LANES), jnp.bfloat16),
            pltpu.VMEM((rows, LANES), jnp.bfloat16),
            pltpu.VMEM((rows, LANES), jnp.bfloat16),
            pltpu.VMEM((rows, LANES), jnp.float32),
            pltpu.VMEM((rows, LANES), jnp.float32),
            pltpu.VMEM((rows, LANES), jnp.float32),
        ],
        compiler_params=pltpu.CompilerParams(vmem_limit_bytes=40 * 1024 * 1024),
        cost_estimate=pl.CostEstimate(
            flops=flops, bytes_accessed=rows * columns * 8, transcendentals=rows * rows * pairs
        ),
        name="attention",
    )(
        projected,
        projected,
        projected,
        grad_attended,
        segment[:, None],
        segment[None, :],
        keep,
        ahead,
        behind,
    )


def dot_f32(left, right, left_axis, right_axis):
    return lax.dot_general(
        left.astype(jnp.bfloat16),
        right.astype(jnp.bfloat16),
        (((left_axis,), (right_axis,)), ((), ())),
        preferred_element_type=jnp.float32,
    )


def shampoo(weight_block, grad_block, left, right):
    left_new = 0.5 * left[0, 0, 0] + 0.5 * dot_f32(grad_block, grad_block, 1, 1)
    right_new = 0.5 * right[0, 0, 0] + 0.5 * dot_f32(grad_block, grad_block, 0, 0)
    step_block = dot_f32(dot_f32(left[1, 0, 0], grad_block, 1, 0), right[1, 0, 0], 1, 0)
    return (weight_block - matrix_rate * step_block, left_new[None, None], right_new[None, None])


def shampoo_turned(weight_block, turned_grad, left, right):
    left_new = 0.5 * left[0, 0, 0] + 0.5 * dot_f32(turned_grad, turned_grad, 0, 0)
    right_new = 0.5 * right[0, 0, 0] + 0.5 * dot_f32(turned_grad, turned_grad, 1, 1)
    step_block = dot_f32(dot_f32(left[1, 0, 0], turned_grad, 1, 1), right[1, 0, 0], 1, 0)
    return (weight_block - matrix_rate * step_block, left_new[None, None], right_new[None, None])


def vector_update(state, grad):
    stat_new = 0.5 * state[1] + 0.5 * grad * grad
    param_new = state[0] - vector_rate * grad * lax.rsqrt(stat_new)
    return (param_new, stat_new)


def local(
    tokens,
    cotangent,
    seq_lengths,
    w_qkv,
    qkv_bias_state,
    w_out,
    out_bias_state,
    w_up,
    up_bias_state,
    w_down,
    ln_state,
    qkv_left,
    qkv_right,
    out_left,
    out_right,
    up_left,
    up_right,
    down_left,
    down_right,
):
    row_count, share_width = tokens.shape
    mp_size = lax.axis_size("mp")
    dp_size = lax.axis_size("dp")
    model_width = share_width * mp_size
    own_width = w_qkv.shape[2]
    mp_place = lax.axis_index("mp")
    core = lax.axis_index("dp") % 2

    flat_master = jnp.concatenate([w_qkv[:, kind] for kind in range(3)], axis=1)
    block_qkvo = jnp.concatenate([flat_master, w_out.T], axis=1).astype(jnp.bfloat16)
    full_qkvo = lax.all_gather(block_qkvo, "dp", axis=0, tiled=True)
    full_up = lax.all_gather(w_up.astype(jnp.bfloat16), "dp", axis=0, tiled=True)
    turned_down = lax.all_gather(w_down.T.astype(jnp.bfloat16), "dp", axis=0, tiled=True)
    full_qkv = full_qkvo[:, : 3 * own_width]
    turned_out = full_qkvo[:, 3 * own_width :]

    piece = ln_state.shape[2]
    small = jnp.concatenate(
        [
            ln_state[0].reshape(-1),
            qkv_bias_state[0].reshape(-1),
            out_bias_state[0].reshape(-1),
            up_bias_state[0].reshape(-1),
        ]
    )
    small = small.astype(jnp.bfloat16).astype(jnp.float32)
    filled = small.shape[0]
    small = jnp.pad(small, (0, -filled % 1024)).reshape(1, 8, -1)
    spread = exchange(small, ("mp", "dp"), 1, True).reshape(mp_size * dp_size, -1)[:, :filled]
    x_full = mp_gather(tie(tokens, spread))
    upstream = mp_gather(tie(cotangent, spread))
    norm_all = spread[:, : 2 * piece].reshape(-1, 2, piece).transpose(1, 0, 2).reshape(2, -1)
    here = take(spread.reshape(mp_size, dp_size, -1), mp_place)
    bias_qkv = here[:, 2 * piece : 5 * piece].reshape(dp_size, 3, piece)
    bias_qkv = bias_qkv.transpose(1, 0, 2).reshape(-1)
    bias_out = here[:, 5 * piece : 7 * piece].reshape(dp_size, 2, piece)
    bias_out = bias_out.transpose(1, 0, 2).reshape(2, -1)
    bias_up = here[:, 7 * piece :].reshape(-1)

    segment, offsets, is_valid = segment_layout(seq_lengths[0], row_count)
    cosine, sine = rope_tables(offsets)

    inputs = x_full.astype(jnp.float32)
    row_mean = jnp.mean(inputs, axis=1, keepdims=True)
    row_var = jnp.mean(inputs * inputs, axis=1, keepdims=True) - row_mean * row_mean
    inv_std = lax.rsqrt(row_var + norm_eps)
    normed = ((inputs - row_mean) * inv_std * norm_all[0] + norm_all[1]).astype(jnp.bfloat16)
    grad_rows = (upstream.astype(jnp.float32) * is_valid[:, None]).astype(jnp.bfloat16)
    gy_near, gy_far = (parity_columns(grad_rows, core), parity_columns(grad_rows, 1 - core))
    xn_near, xn_far = (parity_columns(normed, core), parity_columns(normed, 1 - core))

    projected = jnp.dot(normed, full_qkv, preferred_element_type=jnp.float32) + bias_qkv
    grad_attended = jnp.dot(grad_rows, turned_out, preferred_element_type=jnp.float32)
    attended, grad_projected = attention(
        projected, grad_attended.astype(jnp.bfloat16), segment, cosine, sine
    )
    sum_qkvo = OwnerSum(
        jnp.concatenate([over_rows(xn_far, grad_projected), over_rows(gy_far, attended)], axis=1)
    )
    sends = sum_qkvo.add_near(
        jnp.concatenate([over_rows(xn_near, grad_projected), over_rows(gy_near, attended)], axis=1)
    )

    normed_up = tie(normed, *sends)
    hidden = jnp.dot(normed_up, full_up, preferred_element_type=jnp.float32) + bias_up
    activated, slope = gelu_pair(hidden)
    activated = activated.astype(jnp.bfloat16)
    slope = slope.astype(jnp.bfloat16)
    sends = sum_qkvo.advance()
    sum_down = OwnerSum(over_rows(gy_far, activated))
    gy_near = tie(gy_near, *sends)
    sends = sum_down.add_near(over_rows(gy_near, activated))
    more = sum_qkvo.advance()
    grad_rows_down = tie(grad_rows, *sends, *more)

    grad_act = jnp.dot(grad_rows_down, turned_down, preferred_element_type=jnp.float32)
    grad_hidden = (grad_act * slope.astype(jnp.float32)).astype(jnp.bfloat16)
    sends = sum_down.advance()
    xn_far, xn_near = lax.optimization_barrier((xn_far, xn_near) + tuple(sends))[:2]
    sum_up = OwnerSum(over_rows(xn_far, grad_hidden))
    sends_up = sum_up.add_near(over_rows(xn_near, grad_hidden))
    attended_late = tie(attended, *sends_up)

    partial_sum = contract(attended_late, turned_out, 1, 1) + contract(activated, turned_down, 1, 1)
    branches = mp_scatter(partial_sum.astype(jnp.bfloat16))
    grad_projected_late = tie(grad_projected, partial_sum)
    grad_normed_part = contract(grad_projected_late, full_qkv, 1, 1) + contract(grad_hidden, full_up, 1, 1)
    gained_part = grad_normed_part * norm_all[0]
    row_terms = jnp.stack(
        [
            jnp.sum(gained_part, axis=1),
            jnp.sum(gained_part * ((inputs - row_mean) * inv_std), axis=1),
        ]
    )
    row_terms = jnp.sum(exchange(row_terms.reshape(1, 16, -1), ("mp",), 2, True), axis=0)
    row_terms = row_terms.reshape(2, -1)
    grad_normed = mp_scatter(grad_normed_part.astype(jnp.bfloat16))

    own_inputs = tokens.astype(jnp.float32)
    output = (own_inputs + branches + bias_out[0] + bias_out[1]).astype(jnp.bfloat16)

    normalized = (own_inputs - row_mean) * inv_std
    norm_here = lax.dynamic_slice_in_dim(norm_all, mp_place * share_width, share_width, 1)
    gained = grad_normed * norm_here[0]
    local_grad = cotangent.astype(jnp.float32) * is_valid[:, None]
    input_grad = local_grad + inv_std * (
        gained
        - row_terms[0][:, None] / model_width
        - normalized * row_terms[1][:, None] / model_width
    )

    def owner_rows(values, count):
        return values.reshape(count, dp_size, -1).transpose(1, 0, 2).reshape(dp_size, -1)

    vector_grads = jnp.concatenate(
        [
            owner_rows(jnp.sum(grad_normed * normalized, axis=0), 1),
            owner_rows(jnp.sum(grad_normed, axis=0), 1),
            owner_rows(jnp.sum(grad_projected.astype(jnp.float32), axis=0), 3),
            owner_rows(jnp.sum(local_grad, axis=0), 1),
            owner_rows(jnp.sum(grad_hidden.astype(jnp.float32), axis=0), 1),
        ],
        axis=1,
    )
    width = vector_grads.shape[1]
    vector_grads = jnp.pad(vector_grads, ((0, 0), (0, -width % 1024))).reshape(dp_size, 8, -1)
    vector_sums = jnp.sum(exchange(vector_grads, ("dp",), 3, False), axis=0).reshape(-1)[:width]
    owned_norm = vector_sums[: 2 * piece].reshape(2, piece)
    owned_bqkv = vector_sums[2 * piece : 5 * piece].reshape(3, piece)
    bias_total = vector_sums[5 * piece : 6 * piece]
    owned_obias = jnp.stack([bias_total, bias_total])
    owned_bup = vector_sums[6 * piece :]

    owned_qkvo = sum_qkvo.rest().total()
    owned_down = sum_down.rest().total()
    owned_up = sum_up.rest().total()
    owned_qkv = owned_qkvo[:, : 3 * own_width]
    owned_out = owned_qkvo[:, 3 * own_width :]
    new_w_down, down_left_new, down_right_new = shampoo_turned(
        w_down, owned_down, down_left, down_right
    )
    new_w_out, out_left_new, out_right_new = shampoo_turned(w_out, owned_out, out_left, out_right)
    new_qkv_block, qkv_left_new, qkv_right_new = shampoo(
        flat_master, owned_qkv, qkv_left, qkv_right
    )
    new_w_qkv = jnp.stack(
        [new_qkv_block[:, kind * own_width : (kind + 1) * own_width] for kind in range(3)], axis=1
    )
    new_w_up, up_left_new, up_right_new = shampoo(w_up, owned_up, up_left, up_right)
    qkv_params, qkv_stats = vector_update(qkv_bias_state, owned_bqkv)
    obias_params, obias_stats = vector_update(out_bias_state, owned_obias)
    norm_new_params, norm_new_stats = vector_update(ln_state, owned_norm)
    new_up_bias, new_up_stat = vector_update(up_bias_state, owned_bup)
    new_vector_params = jnp.concatenate([qkv_params, obias_params, norm_new_params], axis=0)
    new_vector_stats = jnp.concatenate([qkv_stats, obias_stats, norm_new_stats], axis=0)
    return (
        output,
        input_grad,
        new_w_qkv,
        new_w_out,
        new_w_up,
        new_w_down,
        new_vector_params,
        new_vector_stats,
        new_up_bias,
        new_up_stat,
        qkv_left_new,
        qkv_right_new,
        out_left_new,
        out_right_new,
        up_left_new,
        up_right_new,
        down_left_new,
        down_right_new,
    )


def solution(mesh):
    return jax.shard_map(
        local,
        mesh=mesh,
        in_specs=(
            P("dp", "mp"),
            P("dp", "mp"),
            P("dp", None),
            P("dp", None, "mp"),
            P(None, None, ("mp", "dp")),
            P("mp", "dp"),
            P(None, None, ("mp", "dp")),
            P("dp", "mp"),
            P(None, ("mp", "dp")),
            P("mp", "dp"),
            P(None, None, ("mp", "dp")),
            P(None, "mp", "dp", None, None),
            P(None, "mp", "dp", None, None),
            P(None, "mp", "dp", None, None),
            P(None, "mp", "dp", None, None),
            P(None, "mp", "dp", None, None),
            P(None, "mp", "dp", None, None),
            P(None, "mp", "dp", None, None),
            P(None, "mp", "dp", None, None),
        ),
        out_specs=(
            P("dp", "mp"),
            P("dp", "mp"),
            P("dp", None, "mp"),
            P("mp", "dp"),
            P("dp", "mp"),
            P("mp", "dp"),
            P(None, ("mp", "dp")),
            P(None, ("mp", "dp")),
            P(("mp", "dp")),
            P(("mp", "dp")),
            P("mp", "dp", None, None),
            P("mp", "dp", None, None),
            P("mp", "dp", None, None),
            P("mp", "dp", None, None),
            P("mp", "dp", None, None),
            P("mp", "dp", None, None),
            P("mp", "dp", None, None),
            P("mp", "dp", None, None),
        ),
        check_vma=False,
    )
```

```python
import functools
import math

import jax
import jax.numpy as jnp
from jax import lax
from jax.experimental import pallas as pl
from jax.experimental.pallas import tpu as pltpu
from jax.sharding import PartitionSpec as P

HEAD_DIM = 64
ROT_DIM = 32
LANES = 128
ROW_TILE = 256


norm_eps = 1e-05
matrix_rate = 1.0
vector_rate = 0.4
masked_score = -1e30


def segment_layout(lengths, row_count):
    positions = jnp.arange(row_count, dtype=jnp.int32)
    seq_ends = jnp.cumsum(lengths)
    finished = seq_ends[None, :] <= positions[:, None]
    segment = jnp.sum(finished.astype(jnp.int32), axis=1)
    starting = jnp.max(jnp.where(finished, seq_ends[None, :], 0), axis=1)
    is_valid = positions < seq_ends[-1]
    segment = jnp.where(is_valid, segment, lengths.shape[0] + positions)
    offsets = (positions - starting).astype(jnp.float32)
    return (segment, offsets, is_valid.astype(jnp.float32))


def rope_tables(offsets):
    half_rot = ROT_DIM // 2
    freq_index = jnp.arange(half_rot, dtype=jnp.float32)
    inverse = jnp.exp(-(2.0 * freq_index / ROT_DIM) * math.log(10000.0))
    angles = offsets[:, None] * inverse[None, :]
    return (jnp.cos(angles), jnp.sin(angles))


def gelu_pair(values):
    square = values * values
    inner = math.sqrt(2.0 / math.pi) * values * (1.0 + 0.044715 * square)
    bent = jnp.tanh(inner)
    half = 0.5 * (1.0 + bent)
    slope = half + 0.5 * values * (1.0 - bent * bent) * math.sqrt(2.0 / math.pi) * (
        1.0 + 3.0 * 0.044715 * square
    )
    return (values * half, slope)


def take(array, index, axis=0):
    return lax.dynamic_index_in_dim(array, index, axis, keepdims=False)


def summed(*terms):
    total = terms[0].astype(jnp.float32)
    for term in terms[1:]:
        total = total + term.astype(jnp.float32)
    return total


def exchange_kernel(axes, count, same, in_ref, out_ref, send_sems, recv_sems):
    sizes = [lax.axis_size(axis) for axis in axes]
    place = lax.axis_index(axes[0])
    for axis, size in zip(axes[1:], sizes[1:]):
        place = place * size + lax.axis_index(axis)

    def device(peer):
        if len(axes) == 1:
            return {axes[0]: peer}
        return {axes[0]: peer // sizes[1], axes[1]: lax.rem(peer, sizes[1])}

    barrier = pltpu.get_barrier_semaphore()

    def greet(step, carry):
        peer = lax.rem(place + step, count)
        pl.semaphore_signal(
            barrier, inc=1, device_id=device(peer), device_id_type=pl.DeviceIdType.MESH
        )
        return carry

    lax.fori_loop(1, count, greet, 0)
    pl.semaphore_wait(barrier, count - 1)

    def copy_to(step):
        peer = lax.rem(place + step, count)
        source = in_ref.at[0] if same else in_ref.at[peer]
        return pltpu.make_async_remote_copy(
            src_ref=source,
            dst_ref=out_ref.at[place],
            send_sem=send_sems.at[step],
            recv_sem=recv_sems.at[step],
            device_id=device(peer),
            device_id_type=pl.DeviceIdType.MESH,
        )

    def begin(step, carry):
        copy_to(step).start()
        return carry

    def finish(step, carry):
        copy_to(step).wait()
        return carry

    lax.fori_loop(1, count, begin, 0)
    out_ref[place] = in_ref[0] if same else in_ref[place]
    lax.fori_loop(1, count, finish, 0)


def exchange(values, axes, collective_id, same):
    count = 1
    for axis in axes:
        count *= lax.axis_size(axis)
    return pl.pallas_call(
        functools.partial(exchange_kernel, axes, count, same),
        out_shape=jax.ShapeDtypeStruct((count,) + values.shape[1:], values.dtype),
        in_specs=[pl.BlockSpec(memory_space=pltpu.VMEM)],
        out_specs=pl.BlockSpec(memory_space=pltpu.VMEM),
        scratch_shapes=[pltpu.SemaphoreType.DMA((count,)), pltpu.SemaphoreType.DMA((count,))],
        compiler_params=pltpu.CompilerParams(collective_id=collective_id, has_side_effects=True),
        name="exchange",
    )(values)


def contract(left, right, left_axis, right_axis):
    return lax.dot_general(
        left, right, (((left_axis,), (right_axis,)), ((), ())), preferred_element_type=jnp.float32
    )


MESH_ID = pl.DeviceIdType.MESH


def remote(source, target, send_sem, recv_sem, axis, peer):
    return pltpu.make_async_remote_copy(
        src_ref=source,
        dst_ref=target,
        send_sem=send_sem,
        recv_sem=recv_sem,
        device_id={axis: peer},
        device_id_type=MESH_ID,
    )


def greet_line():
    size = lax.axis_size("dp")
    place = lax.axis_index("dp")
    barrier = pltpu.get_barrier_semaphore()
    core = lax.rem(place, 2)
    peers = [place + 1 - 2 * core, lax.rem(place + 2, size), lax.rem(place + size - 2, size)]
    for peer in peers:
        pl.semaphore_signal(barrier, inc=1, device_id={"dp": peer}, device_id_type=MESH_ID)
    return (barrier, len(peers))


class LineGather:
    def __init__(self, own, full, send, recv):
        self.count = lax.axis_size("dp") // 2
        self.place = lax.axis_index("dp")
        self.spot = self.place // 2
        self.core = lax.rem(self.place, 2)
        self.own, self.full, self.send, self.recv = own, full, send, recv
        self.rows = own.shape[0]

    def block(self, chip, core):
        start = pl.multiple_of((2 * chip + core) * self.rows, self.rows)
        return self.full.at[pl.ds(start, self.rows), :]

    def copy(self, kind, step, chip, peer, from_own=False):
        block = self.block(chip, self.core)
        source = self.own if from_own else block
        return remote(
            source, block, self.send.at[kind, step], self.recv.at[kind, step], "dp", peer
        )

    def rise(self, step):
        return self.copy(0, step, self.spot - step + 1, self.place + 2, step == 1)

    def fall(self, step):
        return self.copy(1, step, self.spot + step - 1, self.place - 2, step == 1)

    def show(self, kind, step):
        chip = self.spot - step if kind == 2 else self.spot + step
        return self.copy(kind, step, chip, self.place + 1 - 2 * self.core, step == 0)

    def keep(self):
        return pltpu.make_async_copy(
            self.own, self.block(self.spot, self.core), self.send.at[3, 0]
        )

    def start(self):
        pl.when(self.spot + 1 < self.count)(lambda: self.rise(1).start())
        pl.when(self.spot > 0)(lambda: self.fall(1).start())
        self.show(2, 0).start()
        self.keep().start()

    def advance(self, step):
        @pl.when(self.spot >= step)
        def _():
            self.rise(step).wait_recv()
            pl.when(self.spot + 1 < self.count)(lambda: self.rise(step + 1).start())
            self.show(2, step).start()

        @pl.when(self.spot + step < self.count)
        def _():
            self.fall(step).wait_recv()
            pl.when(self.spot > 0)(lambda: self.fall(step + 1).start())
            self.show(3, step).start()

    def finish(self):
        self.keep().wait()
        self.show(2, 0).wait()
        for step in range(1, self.count):
            rises = (self.spot + 1 < self.count) & (self.spot >= step - 1)
            falls = (self.spot > 0) & (self.spot + step - 1 < self.count)
            pl.when(rises)(lambda step=step: self.rise(step).wait_send())
            pl.when(falls)(lambda step=step: self.fall(step).wait_send())
            pl.when(self.spot >= step)(lambda step=step: self.show(2, step).wait())
            pl.when(self.spot + step < self.count)(lambda step=step: self.show(3, step).wait())


def gather_sems():
    count = lax.axis_size("dp") // 2
    return [pltpu.SemaphoreType.DMA((4, count + 1)), pltpu.SemaphoreType.DMA((4, count + 1))]


def by_rows(rows, step, body):
    def once(index, carry):
        body(pl.ds(pl.multiple_of(index * step, step), step))
        return carry

    lax.fori_loop(0, rows // step, once, 0)


class LineSum:
    def __init__(self, blocks, from_below, from_above, send, recv):
        self.count = lax.axis_size("dp") // 2
        self.place = lax.axis_index("dp")
        self.spot = self.place // 2
        self.blocks, self.below, self.above = blocks, from_below, from_above
        self.send, self.recv = send, recv

    def rise(self, step, source):
        target = self.below.at[step - 1]
        sems = (self.send.at[0, step], self.recv.at[0, step])
        return remote(source, target, *sems, "dp", self.place + 2)

    def fall(self, step, source):
        target = self.above.at[step - 1]
        sems = (self.send.at[1, step], self.recv.at[1, step])
        return remote(source, target, *sems, "dp", self.place - 2)

    def add(self, slot, block):
        def body(rows):
            total = slot[rows, :].astype(jnp.float32) + self.blocks[block, rows, :].astype(jnp.float32)
            slot[rows, :] = total.astype(jnp.bfloat16)

        by_rows(slot.shape[0], 32, body)

    def advance(self, step):
        last = self.count - 1
        up_block = self.count + self.spot - step
        down_block = self.spot - self.count + step
        mirrored = last - self.spot

        @pl.when(self.spot == 0)
        def _():
            self.rise(step, self.blocks.at[self.count - step]).start()

        @pl.when(mirrored == 0)
        def _():
            self.fall(step, self.blocks.at[step - 1]).start()

        if step > 1:

            @pl.when((self.spot > 0) & (self.spot < last) & (self.spot < step))
            def _():
                slot = self.below.at[step - 2]
                self.rise(step - 1, slot).wait_recv()
                self.add(slot, up_block)
                self.rise(step, slot).start()

            @pl.when((mirrored > 0) & (mirrored < last) & (mirrored < step))
            def _():
                slot = self.above.at[step - 2]
                self.fall(step - 1, slot).wait_recv()
                self.add(slot, down_block)
                self.fall(step, slot).start()

    def finish(self, out):
        last = self.count - 1

        def body(rows):
            out[rows, :] = self.blocks[self.spot, rows, :].astype(jnp.float32)

        by_rows(out.shape[0], 32, body)

        def gain(slot):
            def body(rows):
                out[rows, :] = out[rows, :] + slot[rows, :].astype(jnp.float32)

            by_rows(out.shape[0], 32, body)

        @pl.when(self.spot > 0)
        def _():
            slot = self.below.at[last - 1]
            self.rise(last, slot).wait_recv()
            gain(slot)

        @pl.when(self.spot < last)
        def _():
            slot = self.above.at[last - 1]
            self.fall(last, slot).wait_recv()
            gain(slot)

        for step in range(1, self.count):
            block = self.blocks.at[0]
            mirrored = last - self.spot
            rises = (self.spot < step) & (self.spot < last)
            falls = (mirrored < step) & (mirrored < last)
            pl.when(rises)(lambda step=step, block=block: self.rise(step, block).wait_send())
            pl.when(falls)(lambda step=step, block=block: self.fall(step, block).wait_send())


def sum_scratch(rows, columns):
    count = lax.axis_size("dp") // 2
    return [
        pltpu.VMEM((count - 1, rows, columns), jnp.bfloat16),
        pltpu.VMEM((count - 1, rows, columns), jnp.bfloat16),
        pltpu.SemaphoreType.DMA((2, count)),
        pltpu.SemaphoreType.DMA((2, count)),
    ]


class PairProducts:
    def __init__(self, lefts, rights, parcel, sums, send, recv):
        self.count = lax.axis_size("dp") // 2
        self.place = lax.axis_index("dp")
        self.core = lax.rem(self.place, 2)
        self.lefts, self.rights = lefts, rights
        self.parcel, self.sums, self.send, self.recv = parcel, sums, send, recv

    def copy(self, chip):
        return remote(
            self.parcel.at[chip],
            self.sums.at[chip],
            self.send.at[chip],
            self.recv.at[chip],
            "dp",
            self.place + 1 - 2 * self.core,
        )

    def product(self, chip, core, quarter):
        rows = self.sums.shape[1]
        width = self.sums.shape[2] // 4
        start = pl.multiple_of((2 * chip + core) * rows, rows)
        left = self.lefts[quarter][:, pl.ds(start, rows)]
        ref, first = self.rights[quarter]
        return contract(left, ref[:, pl.ds(first, width)], 0, 0)

    def far(self):
        width = self.sums.shape[2] // 4

        def once(chip, carry):
            for quarter in range(4):
                piece = self.product(chip, 1 - self.core, quarter)
                self.parcel[chip, :, pl.ds(quarter * width, width)] = piece.astype(jnp.bfloat16)
            self.copy(chip).start()
            return carry

        lax.fori_loop(0, self.count, once, 0)

    def near(self):
        width = self.sums.shape[2] // 4

        def once(chip, carry):
            self.copy(chip).wait()
            for quarter in range(4):
                columns = pl.ds(quarter * width, width)
                piece = self.product(chip, self.core, quarter)
                total = piece + self.sums[chip, :, columns].astype(jnp.float32)
                self.sums[chip, :, columns] = total.astype(jnp.bfloat16)
            return carry

        lax.fori_loop(0, self.count, once, 0)


def pair_scratch(rows, columns):
    count = lax.axis_size("dp") // 2
    return [
        pltpu.VMEM((count, rows, columns), jnp.bfloat16),
        pltpu.SemaphoreType.DMA((count,)),
        pltpu.SemaphoreType.DMA((count,)),
    ]


class BlockGather:
    def __init__(self, own, full, send, recv):
        self.size = lax.axis_size("mp")
        self.place = lax.axis_index("mp")
        self.own, self.full, self.send, self.recv = own, full, send, recv
        self.rows, self.width = own.shape

    def spread(self, index, rows, owner, peer, first):
        start = pl.multiple_of(owner * self.width, self.width)
        target = self.full.at[rows, pl.ds(start, self.width)]
        source = self.own if first else target
        return remote(source, target, self.send.at[index], self.recv.at[index], "mp", peer)

    def copies(self):
        every = pl.ds(0, self.rows)
        if self.size != 4:
            peers = [lax.rem(self.place + step, self.size) for step in range(1, self.size)]
            return [
                self.spread(index, every, self.place, peer, True)
                for index, peer in enumerate(peers)
            ]
        beside = self.place + 1 - 2 * lax.rem(self.place, 2)
        above = lax.rem(self.place + 2, 4)
        half = self.rows // 2
        return [
            self.spread(0, every, self.place, beside, True),
            self.spread(1, every, self.place, above, True),
            self.spread(2, pl.ds(0, half), above, beside, False),
            self.spread(3, pl.ds(half, half), beside, above, False),
        ]

    def keep(self):
        start = pl.multiple_of(self.place * self.width, self.width)
        target = self.full.at[:, pl.ds(start, self.width)]
        return pltpu.make_async_copy(self.own, target, self.send.at[self.size])

    def start(self):
        copies = self.copies()
        for copy in copies[:2] if self.size == 4 else copies:
            copy.start()
        self.keep().start()

    def forward(self):
        copies = self.copies()
        if self.size == 4:
            copies[1].wait_recv()
            copies[2].start()
            copies[0].wait_recv()
            copies[3].start()

    def finish(self):
        copies = self.copies()
        self.keep().wait()
        for index, copy in enumerate(copies):
            copy.wait_send()
            if index > 1 or self.size != 4:
                copy.wait_recv()


def block_sems():
    size = lax.axis_size("mp") + 1
    return [pltpu.SemaphoreType.DMA((size,)), pltpu.SemaphoreType.DMA((size,))]


def first_kernel(
    block_ref,
    x_ref,
    gy_ref,
    small_ref,
    full_ref,
    x_full,
    gy_full,
    spread_ref,
    gather_send,
    gather_recv,
    x_send,
    x_recv,
    gy_send,
    gy_recv,
    small_send,
    small_recv,
):
    columns = lax.axis_size("dp")
    total = columns * lax.axis_size("mp")
    place = lax.axis_index("mp") * columns + lax.axis_index("dp")
    barrier = pltpu.get_barrier_semaphore()

    def device(step):
        peer = lax.rem(place + step, total)
        return {"mp": peer // columns, "dp": lax.rem(peer, columns)}

    def greet(step, carry):
        pl.semaphore_signal(barrier, inc=1, device_id=device(step), device_id_type=MESH_ID)
        return carry

    lax.fori_loop(1, total, greet, 0)
    pl.semaphore_wait(barrier, total - 1)

    def small_copy(step):
        return pltpu.make_async_remote_copy(
            src_ref=small_ref.at[0],
            dst_ref=spread_ref.at[place],
            send_sem=small_send.at[step],
            recv_sem=small_recv.at[step],
            device_id=device(step),
            device_id_type=MESH_ID,
        )

    def begin(step, carry):
        small_copy(step).start()
        return carry

    def end(step, carry):
        small_copy(step).wait()
        return carry

    weight = LineGather(block_ref, full_ref, gather_send, gather_recv)
    rows_x = BlockGather(x_ref, x_full, x_send, x_recv)
    rows_gy = BlockGather(gy_ref, gy_full, gy_send, gy_recv)
    lax.fori_loop(1, total, begin, 0)
    weight.start()
    rows_x.start()
    spread_ref[place] = small_ref[0]
    lax.fori_loop(1, total, end, 0)
    weight.advance(1)
    rows_x.forward()
    rows_gy.start()
    for step in range(2, weight.count):
        weight.advance(step)
        if step == 2:
            rows_gy.forward()
    weight.finish()
    rows_x.finish()
    rows_gy.finish()


def first_gathers(block, tokens, cotangent, small):
    hbm = pl.BlockSpec(memory_space=pl.ANY)
    vmem = pl.BlockSpec(memory_space=pltpu.VMEM)
    mp_size, dp_size = (lax.axis_size("mp"), lax.axis_size("dp"))
    wide = (tokens.shape[0], tokens.shape[1] * mp_size)
    total = mp_size * dp_size
    return pl.pallas_call(
        first_kernel,
        in_specs=[hbm, hbm, hbm, vmem],
        out_specs=[hbm, hbm, hbm, vmem],
        out_shape=[
            jax.ShapeDtypeStruct((block.shape[0] * dp_size, block.shape[1]), block.dtype),
            jax.ShapeDtypeStruct(wide, tokens.dtype),
            jax.ShapeDtypeStruct(wide, cotangent.dtype),
            jax.ShapeDtypeStruct((total,) + small.shape[1:], small.dtype),
        ],
        scratch_shapes=gather_sems()
        + block_sems()
        + block_sems()
        + [pltpu.SemaphoreType.DMA((total,)), pltpu.SemaphoreType.DMA((total,))],
        compiler_params=pltpu.CompilerParams(collective_id=1, has_side_effects=True),
        name="first_gathers",
    )(block, tokens, cotangent, small)


def greet_and_wait():
    barrier, count = greet_line()
    pl.semaphore_wait(barrier, count)


def second_kernel(
    block_ref,
    xn_ref,
    gy_ref,
    up_ref,
    bias_ref,
    full_ref,
    act_ref,
    slope_ref,
    sums_ref,
    gather_send,
    gather_recv,
    parcel,
    pair_send,
    pair_recv,
):
    weight = LineGather(block_ref, full_ref, gather_send, gather_recv)
    products = PairProducts(
        [gy_ref] * 4, quarters(act_ref), parcel, sums_ref, pair_send, pair_recv
    )
    greet_and_wait()
    weight.start()
    width = up_ref.shape[1] // 4

    def tile(rows):
        for quarter in range(4):
            columns = pl.ds(quarter * width, width)
            hidden = contract(xn_ref[rows, :], up_ref[:, columns], 1, 0) + bias_ref[:, columns]
            activated, slope = gelu_pair(hidden)
            act_ref[rows, columns] = activated.astype(jnp.bfloat16)
            slope_ref[rows, columns] = slope.astype(jnp.bfloat16)

    by_rows(xn_ref.shape[0], ROW_TILE, tile)
    products.far()
    weight.advance(1)
    products.near()
    for step in range(2, weight.count):
        weight.advance(step)
    weight.finish()


def quarters(ref):
    width = ref.shape[1] // 4
    return [(ref, quarter * width) for quarter in range(4)]


VMEM_LIMIT = 60 * 1024 * 1024


def carrying(kernel, collective_id, operands, in_places, outs, out_places, scratch, flops, name):
    spaces = {"h": pl.BlockSpec(memory_space=pl.ANY), "v": pl.BlockSpec(memory_space=pltpu.VMEM)}
    return pl.pallas_call(
        kernel,
        in_specs=[spaces[place] for place in in_places],
        out_specs=[spaces[place] for place in out_places],
        out_shape=[jax.ShapeDtypeStruct(shape, dtype) for shape, dtype in outs],
        scratch_shapes=scratch,
        compiler_params=pltpu.CompilerParams(
            collective_id=collective_id, has_side_effects=True, vmem_limit_bytes=VMEM_LIMIT
        ),
        cost_estimate=pl.CostEstimate(flops=flops, bytes_accessed=1 << 25, transcendentals=0),
        name=name,
    )(*operands)


def second_step(block, normed, grad_rows, full_up, bias_up):
    rows, width = normed.shape
    count = lax.axis_size("dp") // 2
    columns = full_up.shape[1]
    low = jnp.bfloat16
    return carrying(
        second_kernel,
        4,
        (block, normed, grad_rows, full_up, bias_up[None, :]),
        "hvvvv",
        [
            ((width, block.shape[1]), low),
            ((rows, columns), low),
            ((rows, columns), low),
            ((count, width // (2 * count), columns), low),
        ],
        "hvvv",
        gather_sems() + pair_scratch(width // (2 * count), columns),
        4 * rows * width * columns,
        "gather_beside_hidden",
    )


def third_kernel(
    head_cols,
    block_ref,
    ready_ref,
    xn_ref,
    gy_ref,
    weight_ref,
    bias_ref,
    seg_col_ref,
    seg_row_ref,
    keep_ref,
    ahead_ref,
    behind_ref,
    full_ref,
    grad_ref,
    or_ref,
    sums_ref,
    owned_ref,
    gather_send,
    gather_recv,
    below,
    above,
    line_send,
    line_recv,
    parcel,
    pair_send,
    pair_recv,
    mask_ref,
    low_ref,
    go_ref,
    dq_acc,
    dk_acc,
    dv_acc,
):
    weight = LineGather(block_ref, full_ref, gather_send, gather_recv)
    line = LineSum(ready_ref, below, above, line_send, line_recv)
    rights = [(grad_ref, kind * head_cols) for kind in range(3)] + [(or_ref, 0)]
    products = PairProducts(
        [xn_ref] * 3 + [gy_ref], rights, parcel, sums_ref, pair_send, pair_recv
    )
    greet_and_wait()
    weight.start()
    line.advance(1)

    rows = xn_ref.shape[0]
    tiles = rows // ROW_TILE
    scale = HEAD_DIM ** (-0.5)
    for tile in range(tiles):
        here = pl.ds(tile * ROW_TILE, ROW_TILE)
        reach = (tile + 1) * ROW_TILE
        shape = (ROW_TILE, reach)
        row_ids = lax.broadcasted_iota(jnp.int32, shape, 0) + tile * ROW_TILE
        key_ids = lax.broadcasted_iota(jnp.int32, shape, 1)
        allowed = (seg_col_ref[here, :] == seg_row_ref[:, pl.ds(0, reach)]) & (key_ids <= row_ids)
        mask_ref[here, pl.ds(0, reach)] = jnp.where(allowed, 0.0, masked_score)

    def turned(values, here, direction):
        ahead = pltpu.roll(values, LANES - ROT_DIM // 2, 1)
        behind = pltpu.roll(values, ROT_DIM // 2, 1)
        return values * keep_ref[here, :] + direction * (
            ahead * ahead_ref[here, :] + behind * behind_ref[here, :]
        )

    def project(here):
        for kind in range(3):
            columns = pl.ds(kind * head_cols, head_cols)
            values = contract(xn_ref[here, :], weight_ref[:, columns], 1, 0) + bias_ref[:, columns]
            if kind == 2:
                low_ref[here, columns] = values.astype(jnp.bfloat16)
                continue
            for first in range(0, head_cols, LANES):
                part = turned(values[:, first : first + LANES], here, 1.0).astype(jnp.bfloat16)
                if kind == 0:
                    part = part * scale
                low_ref[here, pl.ds(kind * head_cols + first, LANES)] = part
        columns = pl.ds(3 * head_cols, head_cols)
        values = contract(gy_ref[here, :], weight_ref[:, columns], 1, 0)
        go_ref[here, :] = values.astype(jnp.bfloat16)

    by_rows(rows, ROW_TILE, project)

    lane = lax.broadcasted_iota(jnp.int32, (ROW_TILE, LANES), 1)
    first_head = lane < HEAD_DIM

    def one_pair(pair, carry):
        column = pl.multiple_of(pair * LANES, LANES)
        q_lanes = pl.ds(column, LANES)
        k_lanes = pl.ds(pl.multiple_of(head_cols + column, LANES), LANES)
        v_lanes = pl.ds(pl.multiple_of(2 * head_cols + column, LANES), LANES)
        dk_acc[...] = jnp.zeros_like(dk_acc)
        dv_acc[...] = jnp.zeros_like(dv_acc)
        for tile in range(tiles):
            here = pl.ds(tile * ROW_TILE, ROW_TILE)
            keys = pl.ds(0, (tile + 1) * ROW_TILE)
            outs = []
            query_grads = []
            for head in range(LANES // HEAD_DIM):
                mine = first_head if head == 0 else jnp.logical_not(first_head)
                none = jnp.zeros((ROW_TILE, LANES), jnp.bfloat16)
                query = jnp.where(mine, low_ref[here, q_lanes], none)
                grad_out = jnp.where(mine, go_ref[here, q_lanes], none)
                scores = contract(query, low_ref[keys, k_lanes], 1, 1) + mask_ref[here, keys]
                peak = jnp.max(scores, axis=1, keepdims=True)
                weights = jnp.exp(scores - peak)
                share = 1.0 / jnp.sum(weights, axis=1, keepdims=True)
                probs = weights * share
                probs_low = probs.astype(jnp.bfloat16)
                outs.append(contract(probs_low, low_ref[keys, v_lanes], 1, 0))
                grad_probs = contract(grad_out, low_ref[keys, v_lanes], 1, 1)
                delta = jnp.sum(probs * grad_probs, axis=1, keepdims=True)
                grad_scores = (probs * (grad_probs - delta)).astype(jnp.bfloat16)
                query_grads.append(contract(grad_scores, low_ref[keys, k_lanes], 1, 0))
                dk_acc[keys, :] += contract(grad_scores, query, 0, 0)
                dv_acc[keys, :] += contract(probs_low, grad_out, 0, 0)
            or_ref[here, q_lanes] = jnp.where(first_head, outs[0], outs[1]).astype(jnp.bfloat16)
            dq_acc[here, :] = jnp.where(first_head, query_grads[0], query_grads[1])
        for tile in range(tiles):
            here = pl.ds(tile * ROW_TILE, ROW_TILE)
            query_grad = turned(dq_acc[here, :], here, -1.0) * scale
            grad_ref[here, q_lanes] = query_grad.astype(jnp.bfloat16)
            key_grad = turned(dk_acc[here, :], here, -1.0)
            grad_ref[here, k_lanes] = key_grad.astype(jnp.bfloat16)
            grad_ref[here, v_lanes] = dv_acc[here, :].astype(jnp.bfloat16)

        @pl.when(pair == 0)
        def _():
            weight.advance(1)
            line.advance(2)

        return carry

    lax.fori_loop(0, head_cols // LANES, one_pair, 0)
    weight.advance(2)
    line.advance(3)
    products.far()
    products.near()
    for step in range(3, weight.count):
        weight.advance(step)
    for step in range(4, weight.count):
        line.advance(step)
    line.finish(owned_ref)
    weight.finish()


def third_step(block, ready, normed, grad_rows, full_qkvo, bias_qkv, segment, cosine, sine):
    rows, width = normed.shape
    count = lax.axis_size("dp") // 2
    columns = full_qkvo.shape[1]
    head_cols = columns // 4
    part = width // (2 * count)
    low = jnp.bfloat16
    still = jnp.ones((rows, HEAD_DIM - ROT_DIM), jnp.float32)
    zero = jnp.zeros((rows, ROT_DIM // 2), jnp.float32)
    repeat = (1, LANES // HEAD_DIM)
    keep = jnp.tile(jnp.concatenate([cosine, cosine, still], axis=1), repeat)
    ahead = jnp.tile(jnp.concatenate([-sine, zero, 0.0 * still], axis=1), repeat)
    behind = jnp.tile(jnp.concatenate([zero, sine, 0.0 * still], axis=1), repeat)
    return carrying(
        functools.partial(third_kernel, head_cols),
        5,
        (
            block,
            ready,
            normed,
            grad_rows,
            full_qkvo,
            bias_qkv[None, :],
            segment[:, None],
            segment[None, :],
            keep,
            ahead,
            behind,
        ),
        "hvvvvvvvvvv",
        [
            ((width, block.shape[1]), low),
            ((rows, 3 * head_cols), low),
            ((rows, head_cols), low),
            ((count, part, columns), low),
            ((part, ready.shape[2]), jnp.float32),
        ],
        "hvvvv",
        gather_sems()
        + sum_scratch(part, ready.shape[2])
        + pair_scratch(part, columns)
        + [
            pltpu.VMEM((rows, rows), jnp.float32),
            pltpu.VMEM((rows, 3 * head_cols), low),
            pltpu.VMEM((rows, head_cols), low),
            pltpu.VMEM((rows, LANES), jnp.float32),
            pltpu.VMEM((rows, LANES), jnp.float32),
            pltpu.VMEM((rows, LANES), jnp.float32),
        ],
        4 * rows * width * columns + 12 * rows * rows * head_cols,
        "lines_beside_attention",
    )


def fourth_kernel(
    ready_ref,
    xn_ref,
    gy_ref,
    down_ref,
    slope_ref,
    gh_ref,
    sums_ref,
    owned_ref,
    below,
    above,
    line_send,
    line_recv,
    parcel,
    pair_send,
    pair_recv,
):
    line = LineSum(ready_ref, below, above, line_send, line_recv)
    products = PairProducts(
        [xn_ref] * 4, quarters(gh_ref), parcel, sums_ref, pair_send, pair_recv
    )
    greet_and_wait()
    line.advance(1)
    width = down_ref.shape[1] // 4

    def tile(rows):
        for quarter in range(4):
            columns = pl.ds(quarter * width, width)
            grad_act = contract(gy_ref[rows, :], down_ref[:, columns], 1, 0)
            grad_hidden = grad_act * slope_ref[rows, columns].astype(jnp.float32)
            gh_ref[rows, columns] = grad_hidden.astype(jnp.bfloat16)

    by_rows(gy_ref.shape[0], ROW_TILE, tile)
    products.far()
    line.advance(2)
    products.near()
    for step in range(3, line.count):
        line.advance(step)
    line.finish(owned_ref)


def fourth_step(ready, normed, grad_rows, turned_down, slope):
    rows, width = normed.shape
    count = lax.axis_size("dp") // 2
    columns = turned_down.shape[1]
    part = width // (2 * count)
    low = jnp.bfloat16
    return carrying(
        fourth_kernel,
        6,
        (ready, normed, grad_rows, turned_down, slope),
        "vvvvv",
        [
            ((rows, columns), low),
            ((count, part, columns), low),
            ((part, ready.shape[2]), jnp.float32),
        ],
        "vvv",
        sum_scratch(part, ready.shape[2]) + pair_scratch(part, columns),
        4 * rows * width * columns,
        "line_beside_hidden_grad",
    )


def greet_block():
    size = lax.axis_size("mp")
    place = lax.axis_index("mp")
    barrier = pltpu.get_barrier_semaphore()
    for step in range(1, size):
        peer = lax.rem(place + step, size)
        pl.semaphore_signal(barrier, inc=1, device_id={"mp": peer}, device_id_type=MESH_ID)
    return size - 1


class BlockScatter:
    def __init__(self, parts, got, send, recv):
        self.size = lax.axis_size("mp")
        self.place = lax.axis_index("mp")
        self.parts, self.got, self.send, self.recv = parts, got, send, recv
        self.half = parts.shape[1] // 2
        self.beside = self.place + 1 - 2 * lax.rem(self.place, 2)
        self.above = lax.rem(self.place + 2, 4)

    def owner(self, index):
        if self.size == 4:
            return [lax.rem(self.beside + 2, 4), self.beside, self.above, self.place][index]
        return lax.rem(self.place + 1 + index, self.size)

    def copy(self, index):
        if self.size == 4:
            part, bottom, peer = [
                (0, 0, self.beside),
                (0, 1, self.above),
                (1, 0, self.beside),
                (2, 1, self.above),
                (2, 0, self.above),
                (1, 1, self.beside),
            ][index]
            source = self.parts.at[part, pl.ds(bottom * self.half, self.half), :]
        else:
            source = self.parts.at[index]
            peer = self.owner(index)
        sems = (self.send.at[index], self.recv.at[index])
        return remote(source, self.got.at[index], *sems, "mp", peer)

    def after(self, index):
        if self.size != 4:
            if index < self.size - 1:
                self.copy(index).start()
            return
        for number in ((0, 1), (2,), (3,), ())[index]:
            self.copy(number).start()

    def second(self):
        if self.size != 4:
            return
        for number, part, bottom in ((0, 2, 0), (1, 1, 1)):
            self.copy(number).wait_recv()

            def body(rows, number=number, part=part, bottom=bottom):
                here = pl.ds(bottom * self.half + rows.start, rows.size)
                total = summed(self.parts[part, here, :], self.got[number, rows, :])
                self.parts[part, here, :] = total.astype(jnp.bfloat16)

            by_rows(self.half, 64, body)
            self.copy(number + 4).start()

    def finish(self):
        if self.size != 4:
            for index in range(self.size - 1):
                self.copy(index).wait()
            return
        for index in range(6):
            if index > 1:
                self.copy(index).wait_recv()
            self.copy(index).wait_send()

    def total(self, tile, rows):
        here = pl.ds(tile * rows, rows)
        own = self.parts[self.size - 1, here, :]
        if self.size != 4:
            return summed(own, *[self.got[index, here, :] for index in range(self.size - 1)])
        bottom = (tile * rows) // self.half
        there = pl.ds(tile * rows - bottom * self.half, rows)
        return summed(own, self.got[2 + bottom, there, :], self.got[4 + bottom, there, :])


def scatter_scratch(rows, width):
    size = lax.axis_size("mp")
    slots = (6, rows // 2, width) if size == 4 else (size - 1, rows, width)
    return [
        pltpu.VMEM((size, rows, width), jnp.bfloat16),
        pltpu.VMEM(slots, jnp.bfloat16),
        pltpu.SemaphoreType.DMA((slots[0],)),
        pltpu.SemaphoreType.DMA((slots[0],)),
    ]


def fifth_kernel(
    head_cols,
    ready_ref,
    act_ref,
    gh_ref,
    grad_ref,
    or_ref,
    down_ref,
    qkvo_ref,
    up_ref,
    x_ref,
    gy_ref,
    stats_ref,
    vectors_ref,
    out_ref,
    dx_ref,
    owned_ref,
    sums_ref,
    below,
    above,
    line_send,
    line_recv,
    g_parts,
    g_got,
    g_send,
    g_recv,
    t_parts,
    t_got,
    t_send,
    t_recv,
    one_ref,
    two_ref,
    load_sems,
    terms_ref,
    terms_got,
    terms_send,
    terms_recv,
):
    line = LineSum(ready_ref, below, above, line_send, line_recv)
    from_norm = BlockScatter(g_parts, g_got, g_send, g_recv)
    branches = BlockScatter(t_parts, t_got, t_send, t_recv)
    mp_size = from_norm.size
    mp_place = from_norm.place
    rows, width = x_ref.shape
    model_width = width * mp_size
    tiles = rows // ROW_TILE

    def load(index):
        late, share = divmod(index, mp_size)
        start = pl.multiple_of(from_norm.owner(share) * width, width)
        slot = index % 2
        where = pl.ds(start, width)
        source = down_ref if late else up_ref
        return [
            pltpu.make_async_copy(qkvo_ref.at[where, :], one_ref.at[slot], load_sems.at[0, slot]),
            pltpu.make_async_copy(source.at[where, :], two_ref.at[slot], load_sems.at[1, slot]),
        ]

    for copy in load(0):
        copy.start()
    barrier, count = greet_line()
    count += greet_block()
    pl.semaphore_wait(barrier, count)
    line.advance(1)

    for index in range(2 * mp_size):
        late, share = divmod(index, mp_size)
        slot = index % 2
        for copy in load(index):
            copy.wait()
        if index + 1 < 2 * mp_size:
            for copy in load(index + 1):
                copy.start()

        def tile(here, late=late, share=share, slot=slot):
            if late:
                part = contract(or_ref[here, :], one_ref[slot, :, pl.ds(3 * head_cols, head_cols)], 1, 1)
                part = part + contract(act_ref[here, :], two_ref[slot], 1, 1)
                t_parts[share, here, :] = part.astype(jnp.bfloat16)
            else:
                part = contract(grad_ref[here, :], one_ref[slot, :, pl.ds(0, 3 * head_cols)], 1, 1)
                part = part + contract(gh_ref[here, :], two_ref[slot], 1, 1)
                g_parts[share, here, :] = part.astype(jnp.bfloat16)

        by_rows(rows, ROW_TILE, tile)
        (branches if late else from_norm).after(share)
        if index == mp_size:
            from_norm.second()
        if index == mp_size + 1:
            line.advance(2)
    branches.second()
    from_norm.finish()

    def lane_pair(first, second):
        lane = lax.broadcasted_iota(jnp.int32, (ROW_TILE, LANES), 1)
        return jnp.where(lane == 0, first, jnp.where(lane == 1, second, 0.0))

    gain = vectors_ref[0:1, :]
    columns = [jnp.zeros((1, width), jnp.float32) for _ in range(3)]
    for tile in range(tiles):
        here = pl.ds(tile * ROW_TILE, ROW_TILE)
        normalized = (x_ref[here, :].astype(jnp.float32) - stats_ref[here, 0:1]) * stats_ref[here, 1:2]
        grad = from_norm.total(tile, ROW_TILE)
        gained = grad * gain
        terms = lane_pair(
            jnp.sum(gained, axis=1, keepdims=True),
            jnp.sum(gained * normalized, axis=1, keepdims=True),
        )
        terms_ref[:, here] = jnp.transpose(terms)[:8, :]
        upstream = gy_ref[here, :].astype(jnp.float32) * stats_ref[here, 2:3]
        columns[0] += jnp.sum(grad * normalized, axis=0, keepdims=True)
        columns[1] += jnp.sum(grad, axis=0, keepdims=True)
        columns[2] += jnp.sum(upstream, axis=0, keepdims=True)
    sums_ref[...] = jnp.concatenate(columns + [jnp.zeros((5, width), jnp.float32)], axis=0)

    def terms_copy(step):
        peer = lax.rem(mp_place + step, mp_size)
        slot = step - 1
        sems = (terms_send.at[slot], terms_recv.at[slot])
        return remote(terms_ref, terms_got.at[slot], *sems, "mp", peer)

    for step in range(1, mp_size):
        terms_copy(step).start()
    for step in range(3, line.count):
        line.advance(step)
    for step in range(1, mp_size):
        terms_copy(step).wait()
    for tile in range(tiles):
        here = pl.ds(tile * ROW_TILE, ROW_TILE)
        terms = terms_ref[:, here]
        for slot in range(mp_size - 1):
            terms = terms + terms_got[slot, :, here]
        wide = jnp.concatenate([terms, jnp.zeros((LANES - 8, ROW_TILE), jnp.float32)], axis=0)
        terms = jnp.transpose(wide) * (1.0 / model_width)
        inv_std = stats_ref[here, 1:2]
        normalized = (x_ref[here, :].astype(jnp.float32) - stats_ref[here, 0:1]) * inv_std
        gained = from_norm.total(tile, ROW_TILE) * gain
        upstream = gy_ref[here, :].astype(jnp.float32) * stats_ref[here, 2:3]
        dx_ref[here, :] = upstream + inv_std * (gained - terms[:, 0:1] - normalized * terms[:, 1:2])
    branches.finish()
    for tile in range(tiles):
        here = pl.ds(tile * ROW_TILE, ROW_TILE)
        total = x_ref[here, :].astype(jnp.float32) + branches.total(tile, ROW_TILE)
        total = total + vectors_ref[1:2, :] + vectors_ref[2:3, :]
        out_ref[here, :] = total.astype(jnp.bfloat16)
    line.finish(owned_ref)


def fifth_step(
    ready,
    activated,
    grad_hidden,
    grad_projected,
    attended,
    turned_down,
    full_qkvo,
    full_up,
    tokens,
    cotangent,
    stats,
    vectors,
):
    rows, width = tokens.shape
    head_cols = attended.shape[1]
    count, part, columns = ready.shape
    mp_size = lax.axis_size("mp")
    low = jnp.bfloat16
    return carrying(
        functools.partial(fifth_kernel, head_cols),
        7,
        (
            ready,
            activated,
            grad_hidden,
            grad_projected,
            attended,
            turned_down,
            full_qkvo,
            full_up,
            tokens,
            cotangent,
            stats,
            vectors,
        ),
        "vvvvvhhhvvvv",
        [
            ((rows, width), low),
            ((rows, width), jnp.float32),
            ((part, columns), jnp.float32),
            ((8, width), jnp.float32),
        ],
        "vvvv",
        sum_scratch(part, columns)
        + scatter_scratch(rows, width)
        + scatter_scratch(rows, width)
        + [
            pltpu.VMEM((2, width, columns), low),
            pltpu.VMEM((2, width, columns), low),
            pltpu.SemaphoreType.DMA((2, 2)),
            pltpu.VMEM((8, rows), jnp.float32),
            pltpu.VMEM((mp_size - 1, 8, rows), jnp.float32),
            pltpu.SemaphoreType.DMA((mp_size - 1,)),
            pltpu.SemaphoreType.DMA((mp_size - 1,)),
        ],
        4 * rows * width * mp_size * columns,
        "line_beside_norm_grad",
    )


def dot_f32(left, right, left_axis, right_axis):
    return lax.dot_general(
        left.astype(jnp.bfloat16),
        right.astype(jnp.bfloat16),
        (((left_axis,), (right_axis,)), ((), ())),
        preferred_element_type=jnp.float32,
    )


def shampoo(weight_block, grad_block, left, right):
    left_new = 0.5 * left[0, 0, 0] + 0.5 * dot_f32(grad_block, grad_block, 1, 1)
    right_new = 0.5 * right[0, 0, 0] + 0.5 * dot_f32(grad_block, grad_block, 0, 0)
    step_block = dot_f32(dot_f32(left[1, 0, 0], grad_block, 1, 0), right[1, 0, 0], 1, 0)
    return (weight_block - matrix_rate * step_block, left_new[None, None], right_new[None, None])


def shampoo_turned(weight_block, turned_grad, left, right):
    left_new = 0.5 * left[0, 0, 0] + 0.5 * dot_f32(turned_grad, turned_grad, 0, 0)
    right_new = 0.5 * right[0, 0, 0] + 0.5 * dot_f32(turned_grad, turned_grad, 1, 1)
    step_block = dot_f32(dot_f32(left[1, 0, 0], turned_grad, 1, 1), right[1, 0, 0], 1, 0)
    return (weight_block - matrix_rate * step_block, left_new[None, None], right_new[None, None])


def vector_update(state, grad):
    stat_new = 0.5 * state[1] + 0.5 * grad * grad
    param_new = state[0] - vector_rate * grad * lax.rsqrt(stat_new)
    return (param_new, stat_new)


def local(
    tokens,
    cotangent,
    seq_lengths,
    w_qkv,
    qkv_bias_state,
    w_out,
    out_bias_state,
    w_up,
    up_bias_state,
    w_down,
    ln_state,
    qkv_left,
    qkv_right,
    out_left,
    out_right,
    up_left,
    up_right,
    down_left,
    down_right,
):
    row_count, share_width = tokens.shape
    mp_size = lax.axis_size("mp")
    dp_size = lax.axis_size("dp")
    model_width = share_width * mp_size
    own_width = w_qkv.shape[2]
    mp_place = lax.axis_index("mp")

    flat_master = jnp.concatenate([w_qkv[:, kind] for kind in range(3)], axis=1)
    block_qkvo = jnp.concatenate([flat_master, w_out.T], axis=1).astype(jnp.bfloat16)
    piece = ln_state.shape[2]
    small = jnp.concatenate(
        [
            ln_state[0].reshape(-1),
            qkv_bias_state[0].reshape(-1),
            out_bias_state[0].reshape(-1),
            up_bias_state[0].reshape(-1),
        ]
    )
    small = small.astype(jnp.bfloat16).astype(jnp.float32)
    filled = small.shape[0]
    small = jnp.pad(small, (0, -filled % 1024)).reshape(1, 8, -1)
    full_up, x_full, upstream, spread = first_gathers(
        w_up.astype(jnp.bfloat16), tokens, cotangent, small
    )
    spread = spread.reshape(mp_size * dp_size, -1)[:, :filled]
    norm_all = spread[:, : 2 * piece].reshape(-1, 2, piece).transpose(1, 0, 2).reshape(2, -1)
    here = take(spread.reshape(mp_size, dp_size, -1), mp_place)
    bias_qkv = here[:, 2 * piece : 5 * piece].reshape(dp_size, 3, piece)
    bias_qkv = bias_qkv.transpose(1, 0, 2).reshape(-1)
    bias_out = here[:, 5 * piece : 7 * piece].reshape(dp_size, 2, piece)
    bias_out = bias_out.transpose(1, 0, 2).reshape(2, -1)
    bias_up = here[:, 7 * piece :].reshape(-1)

    segment, offsets, is_valid = segment_layout(seq_lengths[0], row_count)
    cosine, sine = rope_tables(offsets)

    inputs = x_full.astype(jnp.float32)
    row_mean = jnp.mean(inputs, axis=1, keepdims=True)
    row_var = jnp.mean(inputs * inputs, axis=1, keepdims=True) - row_mean * row_mean
    inv_std = lax.rsqrt(row_var + norm_eps)
    normed = ((inputs - row_mean) * inv_std * norm_all[0] + norm_all[1]).astype(jnp.bfloat16)
    grad_rows = (upstream.astype(jnp.float32) * is_valid[:, None]).astype(jnp.bfloat16)
    full_qkvo, activated, slope, ready_down = second_step(
        block_qkvo, normed, grad_rows, full_up, bias_up
    )
    turned_down, grad_projected, attended, ready_qkvo, owned_down = third_step(
        w_down.T.astype(jnp.bfloat16),
        ready_down,
        normed,
        grad_rows,
        full_qkvo,
        bias_qkv,
        segment,
        cosine,
        sine,
    )
    grad_hidden, ready_up, owned_qkvo = fourth_step(
        ready_qkvo, normed, grad_rows, turned_down, slope
    )
    norm_here = lax.dynamic_slice_in_dim(norm_all, mp_place * share_width, share_width, 1)
    vectors = jnp.concatenate(
        [norm_here[:1], bias_out, jnp.zeros((5, share_width), jnp.float32)], axis=0
    )
    stats = jnp.concatenate([row_mean, inv_std, is_valid[:, None]], axis=1)
    output, input_grad, owned_up, column_sums = fifth_step(
        ready_up,
        activated,
        grad_hidden,
        grad_projected,
        attended,
        turned_down,
        full_qkvo,
        full_up,
        tokens,
        cotangent,
        stats,
        vectors,
    )

    def owner_rows(values, count):
        return values.reshape(count, dp_size, -1).transpose(1, 0, 2).reshape(dp_size, -1)

    vector_grads = jnp.concatenate(
        [
            owner_rows(column_sums[0], 1),
            owner_rows(column_sums[1], 1),
            owner_rows(jnp.sum(grad_projected.astype(jnp.float32), axis=0), 3),
            owner_rows(column_sums[2], 1),
            owner_rows(jnp.sum(grad_hidden.astype(jnp.float32), axis=0), 1),
        ],
        axis=1,
    )
    width = vector_grads.shape[1]
    vector_grads = jnp.pad(vector_grads, ((0, 0), (0, -width % 1024))).reshape(dp_size, 8, -1)
    vector_sums = jnp.sum(exchange(vector_grads, ("dp",), 3, False), axis=0).reshape(-1)[:width]
    owned_norm = vector_sums[: 2 * piece].reshape(2, piece)
    owned_bqkv = vector_sums[2 * piece : 5 * piece].reshape(3, piece)
    bias_total = vector_sums[5 * piece : 6 * piece]
    owned_obias = jnp.stack([bias_total, bias_total])
    owned_bup = vector_sums[6 * piece :]

    owned_qkv = owned_qkvo[:, : 3 * own_width]
    owned_out = owned_qkvo[:, 3 * own_width :]
    new_w_down, down_left_new, down_right_new = shampoo_turned(
        w_down, owned_down, down_left, down_right
    )
    new_w_out, out_left_new, out_right_new = shampoo_turned(w_out, owned_out, out_left, out_right)
    new_qkv_block, qkv_left_new, qkv_right_new = shampoo(
        flat_master, owned_qkv, qkv_left, qkv_right
    )
    new_w_qkv = jnp.stack(
        [new_qkv_block[:, kind * own_width : (kind + 1) * own_width] for kind in range(3)], axis=1
    )
    new_w_up, up_left_new, up_right_new = shampoo(w_up, owned_up, up_left, up_right)
    qkv_params, qkv_stats = vector_update(qkv_bias_state, owned_bqkv)
    obias_params, obias_stats = vector_update(out_bias_state, owned_obias)
    norm_new_params, norm_new_stats = vector_update(ln_state, owned_norm)
    new_up_bias, new_up_stat = vector_update(up_bias_state, owned_bup)
    new_vector_params = jnp.concatenate([qkv_params, obias_params, norm_new_params], axis=0)
    new_vector_stats = jnp.concatenate([qkv_stats, obias_stats, norm_new_stats], axis=0)
    return (
        output,
        input_grad,
        new_w_qkv,
        new_w_out,
        new_w_up,
        new_w_down,
        new_vector_params,
        new_vector_stats,
        new_up_bias,
        new_up_stat,
        qkv_left_new,
        qkv_right_new,
        out_left_new,
        out_right_new,
        up_left_new,
        up_right_new,
        down_left_new,
        down_right_new,
    )


def solution(mesh):
    return jax.shard_map(
        local,
        mesh=mesh,
        in_specs=(
            P("dp", "mp"),
            P("dp", "mp"),
            P("dp", None),
            P("dp", None, "mp"),
            P(None, None, ("mp", "dp")),
            P("mp", "dp"),
            P(None, None, ("mp", "dp")),
            P("dp", "mp"),
            P(None, ("mp", "dp")),
            P("mp", "dp"),
            P(None, None, ("mp", "dp")),
            P(None, "mp", "dp", None, None),
            P(None, "mp", "dp", None, None),
            P(None, "mp", "dp", None, None),
            P(None, "mp", "dp", None, None),
            P(None, "mp", "dp", None, None),
            P(None, "mp", "dp", None, None),
            P(None, "mp", "dp", None, None),
            P(None, "mp", "dp", None, None),
        ),
        out_specs=(
            P("dp", "mp"),
            P("dp", "mp"),
            P("dp", None, "mp"),
            P("mp", "dp"),
            P("dp", "mp"),
            P("mp", "dp"),
            P(None, ("mp", "dp")),
            P(None, ("mp", "dp")),
            P(("mp", "dp")),
            P(("mp", "dp")),
            P("mp", "dp", None, None),
            P("mp", "dp", None, None),
            P("mp", "dp", None, None),
            P("mp", "dp", None, None),
            P("mp", "dp", None, None),
            P("mp", "dp", None, None),
            P("mp", "dp", None, None),
            P("mp", "dp", None, None),
        ),
        check_vma=False,
    )
```

```python
import functools
import math

import jax
import jax.numpy as jnp
from jax import lax
from jax.experimental import pallas as pl
from jax.experimental.pallas import tpu as pltpu
from jax.sharding import PartitionSpec as P

HEAD_DIM = 64
ROT_DIM = 32
LANES = 128
ROW_TILE = 256


norm_eps = 1e-05
matrix_rate = 1.0
vector_rate = 0.4
masked_score = -1e30


def segment_of(ends, positions, axis, slots):
    finished = ends <= positions
    segment = jnp.sum(jnp.where(finished, 1, 0), axis=axis, keepdims=True)
    starting = jnp.max(jnp.where(finished, ends, 0), axis=axis, keepdims=True)
    return (segment, starting, segment < slots)


def rope_tables(offsets):
    lane = lax.rem(lax.broadcasted_iota(jnp.int32, (1, LANES), 1), HEAD_DIM)
    half_rot = ROT_DIM // 2
    freq_index = lax.rem(lane, half_rot).astype(jnp.float32)
    inverse = jnp.exp(-(2.0 * freq_index / ROT_DIM) * math.log(10000.0))
    angles = offsets * inverse
    cosine, sine = (jnp.cos(angles), jnp.sin(angles))
    keep = jnp.where(lane < ROT_DIM, cosine, 1.0)
    ahead = jnp.where(lane < half_rot, -sine, 0.0)
    behind = jnp.where((lane >= half_rot) & (lane < ROT_DIM), sine, 0.0)
    return (keep, ahead, behind)


def gelu_pair(values):
    square = values * values
    inner = math.sqrt(2.0 / math.pi) * values * (1.0 + 0.044715 * square)
    bent = jnp.tanh(inner)
    half = 0.5 * (1.0 + bent)
    slope = half + 0.5 * values * (1.0 - bent * bent) * math.sqrt(2.0 / math.pi) * (
        1.0 + 3.0 * 0.044715 * square
    )
    return (values * half, slope)


def take(array, index, axis=0):
    return lax.dynamic_index_in_dim(array, index, axis, keepdims=False)


def summed(*terms):
    total = terms[0].astype(jnp.float32)
    for term in terms[1:]:
        total = total + term.astype(jnp.float32)
    return total


def contract(left, right, left_axis, right_axis):
    return lax.dot_general(
        left, right, (((left_axis,), (right_axis,)), ((), ())), preferred_element_type=jnp.float32
    )


MESH_ID = pl.DeviceIdType.MESH


def remote(source, target, send_sem, recv_sem, axis, peer):
    return pltpu.make_async_remote_copy(
        src_ref=source,
        dst_ref=target,
        send_sem=send_sem,
        recv_sem=recv_sem,
        device_id={axis: peer},
        device_id_type=MESH_ID,
    )


def greet_line():
    size = lax.axis_size("dp")
    place = lax.axis_index("dp")
    barrier = pltpu.get_barrier_semaphore()
    core = lax.rem(place, 2)
    peers = [place + 1 - 2 * core, lax.rem(place + 2, size), lax.rem(place + size - 2, size)]
    for peer in peers:
        pl.semaphore_signal(barrier, inc=1, device_id={"dp": peer}, device_id_type=MESH_ID)
    return (barrier, len(peers))


PIECES = 2
VMEM_LIMIT = 60 * 1024 * 1024


def piecewise(body, first=0, last=PIECES):
    def once(piece, carry):
        body(piece)
        return carry

    lax.fori_loop(first, last, once, 0)


class LineGather:
    def __init__(self, own, full, send, recv):
        self.count = lax.axis_size("dp") // 2
        self.place = lax.axis_index("dp")
        self.spot = self.place // 2
        self.core = lax.rem(self.place, 2)
        self.own, self.full, self.send, self.recv = own, full, send, recv
        self.rows = own.shape[0]
        self.part = self.rows // PIECES

    def copy(self, kind, step, piece, chip, peer, from_own=False):
        offset = piece * self.part
        start = pl.multiple_of((2 * chip + self.core) * self.rows + offset, self.part)
        block = self.full.at[pl.ds(start, self.part), :]
        source = block
        if from_own:
            source = self.own.at[pl.ds(pl.multiple_of(offset, self.part), self.part), :]
        sems = (self.send.at[kind, step, piece], self.recv.at[kind, step, piece])
        return remote(source, block, *sems, "dp", peer)

    def rise(self, step, piece):
        return self.copy(0, step, piece, self.spot - step + 1, self.place + 2, step == 1)

    def fall(self, step, piece):
        return self.copy(1, step, piece, self.spot + step - 1, self.place - 2, step == 1)

    def show(self, kind, step, piece):
        chip = self.spot - step if kind == 2 else self.spot + step
        return self.copy(kind, step, piece, chip, self.place + 1 - 2 * self.core, step == 0)

    def keep(self):
        start = pl.multiple_of(self.place * self.rows, self.rows)
        target = self.full.at[pl.ds(start, self.rows), :]
        return pltpu.make_async_copy(self.own, target, self.send.at[3, 0, 0])

    def start(self):
        def body(piece):
            pl.when(self.spot + 1 < self.count)(lambda: self.rise(1, piece).start())
            pl.when(self.spot > 0)(lambda: self.fall(1, piece).start())
            self.show(2, 0, piece).start()

        piecewise(body)
        self.keep().start()

    def advance(self, step, first=0, last=PIECES):
        def body(piece):
            @pl.when(self.spot >= step)
            def _():
                self.rise(step, piece).wait_recv()
                pl.when(self.spot + 1 < self.count)(lambda: self.rise(step + 1, piece).start())
                self.show(2, step, piece).start()

            @pl.when(self.spot + step < self.count)
            def _():
                self.fall(step, piece).wait_recv()
                pl.when(self.spot > 0)(lambda: self.fall(step + 1, piece).start())
                self.show(3, step, piece).start()

        piecewise(body, first, last)

    def finish(self):
        self.keep().wait()

        def body(piece):
            self.show(2, 0, piece).wait()
            for step in range(1, self.count):
                rises = (self.spot + 1 < self.count) & (self.spot >= step - 1)
                falls = (self.spot > 0) & (self.spot + step - 1 < self.count)
                above = self.spot + step < self.count
                pl.when(rises)(lambda step=step: self.rise(step, piece).wait_send())
                pl.when(falls)(lambda step=step: self.fall(step, piece).wait_send())
                pl.when(self.spot >= step)(lambda step=step: self.show(2, step, piece).wait())
                pl.when(above)(lambda step=step: self.show(3, step, piece).wait())

        piecewise(body)


def gather_sems():
    count = lax.axis_size("dp") // 2
    return [pltpu.SemaphoreType.DMA((4, count + 1, PIECES)) for _ in range(2)]


def by_rows(rows, step, body):
    def once(index, carry):
        body(pl.ds(pl.multiple_of(index * step, step), step))
        return carry

    lax.fori_loop(0, rows // step, once, 0)


class LineSum:
    def __init__(self, blocks, from_below, from_above, send, recv):
        self.count = lax.axis_size("dp") // 2
        self.place = lax.axis_index("dp")
        self.spot = self.place // 2
        self.blocks, self.below, self.above = blocks, from_below, from_above
        self.send, self.recv = send, recv
        self.part = blocks.shape[1] // PIECES

    def rows(self, piece):
        return pl.ds(pl.multiple_of(piece * self.part, self.part), self.part)

    def move(self, kind, slots, step, piece, peer, block=None):
        rows = self.rows(piece)
        source = self.blocks.at[block, rows, :] if block is not None else slots.at[step - 2, rows, :]
        sems = (self.send.at[kind, step, piece], self.recv.at[kind, step, piece])
        return remote(source, slots.at[step - 1, rows, :], *sems, "dp", peer)

    def rise(self, step, piece, block=None):
        return self.move(0, self.below, step, piece, self.place + 2, block)

    def fall(self, step, piece, block=None):
        return self.move(1, self.above, step, piece, self.place - 2, block)

    def add(self, slots, step, block, piece):
        def body(rows):
            here = pl.ds(pl.multiple_of(piece * self.part + rows.start, rows.size), rows.size)
            total = slots[step - 2, here, :].astype(jnp.float32)
            total = total + self.blocks[block, here, :].astype(jnp.float32)
            slots[step - 2, here, :] = total.astype(jnp.bfloat16)

        by_rows(self.part, 16, body)

    def advance(self, step, first=0, last=PIECES):
        end = self.count - 1
        mirrored = end - self.spot

        def body(piece):
            pl.when(self.spot == 0)(lambda: self.rise(step, piece, self.count - step).start())
            pl.when(mirrored == 0)(lambda: self.fall(step, piece, step - 1).start())
            if step == 1:
                return

            @pl.when((self.spot > 0) & (self.spot < end) & (self.spot < step))
            def _():
                self.rise(step - 1, piece, 0).wait_recv()
                self.add(self.below, step, self.count + self.spot - step, piece)
                self.rise(step, piece).start()

            @pl.when((mirrored > 0) & (mirrored < end) & (mirrored < step))
            def _():
                self.fall(step - 1, piece, 0).wait_recv()
                self.add(self.above, step, self.spot - self.count + step, piece)
                self.fall(step, piece).start()

        piecewise(body, first, last)

    def hand_out(self, up_out, down_out):
        end = self.count - 1
        mirrored = end - self.spot

        def body(piece):
            rows = self.rows(piece)

            def move(out, slots, block):
                def once(small):
                    here = pl.ds(pl.multiple_of(rows.start + small.start, small.size), small.size)
                    total = self.blocks[block, here, :].astype(jnp.float32)
                    if slots is not None:
                        total = total + slots[end - 2, here, :].astype(jnp.float32)
                    out[here, :] = total.astype(jnp.bfloat16)

                by_rows(self.part, 16, once)

            pl.when(self.spot == 0)(lambda: move(up_out, None, 1))
            pl.when(mirrored == 0)(lambda: move(down_out, None, end - 1))

            @pl.when((self.spot > 0) & (self.spot < end))
            def _():
                self.rise(end - 1, piece, 0).wait_recv()
                move(up_out, self.below, self.spot + 1)

            @pl.when((mirrored > 0) & (mirrored < end))
            def _():
                self.fall(end - 1, piece, 0).wait_recv()
                move(down_out, self.above, self.spot - 1)

            pl.when(self.spot == end)(lambda: move(up_out, None, 0))
            pl.when(mirrored == end)(lambda: move(down_out, None, 0))
            for step in range(1, end):
                rises = (self.spot < step) & (self.spot < end)
                falls = (mirrored < step) & (mirrored < end)
                pl.when(rises)(lambda step=step: self.rise(step, piece, 0).wait_send())
                pl.when(falls)(lambda step=step: self.fall(step, piece, 0).wait_send())

        piecewise(body)

    def finish(self, out, first=0, last=PIECES):
        end = self.count - 1
        mirrored = end - self.spot

        def body(piece):
            start = piece * self.part

            def small(rows):
                return pl.ds(pl.multiple_of(start + rows.start, rows.size), rows.size)

            def begin(rows):
                out[small(rows), :] = self.blocks[self.spot, small(rows), :].astype(jnp.float32)

            by_rows(self.part, 16, begin)

            def gain(slots):
                def once(rows):
                    here = small(rows)
                    out[here, :] = out[here, :] + slots[end - 1, here, :].astype(jnp.float32)

                by_rows(self.part, 16, once)

            @pl.when(self.spot > 0)
            def _():
                self.rise(end, piece, 0).wait_recv()
                gain(self.below)

            @pl.when(self.spot < end)
            def _():
                self.fall(end, piece, 0).wait_recv()
                gain(self.above)

            for step in range(1, self.count):
                rises = (self.spot < step) & (self.spot < end)
                falls = (mirrored < step) & (mirrored < end)
                pl.when(rises)(lambda step=step: self.rise(step, piece, 0).wait_send())
                pl.when(falls)(lambda step=step: self.fall(step, piece, 0).wait_send())

        piecewise(body, first, last)


def sum_scratch(rows, columns):
    count = lax.axis_size("dp") // 2
    return [
        pltpu.VMEM((count - 1, rows, columns), jnp.bfloat16),
        pltpu.VMEM((count - 1, rows, columns), jnp.bfloat16),
        pltpu.SemaphoreType.DMA((2, count, PIECES)),
        pltpu.SemaphoreType.DMA((2, count, PIECES)),
    ]


class PairProducts:
    def __init__(self, lefts, rights, parcel, sums, send, recv):
        self.count = lax.axis_size("dp") // 2
        self.place = lax.axis_index("dp")
        self.core = lax.rem(self.place, 2)
        self.lefts, self.rights = lefts, rights
        self.parcel, self.sums, self.send, self.recv = parcel, sums, send, recv

    def copy(self, chip):
        return remote(
            self.parcel.at[chip],
            self.sums.at[chip],
            self.send.at[chip],
            self.recv.at[chip],
            "dp",
            self.place + 1 - 2 * self.core,
        )

    def product(self, chip, core, quarter):
        rows = self.sums.shape[1]
        width = self.sums.shape[2] // 4
        start = pl.multiple_of((2 * chip + core) * rows, rows)
        left = self.lefts[quarter][:, pl.ds(start, rows)]
        ref, first = self.rights[quarter]
        return contract(left, ref[:, pl.ds(first, width)], 0, 0)

    def far(self):
        width = self.sums.shape[2] // 4

        def once(chip, carry):
            for quarter in range(4):
                piece = self.product(chip, 1 - self.core, quarter)
                self.parcel[chip, :, pl.ds(quarter * width, width)] = piece.astype(jnp.bfloat16)
            self.copy(chip).start()
            return carry

        lax.fori_loop(0, self.count, once, 0)

    def near(self):
        width = self.sums.shape[2] // 4

        def once(chip, carry):
            self.copy(chip).wait()
            for quarter in range(4):
                columns = pl.ds(quarter * width, width)
                piece = self.product(chip, self.core, quarter)
                total = piece + self.sums[chip, :, columns].astype(jnp.float32)
                self.sums[chip, :, columns] = total.astype(jnp.bfloat16)
            return carry

        lax.fori_loop(0, self.count, once, 0)


def pair_scratch(rows, columns):
    count = lax.axis_size("dp") // 2
    return [
        pltpu.VMEM((count, rows, columns), jnp.bfloat16),
        pltpu.SemaphoreType.DMA((count,)),
        pltpu.SemaphoreType.DMA((count,)),
    ]


class BlockGather:
    def __init__(self, own, full, send, recv):
        self.size = lax.axis_size("mp")
        self.place = lax.axis_index("mp")
        self.own, self.full, self.send, self.recv = own, full, send, recv
        self.rows, self.width = own.shape

    def spread(self, index, rows, owner, peer, first):
        start = pl.multiple_of(owner * self.width, self.width)
        target = self.full.at[rows, pl.ds(start, self.width)]
        source = self.own if first else target
        return remote(source, target, self.send.at[index], self.recv.at[index], "mp", peer)

    def copy(self, index):
        every = pl.ds(0, self.rows)
        if self.size != 4:
            return self.spread(index, every, self.place, lax.rem(self.place + 1 + index, self.size), True)
        beside = self.place + 1 - 2 * lax.rem(self.place, 2)
        above = lax.rem(self.place + 2, 4)
        half = self.rows // 2
        if index < 2:
            return self.spread(index, every, self.place, (beside, above)[index], True)
        if index == 2:
            return self.spread(2, pl.ds(0, half), above, beside, False)
        return self.spread(3, pl.ds(half, half), beside, above, False)

    def keep(self):
        start = pl.multiple_of(self.place * self.width, self.width)
        target = self.full.at[:, pl.ds(start, self.width)]
        return pltpu.make_async_copy(self.own, target, self.send.at[self.size])

    def start(self):
        for index in range(2 if self.size == 4 else self.size - 1):
            self.copy(index).start()
        self.keep().start()

    def forward(self):
        if self.size == 4:
            self.copy(1).wait_recv()
            self.copy(2).start()
            self.copy(0).wait_recv()
            self.copy(3).start()

    def finish(self):
        self.keep().wait()
        for index in range(4 if self.size == 4 else self.size - 1):
            self.copy(index).wait_send()
            if index > 1 or self.size != 4:
                self.copy(index).wait_recv()


def block_sems():
    size = lax.axis_size("mp") + 1
    return [pltpu.SemaphoreType.DMA((size,)), pltpu.SemaphoreType.DMA((size,))]


def field_rows(spread_ref, first_row, index, piece):
    dp_size = lax.axis_size("dp")
    first = lax.axis_index("mp") * dp_size
    devices = [first + owner for owner in range(dp_size)]
    row, lane = divmod(index * piece, LANES)
    return vector_rows(spread_ref, devices, first_row + row, piece, lane)


def vector_rows(spread_ref, devices, row, piece, turn_to=0):
    if piece >= LANES:
        return [
            spread_ref[device, row + part : row + part + 1, :]
            for device in devices
            for part in range(piece // LANES)
        ]
    lane = lax.broadcasted_iota(jnp.int32, (1, LANES), 1)
    fold = LANES // piece
    groups = []
    for first in range(0, len(devices), fold):
        group = jnp.zeros((1, LANES), jnp.float32)
        for part in range(fold):
            values = spread_ref[devices[first + part], row : row + 1, :]
            turn = (part * piece - turn_to) % LANES
            values = pltpu.roll(values, turn, 1) if turn else values
            mine = (lane >= part * piece) & (lane < (part + 1) * piece)
            group = jnp.where(mine, values, group)
        groups.append(group)
    return groups


def cast_rows(source, target, here):
    target[here, :] = source[here, :].astype(target.dtype)


def first_kernel(
    piece,
    up_piece,
    slots,
    w_up_ref,
    w_qkv_ref,
    w_out_ref,
    w_down_ref,
    x_ref,
    gy_ref,
    small_ref,
    ends_ref,
    turned_out,
    full_ref,
    next_full,
    xn_ref,
    gy_full,
    spread_ref,
    stats_ref,
    act_out,
    slope_out,
    sums_ref,
    gather_send,
    gather_recv,
    next_send,
    next_recv,
    x_send,
    x_recv,
    gy_send,
    gy_recv,
    small_send,
    small_recv,
    parcel,
    pair_send,
    pair_recv,
    x_full,
    up_ref,
    act_ref,
    slope_ref,
    local_sems,
    block_ref,
    next_ref,
    valid_ref,
):
    columns = lax.axis_size("dp")
    total = columns * lax.axis_size("mp")
    mp_place = lax.axis_index("mp")
    place = mp_place * columns + lax.axis_index("dp")
    barrier = pltpu.get_barrier_semaphore()

    def device(step):
        peer = lax.rem(place + step, total)
        return {"mp": peer // columns, "dp": lax.rem(peer, columns)}

    def greet(step, carry):
        pl.semaphore_signal(barrier, inc=1, device_id=device(step), device_id_type=MESH_ID)
        return carry

    lax.fori_loop(1, total, greet, 0)
    by_rows(block_ref.shape[0], 64, lambda here: cast_rows(w_up_ref, block_ref, here))
    pl.semaphore_wait(barrier, total - 1)

    def small_copy(step):
        return pltpu.make_async_remote_copy(
            src_ref=small_ref.at[0],
            dst_ref=spread_ref.at[place],
            send_sem=small_send.at[step],
            recv_sem=small_recv.at[step],
            device_id=device(step),
            device_id_type=MESH_ID,
        )

    def begin(step, carry):
        small_copy(step).start()
        return carry

    def end(step, carry):
        small_copy(step).wait()
        return carry

    weight = LineGather(block_ref, full_ref, gather_send, gather_recv)
    later = LineGather(next_ref, next_full, next_send, next_recv)
    rows_x = BlockGather(x_ref, x_full, x_send, x_recv)
    rows_gy = BlockGather(gy_ref, gy_full, gy_send, gy_recv)
    products = PairProducts(
        [gy_full] * 4, quarters(act_ref), parcel, sums_ref, pair_send, pair_recv
    )
    lax.fori_loop(1, total, begin, 0)
    weight.start()
    rows_x.start()
    rows_gy.start()
    spread_ref[place] = small_ref[0]
    rows, width = xn_ref.shape
    depth = block_ref.shape[0]
    head_cols = w_qkv_ref.shape[2]
    for kind in range(3):
        next_ref[:, pl.ds(kind * head_cols, head_cols)] = w_qkv_ref[kind].astype(jnp.bfloat16)
    turned = jnp.transpose(w_out_ref[...]).astype(jnp.bfloat16)
    next_ref[:, pl.ds(3 * head_cols, head_cols)] = turned

    def turn_down(here):
        turned_out[:, here] = jnp.transpose(w_down_ref[here, :]).astype(jnp.bfloat16)

    by_rows(w_down_ref.shape[0], depth, turn_down)

    def mark(here):
        ids = lax.broadcasted_iota(jnp.int32, (ROW_TILE, 1), 0) + here.start
        valid = segment_of(ends_ref[0:1, :], ids, 1, slots)[2]
        valid_ref[here, :] = jnp.where(valid, 1.0, 0.0)

    by_rows(rows, ROW_TILE, mark)
    lax.fori_loop(1, total, end, 0)
    weight.advance(1)
    weight.advance(2)
    rows_x.forward()
    rows_gy.forward()
    weight.advance(3, 0, 1)
    later.start()
    weight.advance(3, 1)
    for step in range(4, weight.count):
        weight.advance(step)
    rows_x.finish()

    gains = vector_rows(spread_ref, range(total), 0, piece)
    shifts = vector_rows(spread_ref, range(total), 0, piece, piece)

    def normalize(here):
        values = x_full[here, :].astype(jnp.float32)
        mean = jnp.sum(values, axis=1, keepdims=True) * (1.0 / width)
        square = jnp.sum(values * values, axis=1, keepdims=True) * (1.0 / width)
        inv_std = lax.rsqrt(square - mean * mean + norm_eps)
        lanes = lax.broadcasted_iota(jnp.int32, (ROW_TILE, LANES), 1)
        stats_ref[here, :] = jnp.where(
            lanes == 0, mean, jnp.where(lanes == 1, inv_std, valid_ref[here, :])
        )
        for group in range(width // LANES):
            part = (x_full[here, pl.ds(group * LANES, LANES)].astype(jnp.float32) - mean) * inv_std
            part = part * gains[group] + shifts[group]
            xn_ref[here, pl.ds(group * LANES, LANES)] = part.astype(jnp.bfloat16)

    by_rows(rows, ROW_TILE, normalize)
    weight.finish()
    load = pltpu.make_async_copy(full_ref, up_ref, local_sems.at[0])
    load.start()
    rows_gy.finish()

    def blank(here):
        kept = gy_full[here, :].astype(jnp.float32) * valid_ref[here, :]
        gy_full[here, :] = kept.astype(jnp.bfloat16)

    by_rows(rows, ROW_TILE, blank)
    bias = vector_rows(
        spread_ref, [mp_place * columns + owner for owner in range(columns)], 1, up_piece
    )
    quarter_width = up_ref.shape[1] // 4
    groups = quarter_width // LANES
    load.wait()

    def tile(here):
        for quarter in range(4):
            part = pl.ds(quarter * quarter_width, quarter_width)
            shift = jnp.concatenate(bias[quarter * groups : (quarter + 1) * groups], axis=1)
            hidden = contract(xn_ref[here, :], up_ref[:, part], 1, 0) + shift
            activated, slope = gelu_pair(hidden)
            act_ref[here, part] = activated.astype(jnp.bfloat16)
            slope_ref[here, part] = slope.astype(jnp.bfloat16)

    by_rows(rows // 2, ROW_TILE, tile)
    later.advance(1)
    by_rows(rows // 2, ROW_TILE, lambda here: tile(pl.ds(rows // 2 + here.start, here.size)))
    stores = [
        pltpu.make_async_copy(act_ref, act_out, local_sems.at[1]),
        pltpu.make_async_copy(slope_ref, slope_out, local_sems.at[2]),
    ]
    for store in stores:
        store.start()
    later.advance(2, 0, 1)
    products.far()
    later.advance(2, 1)
    products.near()
    for step in range(3, later.count):
        later.advance(step)
    later.finish()
    for store in stores:
        store.wait()


def first_step(weights, tokens, cotangent, small, ends, slots, piece, up_piece):
    mp_size, dp_size = (lax.axis_size("mp"), lax.axis_size("dp"))
    count = dp_size // 2
    rows = tokens.shape[0]
    wide = (rows, tokens.shape[1] * mp_size)
    part, columns = weights[0].shape
    total = mp_size * dp_size
    low = jnp.bfloat16
    return carrying(
        functools.partial(first_kernel, piece, up_piece, slots),
        1,
        weights + (tokens, cotangent, small, ends),
        "vvvvhhvv",
        [
            ((part, columns), low),
            ((part * dp_size, columns), low),
            ((part * dp_size, columns), low),
            (wide, low),
            (wide, low),
            ((total,) + small.shape[1:], jnp.float32),
            ((rows, LANES), jnp.float32),
            ((rows, columns), low),
            ((rows, columns), low),
            ((count, part, columns), low),
        ],
        "vhhvvvvhhv",
        gather_sems()
        + gather_sems()
        + block_sems()
        + block_sems()
        + [pltpu.SemaphoreType.DMA((total,)), pltpu.SemaphoreType.DMA((total,))]
        + pair_scratch(part, columns)
        + [
            pltpu.VMEM(wide, low),
            pltpu.VMEM((part * dp_size, columns), low),
            pltpu.VMEM((rows, columns), low),
            pltpu.VMEM((rows, columns), low),
            pltpu.SemaphoreType.DMA((3,)),
            pltpu.VMEM((part, columns), low),
            pltpu.VMEM((part, columns), low),
            pltpu.VMEM((rows, 1), jnp.float32),
        ],
        4 * rows * wide[1] * columns,
        "gathers_beside_hidden",
    )


def greet_and_wait():
    barrier, count = greet_line()
    pl.semaphore_wait(barrier, count)


def quarters(ref):
    width = ref.shape[1] // 4
    return [(ref, quarter * width) for quarter in range(4)]


def carrying(kernel, collective_id, operands, in_places, outs, out_places, scratch, flops, name):
    spaces = {"h": pl.BlockSpec(memory_space=pl.ANY), "v": pl.BlockSpec(memory_space=pltpu.VMEM)}
    return pl.pallas_call(
        kernel,
        in_specs=[spaces[place] for place in in_places],
        out_specs=[spaces[place] for place in out_places],
        out_shape=[jax.ShapeDtypeStruct(shape, dtype) for shape, dtype in outs],
        scratch_shapes=scratch,
        compiler_params=pltpu.CompilerParams(
            collective_id=collective_id, has_side_effects=True, vmem_limit_bytes=VMEM_LIMIT
        ),
        cost_estimate=pl.CostEstimate(flops=flops, bytes_accessed=1 << 25, transcendentals=0),
        name=name,
    )(*operands)


def third_kernel(
    head_cols,
    slots,
    piece,
    field_row,
    block_ref,
    ready_hbm,
    xn_hbm,
    gy_hbm,
    weight_hbm,
    spread_ref,
    ends_ref,
    ends_col_ref,
    full_ref,
    grad_out,
    or_out,
    sums_ref,
    owned_ref,
    vector_ref,
    gather_send,
    gather_recv,
    below,
    above,
    line_send,
    line_recv,
    parcel,
    pair_send,
    pair_recv,
    mask_ref,
    low_ref,
    go_ref,
    dq_acc,
    dk_acc,
    dv_acc,
    ready_ref,
    xn_ref,
    gy_ref,
    weight_ref,
    grad_ref,
    or_ref,
    local_sems,
    keep_ref,
    ahead_ref,
    behind_ref,
):
    loads = [
        pltpu.make_async_copy(source, target, local_sems.at[index])
        for index, (source, target) in enumerate(
            [(ready_hbm, ready_ref), (xn_hbm, xn_ref), (weight_hbm, weight_ref), (gy_hbm, gy_ref)]
        )
    ]
    for load in loads:
        load.start()
    weight = LineGather(block_ref, full_ref, gather_send, gather_recv)
    line = LineSum(ready_ref, below, above, line_send, line_recv)
    rights = [(grad_ref, kind * head_cols) for kind in range(3)] + [(or_ref, 0)]
    products = PairProducts(
        [xn_ref] * 3 + [gy_ref], rights, parcel, sums_ref, pair_send, pair_recv
    )
    greet_and_wait()
    weight.start()
    loads[0].wait()
    line.advance(1)

    rows = xn_ref.shape[0]
    tiles = rows // ROW_TILE
    scale = HEAD_DIM ** (-0.5)
    row_positions = lax.broadcasted_iota(jnp.int32, (1, rows), 1)
    seg_row, _, row_valid = segment_of(ends_col_ref[...], row_positions, 0, slots)
    seg_row = jnp.where(row_valid, seg_row, slots + row_positions)
    for tile in range(tiles):
        here = pl.ds(tile * ROW_TILE, ROW_TILE)
        reach = (tile + 1) * ROW_TILE
        shape = (ROW_TILE, reach)
        ids = lax.broadcasted_iota(jnp.int32, (ROW_TILE, 1), 0) + tile * ROW_TILE
        seg_col, starting, valid = segment_of(ends_ref[0:1, :], ids, 1, slots)
        seg_col = jnp.where(valid, seg_col, slots + ids)
        tables = rope_tables((ids - starting).astype(jnp.float32))
        for ref, table in zip((keep_ref, ahead_ref, behind_ref), tables):
            ref[here, :] = table
        key_ids = lax.broadcasted_iota(jnp.int32, shape, 1)
        allowed = (seg_col == seg_row[:, :reach]) & (key_ids <= ids)
        mask_ref[here, pl.ds(0, reach)] = jnp.where(allowed, 0.0, masked_score)
    biases = [
        jnp.concatenate(field_rows(spread_ref, field_row, kind, piece), axis=1) for kind in range(3)
    ]

    def turned(values, here, direction):
        ahead = pltpu.roll(values, LANES - ROT_DIM // 2, 1)
        behind = pltpu.roll(values, ROT_DIM // 2, 1)
        return values * keep_ref[here, :] + direction * (
            ahead * ahead_ref[here, :] + behind * behind_ref[here, :]
        )

    def project(here):
        for kind in range(3):
            columns = pl.ds(kind * head_cols, head_cols)
            values = contract(xn_ref[here, :], weight_ref[:, columns], 1, 0) + biases[kind]
            if kind == 2:
                low_ref[here, columns] = values.astype(jnp.bfloat16)
                continue
            for first in range(0, head_cols, LANES):
                part = turned(values[:, first : first + LANES], here, 1.0).astype(jnp.bfloat16)
                if kind == 0:
                    part = part * scale
                low_ref[here, pl.ds(kind * head_cols + first, LANES)] = part
        columns = pl.ds(3 * head_cols, head_cols)
        values = contract(gy_ref[here, :], weight_ref[:, columns], 1, 0)
        go_ref[here, :] = values.astype(jnp.bfloat16)

    for load in loads[1:]:
        load.wait()
    by_rows(rows, ROW_TILE, project)
    vector_ref[...] = jnp.zeros_like(vector_ref)

    lane = lax.broadcasted_iota(jnp.int32, (ROW_TILE, LANES), 1)
    first_head = lane < HEAD_DIM

    def one_pair(pair, carry):
        column = pl.multiple_of(pair * LANES, LANES)
        q_lanes = pl.ds(column, LANES)
        k_lanes = pl.ds(pl.multiple_of(head_cols + column, LANES), LANES)
        v_lanes = pl.ds(pl.multiple_of(2 * head_cols + column, LANES), LANES)
        dk_acc[...] = jnp.zeros_like(dk_acc)
        dv_acc[...] = jnp.zeros_like(dv_acc)
        for tile in range(tiles):
            here = pl.ds(tile * ROW_TILE, ROW_TILE)
            keys = pl.ds(0, (tile + 1) * ROW_TILE)
            outs = []
            query_grads = []
            for head in range(LANES // HEAD_DIM):
                mine = first_head if head == 0 else jnp.logical_not(first_head)
                none = jnp.zeros((ROW_TILE, LANES), jnp.bfloat16)
                query = jnp.where(mine, low_ref[here, q_lanes], none)
                grad_out = jnp.where(mine, go_ref[here, q_lanes], none)
                scores = contract(query, low_ref[keys, k_lanes], 1, 1) + mask_ref[here, keys]
                peak = jnp.max(scores, axis=1, keepdims=True)
                weights = jnp.exp(scores - peak)
                share = 1.0 / jnp.sum(weights, axis=1, keepdims=True)
                probs = weights * share
                probs_low = probs.astype(jnp.bfloat16)
                outs.append(contract(probs_low, low_ref[keys, v_lanes], 1, 0))
                grad_probs = contract(grad_out, low_ref[keys, v_lanes], 1, 1)
                delta = jnp.sum(probs * grad_probs, axis=1, keepdims=True)
                grad_scores = (probs * (grad_probs - delta)).astype(jnp.bfloat16)
                query_grads.append(contract(grad_scores, low_ref[keys, k_lanes], 1, 0))
                dk_acc[keys, :] += contract(grad_scores, query, 0, 0)
                dv_acc[keys, :] += contract(probs_low, grad_out, 0, 0)
            or_ref[here, q_lanes] = jnp.where(first_head, outs[0], outs[1]).astype(jnp.bfloat16)
            dq_acc[here, :] = jnp.where(first_head, query_grads[0], query_grads[1])
        for tile in range(tiles):
            here = pl.ds(tile * ROW_TILE, ROW_TILE)
            parts = [
                (q_lanes, turned(dq_acc[here, :], here, -1.0) * scale),
                (k_lanes, turned(dk_acc[here, :], here, -1.0)),
                (v_lanes, dv_acc[here, :]),
            ]
            for lanes, part in parts:
                part = part.astype(jnp.bfloat16)
                grad_ref[here, lanes] = part
                vector_ref[0:1, lanes] += jnp.sum(part.astype(jnp.float32), axis=0, keepdims=True)

        @pl.when(pair == 0)
        def _():
            weight.advance(1)
            line.advance(2)

        @pl.when(pair == 1)
        def _():
            weight.advance(2, 0, 1)
            line.advance(3, 0, 1)

        return carry

    lax.fori_loop(0, head_cols // LANES, one_pair, 0)
    stores = [
        pltpu.make_async_copy(grad_ref, grad_out, local_sems.at[4]),
        pltpu.make_async_copy(or_ref, or_out, local_sems.at[5]),
    ]
    for store in stores:
        store.start()
    weight.advance(2, 1)
    line.advance(3, 1)
    products.far()
    weight.advance(3, 0, 1)
    products.near()
    weight.advance(3, 1)
    for step in range(4, weight.count):
        weight.advance(step)
        line.advance(step)
    line.finish(owned_ref)
    weight.finish()
    for store in stores:
        store.wait()


def third_step(
    block, ready, normed, grad_rows, full_qkvo, spread, ends, ends_col, slots, piece, field_row
):
    rows, width = normed.shape
    count = lax.axis_size("dp") // 2
    columns = full_qkvo.shape[1]
    head_cols = columns // 4
    part = width // (2 * count)
    low = jnp.bfloat16
    return carrying(
        functools.partial(third_kernel, head_cols, slots, piece, field_row),
        5,
        (
            block,
            ready,
            normed,
            grad_rows,
            full_qkvo,
            spread,
            ends,
            ends_col,
        ),
        "hhhhhvvv",
        [
            ((width, block.shape[1]), low),
            ((rows, 3 * head_cols), low),
            ((rows, head_cols), low),
            ((count, part, columns), low),
            ((part, ready.shape[2]), jnp.float32),
            ((8, columns), jnp.float32),
        ],
        "hhhvvv",
        gather_sems()
        + sum_scratch(part, ready.shape[2])
        + pair_scratch(part, columns)
        + [
            pltpu.VMEM((rows, rows), jnp.float32),
            pltpu.VMEM((rows, 3 * head_cols), low),
            pltpu.VMEM((rows, head_cols), low),
            pltpu.VMEM((rows, LANES), jnp.float32),
            pltpu.VMEM((rows, LANES), jnp.float32),
            pltpu.VMEM((rows, LANES), jnp.float32),
            pltpu.VMEM(ready.shape, low),
            pltpu.VMEM((rows, width), low),
            pltpu.VMEM((rows, width), low),
            pltpu.VMEM((width, columns), low),
            pltpu.VMEM((rows, 3 * head_cols), low),
            pltpu.VMEM((rows, head_cols), low),
            pltpu.SemaphoreType.DMA((6,)),
            pltpu.VMEM((rows, LANES), jnp.float32),
            pltpu.VMEM((rows, LANES), jnp.float32),
            pltpu.VMEM((rows, LANES), jnp.float32),
        ],
        4 * rows * width * columns + 12 * rows * rows * head_cols,
        "lines_beside_attention",
    )


def fourth_kernel(
    head_cols,
    piece,
    field_row,
    ready_hbm,
    xn_hbm,
    gy_hbm,
    down_hbm,
    slope_hbm,
    act_hbm,
    or_hbm,
    qkvo_hbm,
    x_ref,
    spread_ref,
    gh_out,
    sums_ref,
    owned_ref,
    vector_ref,
    out_ref,
    below,
    above,
    line_send,
    line_recv,
    parcel,
    pair_send,
    pair_recv,
    t_parts,
    t_got,
    t_send,
    t_recv,
    ready_ref,
    xn_ref,
    gy_ref,
    down_ref,
    wide_ref,
    or_ref,
    weight_ref,
    gh_ref,
    local_sems,
):
    loads = [
        pltpu.make_async_copy(source, target, local_sems.at[index])
        for index, (source, target) in enumerate(
            [
                (ready_hbm, ready_ref),
                (gy_hbm, gy_ref),
                (down_hbm, down_ref),
                (slope_hbm, wide_ref),
                (xn_hbm, xn_ref),
                (or_hbm, or_ref),
                (qkvo_hbm.at[:, pl.ds(3 * head_cols, head_cols)], weight_ref),
            ]
        )
    ]
    for load in loads:
        load.start()
    line = LineSum(ready_ref, below, above, line_send, line_recv)
    branches = BlockScatter(t_parts, t_got, t_send, t_recv)
    products = PairProducts(
        [xn_ref] * 4, quarters(gh_ref), parcel, sums_ref, pair_send, pair_recv
    )
    barrier, count = greet_line()
    count += greet_block()
    pl.semaphore_wait(barrier, count)
    loads[0].wait()
    line.advance(1)
    for load in loads[1:4]:
        load.wait()
    rows, share_width = x_ref.shape
    width = down_ref.shape[1] // 4
    vector_ref[...] = jnp.zeros_like(vector_ref)

    def tile(here):
        for quarter in range(4):
            columns = pl.ds(quarter * width, width)
            grad_act = contract(gy_ref[here, :], down_ref[:, columns], 1, 0)
            grad_hidden = grad_act * wide_ref[here, columns].astype(jnp.float32)
            grad_hidden = grad_hidden.astype(jnp.bfloat16)
            gh_ref[here, columns] = grad_hidden
            vector_ref[0:1, columns] += jnp.sum(
                grad_hidden.astype(jnp.float32), axis=0, keepdims=True
            )

    by_rows(rows, ROW_TILE, tile)
    late = pltpu.make_async_copy(act_hbm, wide_ref, local_sems.at[7])
    late.start()
    store = pltpu.make_async_copy(gh_ref, gh_out, local_sems.at[8])
    store.start()
    for load in loads[4:]:
        load.wait()
    line.advance(2, 0, 1)
    late.wait()

    def branch(share):
        start = pl.multiple_of(branches.owner(share) * share_width, share_width)
        where = pl.ds(start, share_width)

        def once(here):
            part = contract(or_ref[here, :], weight_ref[where, :], 1, 1)
            part = part + contract(wide_ref[here, :], down_ref[where, :], 1, 1)
            t_parts[share, here, :] = part.astype(jnp.bfloat16)

        by_rows(rows, ROW_TILE, once)
        branches.after(share)

    shares = branches.size
    for share in range(shares - 1):
        branch(share)
    line.advance(2, 1)
    branches.second()
    products.far()
    line.advance(3, 0, 1)
    products.near()
    line.advance(3, 1)
    for step in range(4, line.count):
        line.advance(step)
    branch(shares - 1)
    branches.finish()
    biases = [
        jnp.concatenate(field_rows(spread_ref, field_row, kind, piece), axis=1) for kind in (3, 4)
    ]
    for tile_index in range(rows // ROW_TILE):
        here = pl.ds(tile_index * ROW_TILE, ROW_TILE)
        total = x_ref[here, :].astype(jnp.float32) + branches.total(tile_index, ROW_TILE)
        total = total + biases[0] + biases[1]
        out_ref[here, :] = total.astype(jnp.bfloat16)
    line.finish(owned_ref)
    store.wait()


def fourth_step(
    ready,
    normed,
    grad_rows,
    turned_down,
    slope,
    activated,
    attended,
    full_qkvo,
    tokens,
    spread,
    piece,
    field_row,
):
    rows, width = normed.shape
    head_cols = attended.shape[1]
    count, part, columns = ready.shape
    low = jnp.bfloat16
    return carrying(
        functools.partial(fourth_kernel, head_cols, piece, field_row),
        6,
        (
            ready,
            normed,
            grad_rows,
            turned_down,
            slope,
            activated,
            attended,
            full_qkvo,
            tokens,
            spread,
        ),
        "hhhhhhhhvv",
        [
            ((rows, columns), low),
            ((count, part, columns), low),
            ((part, columns), jnp.float32),
            ((8, columns), jnp.float32),
            (tokens.shape, low),
        ],
        "hvvvv",
        sum_scratch(part, columns)
        + pair_scratch(part, columns)
        + scatter_scratch(rows, tokens.shape[1])
        + [
            pltpu.VMEM(ready.shape, low),
            pltpu.VMEM((rows, width), low),
            pltpu.VMEM((rows, width), low),
            pltpu.VMEM((width, columns), low),
            pltpu.VMEM((rows, columns), low),
            pltpu.VMEM((rows, head_cols), low),
            pltpu.VMEM((width, head_cols), low),
            pltpu.VMEM((rows, columns), low),
            pltpu.SemaphoreType.DMA((9,)),
        ],
        6 * rows * width * columns,
        "line_beside_hidden_grad",
    )


def greet_block():
    size = lax.axis_size("mp")
    place = lax.axis_index("mp")
    barrier = pltpu.get_barrier_semaphore()
    for step in range(1, size):
        peer = lax.rem(place + step, size)
        pl.semaphore_signal(barrier, inc=1, device_id={"mp": peer}, device_id_type=MESH_ID)
    return size - 1


class BlockScatter:
    def __init__(self, parts, got, send, recv):
        self.size = lax.axis_size("mp")
        self.place = lax.axis_index("mp")
        self.parts, self.got, self.send, self.recv = parts, got, send, recv
        self.half = parts.shape[1] // 2
        self.beside = self.place + 1 - 2 * lax.rem(self.place, 2)
        self.above = lax.rem(self.place + 2, 4)

    def owner(self, index):
        if self.size == 4:
            return [lax.rem(self.beside + 2, 4), self.beside, self.above, self.place][index]
        return lax.rem(self.place + 1 + index, self.size)

    def copy(self, index):
        if self.size == 4:
            part, bottom, peer = [
                (0, 0, self.beside),
                (0, 1, self.above),
                (1, 0, self.beside),
                (2, 1, self.above),
                (2, 0, self.above),
                (1, 1, self.beside),
            ][index]
            source = self.parts.at[part, pl.ds(bottom * self.half, self.half), :]
        else:
            source = self.parts.at[index]
            peer = self.owner(index)
        sems = (self.send.at[index], self.recv.at[index])
        return remote(source, self.got.at[index], *sems, "mp", peer)

    def after(self, index):
        if self.size != 4:
            if index < self.size - 1:
                self.copy(index).start()
            return
        for number in ((0, 1), (2,), (3,), ())[index]:
            self.copy(number).start()

    def second(self):
        if self.size != 4:
            return
        for number, part, bottom in ((0, 2, 0), (1, 1, 1)):
            self.copy(number).wait_recv()

            def body(rows, number=number, part=part, bottom=bottom):
                here = pl.ds(bottom * self.half + rows.start, rows.size)
                total = summed(self.parts[part, here, :], self.got[number, rows, :])
                self.parts[part, here, :] = total.astype(jnp.bfloat16)

            by_rows(self.half, 64, body)
            self.copy(number + 4).start()

    def finish(self):
        if self.size != 4:
            for index in range(self.size - 1):
                self.copy(index).wait()
            return
        for index in range(6):
            if index > 1:
                self.copy(index).wait_recv()
            self.copy(index).wait_send()

    def total(self, tile, rows):
        here = pl.ds(tile * rows, rows)
        own = self.parts[self.size - 1, here, :]
        if self.size != 4:
            return summed(own, *[self.got[index, here, :] for index in range(self.size - 1)])
        bottom = (tile * rows) // self.half
        there = pl.ds(tile * rows - bottom * self.half, rows)
        return summed(own, self.got[2 + bottom, there, :], self.got[4 + bottom, there, :])


def scatter_scratch(rows, width):
    size = lax.axis_size("mp")
    slots = (6, rows // 2, width) if size == 4 else (size - 1, rows, width)
    return [
        pltpu.VMEM((size, rows, width), jnp.bfloat16),
        pltpu.VMEM(slots, jnp.bfloat16),
        pltpu.SemaphoreType.DMA((slots[0],)),
        pltpu.SemaphoreType.DMA((slots[0],)),
    ]


STREAM = 256
SLOTS = 3


def stream(tiles, loads, stores, compute, primed=False):
    ahead = SLOTS - 1
    if not primed:
        prime(tiles, loads)

    def once(tile, carry):
        slot = lax.rem(tile, SLOTS)

        @pl.when(tile + ahead < tiles)
        def _():
            for copy in loads(tile + ahead, lax.rem(tile + ahead, SLOTS)):
                copy.start()

        for copy in loads(tile, slot):
            copy.wait()

        @pl.when(tile >= SLOTS)
        def _():
            for copy in stores(tile - SLOTS, slot):
                copy.wait()

        compute(tile, slot)
        for copy in stores(tile, slot):
            copy.start()
        return carry

    lax.fori_loop(0, tiles, once, 0)
    for tile in range(max(tiles - SLOTS, 0), tiles):
        for copy in stores(tile, tile % SLOTS):
            copy.wait()


def prime(tiles, loads):
    for tile in range(min(SLOTS - 1, tiles)):
        for copy in loads(tile, tile):
            copy.start()


def fetch(pairs, sems):
    copies = [
        pltpu.make_async_copy(source, target, sems.at[index])
        for index, (source, target) in enumerate(pairs)
    ]
    for copy in copies:
        copy.start()
    return copies


def step_tall(grad, root_left, root_right, master, master_out):
    depth, size = grad.shape
    tile_rows = min(STREAM, size)

    def scope(root_in, side_in, side_new, sems):
        root = root_right[1, 0, 0].astype(jnp.bfloat16)

        def where(tile):
            return pl.ds(pl.multiple_of(tile * tile_rows, tile_rows), tile_rows)

        def loads(tile, slot):
            here = where(tile)
            source = root_left.at[1, 0, 0, here, :]
            return [
                pltpu.make_async_copy(source, root_in.at[slot], sems.at[0, slot]),
                pltpu.make_async_copy(master.at[here, :], side_in.at[slot], sems.at[1, slot]),
            ]

        def stores(tile, slot):
            target = master_out.at[where(tile), :]
            return [pltpu.make_async_copy(side_new.at[slot], target, sems.at[2, slot])]

        def compute(tile, slot):
            first = contract(root_in[slot].astype(jnp.bfloat16), grad[...], 1, 1)
            step = contract(first.astype(jnp.bfloat16), root, 1, 0)
            side_new[slot] = side_in[slot] - matrix_rate * step

        stream(size // tile_rows, loads, stores, compute)

    pl.run_scoped(
        scope,
        pltpu.VMEM((SLOTS, tile_rows, size), jnp.float32),
        pltpu.VMEM((SLOTS, tile_rows, depth), jnp.float32),
        pltpu.VMEM((SLOTS, tile_rows, depth), jnp.float32),
        pltpu.SemaphoreType.DMA((3, SLOTS)),
    )


def step_wide(grad, root_left, root_right, master, master_out):
    depth, size = grad.shape
    tile_rows = min(STREAM, size)
    plane = master.shape[2]

    def scope(root_in, low, sems):
        first = contract(root_left[1, 0, 0].astype(jnp.bfloat16), grad[...], 1, 0)
        low[...] = first.astype(jnp.bfloat16)

        def where(tile):
            return pl.ds(pl.multiple_of(tile * tile_rows, tile_rows), tile_rows)

        def loads(tile, slot):
            source = root_right.at[1, 0, 0, :, where(tile)]
            return [pltpu.make_async_copy(source, root_in.at[slot], sems.at[slot])]

        def compute(tile, slot):
            step = contract(low[...], root_in[slot].astype(jnp.bfloat16), 1, 0)
            start = tile * tile_rows
            here = pl.ds(pl.multiple_of(lax.rem(start, plane), tile_rows), tile_rows)
            kind = start // plane
            master_out[kind, :, here] = master[kind, :, here] - matrix_rate * step

        stream(size // tile_rows, loads, lambda tile, slot: [], compute)

    pl.run_scoped(
        scope,
        pltpu.VMEM((SLOTS, size, tile_rows), jnp.float32),
        pltpu.VMEM((depth, size), jnp.bfloat16),
        pltpu.SemaphoreType.DMA((SLOTS,)),
    )


def fifth_kernel(
    head_cols,
    piece,
    ready_hbm,
    gh_hbm,
    grad_hbm,
    qkvo_ref,
    up_ref,
    x_hbm,
    gy_hbm,
    stats_hbm,
    spread_ref,
    vector_three,
    vector_four,
    down_hbm,
    owned_hbm,
    down_left,
    down_right,
    w_down,
    qkv_left,
    qkv_right,
    w_qkv_hbm,
    out_left,
    out_right,
    w_out,
    dx_out,
    up_send,
    down_send,
    own_ref,
    sums_ref,
    w_down_new,
    w_qkv_out,
    w_out_new,
    below,
    above,
    line_send,
    line_recv,
    g_parts,
    g_got,
    g_send,
    g_recv,
    terms_ref,
    terms_got,
    terms_send,
    terms_recv,
    vector_ref,
    vector_got,
    vector_send,
    vector_recv,
    ready_ref,
    gh_ref,
    grad_ref,
    low_down,
    low_qkv,
    low_out,
    x_ref,
    gy_ref,
    stats_ref,
    owned_down,
    owned_qkvo,
    w_qkv,
    w_qkv_new,
    dx_ref,
    load_sems,
):
    loads = fetch(
        [
            (ready_hbm, ready_ref),
            (grad_hbm, grad_ref),
            (gh_hbm, gh_ref),
            (owned_hbm, owned_qkvo),
            (down_hbm, owned_down),
            (w_qkv_hbm, w_qkv),
            (x_hbm, x_ref),
            (gy_hbm, gy_ref),
            (stats_hbm, stats_ref),
        ],
        load_sems,
    )
    line = LineSum(ready_ref, below, above, line_send, line_recv)
    from_norm = BlockScatter(g_parts, g_got, g_send, g_recv)
    mp_size = from_norm.size
    mp_place = from_norm.place
    dp_size = lax.axis_size("dp")
    dp_place = lax.axis_index("dp")
    rows, width = x_ref.shape
    model_width = width * mp_size
    tiles = rows // ROW_TILE
    barrier = pltpu.get_barrier_semaphore()

    def greet(step, carry):
        peer = lax.rem(dp_place + step, dp_size)
        pl.semaphore_signal(barrier, inc=1, device_id={"dp": peer}, device_id_type=MESH_ID)
        return carry

    lax.fori_loop(1, dp_size, greet, 0)
    pl.semaphore_wait(barrier, dp_size - 1 + greet_block())
    loads[0].wait()
    line.advance(1)
    for load in loads[1:3]:
        load.wait()

    def parts(one_ref, two_ref, sems):
        def load(share):
            start = pl.multiple_of(from_norm.owner(share) * width, width)
            slot = share % 2
            where = pl.ds(start, width)
            narrow = pl.ds(0, 3 * head_cols)
            return [
                pltpu.make_async_copy(qkvo_ref.at[where, narrow], one_ref.at[slot], sems.at[0, slot]),
                pltpu.make_async_copy(up_ref.at[where, :], two_ref.at[slot], sems.at[1, slot]),
            ]

        for copy in load(0):
            copy.start()
        for share in range(mp_size):
            slot = share % 2
            for copy in load(share):
                copy.wait()
            if share + 1 < mp_size:
                for copy in load(share + 1):
                    copy.start()

            def tile(here, share=share, slot=slot):
                part = contract(grad_ref[here, :], one_ref[slot], 1, 1)
                part = part + contract(gh_ref[here, :], two_ref[slot], 1, 1)
                g_parts[share, here, :] = part.astype(jnp.bfloat16)

            by_rows(rows, ROW_TILE, tile)
            from_norm.after(share)

    columns = up_ref.shape[1]
    pl.run_scoped(
        parts,
        pltpu.VMEM((2, width, 3 * head_cols), jnp.bfloat16),
        pltpu.VMEM((2, width, columns), jnp.bfloat16),
        pltpu.SemaphoreType.DMA((2, 2)),
    )
    for step in range(2, line.count - 1):
        line.advance(step)
    from_norm.second()
    for load in loads[3:]:
        load.wait()
    low_down[...] = owned_down[...].astype(jnp.bfloat16)
    low_qkv[...] = owned_qkvo[:, pl.ds(0, 3 * head_cols)].astype(jnp.bfloat16)
    low_out[...] = owned_qkvo[:, pl.ds(3 * head_cols, head_cols)].astype(jnp.bfloat16)
    step_tall(low_out, out_left, out_right, w_out, w_out_new)
    from_norm.finish()

    def lane_pair(first, second):
        lane = lax.broadcasted_iota(jnp.int32, (ROW_TILE, LANES), 1)
        return jnp.where(lane == 0, first, jnp.where(lane == 1, second, 0.0))

    owners = [mp_place * dp_size + owner for owner in range(dp_size)]
    gain = jnp.concatenate(vector_rows(spread_ref, owners, 0, piece), axis=1)
    sums = [jnp.zeros((1, width), jnp.float32) for _ in range(3)]
    for tile in range(tiles):
        here = pl.ds(tile * ROW_TILE, ROW_TILE)
        normalized = (x_ref[here, :].astype(jnp.float32) - stats_ref[here, 0:1]) * stats_ref[here, 1:2]
        grad = from_norm.total(tile, ROW_TILE)
        gained = grad * gain
        terms = lane_pair(
            jnp.sum(gained, axis=1, keepdims=True),
            jnp.sum(gained * normalized, axis=1, keepdims=True),
        )
        terms_ref[:, here] = jnp.transpose(terms)[:8, :]
        upstream = gy_ref[here, :].astype(jnp.float32) * stats_ref[here, 2:3]
        sums[0] += jnp.sum(grad * normalized, axis=0, keepdims=True)
        sums[1] += jnp.sum(grad, axis=0, keepdims=True)
        sums[2] += jnp.sum(upstream, axis=0, keepdims=True)

    vector_ref[...] = jnp.zeros_like(vector_ref)
    vector_ref[0:1, :] = vector_three[0:1, :]
    vector_ref[1:2, :] = vector_four[0:1, :]
    for index in range(3):
        vector_ref[2 + index : 3 + index, pl.ds(0, width)] = sums[index]

    def terms_copy(step):
        peer = lax.rem(mp_place + step, mp_size)
        slot = step - 1
        sems = (terms_send.at[slot], terms_recv.at[slot])
        return remote(terms_ref, terms_got.at[slot], *sems, "mp", peer)

    def vector_copy(step):
        peer = lax.rem(dp_place + step, dp_size)
        slot = step - 1
        sems = (vector_send.at[slot], vector_recv.at[slot])
        return remote(vector_ref, vector_got.at[slot], *sems, "dp", peer)

    def vector_begin(step, carry):
        vector_copy(step).start()
        return carry

    for step in range(1, mp_size):
        terms_copy(step).start()
    lax.fori_loop(1, dp_size, vector_begin, 0)
    step_wide(low_qkv, qkv_left, qkv_right, w_qkv, w_qkv_new)
    stores = [pltpu.make_async_copy(w_qkv_new, w_qkv_out, load_sems.at[len(loads)])]
    stores[0].start()
    for step in range(1, mp_size):
        terms_copy(step).wait()
    for tile in range(tiles):
        here = pl.ds(tile * ROW_TILE, ROW_TILE)
        terms = terms_ref[:, here]
        for slot in range(mp_size - 1):
            terms = terms + terms_got[slot, :, here]
        wide = jnp.concatenate([terms, jnp.zeros((LANES - 8, ROW_TILE), jnp.float32)], axis=0)
        terms = jnp.transpose(wide) * (1.0 / model_width)
        inv_std = stats_ref[here, 1:2]
        normalized = (x_ref[here, :].astype(jnp.float32) - stats_ref[here, 0:1]) * inv_std
        gained = from_norm.total(tile, ROW_TILE) * gain
        upstream = gy_ref[here, :].astype(jnp.float32) * stats_ref[here, 2:3]
        dx_ref[here, :] = upstream + inv_std * (gained - terms[:, 0:1] - normalized * terms[:, 1:2])
    stores.append(pltpu.make_async_copy(dx_ref, dx_out, load_sems.at[len(loads) + 1]))
    stores[1].start()
    step_tall(low_down, down_left, down_right, w_down, w_down_new)

    def vector_end(step, carry):
        vector_copy(step).wait()
        return carry

    lax.fori_loop(1, dp_size, vector_end, 0)
    total = vector_ref[...]
    for slot in range(dp_size - 1):
        total = total + vector_got[slot]
    sums_ref[...] = total
    by_rows(own_ref.shape[0], 32, lambda here: keep_block(ready_ref, line.spot, own_ref, here))
    line.hand_out(up_send, down_send)
    for store in stores:
        store.wait()


def keep_block(blocks, index, out, here):
    out[here, :] = blocks[index, here, :]


def fifth_step(
    ready,
    grad_hidden,
    grad_projected,
    full_qkvo,
    full_up,
    tokens,
    cotangent,
    stats,
    spread,
    vector_three,
    vector_four,
    owned_down,
    owned_qkvo,
    down,
    qkv,
    out,
    piece,
):
    rows, width = tokens.shape
    head_cols = grad_projected.shape[1] // 3
    count, part, columns = ready.shape
    mp_size = lax.axis_size("mp")
    dp_size = lax.axis_size("dp")
    low = jnp.bfloat16
    exact = jnp.float32
    return carrying(
        functools.partial(fifth_kernel, head_cols, piece),
        7,
        (
            ready,
            grad_hidden,
            grad_projected,
            full_qkvo,
            full_up,
            tokens,
            cotangent,
            stats,
            spread,
            vector_three,
            vector_four,
            owned_down,
            owned_qkvo,
        )
        + down
        + qkv
        + out,
        "hhhhhhhhvvvhh" + "hvh" + "vhh" + "hvh",
        [
            ((rows, width), exact),
            ((part, columns), low),
            ((part, columns), low),
            ((part, columns), low),
            ((8, columns), exact),
            (down[2].shape, exact),
            (qkv[2].shape, exact),
            (out[2].shape, exact),
        ],
        "hvvvvhhh",
        sum_scratch(part, columns)
        + scatter_scratch(rows, width)
        + [
            pltpu.VMEM((8, rows), exact),
            pltpu.VMEM((mp_size - 1, 8, rows), exact),
            pltpu.SemaphoreType.DMA((mp_size - 1,)),
            pltpu.SemaphoreType.DMA((mp_size - 1,)),
            pltpu.VMEM((8, columns), exact),
            pltpu.VMEM((dp_size - 1, 8, columns), exact),
            pltpu.SemaphoreType.DMA((dp_size - 1,)),
            pltpu.SemaphoreType.DMA((dp_size - 1,)),
            pltpu.VMEM(ready.shape, low),
            pltpu.VMEM((rows, columns), low),
            pltpu.VMEM((rows, 3 * head_cols), low),
            pltpu.VMEM((part, columns), low),
            pltpu.VMEM((part, 3 * head_cols), low),
            pltpu.VMEM((part, head_cols), low),
            pltpu.VMEM((rows, width), low),
            pltpu.VMEM((rows, width), low),
            pltpu.VMEM(stats.shape, exact),
            pltpu.VMEM((part, columns), exact),
            pltpu.VMEM((part, columns), exact),
            pltpu.VMEM(qkv[2].shape, exact),
            pltpu.VMEM(qkv[2].shape, exact),
            pltpu.VMEM((rows, width), exact),
            pltpu.SemaphoreType.DMA((11,)),
        ],
        4 * rows * width * mp_size * columns,
        "line_beside_norm_grad",
    )


class Averager:
    def __init__(self, grad, stats, stats_out, buffers, sems):
        self.grad, self.stats, self.stats_out = grad, stats, stats_out
        self.stat_in, self.stat_new = buffers
        self.sems = sems
        self.tile_rows = self.stat_in.shape[1]
        self.tiles = grad.shape[1] // self.tile_rows

    def where(self, tile):
        return pl.ds(pl.multiple_of(tile * self.tile_rows, self.tile_rows), self.tile_rows)

    def loads(self, tile, slot):
        source = self.stats.at[0, 0, 0, self.where(tile), :]
        return [pltpu.make_async_copy(source, self.stat_in.at[slot], self.sems.at[0, slot])]

    def stores(self, tile, slot):
        target = self.stats_out.at[0, 0, self.where(tile), :]
        return [pltpu.make_async_copy(self.stat_new.at[slot], target, self.sems.at[1, slot])]

    def compute(self, tile, slot):
        product = contract(self.grad[:, self.where(tile)], self.grad[...], 0, 0)
        self.stat_new[slot] = 0.5 * self.stat_in[slot] + 0.5 * product

    def run(self):
        stream(self.tiles, self.loads, self.stores, self.compute, True)


class Updater(Averager):
    def __init__(self, grad, stats, stats_out, buffers, sems, first, master, master_out, more):
        super().__init__(grad, stats, stats_out, buffers, sems)
        self.first, self.master, self.master_out = first, master, master_out
        self.root_in, self.side_in, self.side_new = more

    def loads(self, tile, slot):
        here = self.where(tile)
        source = self.stats.at[1, 0, 0, :, here]
        return super().loads(tile, slot) + [
            pltpu.make_async_copy(source, self.root_in.at[slot], self.sems.at[2, slot]),
            pltpu.make_async_copy(
                self.master.at[:, here], self.side_in.at[slot], self.sems.at[3, slot]
            ),
        ]

    def stores(self, tile, slot):
        target = self.master_out.at[:, self.where(tile)]
        return super().stores(tile, slot) + [
            pltpu.make_async_copy(self.side_new.at[slot], target, self.sems.at[4, slot])
        ]

    def compute(self, tile, slot):
        super().compute(tile, slot)
        step = contract(self.first[...], self.root_in[slot].astype(jnp.bfloat16), 1, 0)
        self.side_new[slot] = self.side_in[slot] - matrix_rate * step


def average_small(small, small_new, grad):
    small_new[0, 0] = 0.5 * small[0, 0, 0] + 0.5 * contract(grad[...], grad[...], 1, 1)


def statistics_kernel(
    passed,
    owned_down,
    owned_qkvo,
    down_left,
    down_right,
    qkv_left,
    qkv_right,
    out_left,
    out_right,
    *refs,
):
    sources, refs = (refs[:passed], refs[passed:])
    targets, refs = (refs[:passed], refs[passed:])
    held, refs = (refs[:passed], refs[passed:])
    (
        down_left_new,
        down_right_new,
        qkv_left_new,
        qkv_right_new,
        out_left_new,
        out_right_new,
        low_down,
        low_qkv,
        low_out,
        down_in,
        down_new,
        qkv_in,
        qkv_new,
        out_in,
        out_new,
        sems,
        pass_sems,
    ) = refs
    units = [
        Averager(low_down, down_left, down_left_new, (down_in, down_new), sems.at[0]),
        Averager(low_qkv, qkv_right, qkv_right_new, (qkv_in, qkv_new), sems.at[1]),
        Averager(low_out, out_left, out_left_new, (out_in, out_new), sems.at[2]),
    ]
    for unit in units:
        prime(unit.tiles, unit.loads)
    into = fetch(zip(sources, held), pass_sems.at[0])
    edge = low_qkv.shape[1]
    low_down[...] = owned_down[...].astype(jnp.bfloat16)
    low_qkv[...] = owned_qkvo[:, pl.ds(0, edge)].astype(jnp.bfloat16)
    low_out[...] = owned_qkvo[:, pl.ds(edge, low_out.shape[1])].astype(jnp.bfloat16)
    average_small(down_right, down_right_new, low_down)
    average_small(qkv_left, qkv_left_new, low_qkv)
    average_small(out_right, out_right_new, low_out)
    for copy in into:
        copy.wait()
    onward = fetch(zip(held, targets), pass_sems.at[1])
    for unit in units:
        unit.run()
    for copy in onward:
        copy.wait()


def statistics_step(owned, stats, passed):
    exact = jnp.float32
    low = jnp.bfloat16
    spaces = {"h": pl.BlockSpec(memory_space=pl.ANY), "v": pl.BlockSpec(memory_space=pltpu.VMEM)}
    depth = owned[0].shape[0]
    sizes = [stats[0].shape[-1], stats[3].shape[-1], stats[4].shape[-1]]
    shapes = [jax.ShapeDtypeStruct(array.shape, array.dtype) for array in passed]
    scratch = [pltpu.VMEM(array.shape, array.dtype) for array in passed]
    shapes += [jax.ShapeDtypeStruct(array.shape[1:], exact) for array in stats]
    averages = [pltpu.VMEM((depth, size), low) for size in sizes]
    for size in sizes:
        averages += [pltpu.VMEM((SLOTS, min(STREAM, size), size), exact) for _ in range(2)]
    averages += [
        pltpu.SemaphoreType.DMA((3, 2, SLOTS)),
        pltpu.SemaphoreType.DMA((2, len(passed))),
    ]
    count = len(passed)

    def kernel(*refs):
        inputs, rest = (refs[: 8 + count], refs[8 + count :])
        targets, rest = (rest[:count], rest[count:])
        stats_new, rest = (rest[:6], rest[6:])
        statistics_kernel(count, *inputs, *targets, *rest[:count], *stats_new, *rest[count:])

    return pl.pallas_call(
        kernel,
        in_specs=[spaces[place] for place in "vv" + "hvvhhv" + "h" * count],
        out_specs=[spaces[place] for place in "h" * count + "hvvhhv"],
        out_shape=shapes,
        scratch_shapes=scratch + averages,
        compiler_params=pltpu.CompilerParams(vmem_limit_bytes=VMEM_LIMIT),
        cost_estimate=pl.CostEstimate(
            flops=1 << 33, bytes_accessed=sum(array.size * 4 for array in stats), transcendentals=0
        ),
        name="statistics",
    )(*owned, *stats, *passed)


def last_kernel(
    own_ref,
    rising_ref,
    falling_ref,
    up_left,
    up_right,
    w_up,
    up_left_new,
    up_right_new,
    w_up_new,
    low_up,
    first,
    up_in,
    up_new,
    root_in,
    side_in,
    side_new,
    sems,
):
    unit = Updater(
        low_up,
        up_right,
        up_right_new,
        (up_in, up_new),
        sems,
        first,
        w_up,
        w_up_new,
        (root_in, side_in, side_new),
    )
    prime(unit.tiles, unit.loads)
    low_up[...] = summed(own_ref[...], rising_ref[...], falling_ref[...]).astype(jnp.bfloat16)
    root = up_left[1, 0, 0].astype(jnp.bfloat16)
    first[...] = contract(root, low_up[...], 1, 0).astype(jnp.bfloat16)
    average_small(up_left, up_left_new, low_up)
    unit.run()


def last_step(blocks, up_left, up_right, w_up):
    exact = jnp.float32
    low = jnp.bfloat16
    spaces = {"h": pl.BlockSpec(memory_space=pl.ANY), "v": pl.BlockSpec(memory_space=pltpu.VMEM)}
    depth, columns = w_up.shape
    tile_rows = min(STREAM, columns)
    return pl.pallas_call(
        last_kernel,
        in_specs=[spaces[place] for place in "vvvvhh"],
        out_specs=[spaces[place] for place in "vhh"],
        out_shape=[
            jax.ShapeDtypeStruct(up_left.shape[1:], exact),
            jax.ShapeDtypeStruct(up_right.shape[1:], exact),
            jax.ShapeDtypeStruct(w_up.shape, exact),
        ],
        scratch_shapes=[
            pltpu.VMEM((depth, columns), low),
            pltpu.VMEM((depth, columns), low),
            pltpu.VMEM((SLOTS, tile_rows, columns), exact),
            pltpu.VMEM((SLOTS, tile_rows, columns), exact),
            pltpu.VMEM((SLOTS, columns, tile_rows), exact),
            pltpu.VMEM((SLOTS, depth, tile_rows), exact),
            pltpu.VMEM((SLOTS, depth, tile_rows), exact),
            pltpu.SemaphoreType.DMA((5, SLOTS)),
        ],
        compiler_params=pltpu.CompilerParams(vmem_limit_bytes=VMEM_LIMIT),
        cost_estimate=pl.CostEstimate(
            flops=1 << 33, bytes_accessed=12 * columns * columns, transcendentals=0
        ),
        name="last_weight",
    )(*blocks, up_left, up_right, w_up)


def vector_update(state, grad):
    stat_new = 0.5 * state[1] + 0.5 * grad * grad
    param_new = state[0] - vector_rate * grad * lax.rsqrt(stat_new)
    return (param_new, stat_new)


def local(
    tokens,
    cotangent,
    seq_lengths,
    w_qkv,
    qkv_bias_state,
    w_out,
    out_bias_state,
    w_up,
    up_bias_state,
    w_down,
    ln_state,
    qkv_left,
    qkv_right,
    out_left,
    out_right,
    up_left,
    up_right,
    down_left,
    down_right,
):
    row_count, share_width = tokens.shape
    mp_size = lax.axis_size("mp")
    dp_size = lax.axis_size("dp")
    model_width = share_width * mp_size
    own_width = w_qkv.shape[2]
    mp_place = lax.axis_index("mp")

    piece = ln_state.shape[2]
    up_piece = up_bias_state.shape[1]

    def lane_rows(*values):
        flat = jnp.concatenate([value.reshape(-1) for value in values])
        return jnp.pad(flat, (0, -flat.shape[0] % LANES)).reshape(-1, LANES)

    small = jnp.concatenate(
        [
            lane_rows(ln_state[0]),
            lane_rows(up_bias_state[0]),
            lane_rows(qkv_bias_state[0], out_bias_state[0]),
        ],
        axis=0,
    )
    up_rows = lane_rows(up_bias_state[0]).shape[0]
    small = jnp.pad(small, ((0, 8 - small.shape[0]), (0, 0))).astype(jnp.bfloat16)
    slots = seq_lengths.shape[1]
    ends = jnp.pad(
        jnp.cumsum(seq_lengths[0]), (0, LANES - slots), constant_values=2 * row_count
    ).astype(jnp.int32)
    planes = w_qkv.transpose(1, 0, 2)
    (
        turned_block,
        full_up,
        full_qkvo,
        normed,
        grad_rows,
        spread,
        stats,
        activated,
        slope,
        ready_down,
    ) = first_step(
        (w_up, planes, w_out, w_down),
        tokens,
        cotangent,
        small.astype(jnp.float32)[None],
        jnp.broadcast_to(ends[None, :], (8, LANES)),
        slots,
        piece,
        up_piece,
    )
    field_row = 1 + up_rows
    turned_down, grad_projected, attended, ready_qkvo, owned_down, vector_three = third_step(
        turned_block,
        ready_down,
        normed,
        grad_rows,
        full_qkvo,
        spread,
        jnp.broadcast_to(ends[None, :], (8, LANES)),
        ends[:, None],
        slots,
        piece,
        field_row,
    )
    grad_hidden, ready_up, owned_qkvo, vector_four, output = fourth_step(
        ready_qkvo,
        normed,
        grad_rows,
        turned_down,
        slope,
        activated,
        attended,
        full_qkvo,
        tokens,
        spread,
        piece,
        field_row,
    )
    input_grad, up_send, down_send, up_own, sums, new_w_down, new_planes, new_w_out = fifth_step(
        ready_up,
        grad_hidden,
        grad_projected,
        full_qkvo,
        full_up,
        tokens,
        cotangent,
        stats,
        spread,
        vector_three,
        vector_four,
        owned_down,
        owned_qkvo,
        (down_left, down_right, w_down),
        (qkv_left, qkv_right, planes),
        (out_left, out_right, w_out),
        piece,
    )
    steps = range(dp_size - 2)
    rising = lax.ppermute(up_send, "dp", [(place, place + 2) for place in steps])
    falling = lax.ppermute(down_send, "dp", [(place + 2, place) for place in steps])
    (
        output,
        input_grad,
        new_w_down,
        new_planes,
        new_w_out,
        down_left_new,
        down_right_new,
        qkv_left_new,
        qkv_right_new,
        out_left_new,
        out_right_new,
    ) = statistics_step(
        (owned_down, owned_qkvo),
        (down_left, down_right, qkv_left, qkv_right, out_left, out_right),
        (output, input_grad, new_w_down, new_planes, new_w_out),
    )
    up_left_new, up_right_new, new_w_up = last_step(
        (up_own, rising, falling), up_left, up_right, w_up
    )
    new_w_qkv = new_planes.transpose(1, 0, 2)

    dp_place = lax.axis_index("dp")

    def mine(values, count):
        return take(values.reshape(count, dp_size, -1), dp_place, 1)

    owned_bqkv = mine(sums[0, : 3 * own_width], 3)
    owned_bup = mine(sums[1], 1)[0]
    owned_norm = jnp.concatenate([mine(sums[2, :share_width], 1), mine(sums[3, :share_width], 1)])
    bias_total = mine(sums[4, :share_width], 1)
    owned_obias = jnp.concatenate([bias_total, bias_total])
    qkv_params, qkv_stats = vector_update(qkv_bias_state, owned_bqkv)
    obias_params, obias_stats = vector_update(out_bias_state, owned_obias)
    norm_new_params, norm_new_stats = vector_update(ln_state, owned_norm)
    new_up_bias, new_up_stat = vector_update(up_bias_state, owned_bup)
    new_vector_params = jnp.concatenate([qkv_params, obias_params, norm_new_params], axis=0)
    new_vector_stats = jnp.concatenate([qkv_stats, obias_stats, norm_new_stats], axis=0)
    return (
        output,
        input_grad,
        new_w_qkv,
        new_w_out,
        new_w_up,
        new_w_down,
        new_vector_params,
        new_vector_stats,
        new_up_bias,
        new_up_stat,
        qkv_left_new,
        qkv_right_new,
        out_left_new,
        out_right_new,
        up_left_new,
        up_right_new,
        down_left_new,
        down_right_new,
    )


def solution(mesh):
    return jax.shard_map(
        local,
        mesh=mesh,
        in_specs=(
            P("dp", "mp"),
            P("dp", "mp"),
            P("dp", None),
            P("dp", None, "mp"),
            P(None, None, ("mp", "dp")),
            P("mp", "dp"),
            P(None, None, ("mp", "dp")),
            P("dp", "mp"),
            P(None, ("mp", "dp")),
            P("mp", "dp"),
            P(None, None, ("mp", "dp")),
            P(None, "mp", "dp", None, None),
            P(None, "mp", "dp", None, None),
            P(None, "mp", "dp", None, None),
            P(None, "mp", "dp", None, None),
            P(None, "mp", "dp", None, None),
            P(None, "mp", "dp", None, None),
            P(None, "mp", "dp", None, None),
            P(None, "mp", "dp", None, None),
        ),
        out_specs=(
            P("dp", "mp"),
            P("dp", "mp"),
            P("dp", None, "mp"),
            P("mp", "dp"),
            P("dp", "mp"),
            P("mp", "dp"),
            P(None, ("mp", "dp")),
            P(None, ("mp", "dp")),
            P(("mp", "dp")),
            P(("mp", "dp")),
            P("mp", "dp", None, None),
            P("mp", "dp", None, None),
            P("mp", "dp", None, None),
            P("mp", "dp", None, None),
            P("mp", "dp", None, None),
            P("mp", "dp", None, None),
            P("mp", "dp", None, None),
            P("mp", "dp", None, None),
        ),
        check_vma=False,
    )
```

```python
import functools
import math

import jax
import jax.numpy as jnp
from jax import lax
from jax.experimental import pallas as pl
from jax.experimental.pallas import tpu as pltpu
from jax.sharding import PartitionSpec as P

HEAD_DIM = 64
ROT_DIM = 32
LANES = 128
ROW_TILE = 256


norm_eps = 1e-05
matrix_rate = 1.0
vector_rate = 0.4
masked_score = -1e30


def segment_of(ends, positions, axis, slots):
    finished = ends <= positions
    segment = jnp.sum(jnp.where(finished, 1, 0), axis=axis, keepdims=True)
    starting = jnp.max(jnp.where(finished, ends, 0), axis=axis, keepdims=True)
    return (segment, starting, segment < slots)


def rope_tables(offsets):
    lane = lax.rem(lax.broadcasted_iota(jnp.int32, (1, LANES), 1), HEAD_DIM)
    half_rot = ROT_DIM // 2
    freq_index = lax.rem(lane, half_rot).astype(jnp.float32)
    inverse = jnp.exp(-(2.0 * freq_index / ROT_DIM) * math.log(10000.0))
    angles = offsets * inverse
    cosine, sine = (jnp.cos(angles), jnp.sin(angles))
    keep = jnp.where(lane < ROT_DIM, cosine, 1.0)
    ahead = jnp.where(lane < half_rot, -sine, 0.0)
    behind = jnp.where((lane >= half_rot) & (lane < ROT_DIM), sine, 0.0)
    return (keep, ahead, behind)


def gelu_pair(values):
    square = values * values
    inner = math.sqrt(2.0 / math.pi) * values * (1.0 + 0.044715 * square)
    bent = jnp.tanh(inner)
    half = 0.5 * (1.0 + bent)
    slope = half + 0.5 * values * (1.0 - bent * bent) * math.sqrt(2.0 / math.pi) * (
        1.0 + 3.0 * 0.044715 * square
    )
    return (values * half, slope)


def take(array, index, axis=0):
    return lax.dynamic_index_in_dim(array, index, axis, keepdims=False)


def summed(*terms):
    total = terms[0].astype(jnp.float32)
    for term in terms[1:]:
        total = total + term.astype(jnp.float32)
    return total


def contract(left, right, left_axis, right_axis):
    return lax.dot_general(
        left, right, (((left_axis,), (right_axis,)), ((), ())), preferred_element_type=jnp.float32
    )


MESH_ID = pl.DeviceIdType.MESH


def remote(source, target, send_sem, recv_sem, axis, peer):
    return pltpu.make_async_remote_copy(
        src_ref=source,
        dst_ref=target,
        send_sem=send_sem,
        recv_sem=recv_sem,
        device_id={axis: peer},
        device_id_type=MESH_ID,
    )


def greet_line():
    size = lax.axis_size("dp")
    place = lax.axis_index("dp")
    barrier = pltpu.get_barrier_semaphore()
    core = lax.rem(place, 2)
    peers = [place + 1 - 2 * core, lax.rem(place + 2, size), lax.rem(place + size - 2, size)]
    for peer in peers:
        pl.semaphore_signal(barrier, inc=1, device_id={"dp": peer}, device_id_type=MESH_ID)
    return (barrier, len(peers))


PIECES = 2
VMEM_LIMIT = 60 * 1024 * 1024


def piecewise(body, first=0, last=PIECES):
    def once(piece, carry):
        body(piece)
        return carry

    lax.fori_loop(first, last, once, 0)


class LineGather:
    def __init__(self, own, full, send, recv):
        self.count = lax.axis_size("dp") // 2
        self.place = lax.axis_index("dp")
        self.spot = self.place // 2
        self.core = lax.rem(self.place, 2)
        self.own, self.full, self.send, self.recv = own, full, send, recv
        self.rows = own.shape[0]
        self.part = self.rows // PIECES

    def copy(self, kind, step, piece, chip, peer, from_own=False):
        offset = piece * self.part
        start = pl.multiple_of((2 * chip + self.core) * self.rows + offset, self.part)
        block = self.full.at[pl.ds(start, self.part), :]
        source = block
        if from_own:
            source = self.own.at[pl.ds(pl.multiple_of(offset, self.part), self.part), :]
        sems = (self.send.at[kind, step, piece], self.recv.at[kind, step, piece])
        return remote(source, block, *sems, "dp", peer)

    def rise(self, step, piece):
        return self.copy(0, step, piece, self.spot - step + 1, self.place + 2, step == 1)

    def fall(self, step, piece):
        return self.copy(1, step, piece, self.spot + step - 1, self.place - 2, step == 1)

    def show(self, kind, step, piece):
        chip = self.spot - step if kind == 2 else self.spot + step
        return self.copy(kind, step, piece, chip, self.place + 1 - 2 * self.core, step == 0)

    def keep(self):
        start = pl.multiple_of(self.place * self.rows, self.rows)
        target = self.full.at[pl.ds(start, self.rows), :]
        return pltpu.make_async_copy(self.own, target, self.send.at[3, 0, 0])

    def start(self):
        def body(piece):
            pl.when(self.spot + 1 < self.count)(lambda: self.rise(1, piece).start())
            pl.when(self.spot > 0)(lambda: self.fall(1, piece).start())
            self.show(2, 0, piece).start()

        piecewise(body)
        self.keep().start()

    def advance(self, step, first=0, last=PIECES):
        def body(piece):
            @pl.when(self.spot >= step)
            def _():
                self.rise(step, piece).wait_recv()
                pl.when(self.spot + 1 < self.count)(lambda: self.rise(step + 1, piece).start())
                self.show(2, step, piece).start()

            @pl.when(self.spot + step < self.count)
            def _():
                self.fall(step, piece).wait_recv()
                pl.when(self.spot > 0)(lambda: self.fall(step + 1, piece).start())
                self.show(3, step, piece).start()

        piecewise(body, first, last)

    def finish(self):
        self.keep().wait()

        def body(piece):
            self.show(2, 0, piece).wait()
            for step in range(1, self.count):
                rises = (self.spot + 1 < self.count) & (self.spot >= step - 1)
                falls = (self.spot > 0) & (self.spot + step - 1 < self.count)
                above = self.spot + step < self.count
                pl.when(rises)(lambda step=step: self.rise(step, piece).wait_send())
                pl.when(falls)(lambda step=step: self.fall(step, piece).wait_send())
                pl.when(self.spot >= step)(lambda step=step: self.show(2, step, piece).wait())
                pl.when(above)(lambda step=step: self.show(3, step, piece).wait())

        piecewise(body)


def gather_sems():
    count = lax.axis_size("dp") // 2
    return [pltpu.SemaphoreType.DMA((4, count + 1, PIECES)) for _ in range(2)]


def by_rows(rows, step, body):
    def once(index, carry):
        body(pl.ds(pl.multiple_of(index * step, step), step))
        return carry

    lax.fori_loop(0, rows // step, once, 0)


class LineSum:
    def __init__(self, blocks, from_below, from_above, send, recv):
        self.count = lax.axis_size("dp") // 2
        self.place = lax.axis_index("dp")
        self.spot = self.place // 2
        self.blocks, self.below, self.above = blocks, from_below, from_above
        self.send, self.recv = send, recv
        self.part = blocks.shape[1] // PIECES

    def rows(self, piece):
        return pl.ds(pl.multiple_of(piece * self.part, self.part), self.part)

    def move(self, kind, slots, step, piece, peer, block=None):
        rows = self.rows(piece)
        source = self.blocks.at[block, rows, :] if block is not None else slots.at[step - 2, rows, :]
        sems = (self.send.at[kind, step, piece], self.recv.at[kind, step, piece])
        return remote(source, slots.at[step - 1, rows, :], *sems, "dp", peer)

    def rise(self, step, piece, block=None):
        return self.move(0, self.below, step, piece, self.place + 2, block)

    def fall(self, step, piece, block=None):
        return self.move(1, self.above, step, piece, self.place - 2, block)

    def add(self, slots, step, block, piece):
        def body(rows):
            here = pl.ds(pl.multiple_of(piece * self.part + rows.start, rows.size), rows.size)
            total = slots[step - 2, here, :].astype(jnp.float32)
            total = total + self.blocks[block, here, :].astype(jnp.float32)
            slots[step - 2, here, :] = total.astype(jnp.bfloat16)

        by_rows(self.part, 16, body)

    def advance(self, step, first=0, last=PIECES):
        end = self.count - 1
        mirrored = end - self.spot

        def body(piece):
            pl.when(self.spot == 0)(lambda: self.rise(step, piece, self.count - step).start())
            pl.when(mirrored == 0)(lambda: self.fall(step, piece, step - 1).start())
            if step == 1:
                return

            @pl.when((self.spot > 0) & (self.spot < end) & (self.spot < step))
            def _():
                self.rise(step - 1, piece, 0).wait_recv()
                self.add(self.below, step, self.count + self.spot - step, piece)
                self.rise(step, piece).start()

            @pl.when((mirrored > 0) & (mirrored < end) & (mirrored < step))
            def _():
                self.fall(step - 1, piece, 0).wait_recv()
                self.add(self.above, step, self.spot - self.count + step, piece)
                self.fall(step, piece).start()

        piecewise(body, first, last)

    def hand_out(self, up_out, down_out):
        end = self.count - 1
        mirrored = end - self.spot

        def body(piece):
            rows = self.rows(piece)

            def move(out, slots, block):
                def once(small):
                    here = pl.ds(pl.multiple_of(rows.start + small.start, small.size), small.size)
                    total = self.blocks[block, here, :].astype(jnp.float32)
                    if slots is not None:
                        total = total + slots[end - 2, here, :].astype(jnp.float32)
                    out[here, :] = total.astype(jnp.bfloat16)

                by_rows(self.part, 16, once)

            pl.when(self.spot == 0)(lambda: move(up_out, None, 1))
            pl.when(mirrored == 0)(lambda: move(down_out, None, end - 1))

            @pl.when((self.spot > 0) & (self.spot < end))
            def _():
                self.rise(end - 1, piece, 0).wait_recv()
                move(up_out, self.below, self.spot + 1)

            @pl.when((mirrored > 0) & (mirrored < end))
            def _():
                self.fall(end - 1, piece, 0).wait_recv()
                move(down_out, self.above, self.spot - 1)

            pl.when(self.spot == end)(lambda: move(up_out, None, 0))
            pl.when(mirrored == end)(lambda: move(down_out, None, 0))
            for step in range(1, end):
                rises = (self.spot < step) & (self.spot < end)
                falls = (mirrored < step) & (mirrored < end)
                pl.when(rises)(lambda step=step: self.rise(step, piece, 0).wait_send())
                pl.when(falls)(lambda step=step: self.fall(step, piece, 0).wait_send())

        piecewise(body)

    def finish(self, out, first=0, last=PIECES):
        end = self.count - 1
        mirrored = end - self.spot

        def body(piece):
            start = piece * self.part

            def small(rows):
                return pl.ds(pl.multiple_of(start + rows.start, rows.size), rows.size)

            def begin(rows):
                out[small(rows), :] = self.blocks[self.spot, small(rows), :].astype(out.dtype)

            by_rows(self.part, 16, begin)

            def gain(slots):
                def once(rows):
                    here = small(rows)
                    total = summed(out[here, :], slots[end - 1, here, :])
                    out[here, :] = total.astype(out.dtype)

                by_rows(self.part, 16, once)

            @pl.when(self.spot > 0)
            def _():
                self.rise(end, piece, 0).wait_recv()
                gain(self.below)

            @pl.when(self.spot < end)
            def _():
                self.fall(end, piece, 0).wait_recv()
                gain(self.above)

            for step in range(1, self.count):
                rises = (self.spot < step) & (self.spot < end)
                falls = (mirrored < step) & (mirrored < end)
                pl.when(rises)(lambda step=step: self.rise(step, piece, 0).wait_send())
                pl.when(falls)(lambda step=step: self.fall(step, piece, 0).wait_send())

        piecewise(body, first, last)


def sum_scratch(rows, columns):
    count = lax.axis_size("dp") // 2
    return [
        pltpu.VMEM((count - 1, rows, columns), jnp.bfloat16),
        pltpu.VMEM((count - 1, rows, columns), jnp.bfloat16),
        pltpu.SemaphoreType.DMA((2, count, PIECES)),
        pltpu.SemaphoreType.DMA((2, count, PIECES)),
    ]


class PairProducts:
    def __init__(self, lefts, rights, parcel, sums, send, recv):
        self.count = lax.axis_size("dp") // 2
        self.place = lax.axis_index("dp")
        self.core = lax.rem(self.place, 2)
        self.lefts, self.rights = lefts, rights
        self.parcel, self.sums, self.send, self.recv = parcel, sums, send, recv

    def copy(self, chip):
        return remote(
            self.parcel.at[chip],
            self.sums.at[chip],
            self.send.at[chip],
            self.recv.at[chip],
            "dp",
            self.place + 1 - 2 * self.core,
        )

    def product(self, chip, core, quarter):
        rows = self.sums.shape[1]
        width = self.sums.shape[2] // 4
        start = pl.multiple_of((2 * chip + core) * rows, rows)
        left = self.lefts[quarter][:, pl.ds(start, rows)]
        ref, first = self.rights[quarter]
        return contract(left, ref[:, pl.ds(first, width)], 0, 0)

    def far(self):
        width = self.sums.shape[2] // 4

        def once(chip, carry):
            for quarter in range(4):
                piece = self.product(chip, 1 - self.core, quarter)
                self.parcel[chip, :, pl.ds(quarter * width, width)] = piece.astype(jnp.bfloat16)
            self.copy(chip).start()
            return carry

        lax.fori_loop(0, self.count, once, 0)

    def near(self):
        width = self.sums.shape[2] // 4

        def once(chip, carry):
            self.copy(chip).wait()
            for quarter in range(4):
                columns = pl.ds(quarter * width, width)
                piece = self.product(chip, self.core, quarter)
                total = piece + self.sums[chip, :, columns].astype(jnp.float32)
                self.sums[chip, :, columns] = total.astype(jnp.bfloat16)
            return carry

        lax.fori_loop(0, self.count, once, 0)


def pair_scratch(rows, columns):
    count = lax.axis_size("dp") // 2
    return [
        pltpu.VMEM((count, rows, columns), jnp.bfloat16),
        pltpu.SemaphoreType.DMA((count,)),
        pltpu.SemaphoreType.DMA((count,)),
    ]


class BlockGather:
    def __init__(self, own, full, send, recv):
        self.size = lax.axis_size("mp")
        self.place = lax.axis_index("mp")
        self.own, self.full, self.send, self.recv = own, full, send, recv
        self.rows, self.width = own.shape

    def spread(self, index, rows, owner, peer, first):
        start = pl.multiple_of(owner * self.width, self.width)
        target = self.full.at[rows, pl.ds(start, self.width)]
        source = self.own if first else target
        return remote(source, target, self.send.at[index], self.recv.at[index], "mp", peer)

    def copy(self, index):
        every = pl.ds(0, self.rows)
        if self.size != 4:
            return self.spread(index, every, self.place, lax.rem(self.place + 1 + index, self.size), True)
        beside = self.place + 1 - 2 * lax.rem(self.place, 2)
        above = lax.rem(self.place + 2, 4)
        half = self.rows // 2
        if index < 2:
            return self.spread(index, every, self.place, (beside, above)[index], True)
        if index == 2:
            return self.spread(2, pl.ds(0, half), above, beside, False)
        return self.spread(3, pl.ds(half, half), beside, above, False)

    def keep(self):
        start = pl.multiple_of(self.place * self.width, self.width)
        target = self.full.at[:, pl.ds(start, self.width)]
        return pltpu.make_async_copy(self.own, target, self.send.at[self.size])

    def start(self):
        for index in range(2 if self.size == 4 else self.size - 1):
            self.copy(index).start()
        self.keep().start()

    def forward(self):
        if self.size == 4:
            self.copy(1).wait_recv()
            self.copy(2).start()
            self.copy(0).wait_recv()
            self.copy(3).start()

    def finish(self):
        self.keep().wait()
        for index in range(4 if self.size == 4 else self.size - 1):
            self.copy(index).wait_send()
            if index > 1 or self.size != 4:
                self.copy(index).wait_recv()


def block_sems():
    size = lax.axis_size("mp") + 1
    return [pltpu.SemaphoreType.DMA((size,)), pltpu.SemaphoreType.DMA((size,))]


def field_rows(spread_ref, first_row, index, piece):
    dp_size = lax.axis_size("dp")
    first = lax.axis_index("mp") * dp_size
    devices = [first + owner for owner in range(dp_size)]
    row, lane = divmod(index * piece, LANES)
    return vector_rows(spread_ref, devices, first_row + row, piece, lane)


def vector_rows(spread_ref, devices, row, piece, turn_to=0):
    if piece >= LANES:
        return [
            spread_ref[device, row + part : row + part + 1, :]
            for device in devices
            for part in range(piece // LANES)
        ]
    lane = lax.broadcasted_iota(jnp.int32, (1, LANES), 1)
    fold = LANES // piece
    groups = []
    for first in range(0, len(devices), fold):
        group = jnp.zeros((1, LANES), jnp.float32)
        for part in range(fold):
            values = spread_ref[devices[first + part], row : row + 1, :]
            turn = (part * piece - turn_to) % LANES
            values = pltpu.roll(values, turn, 1) if turn else values
            mine = (lane >= part * piece) & (lane < (part + 1) * piece)
            group = jnp.where(mine, values, group)
        groups.append(group)
    return groups


def cast_rows(source, target, here):
    target[here, :] = source[here, :].astype(target.dtype)


def first_kernel(
    piece,
    up_piece,
    slots,
    w_up_ref,
    w_qkv_hbm,
    w_out_hbm,
    w_down_hbm,
    x_ref,
    gy_ref,
    small_ref,
    ends_ref,
    turned_out,
    full_ref,
    next_full,
    xn_out,
    gy_out,
    spread_ref,
    stats_ref,
    act_out,
    slope_out,
    sums_out,
    gather_send,
    gather_recv,
    next_send,
    next_recv,
    x_send,
    x_recv,
    gy_send,
    gy_recv,
    small_send,
    small_recv,
    parcel,
    pair_send,
    pair_recv,
    x_full,
    up_ref,
    act_ref,
    slope_ref,
    local_sems,
    block_ref,
    next_ref,
    valid_ref,
    xn_ref,
    gy_full,
    sums_ref,
    w_qkv_ref,
    w_out_ref,
    w_down_ref,
):
    loads = fetch(
        [(w_qkv_hbm, w_qkv_ref), (w_out_hbm, w_out_ref), (w_down_hbm, w_down_ref)],
        local_sems.at[pl.ds(6, 3)],
    )
    columns = lax.axis_size("dp")
    total = columns * lax.axis_size("mp")
    mp_place = lax.axis_index("mp")
    place = mp_place * columns + lax.axis_index("dp")
    barrier = pltpu.get_barrier_semaphore()

    def device(step):
        peer = lax.rem(place + step, total)
        return {"mp": peer // columns, "dp": lax.rem(peer, columns)}

    def greet(step, carry):
        pl.semaphore_signal(barrier, inc=1, device_id=device(step), device_id_type=MESH_ID)
        return carry

    lax.fori_loop(1, total, greet, 0)
    by_rows(block_ref.shape[0], 64, lambda here: cast_rows(w_up_ref, block_ref, here))
    pl.semaphore_wait(barrier, total - 1)

    def small_copy(step):
        return pltpu.make_async_remote_copy(
            src_ref=small_ref.at[0],
            dst_ref=spread_ref.at[place],
            send_sem=small_send.at[step],
            recv_sem=small_recv.at[step],
            device_id=device(step),
            device_id_type=MESH_ID,
        )

    def begin(step, carry):
        small_copy(step).start()
        return carry

    def end(step, carry):
        small_copy(step).wait()
        return carry

    weight = LineGather(block_ref, full_ref, gather_send, gather_recv)
    later = LineGather(next_ref, next_full, next_send, next_recv)
    rows_x = BlockGather(x_ref, x_full, x_send, x_recv)
    rows_gy = BlockGather(gy_ref, gy_full, gy_send, gy_recv)
    products = PairProducts(
        [gy_full] * 4, quarters(act_ref), parcel, sums_ref, pair_send, pair_recv
    )
    lax.fori_loop(1, total, begin, 0)
    weight.start()
    rows_x.start()
    rows_gy.start()
    spread_ref[place] = small_ref[0]
    rows, width = xn_ref.shape
    depth = block_ref.shape[0]
    head_cols = w_qkv_ref.shape[2]
    for copy in loads:
        copy.wait()
    for kind in range(3):
        next_ref[:, pl.ds(kind * head_cols, head_cols)] = w_qkv_ref[kind].astype(jnp.bfloat16)
    turned = jnp.transpose(w_out_ref[...]).astype(jnp.bfloat16)
    next_ref[:, pl.ds(3 * head_cols, head_cols)] = turned

    def turn_down(here):
        turned_out[:, here] = jnp.transpose(w_down_ref[here, :]).astype(jnp.bfloat16)

    by_rows(w_down_ref.shape[0], depth, turn_down)

    def mark(here):
        ids = lax.broadcasted_iota(jnp.int32, (ROW_TILE, 1), 0) + here.start
        valid = segment_of(ends_ref[0:1, :], ids, 1, slots)[2]
        valid_ref[here, :] = jnp.where(valid, 1.0, 0.0)

    by_rows(rows, ROW_TILE, mark)
    lax.fori_loop(1, total, end, 0)
    weight.advance(1)
    weight.advance(2)
    rows_x.forward()
    rows_gy.forward()
    weight.advance(3, 0, 1)
    later.start()
    weight.advance(3, 1)
    for step in range(4, weight.count):
        weight.advance(step)
    rows_x.finish()

    gains = vector_rows(spread_ref, range(total), 0, piece)
    shifts = vector_rows(spread_ref, range(total), 0, piece, piece)

    def normalize(here):
        values = x_full[here, :].astype(jnp.float32)
        mean = jnp.sum(values, axis=1, keepdims=True) * (1.0 / width)
        square = jnp.sum(values * values, axis=1, keepdims=True) * (1.0 / width)
        inv_std = lax.rsqrt(square - mean * mean + norm_eps)
        lanes = lax.broadcasted_iota(jnp.int32, (ROW_TILE, LANES), 1)
        stats_ref[here, :] = jnp.where(
            lanes == 0, mean, jnp.where(lanes == 1, inv_std, valid_ref[here, :])
        )
        for group in range(width // LANES):
            part = (x_full[here, pl.ds(group * LANES, LANES)].astype(jnp.float32) - mean) * inv_std
            part = part * gains[group] + shifts[group]
            xn_ref[here, pl.ds(group * LANES, LANES)] = part.astype(jnp.bfloat16)

    by_rows(rows, ROW_TILE, normalize)
    stores = fetch([(xn_ref, xn_out)], local_sems.at[pl.ds(3, 1)])
    weight.finish()
    load = pltpu.make_async_copy(full_ref, up_ref, local_sems.at[0])
    load.start()
    rows_gy.finish()

    def blank(here):
        kept = gy_full[here, :].astype(jnp.float32) * valid_ref[here, :]
        gy_full[here, :] = kept.astype(jnp.bfloat16)

    by_rows(rows, ROW_TILE, blank)
    stores += fetch([(gy_full, gy_out)], local_sems.at[pl.ds(4, 1)])
    bias = vector_rows(
        spread_ref, [mp_place * columns + owner for owner in range(columns)], 1, up_piece
    )
    quarter_width = up_ref.shape[1] // 4
    groups = quarter_width // LANES
    load.wait()

    def tile(here):
        for quarter in range(4):
            part = pl.ds(quarter * quarter_width, quarter_width)
            shift = jnp.concatenate(bias[quarter * groups : (quarter + 1) * groups], axis=1)
            hidden = contract(xn_ref[here, :], up_ref[:, part], 1, 0) + shift
            activated, slope = gelu_pair(hidden)
            act_ref[here, part] = activated.astype(jnp.bfloat16)
            slope_ref[here, part] = slope.astype(jnp.bfloat16)

    by_rows(rows // 2, ROW_TILE, tile)
    later.advance(1)
    by_rows(rows // 2, ROW_TILE, lambda here: tile(pl.ds(rows // 2 + here.start, here.size)))
    stores += fetch([(act_ref, act_out), (slope_ref, slope_out)], local_sems.at[pl.ds(1, 2)])
    later.advance(2, 0, 1)
    products.far()
    later.advance(2, 1)
    products.near()
    stores += fetch([(sums_ref, sums_out)], local_sems.at[pl.ds(5, 1)])
    for step in range(3, later.count):
        later.advance(step)
    later.finish()
    for store in stores:
        store.wait()


def first_step(weights, tokens, cotangent, small, ends, slots, piece, up_piece):
    mp_size, dp_size = (lax.axis_size("mp"), lax.axis_size("dp"))
    count = dp_size // 2
    rows = tokens.shape[0]
    wide = (rows, tokens.shape[1] * mp_size)
    part, columns = weights[0].shape
    total = mp_size * dp_size
    low = jnp.bfloat16
    return carrying(
        functools.partial(first_kernel, piece, up_piece, slots),
        1,
        weights + (tokens, cotangent, small, ends),
        "vhhhhhvv",
        [
            ((part, columns), low),
            ((part * dp_size, columns), low),
            ((part * dp_size, columns), low),
            (wide, low),
            (wide, low),
            ((total,) + small.shape[1:], jnp.float32),
            ((rows, LANES), jnp.float32),
            ((rows, columns), low),
            ((rows, columns), low),
            ((count, part, columns), low),
        ],
        "vhhhhvvhhh",
        gather_sems()
        + gather_sems()
        + block_sems()
        + block_sems()
        + [pltpu.SemaphoreType.DMA((total,)), pltpu.SemaphoreType.DMA((total,))]
        + pair_scratch(part, columns)
        + [
            pltpu.VMEM(wide, low),
            pltpu.VMEM((part * dp_size, columns), low),
            pltpu.VMEM((rows, columns), low),
            pltpu.VMEM((rows, columns), low),
            pltpu.SemaphoreType.DMA((9,)),
            pltpu.VMEM((part, columns), low),
            pltpu.VMEM((part, columns), low),
            pltpu.VMEM((rows, 1), jnp.float32),
            pltpu.VMEM(wide, low),
            pltpu.VMEM(wide, low),
            pltpu.VMEM((count, part, columns), low),
        ]
        + [pltpu.VMEM(weight.shape, weight.dtype) for weight in weights[1:]],
        4 * rows * wide[1] * columns,
        "gathers_beside_hidden",
    )


def greet_and_wait():
    barrier, count = greet_line()
    pl.semaphore_wait(barrier, count)


def quarters(ref):
    width = ref.shape[1] // 4
    return [(ref, quarter * width) for quarter in range(4)]


def carrying(kernel, collective_id, operands, in_places, outs, out_places, scratch, flops, name):
    spaces = {"h": pl.BlockSpec(memory_space=pl.ANY), "v": pl.BlockSpec(memory_space=pltpu.VMEM)}
    return pl.pallas_call(
        kernel,
        in_specs=[spaces[place] for place in in_places],
        out_specs=[spaces[place] for place in out_places],
        out_shape=[jax.ShapeDtypeStruct(shape, dtype) for shape, dtype in outs],
        scratch_shapes=scratch,
        compiler_params=pltpu.CompilerParams(
            collective_id=collective_id, has_side_effects=True, vmem_limit_bytes=VMEM_LIMIT
        ),
        cost_estimate=pl.CostEstimate(flops=flops, bytes_accessed=1 << 25, transcendentals=0),
        name=name,
    )(*operands)


PLAN = {
    "projected": (),
    0: ((1, 0), (1, 1)),
    1: ((2, 0),),
    "attended": ((2, 1),),
    "far": ((3, 0),),
}


def third_kernel(
    head_cols,
    slots,
    piece,
    field_row,
    block_ref,
    ready_hbm,
    xn_hbm,
    gy_hbm,
    weight_hbm,
    spread_ref,
    ends_ref,
    ends_col_ref,
    full_ref,
    grad_out,
    or_out,
    sums_out,
    owned_ref,
    vector_ref,
    gather_send,
    gather_recv,
    below,
    above,
    line_send,
    line_recv,
    parcel,
    pair_send,
    pair_recv,
    mask_ref,
    low_ref,
    go_ref,
    dq_acc,
    dk_acc,
    dv_acc,
    ready_ref,
    xn_ref,
    gy_ref,
    weight_ref,
    grad_ref,
    or_ref,
    local_sems,
    keep_ref,
    ahead_ref,
    behind_ref,
    sums_ref,
):
    loads = [
        pltpu.make_async_copy(source, target, local_sems.at[index])
        for index, (source, target) in enumerate(
            [(ready_hbm, ready_ref), (xn_hbm, xn_ref), (weight_hbm, weight_ref), (gy_hbm, gy_ref)]
        )
    ]
    for load in loads:
        load.start()
    weight = LineGather(block_ref, full_ref, gather_send, gather_recv)
    line = LineSum(ready_ref, below, above, line_send, line_recv)
    rights = [(grad_ref, kind * head_cols) for kind in range(3)] + [(or_ref, 0)]
    products = PairProducts(
        [xn_ref] * 3 + [gy_ref], rights, parcel, sums_ref, pair_send, pair_recv
    )
    greet_and_wait()
    weight.start()
    loads[0].wait()
    line.advance(1)

    rows = xn_ref.shape[0]
    tiles = rows // ROW_TILE
    scale = HEAD_DIM ** (-0.5)
    row_positions = lax.broadcasted_iota(jnp.int32, (1, rows), 1)
    seg_row, _, row_valid = segment_of(ends_col_ref[...], row_positions, 0, slots)
    seg_row = jnp.where(row_valid, seg_row, slots + row_positions)
    for tile in range(tiles):
        here = pl.ds(tile * ROW_TILE, ROW_TILE)
        reach = (tile + 1) * ROW_TILE
        shape = (ROW_TILE, reach)
        ids = lax.broadcasted_iota(jnp.int32, (ROW_TILE, 1), 0) + tile * ROW_TILE
        seg_col, starting, valid = segment_of(ends_ref[0:1, :], ids, 1, slots)
        seg_col = jnp.where(valid, seg_col, slots + ids)
        tables = rope_tables((ids - starting).astype(jnp.float32))
        for ref, table in zip((keep_ref, ahead_ref, behind_ref), tables):
            ref[here, :] = table
        key_ids = lax.broadcasted_iota(jnp.int32, shape, 1)
        allowed = (seg_col == seg_row[:, :reach]) & (key_ids <= ids)
        mask_ref[here, pl.ds(0, reach)] = jnp.where(allowed, 0.0, masked_score)
    biases = [
        jnp.concatenate(field_rows(spread_ref, field_row, kind, piece), axis=1) for kind in range(3)
    ]

    def turned(values, here, direction):
        ahead = pltpu.roll(values, LANES - ROT_DIM // 2, 1)
        behind = pltpu.roll(values, ROT_DIM // 2, 1)
        return values * keep_ref[here, :] + direction * (
            ahead * ahead_ref[here, :] + behind * behind_ref[here, :]
        )

    def project(here):
        for kind in range(3):
            columns = pl.ds(kind * head_cols, head_cols)
            values = contract(xn_ref[here, :], weight_ref[:, columns], 1, 0) + biases[kind]
            if kind == 2:
                low_ref[here, columns] = values.astype(jnp.bfloat16)
                continue
            for first in range(0, head_cols, LANES):
                part = turned(values[:, first : first + LANES], here, 1.0).astype(jnp.bfloat16)
                if kind == 0:
                    part = part * scale
                low_ref[here, pl.ds(kind * head_cols + first, LANES)] = part
        columns = pl.ds(3 * head_cols, head_cols)
        values = contract(gy_ref[here, :], weight_ref[:, columns], 1, 0)
        go_ref[here, :] = values.astype(jnp.bfloat16)

    for load in loads[1:]:
        load.wait()
    by_rows(rows, ROW_TILE, project)
    vector_ref[...] = jnp.zeros_like(vector_ref)

    done = set()
    pairs = head_cols // LANES

    def events(wanted):
        for step, piece in wanted:
            if (step, piece) not in done and step < weight.count:
                done.add((step, piece))
                weight.advance(step, piece, piece + 1)
                if step + 1 < weight.count:
                    line.advance(step + 1, piece, piece + 1)

    lane = lax.broadcasted_iota(jnp.int32, (ROW_TILE, LANES), 1)
    first_head = lane < HEAD_DIM

    def one_pair(pair, carry):
        column = pl.multiple_of(pair * LANES, LANES)
        q_lanes = pl.ds(column, LANES)
        k_lanes = pl.ds(pl.multiple_of(head_cols + column, LANES), LANES)
        v_lanes = pl.ds(pl.multiple_of(2 * head_cols + column, LANES), LANES)
        dk_acc[...] = jnp.zeros_like(dk_acc)
        dv_acc[...] = jnp.zeros_like(dv_acc)
        for tile in range(tiles):
            here = pl.ds(tile * ROW_TILE, ROW_TILE)
            keys = pl.ds(0, (tile + 1) * ROW_TILE)
            outs = []
            query_grads = []
            for head in range(LANES // HEAD_DIM):
                mine = first_head if head == 0 else jnp.logical_not(first_head)
                none = jnp.zeros((ROW_TILE, LANES), jnp.bfloat16)
                query = jnp.where(mine, low_ref[here, q_lanes], none)
                grad_out = jnp.where(mine, go_ref[here, q_lanes], none)
                scores = contract(query, low_ref[keys, k_lanes], 1, 1) + mask_ref[here, keys]
                peak = jnp.max(scores, axis=1, keepdims=True)
                weights = jnp.exp(scores - peak)
                share = 1.0 / jnp.sum(weights, axis=1, keepdims=True)
                probs = weights * share
                probs_low = probs.astype(jnp.bfloat16)
                outs.append(contract(probs_low, low_ref[keys, v_lanes], 1, 0))
                grad_probs = contract(grad_out, low_ref[keys, v_lanes], 1, 1)
                delta = jnp.sum(probs * grad_probs, axis=1, keepdims=True)
                grad_scores = (probs * (grad_probs - delta)).astype(jnp.bfloat16)
                query_grads.append(contract(grad_scores, low_ref[keys, k_lanes], 1, 0))
                dk_acc[keys, :] += contract(grad_scores, query, 0, 0)
                dv_acc[keys, :] += contract(probs_low, grad_out, 0, 0)
            or_ref[here, q_lanes] = jnp.where(first_head, outs[0], outs[1]).astype(jnp.bfloat16)
            dq_acc[here, :] = jnp.where(first_head, query_grads[0], query_grads[1])
        for tile in range(tiles):
            here = pl.ds(tile * ROW_TILE, ROW_TILE)
            parts = [
                (q_lanes, turned(dq_acc[here, :], here, -1.0) * scale),
                (k_lanes, turned(dk_acc[here, :], here, -1.0)),
                (v_lanes, dv_acc[here, :]),
            ]
            for lanes, part in parts:
                part = part.astype(jnp.bfloat16)
                grad_ref[here, lanes] = part
                vector_ref[0:1, lanes] += jnp.sum(part.astype(jnp.float32), axis=0, keepdims=True)

        for index in range(pairs):
            if index in PLAN:
                pl.when(pair == index)(functools.partial(events, PLAN[index]))
        return carry

    events(PLAN["projected"])
    lax.fori_loop(0, pairs, one_pair, 0)
    stores = [
        pltpu.make_async_copy(grad_ref, grad_out, local_sems.at[4]),
        pltpu.make_async_copy(or_ref, or_out, local_sems.at[5]),
    ]
    for store in stores:
        store.start()
    events(PLAN["attended"])
    products.far()
    events(PLAN["far"])
    products.near()
    stores += fetch([(sums_ref, sums_out)], local_sems.at[pl.ds(6, 1)])
    events([(step, piece) for step in range(1, weight.count) for piece in range(PIECES)])
    line.finish(owned_ref)
    weight.finish()
    for store in stores:
        store.wait()


def third_step(
    block, ready, normed, grad_rows, full_qkvo, spread, ends, ends_col, slots, piece, field_row
):
    rows, width = normed.shape
    count = lax.axis_size("dp") // 2
    columns = full_qkvo.shape[1]
    head_cols = columns // 4
    part = width // (2 * count)
    low = jnp.bfloat16
    return carrying(
        functools.partial(third_kernel, head_cols, slots, piece, field_row),
        5,
        (
            block,
            ready,
            normed,
            grad_rows,
            full_qkvo,
            spread,
            ends,
            ends_col,
        ),
        "hhhhhvvv",
        [
            ((width, block.shape[1]), low),
            ((rows, 3 * head_cols), low),
            ((rows, head_cols), low),
            ((count, part, columns), low),
            ((part, ready.shape[2]), low),
            ((8, columns), jnp.float32),
        ],
        "hhhhvv",
        gather_sems()
        + sum_scratch(part, ready.shape[2])
        + pair_scratch(part, columns)
        + [
            pltpu.VMEM((rows, rows), jnp.float32),
            pltpu.VMEM((rows, 3 * head_cols), low),
            pltpu.VMEM((rows, head_cols), low),
            pltpu.VMEM((rows, LANES), jnp.float32),
            pltpu.VMEM((rows, LANES), jnp.float32),
            pltpu.VMEM((rows, LANES), jnp.float32),
            pltpu.VMEM(ready.shape, low),
            pltpu.VMEM((rows, width), low),
            pltpu.VMEM((rows, width), low),
            pltpu.VMEM((width, columns), low),
            pltpu.VMEM((rows, 3 * head_cols), low),
            pltpu.VMEM((rows, head_cols), low),
            pltpu.SemaphoreType.DMA((7,)),
            pltpu.VMEM((rows, LANES), jnp.float32),
            pltpu.VMEM((rows, LANES), jnp.float32),
            pltpu.VMEM((rows, LANES), jnp.float32),
            pltpu.VMEM((count, part, columns), low),
        ],
        4 * rows * width * columns + 12 * rows * rows * head_cols,
        "lines_beside_attention",
    )


def fourth_kernel(
    head_cols,
    piece,
    field_row,
    ready_hbm,
    xn_hbm,
    gy_hbm,
    down_hbm,
    slope_hbm,
    act_hbm,
    or_hbm,
    qkvo_hbm,
    x_ref,
    spread_ref,
    gh_out,
    sums_out,
    up_send,
    down_send,
    own_ref,
    vector_ref,
    out_ref,
    below,
    above,
    line_send,
    line_recv,
    parcel,
    pair_send,
    pair_recv,
    t_parts,
    t_got,
    t_send,
    t_recv,
    ready_ref,
    xn_ref,
    gy_ref,
    down_ref,
    wide_ref,
    or_ref,
    weight_ref,
    gh_ref,
    local_sems,
    sums_ref,
):
    loads = [
        pltpu.make_async_copy(source, target, local_sems.at[index])
        for index, (source, target) in enumerate(
            [
                (ready_hbm, ready_ref),
                (down_hbm, down_ref),
                (act_hbm, wide_ref),
                (or_hbm, or_ref),
                (qkvo_hbm.at[:, pl.ds(3 * head_cols, head_cols)], weight_ref),
                (gy_hbm, gy_ref),
                (xn_hbm, xn_ref),
            ]
        )
    ]
    for load in loads:
        load.start()
    line = LineSum(ready_ref, below, above, line_send, line_recv)
    branches = BlockScatter(t_parts, t_got, t_send, t_recv)
    products = PairProducts(
        [xn_ref] * 4, quarters(gh_ref), parcel, sums_ref, pair_send, pair_recv
    )
    barrier, count = greet_line()
    count += greet_block()
    pl.semaphore_wait(barrier, count)
    loads[0].wait()
    line.advance(1)
    for load in loads[1:5]:
        load.wait()
    rows, share_width = x_ref.shape
    width = down_ref.shape[1] // 4
    vector_ref[...] = jnp.zeros_like(vector_ref)

    def tile(here):
        for quarter in range(4):
            columns = pl.ds(quarter * width, width)
            grad_act = contract(gy_ref[here, :], down_ref[:, columns], 1, 0)
            grad_hidden = grad_act * wide_ref[here, columns].astype(jnp.float32)
            grad_hidden = grad_hidden.astype(jnp.bfloat16)
            gh_ref[here, columns] = grad_hidden
            vector_ref[0:1, columns] += jnp.sum(
                grad_hidden.astype(jnp.float32), axis=0, keepdims=True
            )

    def branch(share):
        start = pl.multiple_of(branches.owner(share) * share_width, share_width)
        where = pl.ds(start, share_width)

        def once(here):
            part = contract(or_ref[here, :], weight_ref[where, :], 1, 1)
            part = part + contract(wide_ref[here, :], down_ref[where, :], 1, 1)
            t_parts[share, here, :] = part.astype(jnp.bfloat16)

        by_rows(rows, 2 * ROW_TILE, once)
        branches.after(share)

    shares = branches.size
    for share in range(shares):
        branch(share)
        if share == 2:
            line.advance(2, 0, 1)
    late = pltpu.make_async_copy(slope_hbm, wide_ref, local_sems.at[7])
    late.start()
    line.advance(2, 1)
    branches.second()
    for load in loads[5:]:
        load.wait()
    late.wait()
    by_rows(rows, ROW_TILE, tile)
    stores = fetch([(gh_ref, gh_out)], local_sems.at[pl.ds(8, 1)])
    products.far()
    for step in range(3, line.count - 1):
        line.advance(step)
    branches.finish()
    biases = [
        jnp.concatenate(field_rows(spread_ref, field_row, kind, piece), axis=1) for kind in (3, 4)
    ]
    for tile_index in range(rows // ROW_TILE):
        here = pl.ds(tile_index * ROW_TILE, ROW_TILE)
        total = x_ref[here, :].astype(jnp.float32) + branches.total(tile_index, ROW_TILE)
        total = total + biases[0] + biases[1]
        out_ref[here, :] = total.astype(jnp.bfloat16)
    products.near()
    stores += fetch([(sums_ref, sums_out)], local_sems.at[pl.ds(9, 1)])
    by_rows(own_ref.shape[0], 32, lambda here: keep_block(ready_ref, line.spot, own_ref, here))
    line.hand_out(up_send, down_send)
    for store in stores:
        store.wait()


def fourth_step(
    ready,
    normed,
    grad_rows,
    turned_down,
    slope,
    activated,
    attended,
    full_qkvo,
    tokens,
    spread,
    piece,
    field_row,
):
    rows, width = normed.shape
    head_cols = attended.shape[1]
    count, part, columns = ready.shape
    low = jnp.bfloat16
    return carrying(
        functools.partial(fourth_kernel, head_cols, piece, field_row),
        6,
        (
            ready,
            normed,
            grad_rows,
            turned_down,
            slope,
            activated,
            attended,
            full_qkvo,
            tokens,
            spread,
        ),
        "hhhhhhhhvv",
        [
            ((rows, columns), low),
            ((count, part, columns), low),
            ((part, columns), low),
            ((part, columns), low),
            ((part, columns), low),
            ((8, columns), jnp.float32),
            (tokens.shape, low),
        ],
        "hhvvvvv",
        sum_scratch(part, columns)
        + pair_scratch(part, columns)
        + scatter_scratch(rows, tokens.shape[1])
        + [
            pltpu.VMEM(ready.shape, low),
            pltpu.VMEM((rows, width), low),
            pltpu.VMEM((rows, width), low),
            pltpu.VMEM((width, columns), low),
            pltpu.VMEM((rows, columns), low),
            pltpu.VMEM((rows, head_cols), low),
            pltpu.VMEM((width, head_cols), low),
            pltpu.VMEM((rows, columns), low),
            pltpu.SemaphoreType.DMA((10,)),
            pltpu.VMEM((count, part, columns), low),
        ],
        6 * rows * width * columns,
        "line_beside_hidden_grad",
    )


def greet_block():
    size = lax.axis_size("mp")
    place = lax.axis_index("mp")
    barrier = pltpu.get_barrier_semaphore()
    for step in range(1, size):
        peer = lax.rem(place + step, size)
        pl.semaphore_signal(barrier, inc=1, device_id={"mp": peer}, device_id_type=MESH_ID)
    return size - 1


class BlockScatter:
    def __init__(self, parts, got, send, recv):
        self.size = lax.axis_size("mp")
        self.place = lax.axis_index("mp")
        self.parts, self.got, self.send, self.recv = parts, got, send, recv
        self.half = parts.shape[1] // 2
        self.beside = self.place + 1 - 2 * lax.rem(self.place, 2)
        self.above = lax.rem(self.place + 2, 4)

    def owner(self, index):
        if self.size == 4:
            return [lax.rem(self.beside + 2, 4), self.beside, self.above, self.place][index]
        return lax.rem(self.place + 1 + index, self.size)

    def copy(self, index):
        if self.size == 4:
            part, bottom, peer = [
                (0, 0, self.beside),
                (0, 1, self.above),
                (1, 0, self.beside),
                (2, 1, self.above),
                (2, 0, self.above),
                (1, 1, self.beside),
            ][index]
            source = self.parts.at[part, pl.ds(bottom * self.half, self.half), :]
        else:
            source = self.parts.at[index]
            peer = self.owner(index)
        sems = (self.send.at[index], self.recv.at[index])
        return remote(source, self.got.at[index], *sems, "mp", peer)

    def after(self, index):
        if self.size != 4:
            if index < self.size - 1:
                self.copy(index).start()
            return
        for number in ((0, 1), (2,), (3,), ())[index]:
            self.copy(number).start()

    def second(self):
        if self.size != 4:
            return
        for number, part, bottom in ((0, 2, 0), (1, 1, 1)):
            self.copy(number).wait_recv()

            def body(rows, number=number, part=part, bottom=bottom):
                here = pl.ds(bottom * self.half + rows.start, rows.size)
                total = summed(self.parts[part, here, :], self.got[number, rows, :])
                self.parts[part, here, :] = total.astype(jnp.bfloat16)

            by_rows(self.half, 64, body)
            self.copy(number + 4).start()

    def finish(self):
        if self.size != 4:
            for index in range(self.size - 1):
                self.copy(index).wait()
            return
        for index in range(6):
            if index > 1:
                self.copy(index).wait_recv()
            self.copy(index).wait_send()

    def total(self, tile, rows):
        here = pl.ds(tile * rows, rows)
        own = self.parts[self.size - 1, here, :]
        if self.size != 4:
            return summed(own, *[self.got[index, here, :] for index in range(self.size - 1)])
        bottom = (tile * rows) // self.half
        there = pl.ds(tile * rows - bottom * self.half, rows)
        return summed(own, self.got[2 + bottom, there, :], self.got[4 + bottom, there, :])


def scatter_scratch(rows, width):
    size = lax.axis_size("mp")
    slots = (6, rows // 2, width) if size == 4 else (size - 1, rows, width)
    return [
        pltpu.VMEM((size, rows, width), jnp.bfloat16),
        pltpu.VMEM(slots, jnp.bfloat16),
        pltpu.SemaphoreType.DMA((slots[0],)),
        pltpu.SemaphoreType.DMA((slots[0],)),
    ]


STREAM = 256
SLOTS = 3


def stream(tiles, loads, stores, compute, primed=False):
    ahead = SLOTS - 1
    if not primed:
        prime(tiles, loads)

    def once(tile, carry):
        slot = lax.rem(tile, SLOTS)

        @pl.when(tile + ahead < tiles)
        def _():
            for copy in loads(tile + ahead, lax.rem(tile + ahead, SLOTS)):
                copy.start()

        for copy in loads(tile, slot):
            copy.wait()

        @pl.when(tile >= SLOTS)
        def _():
            for copy in stores(tile - SLOTS, slot):
                copy.wait()

        compute(tile, slot)
        for copy in stores(tile, slot):
            copy.start()
        return carry

    lax.fori_loop(0, tiles, once, 0)
    for tile in range(max(tiles - SLOTS, 0), tiles):
        for copy in stores(tile, tile % SLOTS):
            copy.wait()


def prime(tiles, loads):
    for tile in range(min(SLOTS - 1, tiles)):
        for copy in loads(tile, tile):
            copy.start()


def fetch(pairs, sems):
    copies = [
        pltpu.make_async_copy(source, target, sems.at[index])
        for index, (source, target) in enumerate(pairs)
    ]
    for copy in copies:
        copy.start()
    return copies


def fifth_kernel(
    head_cols,
    piece,
    ready_hbm,
    gh_hbm,
    grad_hbm,
    qkvo_ref,
    up_ref,
    x_hbm,
    gy_hbm,
    stats_hbm,
    spread_ref,
    vector_three,
    vector_four,
    earlier,
    earlier_rising,
    earlier_falling,
    gained_out,
    terms_out,
    up_send,
    down_send,
    own_ref,
    sums_ref,
    below,
    above,
    line_send,
    line_recv,
    g_parts,
    g_got,
    g_send,
    g_recv,
    terms_ref,
    terms_got,
    terms_send,
    terms_recv,
    vector_ref,
    vector_got,
    vector_send,
    vector_recv,
    ready_ref,
    gh_ref,
    grad_ref,
    x_ref,
    gy_ref,
    stats_ref,
    gained_ref,
    load_sems,
):
    loads = fetch(
        [
            (ready_hbm, ready_ref),
            (grad_hbm, grad_ref),
            (gh_hbm, gh_ref),
            (x_hbm, x_ref),
            (gy_hbm, gy_ref),
            (stats_hbm, stats_ref),
        ],
        load_sems,
    )
    line = LineSum(ready_ref, below, above, line_send, line_recv)
    from_norm = BlockScatter(g_parts, g_got, g_send, g_recv)
    mp_size = from_norm.size
    mp_place = from_norm.place
    dp_size = lax.axis_size("dp")
    dp_place = lax.axis_index("dp")
    rows, width = x_ref.shape
    tiles = rows // ROW_TILE
    barrier = pltpu.get_barrier_semaphore()

    def greet(step, carry):
        peer = lax.rem(dp_place + step, dp_size)
        pl.semaphore_signal(barrier, inc=1, device_id={"dp": peer}, device_id_type=MESH_ID)
        return carry

    lax.fori_loop(1, dp_size, greet, 0)
    pl.semaphore_wait(barrier, dp_size - 1 + greet_block())
    loads[0].wait()
    line.advance(1)
    for load in loads[1:3]:
        load.wait()

    def parts(one_ref, two_ref, sems):
        def load(share):
            start = pl.multiple_of(from_norm.owner(share) * width, width)
            slot = share % 2
            where = pl.ds(start, width)
            narrow = pl.ds(0, 3 * head_cols)
            return [
                pltpu.make_async_copy(qkvo_ref.at[where, narrow], one_ref.at[slot], sems.at[0, slot]),
                pltpu.make_async_copy(up_ref.at[where, :], two_ref.at[slot], sems.at[1, slot]),
            ]

        for copy in load(0):
            copy.start()
        for share in range(mp_size):
            slot = share % 2
            for copy in load(share):
                copy.wait()
            if share + 1 < mp_size:
                for copy in load(share + 1):
                    copy.start()

            def tile(here, share=share, slot=slot):
                part = contract(grad_ref[here, :], one_ref[slot], 1, 1)
                part = part + contract(gh_ref[here, :], two_ref[slot], 1, 1)
                g_parts[share, here, :] = part.astype(jnp.bfloat16)

            by_rows(rows, 2 * ROW_TILE, tile)
            from_norm.after(share)

    columns = up_ref.shape[1]
    pl.run_scoped(
        parts,
        pltpu.VMEM((2, width, 3 * head_cols), jnp.bfloat16),
        pltpu.VMEM((2, width, columns), jnp.bfloat16),
        pltpu.SemaphoreType.DMA((2, 2)),
    )
    for step in range(2, line.count - 1):
        line.advance(step)
    from_norm.second()
    for load in loads[3:]:
        load.wait()
    from_norm.finish()

    def lane_pair(first, second):
        lane = lax.broadcasted_iota(jnp.int32, (ROW_TILE, LANES), 1)
        return jnp.where(lane == 0, first, jnp.where(lane == 1, second, 0.0))

    owners = [mp_place * dp_size + owner for owner in range(dp_size)]
    gain = jnp.concatenate(vector_rows(spread_ref, owners, 0, piece), axis=1)
    sums = [jnp.zeros((1, width), jnp.float32) for _ in range(3)]
    for tile in range(tiles):
        here = pl.ds(tile * ROW_TILE, ROW_TILE)
        normalized = (x_ref[here, :].astype(jnp.float32) - stats_ref[here, 0:1]) * stats_ref[here, 1:2]
        grad = from_norm.total(tile, ROW_TILE)
        gained = grad * gain
        gained_ref[here, :] = gained
        terms = lane_pair(
            jnp.sum(gained, axis=1, keepdims=True),
            jnp.sum(gained * normalized, axis=1, keepdims=True),
        )
        terms_ref[:, here] = jnp.transpose(terms)[:8, :]
        upstream = gy_ref[here, :].astype(jnp.float32) * stats_ref[here, 2:3]
        sums[0] += jnp.sum(grad * normalized, axis=0, keepdims=True)
        sums[1] += jnp.sum(grad, axis=0, keepdims=True)
        sums[2] += jnp.sum(upstream, axis=0, keepdims=True)

    store = pltpu.make_async_copy(gained_ref, gained_out, load_sems.at[len(loads)])
    store.start()
    three_width = vector_three.shape[1]
    fields = [vector_three[0:1, pl.ds(0, three_width - head_cols)], vector_four[0:1, :]] + sums
    flat = jnp.concatenate(fields, axis=1)
    per_row = vector_ref.shape[1]
    for row in range(8):
        part = flat[:, row * per_row : (row + 1) * per_row]
        if part.shape[1]:
            vector_ref[row : row + 1, pl.ds(0, part.shape[1])] = part
    def terms_copy(step):
        peer = lax.rem(mp_place + step, mp_size)
        slot = step - 1
        sems = (terms_send.at[slot], terms_recv.at[slot])
        return remote(terms_ref, terms_got.at[slot], *sems, "mp", peer)

    def vector_copy(step):
        peer = lax.rem(dp_place + step, dp_size)
        slot = step - 1
        sems = (vector_send.at[slot], vector_recv.at[slot])
        return remote(vector_ref, vector_got.at[slot], *sems, "dp", peer)

    def vector_begin(step, carry):
        vector_copy(step).start()
        return carry

    for step in range(1, mp_size):
        terms_copy(step).start()
    lax.fori_loop(1, dp_size, vector_begin, 0)
    def vector_end(step, carry):
        vector_copy(step).wait()
        return carry

    by_rows(own_ref.shape[0], 32, lambda here: keep_block(ready_ref, line.spot, own_ref, here))
    line.hand_out(up_send, down_send)
    terms = terms_ref[...]
    for step in range(1, mp_size):
        terms_copy(step).wait()
        terms = terms + terms_got[step - 1]
    terms_out[...] = terms
    lax.fori_loop(1, dp_size, vector_end, 0)
    total = vector_ref[...]
    for slot in range(dp_size - 1):
        total = total + vector_got[slot]
    flat = jnp.concatenate([total[row : row + 1, :] for row in range(8)], axis=1)
    start = 0
    for row, field in enumerate(fields):
        sums_ref[row : row + 1, pl.ds(0, field.shape[1])] = flat[:, start : start + field.shape[1]]
        start += field.shape[1]
    store.wait()


def keep_block(blocks, index, out, here):
    out[here, :] = blocks[index, here, :]


def fifth_step(
    ready,
    grad_hidden,
    grad_projected,
    full_qkvo,
    full_up,
    tokens,
    cotangent,
    stats,
    spread,
    vector_three,
    vector_four,
    earlier,
    piece,
):
    rows, width = tokens.shape
    head_cols = grad_projected.shape[1] // 3
    count, part, columns = ready.shape
    mp_size = lax.axis_size("mp")
    dp_size = lax.axis_size("dp")
    low = jnp.bfloat16
    exact = jnp.float32
    packed = 3 * head_cols + columns + 3 * width
    packed = -(-packed // (8 * LANES)) * LANES
    return carrying(
        functools.partial(fifth_kernel, head_cols, piece),
        7,
        (
            ready,
            grad_hidden,
            grad_projected,
            full_qkvo,
            full_up,
            tokens,
            cotangent,
            stats,
            spread,
            vector_three,
            vector_four,
        )
        + earlier,
        "hhhhhhhhvvvhhh",
        [
            ((rows, width), exact),
            ((8, rows), exact),
            ((part, columns), low),
            ((part, columns), low),
            ((part, columns), low),
            ((8, columns), exact),
        ],
        "hvvvvv",
        sum_scratch(part, columns)
        + scatter_scratch(rows, width)
        + [
            pltpu.VMEM((8, rows), exact),
            pltpu.VMEM((mp_size - 1, 8, rows), exact),
            pltpu.SemaphoreType.DMA((mp_size - 1,)),
            pltpu.SemaphoreType.DMA((mp_size - 1,)),
            pltpu.VMEM((8, packed), exact),
            pltpu.VMEM((dp_size - 1, 8, packed), exact),
            pltpu.SemaphoreType.DMA((dp_size - 1,)),
            pltpu.SemaphoreType.DMA((dp_size - 1,)),
            pltpu.VMEM(ready.shape, low),
            pltpu.VMEM((rows, columns), low),
            pltpu.VMEM((rows, 3 * head_cols), low),
            pltpu.VMEM((rows, width), low),
            pltpu.VMEM((rows, width), low),
            pltpu.VMEM(stats.shape, exact),
            pltpu.VMEM((rows, width), exact),
            pltpu.SemaphoreType.DMA((7,)),
        ],
        4 * rows * width * mp_size * columns,
        "line_beside_norm_grad",
    )


class Averager:
    def __init__(self, grad, stats, stats_out, buffers, sems):
        self.grad, self.stats, self.stats_out = grad, stats, stats_out
        self.stat_in, self.stat_new, self.root_in, self.side_in, self.side_new = buffers
        self.sems = sems
        self.tile_rows = self.stat_in.shape[1]
        self.tiles = grad.shape[1] // self.tile_rows

    def where(self, tile):
        return pl.ds(pl.multiple_of(tile * self.tile_rows, self.tile_rows), self.tile_rows)

    def loads(self, tile, slot):
        pairs = [
            (self.stats.at[0, 0, 0, self.where(tile), :], self.stat_in),
            (self.root_tile(tile), self.root_in),
            (self.side(self.master, tile), self.side_in),
        ]
        return [
            pltpu.make_async_copy(source, target.at[slot], self.sems.at[index, slot])
            for index, (source, target) in enumerate(pairs)
        ]

    def stores(self, tile, slot):
        pairs = [
            (self.stat_new, self.stats_out.at[0, 0, self.where(tile), :]),
            (self.side_new, self.side(self.master_out, tile)),
        ]
        return [
            pltpu.make_async_copy(source.at[slot], target, self.sems.at[3 + index, slot])
            for index, (source, target) in enumerate(pairs)
        ]

    def compute(self, tile, slot):
        product = contract(self.grad[:, self.where(tile)], self.grad[...], 0, 0)
        self.stat_new[slot] = 0.5 * self.stat_in[slot] + 0.5 * product
        step = self.step(self.root_in[slot].astype(jnp.bfloat16))
        self.side_new[slot] = self.side_in[slot] - matrix_rate * step

    def start(self):
        prime(self.tiles, self.loads)

    def run(self):
        stream(self.tiles, self.loads, self.stores, self.compute, True)


class WideUnit(Averager):
    def __init__(self, grad, stats, stats_out, buffers, sems, first, small, small_out, master, out):
        super().__init__(grad, stats, stats_out, buffers, sems)
        self.first, self.small, self.small_out = first, small, small_out
        self.master, self.master_out = master, out

    def root_tile(self, tile):
        return self.stats.at[1, 0, 0, :, self.where(tile)]

    def side(self, ref, tile):
        if len(ref.shape) == 2:
            return ref.at[:, self.where(tile)]
        per_plane = ref.shape[2] // self.tile_rows
        return ref.at[tile // per_plane, :, self.where(lax.rem(tile, per_plane))]

    def prepare(self):
        root = self.small[1, 0, 0].astype(jnp.bfloat16)
        self.first[...] = contract(root, self.grad[...], 1, 0).astype(jnp.bfloat16)
        average_small(self.small, self.small_out, self.grad)

    def step(self, root):
        return contract(self.first[...], root, 1, 0)


class TallUnit(Averager):
    def __init__(self, grad, stats, stats_out, buffers, sems, small, small_out, master, out):
        super().__init__(grad, stats, stats_out, buffers, sems)
        self.small, self.small_out = small, small_out
        self.master, self.master_out = master, out

    def root_tile(self, tile):
        return self.stats.at[1, 0, 0, self.where(tile), :]

    def side(self, ref, tile):
        return ref.at[self.where(tile), :]

    def prepare(self):
        average_small(self.small, self.small_out, self.grad)

    def step(self, root):
        first = contract(root, self.grad[...], 1, 1).astype(jnp.bfloat16)
        return contract(first, self.small[1, 0, 0].astype(jnp.bfloat16), 1, 0)


def average_small(small, small_out, grad):
    small_out[0, 0] = 0.5 * small[0, 0, 0] + 0.5 * contract(grad[...], grad[...], 1, 1)


def unit_scratch(depth, size, wide):
    tile_rows = min(STREAM, size)
    exact = jnp.float32
    root = (size, tile_rows) if wide else (tile_rows, size)
    side = (depth, tile_rows) if wide else (tile_rows, depth)
    shapes = [(tile_rows, size), (tile_rows, size), root, side, side]
    return [pltpu.VMEM((SLOTS,) + shape, exact) for shape in shapes] + [
        pltpu.SemaphoreType.DMA((5, SLOTS))
    ]


def local_call(kernel, operands, in_places, outs, out_places, scratch, name):
    spaces = {"h": pl.BlockSpec(memory_space=pl.ANY), "v": pl.BlockSpec(memory_space=pltpu.VMEM)}
    return pl.pallas_call(
        kernel,
        in_specs=[spaces[place] for place in in_places],
        out_specs=[spaces[place] for place in out_places],
        out_shape=[jax.ShapeDtypeStruct(shape, dtype) for shape, dtype in outs],
        scratch_shapes=scratch,
        compiler_params=pltpu.CompilerParams(vmem_limit_bytes=VMEM_LIMIT),
        cost_estimate=pl.CostEstimate(flops=1 << 33, bytes_accessed=1 << 26, transcendentals=0),
        name=name,
    )(*operands)


def down_kernel(
    grad, stats, small, master, earlier, stats_out, small_out, master_out, *scratch
):
    *buffers, sems = scratch
    unit = TallUnit(
        grad, stats, stats_out, buffers, sems, small, small_out, master, master_out
    )
    unit.start()
    unit.prepare()
    unit.run()


def down_step(grad, left, right, master, earlier):
    exact = jnp.float32
    return local_call(
        down_kernel,
        (grad, left, right, master, earlier),
        "vhvhh",
        [(left.shape[1:], exact), (right.shape[1:], exact), (master.shape, exact)],
        "hvh",
        unit_scratch(grad.shape[0], grad.shape[1], False),
        "down_weight",
    )


def update_vectors(sums, states, up_state, params_out, stats_out, up_out, up_stat_out):
    columns = sums.shape[1]
    place = lax.axis_index("dp")
    qkv_state, out_state, norm_state = states
    piece = qkv_state.shape[2]
    stride = lax.axis_size("dp") * piece
    own = pltpu.roll(sums[...], lax.rem(columns - place * piece, columns), 1)
    picks = [(qkv_state, kind, own[0:1, kind * stride : kind * stride + piece]) for kind in range(3)]
    picks += [(out_state, kind, own[4:5, :piece]) for kind in range(2)]
    picks += [(norm_state, kind, own[2 + kind : 3 + kind, :piece]) for kind in range(2)]

    def update(param, stat, grad):
        stat_new = 0.5 * stat + 0.5 * grad * grad
        return (param - vector_rate * grad * lax.rsqrt(stat_new), stat_new)

    for row, (state, kind, grad) in enumerate(picks):
        param, stat = update(state[0, kind : kind + 1, :], state[1, kind : kind + 1, :], grad)
        params_out[row : row + 1, :] = param
        stats_out[row : row + 1, :] = stat
    piece = up_state.shape[1]
    own = pltpu.roll(sums[...], lax.rem(columns - place * piece, columns), 1)
    param, stat = update(up_state[0:1, :], up_state[1:2, :], own[1:2, :piece])
    up_out[...] = param
    up_stat_out[...] = stat


def attention_weights_kernel(
    passed,
    own_ref,
    rising_ref,
    falling_ref,
    qkv_left,
    qkv_right,
    w_qkv,
    out_left,
    out_right,
    w_out,
    sums,
    qkv_state,
    out_state,
    norm_state,
    up_state,
    x_ref,
    gy_ref,
    stats_ref,
    gained_ref,
    terms_ref,
    *refs,
):
    sources, refs = (refs[:passed], refs[passed:])
    targets, refs = (refs[:passed], refs[passed:])
    (
        qkv_left_new,
        qkv_right_new,
        w_qkv_new,
        out_left_new,
        out_right_new,
        w_out_new,
        params_out,
        stats_out,
        up_out,
        up_stat_out,
        dx_out,
        low_qkv,
        low_out,
        first,
        dx_ref,
        dx_sem,
    ), refs = (refs[:16], refs[16:])
    held, refs = (refs[:passed], refs[passed:])
    pass_sems, *buffers = refs
    qkv = WideUnit(
        low_qkv,
        qkv_right,
        qkv_right_new,
        buffers[:5],
        buffers[5],
        first,
        qkv_left,
        qkv_left_new,
        w_qkv,
        w_qkv_new,
    )
    out = TallUnit(
        low_out,
        out_left,
        out_left_new,
        buffers[6:11],
        buffers[11],
        out_right,
        out_right_new,
        w_out,
        w_out_new,
    )
    qkv.start()
    out.start()
    into = fetch(zip(sources, held), pass_sems.at[0])
    edge = low_qkv.shape[1]
    owned = summed(own_ref[...], rising_ref[...], falling_ref[...]).astype(jnp.bfloat16)
    low_qkv[...] = owned[:, :edge]
    low_out[...] = owned[:, edge:]
    qkv.prepare()
    out.prepare()
    for copy in into:
        copy.wait()
    onward = fetch(zip(held, targets), pass_sems.at[1])
    rows, width = x_ref.shape
    model_width = width * lax.axis_size("mp")
    for tile in range(rows // ROW_TILE):
        here = pl.ds(tile * ROW_TILE, ROW_TILE)
        zeros = jnp.zeros((LANES - 8, ROW_TILE), jnp.float32)
        terms = jnp.transpose(jnp.concatenate([terms_ref[:, here], zeros], axis=0))
        terms = terms * (1.0 / model_width)
        inv_std = stats_ref[here, 1:2]
        normalized = (x_ref[here, :].astype(jnp.float32) - stats_ref[here, 0:1]) * inv_std
        upstream = gy_ref[here, :].astype(jnp.float32) * stats_ref[here, 2:3]
        change = gained_ref[here, :] - terms[:, 0:1] - normalized * terms[:, 1:2]
        dx_ref[here, :] = upstream + inv_std * change
    onward += fetch([(dx_ref, dx_out)], dx_sem)
    qkv.run()
    out.run()
    update_vectors(
        sums, (qkv_state, out_state, norm_state), up_state, params_out, stats_out, up_out, up_stat_out
    )
    for copy in onward:
        copy.wait()


def attention_weights_step(blocks, qkv, out, sums, states, norm, passed):
    exact = jnp.float32
    low = jnp.bfloat16
    depth = blocks[0].shape[0]
    sizes = (qkv[1].shape[-1], out[0].shape[-1])
    count = len(passed)
    piece = states[0].shape[2]
    up_piece = states[3].shape[1]
    return local_call(
        functools.partial(attention_weights_kernel, count),
        blocks + qkv + out + (sums,) + states + norm + passed,
        "vvv" + "vhh" + "hvh" + "v" + "vvvv" + "vvvvv" + "h" * count,
        [(array.shape, array.dtype) for array in passed]
        + [
            (qkv[0].shape[1:], exact),
            (qkv[1].shape[1:], exact),
            (qkv[2].shape, exact),
            (out[0].shape[1:], exact),
            (out[1].shape[1:], exact),
            (out[2].shape, exact),
            ((7, piece), exact),
            ((7, piece), exact),
            ((1, up_piece), exact),
            ((1, up_piece), exact),
            (norm[0].shape, exact),
        ],
        "h" * count + "vhh" + "hvh" + "vvvv" + "h",
        [
            pltpu.VMEM((depth, sizes[0]), low),
            pltpu.VMEM((depth, sizes[1]), low),
            pltpu.VMEM((depth, sizes[0]), low),
            pltpu.VMEM(norm[0].shape, exact),
            pltpu.SemaphoreType.DMA((1,)),
        ]
        + [pltpu.VMEM(array.shape, array.dtype) for array in passed]
        + [pltpu.SemaphoreType.DMA((2, count))]
        + unit_scratch(depth, sizes[0], True)
        + unit_scratch(depth, sizes[1], False),
        "attention_weights",
    )


def up_kernel(
    own_ref,
    rising_ref,
    falling_ref,
    small,
    stats,
    master,
    earlier,
    small_out,
    stats_out,
    master_out,
    grad,
    first,
    *scratch,
):
    *buffers, sems = scratch
    unit = WideUnit(
        grad, stats, stats_out, buffers, sems, first, small, small_out, master, master_out
    )
    unit.start()
    grad[...] = summed(own_ref[...], rising_ref[...], falling_ref[...]).astype(jnp.bfloat16)
    unit.prepare()
    unit.run()


def up_step(blocks, left, right, master, earlier):
    exact = jnp.float32
    depth, columns = master.shape
    return local_call(
        up_kernel,
        blocks + (left, right, master, earlier),
        "vvvvhhh",
        [(left.shape[1:], exact), (right.shape[1:], exact), (master.shape, exact)],
        "vhh",
        [pltpu.VMEM((depth, columns), jnp.bfloat16) for _ in range(2)]
        + unit_scratch(depth, columns, True),
        "up_weight",
    )


def local(
    tokens,
    cotangent,
    seq_lengths,
    w_qkv,
    qkv_bias_state,
    w_out,
    out_bias_state,
    w_up,
    up_bias_state,
    w_down,
    ln_state,
    qkv_left,
    qkv_right,
    out_left,
    out_right,
    up_left,
    up_right,
    down_left,
    down_right,
):
    row_count, share_width = tokens.shape
    mp_size = lax.axis_size("mp")
    dp_size = lax.axis_size("dp")
    model_width = share_width * mp_size
    own_width = w_qkv.shape[2]
    mp_place = lax.axis_index("mp")

    piece = ln_state.shape[2]
    up_piece = up_bias_state.shape[1]

    def lane_rows(*values):
        flat = jnp.concatenate([value.reshape(-1) for value in values])
        return jnp.pad(flat, (0, -flat.shape[0] % LANES)).reshape(-1, LANES)

    small = jnp.concatenate(
        [
            lane_rows(ln_state[0]),
            lane_rows(up_bias_state[0]),
            lane_rows(qkv_bias_state[0], out_bias_state[0]),
        ],
        axis=0,
    )
    up_rows = lane_rows(up_bias_state[0]).shape[0]
    small = jnp.pad(small, ((0, 8 - small.shape[0]), (0, 0))).astype(jnp.bfloat16)
    slots = seq_lengths.shape[1]
    ends = jnp.pad(
        jnp.cumsum(seq_lengths[0]), (0, LANES - slots), constant_values=2 * row_count
    ).astype(jnp.int32)
    planes = w_qkv.transpose(1, 0, 2)
    (
        turned_block,
        full_up,
        full_qkvo,
        normed,
        grad_rows,
        spread,
        stats,
        activated,
        slope,
        ready_down,
    ) = first_step(
        (w_up, planes, w_out, w_down),
        tokens,
        cotangent,
        small.astype(jnp.float32)[None],
        jnp.broadcast_to(ends[None, :], (8, LANES)),
        slots,
        piece,
        up_piece,
    )
    field_row = 1 + up_rows
    turned_down, grad_projected, attended, ready_qkvo, owned_down, vector_three = third_step(
        turned_block,
        ready_down,
        normed,
        grad_rows,
        full_qkvo,
        spread,
        jnp.broadcast_to(ends[None, :], (8, LANES)),
        ends[:, None],
        slots,
        piece,
        field_row,
    )
    grad_hidden, ready_up, *sends, vector_four, output = fourth_step(
        ready_qkvo,
        normed,
        grad_rows,
        turned_down,
        slope,
        activated,
        attended,
        full_qkvo,
        tokens,
        spread,
        piece,
        field_row,
    )
    steps = range(dp_size - 2)

    def last_hop(up_send, down_send, own):
        rising = lax.ppermute(up_send, "dp", [(place, place + 2) for place in steps])
        falling = lax.ppermute(down_send, "dp", [(place + 2, place) for place in steps])
        return (own, rising, falling)

    blocks_qkvo = last_hop(*sends)
    down_left_new, down_right_new, new_w_down = down_step(
        owned_down, down_left, down_right, w_down, ready_up
    )
    gained, terms, *sends, sums = fifth_step(
        ready_up,
        grad_hidden,
        grad_projected,
        full_qkvo,
        full_up,
        tokens,
        cotangent,
        stats,
        spread,
        vector_three,
        vector_four,
        (down_right_new,) + blocks_qkvo[1:],
        piece,
    )
    blocks_up = last_hop(*sends)
    (
        output,
        qkv_left_new,
        qkv_right_new,
        new_planes,
        out_left_new,
        out_right_new,
        new_w_out,
        new_vector_params,
        new_vector_stats,
        new_up_bias,
        new_up_stat,
        input_grad,
    ) = attention_weights_step(
        blocks_qkvo,
        (qkv_left, qkv_right, planes),
        (out_left, out_right, w_out),
        sums,
        (qkv_bias_state, out_bias_state, ln_state, up_bias_state),
        (tokens, cotangent, stats, gained, terms),
        (output,),
    )
    new_w_qkv = new_planes.transpose(1, 0, 2)
    up_left_new, up_right_new, new_w_up = up_step(
        blocks_up, up_left, up_right, w_up, new_vector_params
    )
    new_up_bias = new_up_bias.reshape(-1)
    new_up_stat = new_up_stat.reshape(-1)
    return (
        output,
        input_grad,
        new_w_qkv,
        new_w_out,
        new_w_up,
        new_w_down,
        new_vector_params,
        new_vector_stats,
        new_up_bias,
        new_up_stat,
        qkv_left_new,
        qkv_right_new,
        out_left_new,
        out_right_new,
        up_left_new,
        up_right_new,
        down_left_new,
        down_right_new,
    )


def solution(mesh):
    return jax.shard_map(
        local,
        mesh=mesh,
        in_specs=(
            P("dp", "mp"),
            P("dp", "mp"),
            P("dp", None),
            P("dp", None, "mp"),
            P(None, None, ("mp", "dp")),
            P("mp", "dp"),
            P(None, None, ("mp", "dp")),
            P("dp", "mp"),
            P(None, ("mp", "dp")),
            P("mp", "dp"),
            P(None, None, ("mp", "dp")),
            P(None, "mp", "dp", None, None),
            P(None, "mp", "dp", None, None),
            P(None, "mp", "dp", None, None),
            P(None, "mp", "dp", None, None),
            P(None, "mp", "dp", None, None),
            P(None, "mp", "dp", None, None),
            P(None, "mp", "dp", None, None),
            P(None, "mp", "dp", None, None),
        ),
        out_specs=(
            P("dp", "mp"),
            P("dp", "mp"),
            P("dp", None, "mp"),
            P("mp", "dp"),
            P("dp", "mp"),
            P("mp", "dp"),
            P(None, ("mp", "dp")),
            P(None, ("mp", "dp")),
            P(("mp", "dp")),
            P(("mp", "dp")),
            P("mp", "dp", None, None),
            P("mp", "dp", None, None),
            P("mp", "dp", None, None),
            P("mp", "dp", None, None),
            P("mp", "dp", None, None),
            P("mp", "dp", None, None),
            P("mp", "dp", None, None),
            P("mp", "dp", None, None),
        ),
        check_vma=False,
    )
```

```python
import functools
import math

import jax
import jax.numpy as jnp
from jax import lax
from jax.experimental import pallas as pl
from jax.experimental.pallas import tpu as pltpu
from jax.sharding import PartitionSpec as P

HEAD_DIM = 64
ROT_DIM = 32
LANES = 128
ROW_TILE = 256


norm_eps = 1e-05
matrix_rate = 1.0
vector_rate = 0.4
masked_score = -1e30


def segment_of(ends, positions, axis, slots):
    finished = ends <= positions
    segment = jnp.sum(jnp.where(finished, 1, 0), axis=axis, keepdims=True)
    starting = jnp.max(jnp.where(finished, ends, 0), axis=axis, keepdims=True)
    return (segment, starting, segment < slots)


def ends_of(lengths, padded):
    slots = lengths.shape[1]
    padded[...] = jnp.zeros_like(padded)
    padded[0:1, pl.ds(0, slots)] = lengths[...].astype(jnp.float32)
    shape = (LANES, LANES)
    slot = lax.broadcasted_iota(jnp.int32, shape, 0)
    before = lax.broadcasted_iota(jnp.int32, shape, 1) <= slot
    ends = jnp.sum(jnp.where(before, padded[0:1, :], 0.0), axis=1, keepdims=True)
    ends = jnp.where(slot < slots, ends, 1e9)
    return (jnp.transpose(ends)[0:1, :].astype(jnp.int32), ends[:, 0:1].astype(jnp.int32))


def rope_tables(offsets):
    lane = lax.rem(lax.broadcasted_iota(jnp.int32, (1, LANES), 1), HEAD_DIM)
    half_rot = ROT_DIM // 2
    freq_index = lax.rem(lane, half_rot).astype(jnp.float32)
    inverse = jnp.exp(-(2.0 * freq_index / ROT_DIM) * math.log(10000.0))
    angles = offsets * inverse
    cosine, sine = (jnp.cos(angles), jnp.sin(angles))
    keep = jnp.where(lane < ROT_DIM, cosine, 1.0)
    ahead = jnp.where(lane < half_rot, -sine, 0.0)
    behind = jnp.where((lane >= half_rot) & (lane < ROT_DIM), sine, 0.0)
    return (keep, ahead, behind)


def gelu_pair(values):
    square = values * values
    inner = math.sqrt(2.0 / math.pi) * values * (1.0 + 0.044715 * square)
    bent = jnp.tanh(inner)
    half = 0.5 * (1.0 + bent)
    slope = half + 0.5 * values * (1.0 - bent * bent) * math.sqrt(2.0 / math.pi) * (
        1.0 + 3.0 * 0.044715 * square
    )
    return (values * half, slope)


def take(array, index, axis=0):
    return lax.dynamic_index_in_dim(array, index, axis, keepdims=False)


def summed(*terms):
    total = terms[0].astype(jnp.float32)
    for term in terms[1:]:
        total = total + term.astype(jnp.float32)
    return total


def contract(left, right, left_axis, right_axis):
    return lax.dot_general(
        left, right, (((left_axis,), (right_axis,)), ((), ())), preferred_element_type=jnp.float32
    )


MESH_ID = pl.DeviceIdType.MESH


def remote(source, target, send_sem, recv_sem, axis, peer):
    return pltpu.make_async_remote_copy(
        src_ref=source,
        dst_ref=target,
        send_sem=send_sem,
        recv_sem=recv_sem,
        device_id={axis: peer},
        device_id_type=MESH_ID,
    )


def greet_line():
    size = lax.axis_size("dp")
    place = lax.axis_index("dp")
    barrier = pltpu.get_barrier_semaphore()
    core = lax.rem(place, 2)
    peers = [place + 1 - 2 * core, lax.rem(place + 2, size), lax.rem(place + size - 2, size)]
    for peer in peers:
        pl.semaphore_signal(barrier, inc=1, device_id={"dp": peer}, device_id_type=MESH_ID)
    return (barrier, len(peers))


PIECES = 2
VMEM_LIMIT = 60 * 1024 * 1024


def piecewise(body, first=0, last=PIECES):
    def once(piece, carry):
        body(piece)
        return carry

    lax.fori_loop(first, last, once, 0)


class LineGather:
    def __init__(self, own, full, send, recv):
        self.count = lax.axis_size("dp") // 2
        self.place = lax.axis_index("dp")
        self.spot = self.place // 2
        self.core = lax.rem(self.place, 2)
        self.own, self.full, self.send, self.recv = own, full, send, recv
        self.rows = own.shape[0]
        self.part = self.rows // PIECES

    def copy(self, kind, step, piece, chip, peer, from_own=False):
        offset = piece * self.part
        start = pl.multiple_of((2 * chip + self.core) * self.rows + offset, self.part)
        block = self.full.at[pl.ds(start, self.part), :]
        source = block
        if from_own:
            source = self.own.at[pl.ds(pl.multiple_of(offset, self.part), self.part), :]
        sems = (self.send.at[kind, step, piece], self.recv.at[kind, step, piece])
        return remote(source, block, *sems, "dp", peer)

    def rise(self, step, piece):
        return self.copy(0, step, piece, self.spot - step + 1, self.place + 2, step == 1)

    def fall(self, step, piece):
        return self.copy(1, step, piece, self.spot + step - 1, self.place - 2, step == 1)

    def show(self, kind, step, piece):
        chip = self.spot - step if kind == 2 else self.spot + step
        return self.copy(kind, step, piece, chip, self.place + 1 - 2 * self.core, step == 0)

    def keep(self):
        start = pl.multiple_of(self.place * self.rows, self.rows)
        target = self.full.at[pl.ds(start, self.rows), :]
        return pltpu.make_async_copy(self.own, target, self.send.at[3, 0, 0])

    def start(self):
        def body(piece):
            pl.when(self.spot + 1 < self.count)(lambda: self.rise(1, piece).start())
            pl.when(self.spot > 0)(lambda: self.fall(1, piece).start())
            self.show(2, 0, piece).start()

        piecewise(body)
        self.keep().start()

    def advance(self, step, first=0, last=PIECES):
        def body(piece):
            @pl.when(self.spot >= step)
            def _():
                self.rise(step, piece).wait_recv()
                pl.when(self.spot + 1 < self.count)(lambda: self.rise(step + 1, piece).start())
                self.show(2, step, piece).start()

            @pl.when(self.spot + step < self.count)
            def _():
                self.fall(step, piece).wait_recv()
                pl.when(self.spot > 0)(lambda: self.fall(step + 1, piece).start())
                self.show(3, step, piece).start()

        piecewise(body, first, last)

    def finish(self):
        self.keep().wait()

        def body(piece):
            self.show(2, 0, piece).wait()
            for step in range(1, self.count):
                rises = (self.spot + 1 < self.count) & (self.spot >= step - 1)
                falls = (self.spot > 0) & (self.spot + step - 1 < self.count)
                above = self.spot + step < self.count
                pl.when(rises)(lambda step=step: self.rise(step, piece).wait_send())
                pl.when(falls)(lambda step=step: self.fall(step, piece).wait_send())
                pl.when(self.spot >= step)(lambda step=step: self.show(2, step, piece).wait())
                pl.when(above)(lambda step=step: self.show(3, step, piece).wait())

        piecewise(body)


def gather_sems():
    count = lax.axis_size("dp") // 2
    return [pltpu.SemaphoreType.DMA((4, count + 1, PIECES)) for _ in range(2)]


def by_rows(rows, step, body):
    def once(index, carry):
        body(pl.ds(pl.multiple_of(index * step, step), step))
        return carry

    lax.fori_loop(0, rows // step, once, 0)


class LineSum:
    def __init__(self, blocks, from_below, from_above, send, recv):
        self.count = lax.axis_size("dp") // 2
        self.place = lax.axis_index("dp")
        self.spot = self.place // 2
        self.blocks, self.below, self.above = blocks, from_below, from_above
        self.send, self.recv = send, recv
        self.part = blocks.shape[1] // PIECES

    def rows(self, piece):
        return pl.ds(pl.multiple_of(piece * self.part, self.part), self.part)

    def move(self, kind, slots, step, piece, peer, block=None):
        rows = self.rows(piece)
        source = self.blocks.at[block, rows, :] if block is not None else slots.at[step - 2, rows, :]
        sems = (self.send.at[kind, step, piece], self.recv.at[kind, step, piece])
        return remote(source, slots.at[step - 1, rows, :], *sems, "dp", peer)

    def rise(self, step, piece, block=None):
        return self.move(0, self.below, step, piece, self.place + 2, block)

    def fall(self, step, piece, block=None):
        return self.move(1, self.above, step, piece, self.place - 2, block)

    def add(self, slots, step, block, piece):
        def body(rows):
            here = pl.ds(pl.multiple_of(piece * self.part + rows.start, rows.size), rows.size)
            total = slots[step - 2, here, :].astype(jnp.float32)
            total = total + self.blocks[block, here, :].astype(jnp.float32)
            slots[step - 2, here, :] = total.astype(jnp.bfloat16)

        by_rows(self.part, 16, body)

    def advance(self, step, first=0, last=PIECES):
        end = self.count - 1
        mirrored = end - self.spot

        def body(piece):
            pl.when(self.spot == 0)(lambda: self.rise(step, piece, self.count - step).start())
            pl.when(mirrored == 0)(lambda: self.fall(step, piece, step - 1).start())
            if step == 1:
                return

            @pl.when((self.spot > 0) & (self.spot < end) & (self.spot < step))
            def _():
                self.rise(step - 1, piece, 0).wait_recv()
                self.add(self.below, step, self.count + self.spot - step, piece)
                self.rise(step, piece).start()

            @pl.when((mirrored > 0) & (mirrored < end) & (mirrored < step))
            def _():
                self.fall(step - 1, piece, 0).wait_recv()
                self.add(self.above, step, self.spot - self.count + step, piece)
                self.fall(step, piece).start()

        piecewise(body, first, last)

    def hand_out(self, up_out, down_out):
        end = self.count - 1
        mirrored = end - self.spot

        def body(piece):
            rows = self.rows(piece)

            def move(out, slots, block):
                def once(small):
                    here = pl.ds(pl.multiple_of(rows.start + small.start, small.size), small.size)
                    total = self.blocks[block, here, :].astype(jnp.float32)
                    if slots is not None:
                        total = total + slots[end - 2, here, :].astype(jnp.float32)
                    out[here, :] = total.astype(jnp.bfloat16)

                by_rows(self.part, 16, once)

            pl.when(self.spot == 0)(lambda: move(up_out, None, 1))
            pl.when(mirrored == 0)(lambda: move(down_out, None, end - 1))

            @pl.when((self.spot > 0) & (self.spot < end))
            def _():
                self.rise(end - 1, piece, 0).wait_recv()
                move(up_out, self.below, self.spot + 1)

            @pl.when((mirrored > 0) & (mirrored < end))
            def _():
                self.fall(end - 1, piece, 0).wait_recv()
                move(down_out, self.above, self.spot - 1)

            pl.when(self.spot == end)(lambda: move(up_out, None, 0))
            pl.when(mirrored == end)(lambda: move(down_out, None, 0))
            for step in range(1, end):
                rises = (self.spot < step) & (self.spot < end)
                falls = (mirrored < step) & (mirrored < end)
                pl.when(rises)(lambda step=step: self.rise(step, piece, 0).wait_send())
                pl.when(falls)(lambda step=step: self.fall(step, piece, 0).wait_send())

        piecewise(body)

    def finish(self, out, first=0, last=PIECES):
        end = self.count - 1
        mirrored = end - self.spot

        def body(piece):
            start = piece * self.part

            def small(rows):
                return pl.ds(pl.multiple_of(start + rows.start, rows.size), rows.size)

            def begin(rows):
                out[small(rows), :] = self.blocks[self.spot, small(rows), :].astype(out.dtype)

            by_rows(self.part, 16, begin)

            def gain(slots):
                def once(rows):
                    here = small(rows)
                    total = summed(out[here, :], slots[end - 1, here, :])
                    out[here, :] = total.astype(out.dtype)

                by_rows(self.part, 16, once)

            @pl.when(self.spot > 0)
            def _():
                self.rise(end, piece, 0).wait_recv()
                gain(self.below)

            @pl.when(self.spot < end)
            def _():
                self.fall(end, piece, 0).wait_recv()
                gain(self.above)

            for step in range(1, self.count):
                rises = (self.spot < step) & (self.spot < end)
                falls = (mirrored < step) & (mirrored < end)
                pl.when(rises)(lambda step=step: self.rise(step, piece, 0).wait_send())
                pl.when(falls)(lambda step=step: self.fall(step, piece, 0).wait_send())

        piecewise(body, first, last)


def sum_scratch(rows, columns):
    count = lax.axis_size("dp") // 2
    return [
        pltpu.VMEM((count - 1, rows, columns), jnp.bfloat16),
        pltpu.VMEM((count - 1, rows, columns), jnp.bfloat16),
        pltpu.SemaphoreType.DMA((2, count, PIECES)),
        pltpu.SemaphoreType.DMA((2, count, PIECES)),
    ]


class PairProducts:
    def __init__(self, lefts, rights, parcel, sums, send, recv):
        self.count = lax.axis_size("dp") // 2
        self.place = lax.axis_index("dp")
        self.core = lax.rem(self.place, 2)
        self.lefts, self.rights = lefts, rights
        self.parcel, self.sums, self.send, self.recv = parcel, sums, send, recv

    def copy(self, chip):
        return remote(
            self.parcel.at[chip],
            self.sums.at[chip],
            self.send.at[chip],
            self.recv.at[chip],
            "dp",
            self.place + 1 - 2 * self.core,
        )

    def product(self, chip, core, quarter):
        rows = self.sums.shape[1]
        width = self.sums.shape[2] // 4
        start = pl.multiple_of((2 * chip + core) * rows, rows)
        left = self.lefts[quarter][:, pl.ds(start, rows)]
        ref, first = self.rights[quarter]
        return contract(left, ref[:, pl.ds(first, width)], 0, 0)

    def far(self):
        width = self.sums.shape[2] // 4

        def once(chip, carry):
            for quarter in range(4):
                piece = self.product(chip, 1 - self.core, quarter)
                self.parcel[chip, :, pl.ds(quarter * width, width)] = piece.astype(jnp.bfloat16)
            self.copy(chip).start()
            return carry

        lax.fori_loop(0, self.count, once, 0)

    def near(self):
        width = self.sums.shape[2] // 4

        def once(chip, carry):
            self.copy(chip).wait()
            for quarter in range(4):
                columns = pl.ds(quarter * width, width)
                piece = self.product(chip, self.core, quarter)
                total = piece + self.sums[chip, :, columns].astype(jnp.float32)
                self.sums[chip, :, columns] = total.astype(jnp.bfloat16)
            return carry

        lax.fori_loop(0, self.count, once, 0)


def pair_scratch(rows, columns):
    count = lax.axis_size("dp") // 2
    return [
        pltpu.VMEM((count, rows, columns), jnp.bfloat16),
        pltpu.SemaphoreType.DMA((count,)),
        pltpu.SemaphoreType.DMA((count,)),
    ]


class BlockGather:
    def __init__(self, own, full, send, recv):
        self.size = lax.axis_size("mp")
        self.place = lax.axis_index("mp")
        self.own, self.full, self.send, self.recv = own, full, send, recv
        self.rows, self.width = own.shape

    def spread(self, index, rows, owner, peer, first):
        start = pl.multiple_of(owner * self.width, self.width)
        target = self.full.at[rows, pl.ds(start, self.width)]
        source = self.own if first else target
        return remote(source, target, self.send.at[index], self.recv.at[index], "mp", peer)

    def copy(self, index):
        every = pl.ds(0, self.rows)
        if self.size != 4:
            return self.spread(index, every, self.place, lax.rem(self.place + 1 + index, self.size), True)
        beside = self.place + 1 - 2 * lax.rem(self.place, 2)
        above = lax.rem(self.place + 2, 4)
        half = self.rows // 2
        if index < 2:
            return self.spread(index, every, self.place, (beside, above)[index], True)
        if index == 2:
            return self.spread(2, pl.ds(0, half), above, beside, False)
        return self.spread(3, pl.ds(half, half), beside, above, False)

    def keep(self):
        start = pl.multiple_of(self.place * self.width, self.width)
        target = self.full.at[:, pl.ds(start, self.width)]
        return pltpu.make_async_copy(self.own, target, self.send.at[self.size])

    def start(self):
        for index in range(2 if self.size == 4 else self.size - 1):
            self.copy(index).start()
        self.keep().start()

    def forward(self):
        if self.size == 4:
            self.copy(1).wait_recv()
            self.copy(2).start()
            self.copy(0).wait_recv()
            self.copy(3).start()

    def finish(self):
        self.keep().wait()
        for index in range(4 if self.size == 4 else self.size - 1):
            self.copy(index).wait_send()
            if index > 1 or self.size != 4:
                self.copy(index).wait_recv()


def block_sems():
    size = lax.axis_size("mp") + 1
    return [pltpu.SemaphoreType.DMA((size,)), pltpu.SemaphoreType.DMA((size,))]


def field_rows(spread_ref, first_row, index, piece):
    dp_size = lax.axis_size("dp")
    first = lax.axis_index("mp") * dp_size
    devices = [first + owner for owner in range(dp_size)]
    row, lane = divmod(index * piece, LANES)
    return vector_rows(spread_ref, devices, first_row + row, piece, lane)


def vector_rows(spread_ref, devices, row, piece, turn_to=0):
    if piece >= LANES:
        return [
            spread_ref[device, row + part : row + part + 1, :]
            for device in devices
            for part in range(piece // LANES)
        ]
    lane = lax.broadcasted_iota(jnp.int32, (1, LANES), 1)
    fold = LANES // piece
    groups = []
    for first in range(0, len(devices), fold):
        group = jnp.zeros((1, LANES), jnp.float32)
        for part in range(fold):
            values = spread_ref[devices[first + part], row : row + 1, :]
            turn = (part * piece - turn_to) % LANES
            values = pltpu.roll(values, turn, 1) if turn else values
            mine = (lane >= part * piece) & (lane < (part + 1) * piece)
            group = jnp.where(mine, values, group)
        groups.append(group)
    return groups


def round_matrix(source, target):
    size = source.shape[0]
    tile_rows = min(STREAM, size)

    def scope(before, after, sems):
        def where(tile):
            return pl.ds(pl.multiple_of(tile * tile_rows, tile_rows), tile_rows)

        def loads(tile, slot):
            return [
                pltpu.make_async_copy(source.at[where(tile), :], before.at[slot], sems.at[0, slot])
            ]

        def stores(tile, slot):
            return [
                pltpu.make_async_copy(after.at[slot], target.at[where(tile), :], sems.at[1, slot])
            ]

        def compute(tile, slot):
            after[slot] = before[slot].astype(after.dtype)

        stream(size // tile_rows, loads, stores, compute)

    shape = (SLOTS, tile_rows, size)
    pl.run_scoped(
        scope,
        pltpu.VMEM(shape, source.dtype),
        pltpu.VMEM(shape, target.dtype),
        pltpu.SemaphoreType.DMA((2, SLOTS)),
    )


def cast_rows(source, target, here):
    target[here, :] = source[here, :].astype(target.dtype)


def first_kernel(
    w_up_ref,
    w_qkv_hbm,
    w_out_hbm,
    w_down_hbm,
    x_ref,
    gy_ref,
    norm_state,
    qkv_state,
    out_state,
    up_state,
    lengths_ref,
    right_ref,
    turned_out,
    full_ref,
    next_full,
    xn_out,
    gy_out,
    spread_ref,
    stats_ref,
    act_out,
    slope_out,
    sums_out,
    right_low,
    gather_send,
    gather_recv,
    next_send,
    next_recv,
    x_send,
    x_recv,
    gy_send,
    gy_recv,
    small_send,
    small_recv,
    parcel,
    pair_send,
    pair_recv,
    x_full,
    up_ref,
    act_ref,
    slope_ref,
    local_sems,
    block_ref,
    next_ref,
    valid_ref,
    xn_ref,
    gy_full,
    sums_ref,
    w_qkv_ref,
    w_out_ref,
    w_down_ref,
    small_ref,
    padded_ref,
):
    loads = fetch(
        [(w_qkv_hbm, w_qkv_ref), (w_out_hbm, w_out_ref), (w_down_hbm, w_down_ref)],
        local_sems.at[pl.ds(6, 3)],
    )
    piece = norm_state.shape[2]
    up_piece = up_state.shape[1]
    slots = lengths_ref.shape[1]
    columns = lax.axis_size("dp")
    total = columns * lax.axis_size("mp")
    mp_place = lax.axis_index("mp")
    place = mp_place * columns + lax.axis_index("dp")
    barrier = pltpu.get_barrier_semaphore()

    def device(step):
        peer = lax.rem(place + step, total)
        return {"mp": peer // columns, "dp": lax.rem(peer, columns)}

    def greet(step, carry):
        pl.semaphore_signal(barrier, inc=1, device_id=device(step), device_id_type=MESH_ID)
        return carry

    lax.fori_loop(1, total, greet, 0)
    by_rows(block_ref.shape[0], 64, lambda here: cast_rows(w_up_ref, block_ref, here))
    small_ref[...] = jnp.zeros_like(small_ref)
    up_rows = -(-up_piece // LANES)

    def note(first_row, offset, values):
        values = values.astype(jnp.bfloat16).astype(jnp.float32)
        row, lane = divmod(offset, LANES)
        small_ref[0, first_row + row : first_row + row + 1, pl.ds(lane, values.shape[1])] = values

    for kind in range(2):
        note(0, kind * piece, norm_state[0, kind : kind + 1, :])
        note(1 + up_rows, (3 + kind) * piece, out_state[0, kind : kind + 1, :])
    for kind in range(3):
        note(1 + up_rows, kind * piece, qkv_state[kind, 0:1, :])
    for first in range(0, up_piece, LANES):
        note(1, first, up_state[0:1, first : min(first + LANES, up_piece)])
    pl.semaphore_wait(barrier, total - 1)

    def small_copy(step):
        return pltpu.make_async_remote_copy(
            src_ref=small_ref.at[0],
            dst_ref=spread_ref.at[place],
            send_sem=small_send.at[step],
            recv_sem=small_recv.at[step],
            device_id=device(step),
            device_id_type=MESH_ID,
        )

    def begin(step, carry):
        small_copy(step).start()
        return carry

    def end(step, carry):
        small_copy(step).wait()
        return carry

    weight = LineGather(block_ref, full_ref, gather_send, gather_recv)
    later = LineGather(next_ref, next_full, next_send, next_recv)
    rows_x = BlockGather(x_ref, x_full, x_send, x_recv)
    rows_gy = BlockGather(gy_ref, gy_full, gy_send, gy_recv)
    products = PairProducts(
        [gy_full] * 4, quarters(act_ref), parcel, sums_ref, pair_send, pair_recv
    )
    lax.fori_loop(1, total, begin, 0)
    weight.start()
    rows_x.start()
    rows_gy.start()
    spread_ref[place] = small_ref[0]
    rows, width = xn_ref.shape
    depth = block_ref.shape[0]
    head_cols = w_qkv_ref.shape[2]
    for copy in loads:
        copy.wait()
    for kind in range(3):
        next_ref[:, pl.ds(kind * head_cols, head_cols)] = w_qkv_ref[kind].astype(jnp.bfloat16)
    turned = jnp.transpose(w_out_ref[...]).astype(jnp.bfloat16)
    next_ref[:, pl.ds(3 * head_cols, head_cols)] = turned

    def turn_down(here):
        turned_out[:, here] = jnp.transpose(w_down_ref[here, :]).astype(jnp.bfloat16)

    by_rows(w_down_ref.shape[0], depth, turn_down)

    ends_row, _ = ends_of(lengths_ref, padded_ref)

    def mark(here):
        ids = lax.broadcasted_iota(jnp.int32, (ROW_TILE, 1), 0) + here.start
        valid = segment_of(ends_row, ids, 1, slots)[2]
        valid_ref[here, :] = jnp.where(valid, 1.0, 0.0)

    by_rows(rows, ROW_TILE, mark)
    lax.fori_loop(1, total, end, 0)
    weight.advance(1)
    round_matrix(right_ref.at[0, 0, 0], right_low.at[0, 0, 0])
    weight.advance(2)
    round_matrix(right_ref.at[1, 0, 0], right_low.at[1, 0, 0])
    rows_x.forward()
    rows_gy.forward()
    weight.advance(3, 0, 1)
    later.start()
    weight.advance(3, 1)
    for step in range(4, weight.count):
        weight.advance(step)
    rows_x.finish()

    gains = vector_rows(spread_ref, range(total), 0, piece)
    shifts = vector_rows(spread_ref, range(total), 0, piece, piece)

    def normalize(here):
        values = x_full[here, :].astype(jnp.float32)
        mean = jnp.sum(values, axis=1, keepdims=True) * (1.0 / width)
        square = jnp.sum(values * values, axis=1, keepdims=True) * (1.0 / width)
        inv_std = lax.rsqrt(square - mean * mean + norm_eps)
        lanes = lax.broadcasted_iota(jnp.int32, (ROW_TILE, LANES), 1)
        stats_ref[here, :] = jnp.where(
            lanes == 0, mean, jnp.where(lanes == 1, inv_std, valid_ref[here, :])
        )
        for group in range(width // LANES):
            part = (x_full[here, pl.ds(group * LANES, LANES)].astype(jnp.float32) - mean) * inv_std
            part = part * gains[group] + shifts[group]
            xn_ref[here, pl.ds(group * LANES, LANES)] = part.astype(jnp.bfloat16)

    by_rows(rows, ROW_TILE, normalize)
    stores = fetch([(xn_ref, xn_out)], local_sems.at[pl.ds(3, 1)])
    weight.finish()
    load = pltpu.make_async_copy(full_ref, up_ref, local_sems.at[0])
    load.start()
    rows_gy.finish()

    def blank(here):
        kept = gy_full[here, :].astype(jnp.float32) * valid_ref[here, :]
        gy_full[here, :] = kept.astype(jnp.bfloat16)

    by_rows(rows, ROW_TILE, blank)
    stores += fetch([(gy_full, gy_out)], local_sems.at[pl.ds(4, 1)])
    bias = vector_rows(
        spread_ref, [mp_place * columns + owner for owner in range(columns)], 1, up_piece
    )
    quarter_width = up_ref.shape[1] // 4
    groups = quarter_width // LANES
    load.wait()

    def tile(here):
        for quarter in range(4):
            part = pl.ds(quarter * quarter_width, quarter_width)
            shift = jnp.concatenate(bias[quarter * groups : (quarter + 1) * groups], axis=1)
            hidden = contract(xn_ref[here, :], up_ref[:, part], 1, 0) + shift
            activated, slope = gelu_pair(hidden)
            act_ref[here, part] = activated.astype(jnp.bfloat16)
            slope_ref[here, part] = slope.astype(jnp.bfloat16)

    by_rows(rows // 2, ROW_TILE, tile)
    later.advance(1)
    by_rows(rows // 2, ROW_TILE, lambda here: tile(pl.ds(rows // 2 + here.start, here.size)))
    stores += fetch([(act_ref, act_out), (slope_ref, slope_out)], local_sems.at[pl.ds(1, 2)])
    later.advance(2, 0, 1)
    products.far()
    later.advance(2, 1)
    products.near()
    stores += fetch([(sums_ref, sums_out)], local_sems.at[pl.ds(5, 1)])
    for step in range(3, later.count):
        later.advance(step)
    later.finish()
    for store in stores:
        store.wait()


def first_step(weights, tokens, cotangent, states, lengths, right):
    mp_size, dp_size = (lax.axis_size("mp"), lax.axis_size("dp"))
    count = dp_size // 2
    rows = tokens.shape[0]
    wide = (rows, tokens.shape[1] * mp_size)
    part, columns = weights[0].shape
    total = mp_size * dp_size
    low = jnp.bfloat16
    return carrying(
        first_kernel,
        1,
        weights + (tokens, cotangent) + states + (lengths, right),
        "vhhhhhvvvvvh",
        [
            ((part, columns), low),
            ((part * dp_size, columns), low),
            ((part * dp_size, columns), low),
            (wide, low),
            (wide, low),
            ((total, 8, LANES), jnp.float32),
            ((rows, LANES), jnp.float32),
            ((rows, columns), low),
            ((rows, columns), low),
            ((count, part, columns), low),
            (right.shape, low),
        ],
        "vhhhhvvhhhh",
        gather_sems()
        + gather_sems()
        + block_sems()
        + block_sems()
        + [pltpu.SemaphoreType.DMA((total,)), pltpu.SemaphoreType.DMA((total,))]
        + pair_scratch(part, columns)
        + [
            pltpu.VMEM(wide, low),
            pltpu.VMEM((part * dp_size, columns), low),
            pltpu.VMEM((rows, columns), low),
            pltpu.VMEM((rows, columns), low),
            pltpu.SemaphoreType.DMA((9,)),
            pltpu.VMEM((part, columns), low),
            pltpu.VMEM((part, columns), low),
            pltpu.VMEM((rows, 1), jnp.float32),
            pltpu.VMEM(wide, low),
            pltpu.VMEM(wide, low),
            pltpu.VMEM((count, part, columns), low),
        ]
        + [pltpu.VMEM(weight.shape, weight.dtype) for weight in weights[1:]]
        + [pltpu.VMEM((1, 8, LANES), jnp.float32), pltpu.VMEM((8, LANES), jnp.float32)],
        4 * rows * wide[1] * columns,
        "gathers_beside_hidden",
    )


def greet_and_wait():
    barrier, count = greet_line()
    pl.semaphore_wait(barrier, count)


def quarters(ref):
    width = ref.shape[1] // 4
    return [(ref, quarter * width) for quarter in range(4)]


def carrying(kernel, collective_id, operands, in_places, outs, out_places, scratch, flops, name):
    spaces = {"h": pl.BlockSpec(memory_space=pl.ANY), "v": pl.BlockSpec(memory_space=pltpu.VMEM)}
    return pl.pallas_call(
        kernel,
        in_specs=[spaces[place] for place in in_places],
        out_specs=[spaces[place] for place in out_places],
        out_shape=[jax.ShapeDtypeStruct(shape, dtype) for shape, dtype in outs],
        scratch_shapes=scratch,
        compiler_params=pltpu.CompilerParams(
            collective_id=collective_id, has_side_effects=True, vmem_limit_bytes=VMEM_LIMIT
        ),
        cost_estimate=pl.CostEstimate(flops=flops, bytes_accessed=1 << 25, transcendentals=0),
        name=name,
    )(*operands)


PLAN = {
    "projected": (),
    0: ((1, 0), (1, 1)),
    1: ((2, 0),),
    "attended": ((2, 1),),
    "far": ((3, 0),),
}


def third_kernel(
    head_cols,
    piece,
    field_row,
    block_ref,
    ready_hbm,
    xn_hbm,
    gy_hbm,
    weight_hbm,
    spread_ref,
    lengths_ref,
    full_ref,
    grad_out,
    or_out,
    sums_out,
    owned_ref,
    vector_ref,
    gather_send,
    gather_recv,
    below,
    above,
    line_send,
    line_recv,
    parcel,
    pair_send,
    pair_recv,
    mask_ref,
    low_ref,
    go_ref,
    dq_acc,
    dk_acc,
    dv_acc,
    ready_ref,
    xn_ref,
    gy_ref,
    weight_ref,
    grad_ref,
    or_ref,
    local_sems,
    keep_ref,
    ahead_ref,
    behind_ref,
    sums_ref,
    padded_ref,
):
    loads = [
        pltpu.make_async_copy(source, target, local_sems.at[index])
        for index, (source, target) in enumerate(
            [(ready_hbm, ready_ref), (xn_hbm, xn_ref), (weight_hbm, weight_ref), (gy_hbm, gy_ref)]
        )
    ]
    for load in loads:
        load.start()
    weight = LineGather(block_ref, full_ref, gather_send, gather_recv)
    line = LineSum(ready_ref, below, above, line_send, line_recv)
    rights = [(grad_ref, kind * head_cols) for kind in range(3)] + [(or_ref, 0)]
    products = PairProducts(
        [xn_ref] * 3 + [gy_ref], rights, parcel, sums_ref, pair_send, pair_recv
    )
    greet_and_wait()
    weight.start()
    loads[0].wait()
    line.advance(1)

    rows = xn_ref.shape[0]
    tiles = rows // ROW_TILE
    scale = HEAD_DIM ** (-0.5)
    slots = lengths_ref.shape[1]
    ends_row, ends_col = ends_of(lengths_ref, padded_ref)
    row_positions = lax.broadcasted_iota(jnp.int32, (1, rows), 1)
    seg_row, _, row_valid = segment_of(ends_col, row_positions, 0, slots)
    seg_row = jnp.where(row_valid, seg_row, slots + row_positions)
    for tile in range(tiles):
        here = pl.ds(tile * ROW_TILE, ROW_TILE)
        reach = (tile + 1) * ROW_TILE
        shape = (ROW_TILE, reach)
        ids = lax.broadcasted_iota(jnp.int32, (ROW_TILE, 1), 0) + tile * ROW_TILE
        seg_col, starting, valid = segment_of(ends_row, ids, 1, slots)
        seg_col = jnp.where(valid, seg_col, slots + ids)
        tables = rope_tables((ids - starting).astype(jnp.float32))
        for ref, table in zip((keep_ref, ahead_ref, behind_ref), tables):
            ref[here, :] = table
        key_ids = lax.broadcasted_iota(jnp.int32, shape, 1)
        allowed = (seg_col == seg_row[:, :reach]) & (key_ids <= ids)
        mask_ref[here, pl.ds(0, reach)] = jnp.where(allowed, 0.0, masked_score)
    biases = [
        jnp.concatenate(field_rows(spread_ref, field_row, kind, piece), axis=1) for kind in range(3)
    ]

    def turned(values, here, direction):
        ahead = pltpu.roll(values, LANES - ROT_DIM // 2, 1)
        behind = pltpu.roll(values, ROT_DIM // 2, 1)
        return values * keep_ref[here, :] + direction * (
            ahead * ahead_ref[here, :] + behind * behind_ref[here, :]
        )

    def project(here):
        for kind in range(3):
            columns = pl.ds(kind * head_cols, head_cols)
            values = contract(xn_ref[here, :], weight_ref[:, columns], 1, 0) + biases[kind]
            if kind == 2:
                low_ref[here, columns] = values.astype(jnp.bfloat16)
                continue
            for first in range(0, head_cols, LANES):
                part = turned(values[:, first : first + LANES], here, 1.0).astype(jnp.bfloat16)
                if kind == 0:
                    part = part * scale
                low_ref[here, pl.ds(kind * head_cols + first, LANES)] = part
        columns = pl.ds(3 * head_cols, head_cols)
        values = contract(gy_ref[here, :], weight_ref[:, columns], 1, 0)
        go_ref[here, :] = values.astype(jnp.bfloat16)

    for load in loads[1:]:
        load.wait()
    by_rows(rows, ROW_TILE, project)
    vector_ref[...] = jnp.zeros_like(vector_ref)

    done = set()
    pairs = head_cols // LANES

    def events(wanted):
        for step, piece in wanted:
            if (step, piece) not in done and step < weight.count:
                done.add((step, piece))
                weight.advance(step, piece, piece + 1)
                if step + 1 < weight.count:
                    line.advance(step + 1, piece, piece + 1)

    lane = lax.broadcasted_iota(jnp.int32, (ROW_TILE, LANES), 1)
    first_head = lane < HEAD_DIM

    def one_pair(pair, carry):
        column = pl.multiple_of(pair * LANES, LANES)
        q_lanes = pl.ds(column, LANES)
        k_lanes = pl.ds(pl.multiple_of(head_cols + column, LANES), LANES)
        v_lanes = pl.ds(pl.multiple_of(2 * head_cols + column, LANES), LANES)
        dk_acc[...] = jnp.zeros_like(dk_acc)
        dv_acc[...] = jnp.zeros_like(dv_acc)
        for tile in range(tiles):
            here = pl.ds(tile * ROW_TILE, ROW_TILE)
            keys = pl.ds(0, (tile + 1) * ROW_TILE)
            outs = []
            query_grads = []
            for head in range(LANES // HEAD_DIM):
                mine = first_head if head == 0 else jnp.logical_not(first_head)
                none = jnp.zeros((ROW_TILE, LANES), jnp.bfloat16)
                query = jnp.where(mine, low_ref[here, q_lanes], none)
                grad_out = jnp.where(mine, go_ref[here, q_lanes], none)
                scores = contract(query, low_ref[keys, k_lanes], 1, 1) + mask_ref[here, keys]
                peak = jnp.max(scores, axis=1, keepdims=True)
                weights = jnp.exp(scores - peak)
                share = 1.0 / jnp.sum(weights, axis=1, keepdims=True)
                probs = weights * share
                probs_low = probs.astype(jnp.bfloat16)
                outs.append(contract(probs_low, low_ref[keys, v_lanes], 1, 0))
                grad_probs = contract(grad_out, low_ref[keys, v_lanes], 1, 1)
                delta = jnp.sum(probs * grad_probs, axis=1, keepdims=True)
                grad_scores = (probs * (grad_probs - delta)).astype(jnp.bfloat16)
                query_grads.append(contract(grad_scores, low_ref[keys, k_lanes], 1, 0))
                dk_acc[keys, :] += contract(grad_scores, query, 0, 0)
                dv_acc[keys, :] += contract(probs_low, grad_out, 0, 0)
            or_ref[here, q_lanes] = jnp.where(first_head, outs[0], outs[1]).astype(jnp.bfloat16)
            dq_acc[here, :] = jnp.where(first_head, query_grads[0], query_grads[1])
        for tile in range(tiles):
            here = pl.ds(tile * ROW_TILE, ROW_TILE)
            parts = [
                (q_lanes, turned(dq_acc[here, :], here, -1.0) * scale),
                (k_lanes, turned(dk_acc[here, :], here, -1.0)),
                (v_lanes, dv_acc[here, :]),
            ]
            for lanes, part in parts:
                part = part.astype(jnp.bfloat16)
                grad_ref[here, lanes] = part
                vector_ref[0:1, lanes] += jnp.sum(part.astype(jnp.float32), axis=0, keepdims=True)

        for index in range(pairs):
            if index in PLAN:
                pl.when(pair == index)(functools.partial(events, PLAN[index]))
        return carry

    events(PLAN["projected"])
    lax.fori_loop(0, pairs, one_pair, 0)
    stores = [
        pltpu.make_async_copy(grad_ref, grad_out, local_sems.at[4]),
        pltpu.make_async_copy(or_ref, or_out, local_sems.at[5]),
    ]
    for store in stores:
        store.start()
    events(PLAN["attended"])
    products.far()
    events(PLAN["far"])
    products.near()
    stores += fetch([(sums_ref, sums_out)], local_sems.at[pl.ds(6, 1)])
    events([(step, piece) for step in range(1, weight.count) for piece in range(PIECES)])
    line.finish(owned_ref)
    weight.finish()
    for store in stores:
        store.wait()


def third_step(
    block, ready, normed, grad_rows, full_qkvo, spread, lengths, piece, field_row
):
    rows, width = normed.shape
    count = lax.axis_size("dp") // 2
    columns = full_qkvo.shape[1]
    head_cols = columns // 4
    part = width // (2 * count)
    low = jnp.bfloat16
    return carrying(
        functools.partial(third_kernel, head_cols, piece, field_row),
        5,
        (
            block,
            ready,
            normed,
            grad_rows,
            full_qkvo,
            spread,
            lengths,
        ),
        "hhhhhvv",
        [
            ((width, block.shape[1]), low),
            ((rows, 3 * head_cols), low),
            ((rows, head_cols), low),
            ((count, part, columns), low),
            ((part, ready.shape[2]), low),
            ((8, columns), jnp.float32),
        ],
        "hhhhvv",
        gather_sems()
        + sum_scratch(part, ready.shape[2])
        + pair_scratch(part, columns)
        + [
            pltpu.VMEM((rows, rows), jnp.float32),
            pltpu.VMEM((rows, 3 * head_cols), low),
            pltpu.VMEM((rows, head_cols), low),
            pltpu.VMEM((rows, LANES), jnp.float32),
            pltpu.VMEM((rows, LANES), jnp.float32),
            pltpu.VMEM((rows, LANES), jnp.float32),
            pltpu.VMEM(ready.shape, low),
            pltpu.VMEM((rows, width), low),
            pltpu.VMEM((rows, width), low),
            pltpu.VMEM((width, columns), low),
            pltpu.VMEM((rows, 3 * head_cols), low),
            pltpu.VMEM((rows, head_cols), low),
            pltpu.SemaphoreType.DMA((7,)),
            pltpu.VMEM((rows, LANES), jnp.float32),
            pltpu.VMEM((rows, LANES), jnp.float32),
            pltpu.VMEM((rows, LANES), jnp.float32),
            pltpu.VMEM((count, part, columns), low),
            pltpu.VMEM((8, LANES), jnp.float32),
        ],
        4 * rows * width * columns + 12 * rows * rows * head_cols,
        "lines_beside_attention",
    )


def fourth_kernel(
    head_cols,
    piece,
    field_row,
    ready_hbm,
    xn_hbm,
    gy_hbm,
    down_hbm,
    slope_hbm,
    act_hbm,
    or_hbm,
    qkvo_hbm,
    x_ref,
    spread_ref,
    gh_out,
    sums_out,
    up_send,
    down_send,
    own_ref,
    vector_ref,
    out_ref,
    below,
    above,
    line_send,
    line_recv,
    parcel,
    pair_send,
    pair_recv,
    t_parts,
    t_got,
    t_send,
    t_recv,
    ready_ref,
    xn_ref,
    gy_ref,
    down_ref,
    wide_ref,
    or_ref,
    weight_ref,
    gh_ref,
    local_sems,
    sums_ref,
):
    loads = [
        pltpu.make_async_copy(source, target, local_sems.at[index])
        for index, (source, target) in enumerate(
            [
                (ready_hbm, ready_ref),
                (down_hbm, down_ref),
                (act_hbm, wide_ref),
                (or_hbm, or_ref),
                (qkvo_hbm.at[:, pl.ds(3 * head_cols, head_cols)], weight_ref),
                (gy_hbm, gy_ref),
                (xn_hbm, xn_ref),
            ]
        )
    ]
    for load in loads:
        load.start()
    line = LineSum(ready_ref, below, above, line_send, line_recv)
    branches = BlockScatter(t_parts, t_got, t_send, t_recv)
    products = PairProducts(
        [xn_ref] * 4, quarters(gh_ref), parcel, sums_ref, pair_send, pair_recv
    )
    barrier, count = greet_line()
    count += greet_block()
    pl.semaphore_wait(barrier, count)
    loads[0].wait()
    line.advance(1)
    for load in loads[1:5]:
        load.wait()
    rows, share_width = x_ref.shape
    width = down_ref.shape[1] // 4
    vector_ref[...] = jnp.zeros_like(vector_ref)

    def tile(here):
        for quarter in range(4):
            columns = pl.ds(quarter * width, width)
            grad_act = contract(gy_ref[here, :], down_ref[:, columns], 1, 0)
            grad_hidden = grad_act * wide_ref[here, columns].astype(jnp.float32)
            grad_hidden = grad_hidden.astype(jnp.bfloat16)
            gh_ref[here, columns] = grad_hidden
            vector_ref[0:1, columns] += jnp.sum(
                grad_hidden.astype(jnp.float32), axis=0, keepdims=True
            )

    def branch(share):
        start = pl.multiple_of(branches.owner(share) * share_width, share_width)
        where = pl.ds(start, share_width)

        def once(here):
            part = contract(or_ref[here, :], weight_ref[where, :], 1, 1)
            part = part + contract(wide_ref[here, :], down_ref[where, :], 1, 1)
            t_parts[share, here, :] = part.astype(jnp.bfloat16)

        by_rows(rows, 2 * ROW_TILE, once)
        branches.after(share)

    shares = branches.size
    for share in range(shares):
        branch(share)
        if share == 2:
            line.advance(2, 0, 1)
    late = pltpu.make_async_copy(slope_hbm, wide_ref, local_sems.at[7])
    late.start()
    line.advance(2, 1)
    branches.second()
    for load in loads[5:]:
        load.wait()
    late.wait()
    by_rows(rows, ROW_TILE, tile)
    stores = fetch([(gh_ref, gh_out)], local_sems.at[pl.ds(8, 1)])
    products.far()
    for step in range(3, line.count - 1):
        line.advance(step)
    branches.finish()
    biases = [
        jnp.concatenate(field_rows(spread_ref, field_row, kind, piece), axis=1) for kind in (3, 4)
    ]
    for tile_index in range(rows // ROW_TILE):
        here = pl.ds(tile_index * ROW_TILE, ROW_TILE)
        total = x_ref[here, :].astype(jnp.float32) + branches.total(tile_index, ROW_TILE)
        total = total + biases[0] + biases[1]
        out_ref[here, :] = total.astype(jnp.bfloat16)
    products.near()
    stores += fetch([(sums_ref, sums_out)], local_sems.at[pl.ds(9, 1)])
    by_rows(own_ref.shape[0], 32, lambda here: keep_block(ready_ref, line.spot, own_ref, here))
    line.hand_out(up_send, down_send)
    for store in stores:
        store.wait()


def fourth_step(
    ready,
    normed,
    grad_rows,
    turned_down,
    slope,
    activated,
    attended,
    full_qkvo,
    tokens,
    spread,
    piece,
    field_row,
):
    rows, width = normed.shape
    head_cols = attended.shape[1]
    count, part, columns = ready.shape
    low = jnp.bfloat16
    return carrying(
        functools.partial(fourth_kernel, head_cols, piece, field_row),
        6,
        (
            ready,
            normed,
            grad_rows,
            turned_down,
            slope,
            activated,
            attended,
            full_qkvo,
            tokens,
            spread,
        ),
        "hhhhhhhhvv",
        [
            ((rows, columns), low),
            ((count, part, columns), low),
            ((part, columns), low),
            ((part, columns), low),
            ((part, columns), low),
            ((8, columns), jnp.float32),
            (tokens.shape, low),
        ],
        "hhvvvvv",
        sum_scratch(part, columns)
        + pair_scratch(part, columns)
        + scatter_scratch(rows, tokens.shape[1])
        + [
            pltpu.VMEM(ready.shape, low),
            pltpu.VMEM((rows, width), low),
            pltpu.VMEM((rows, width), low),
            pltpu.VMEM((width, columns), low),
            pltpu.VMEM((rows, columns), low),
            pltpu.VMEM((rows, head_cols), low),
            pltpu.VMEM((width, head_cols), low),
            pltpu.VMEM((rows, columns), low),
            pltpu.SemaphoreType.DMA((10,)),
            pltpu.VMEM((count, part, columns), low),
        ],
        6 * rows * width * columns,
        "line_beside_hidden_grad",
    )


def greet_block():
    size = lax.axis_size("mp")
    place = lax.axis_index("mp")
    barrier = pltpu.get_barrier_semaphore()
    for step in range(1, size):
        peer = lax.rem(place + step, size)
        pl.semaphore_signal(barrier, inc=1, device_id={"mp": peer}, device_id_type=MESH_ID)
    return size - 1


class BlockScatter:
    def __init__(self, parts, got, send, recv):
        self.size = lax.axis_size("mp")
        self.place = lax.axis_index("mp")
        self.parts, self.got, self.send, self.recv = parts, got, send, recv
        self.half = parts.shape[1] // 2
        self.beside = self.place + 1 - 2 * lax.rem(self.place, 2)
        self.above = lax.rem(self.place + 2, 4)

    def owner(self, index):
        if self.size == 4:
            return [lax.rem(self.beside + 2, 4), self.beside, self.above, self.place][index]
        return lax.rem(self.place + 1 + index, self.size)

    def copy(self, index):
        if self.size == 4:
            part, bottom, peer = [
                (0, 0, self.beside),
                (0, 1, self.above),
                (1, 0, self.beside),
                (2, 1, self.above),
                (2, 0, self.above),
                (1, 1, self.beside),
            ][index]
            source = self.parts.at[part, pl.ds(bottom * self.half, self.half), :]
        else:
            source = self.parts.at[index]
            peer = self.owner(index)
        sems = (self.send.at[index], self.recv.at[index])
        return remote(source, self.got.at[index], *sems, "mp", peer)

    def after(self, index):
        if self.size != 4:
            if index < self.size - 1:
                self.copy(index).start()
            return
        for number in ((0, 1), (2,), (3,), ())[index]:
            self.copy(number).start()

    def second(self):
        if self.size != 4:
            return
        for number, part, bottom in ((0, 2, 0), (1, 1, 1)):
            self.copy(number).wait_recv()

            def body(rows, number=number, part=part, bottom=bottom):
                here = pl.ds(bottom * self.half + rows.start, rows.size)
                total = summed(self.parts[part, here, :], self.got[number, rows, :])
                self.parts[part, here, :] = total.astype(jnp.bfloat16)

            by_rows(self.half, 64, body)
            self.copy(number + 4).start()

    def finish(self):
        if self.size != 4:
            for index in range(self.size - 1):
                self.copy(index).wait()
            return
        for index in range(6):
            if index > 1:
                self.copy(index).wait_recv()
            self.copy(index).wait_send()

    def total(self, tile, rows):
        here = pl.ds(tile * rows, rows)
        own = self.parts[self.size - 1, here, :]
        if self.size != 4:
            return summed(own, *[self.got[index, here, :] for index in range(self.size - 1)])
        bottom = (tile * rows) // self.half
        there = pl.ds(tile * rows - bottom * self.half, rows)
        return summed(own, self.got[2 + bottom, there, :], self.got[4 + bottom, there, :])


def scatter_scratch(rows, width):
    size = lax.axis_size("mp")
    slots = (6, rows // 2, width) if size == 4 else (size - 1, rows, width)
    return [
        pltpu.VMEM((size, rows, width), jnp.bfloat16),
        pltpu.VMEM(slots, jnp.bfloat16),
        pltpu.SemaphoreType.DMA((slots[0],)),
        pltpu.SemaphoreType.DMA((slots[0],)),
    ]


STREAM = 256
SLOTS = 3


def stream(tiles, loads, stores, compute, primed=False):
    ahead = SLOTS - 1
    if not primed:
        prime(tiles, loads)

    def once(tile, carry):
        slot = lax.rem(tile, SLOTS)

        @pl.when(tile + ahead < tiles)
        def _():
            for copy in loads(tile + ahead, lax.rem(tile + ahead, SLOTS)):
                copy.start()

        for copy in loads(tile, slot):
            copy.wait()

        @pl.when(tile >= SLOTS)
        def _():
            for copy in stores(tile - SLOTS, slot):
                copy.wait()

        compute(tile, slot)
        for copy in stores(tile, slot):
            copy.start()
        return carry

    lax.fori_loop(0, tiles, once, 0)
    for tile in range(max(tiles - SLOTS, 0), tiles):
        for copy in stores(tile, tile % SLOTS):
            copy.wait()


def prime(tiles, loads):
    for tile in range(min(SLOTS - 1, tiles)):
        for copy in loads(tile, tile):
            copy.start()


def fetch(pairs, sems):
    copies = [
        pltpu.make_async_copy(source, target, sems.at[index])
        for index, (source, target) in enumerate(pairs)
    ]
    for copy in copies:
        copy.start()
    return copies


def fifth_kernel(
    head_cols,
    piece,
    ready_hbm,
    gh_hbm,
    grad_hbm,
    qkvo_ref,
    up_ref,
    x_hbm,
    gy_hbm,
    stats_hbm,
    spread_ref,
    vector_three,
    vector_four,
    earlier,
    earlier_rising,
    earlier_falling,
    gained_out,
    terms_out,
    up_send,
    down_send,
    own_ref,
    sums_ref,
    below,
    above,
    line_send,
    line_recv,
    g_parts,
    g_got,
    g_send,
    g_recv,
    terms_ref,
    terms_got,
    terms_send,
    terms_recv,
    vector_ref,
    vector_got,
    vector_send,
    vector_recv,
    ready_ref,
    gh_ref,
    grad_ref,
    x_ref,
    gy_ref,
    stats_ref,
    gained_ref,
    load_sems,
):
    loads = fetch(
        [
            (ready_hbm, ready_ref),
            (grad_hbm, grad_ref),
            (gh_hbm, gh_ref),
            (x_hbm, x_ref),
            (gy_hbm, gy_ref),
            (stats_hbm, stats_ref),
        ],
        load_sems,
    )
    line = LineSum(ready_ref, below, above, line_send, line_recv)
    from_norm = BlockScatter(g_parts, g_got, g_send, g_recv)
    mp_size = from_norm.size
    mp_place = from_norm.place
    dp_size = lax.axis_size("dp")
    dp_place = lax.axis_index("dp")
    rows, width = x_ref.shape
    tiles = rows // ROW_TILE
    barrier = pltpu.get_barrier_semaphore()

    def greet(step, carry):
        peer = lax.rem(dp_place + step, dp_size)
        pl.semaphore_signal(barrier, inc=1, device_id={"dp": peer}, device_id_type=MESH_ID)
        return carry

    lax.fori_loop(1, dp_size, greet, 0)
    pl.semaphore_wait(barrier, dp_size - 1 + greet_block())
    loads[0].wait()
    line.advance(1)
    for load in loads[1:3]:
        load.wait()

    def parts(one_ref, two_ref, sems):
        def load(share):
            start = pl.multiple_of(from_norm.owner(share) * width, width)
            slot = share % 2
            where = pl.ds(start, width)
            narrow = pl.ds(0, 3 * head_cols)
            return [
                pltpu.make_async_copy(qkvo_ref.at[where, narrow], one_ref.at[slot], sems.at[0, slot]),
                pltpu.make_async_copy(up_ref.at[where, :], two_ref.at[slot], sems.at[1, slot]),
            ]

        for copy in load(0):
            copy.start()
        for share in range(mp_size):
            slot = share % 2
            for copy in load(share):
                copy.wait()
            if share + 1 < mp_size:
                for copy in load(share + 1):
                    copy.start()

            def tile(here, share=share, slot=slot):
                part = contract(grad_ref[here, :], one_ref[slot], 1, 1)
                part = part + contract(gh_ref[here, :], two_ref[slot], 1, 1)
                g_parts[share, here, :] = part.astype(jnp.bfloat16)

            by_rows(rows, 2 * ROW_TILE, tile)
            from_norm.after(share)

    columns = up_ref.shape[1]
    pl.run_scoped(
        parts,
        pltpu.VMEM((2, width, 3 * head_cols), jnp.bfloat16),
        pltpu.VMEM((2, width, columns), jnp.bfloat16),
        pltpu.SemaphoreType.DMA((2, 2)),
    )
    for step in range(2, line.count - 1):
        line.advance(step)
    from_norm.second()
    for load in loads[3:]:
        load.wait()
    from_norm.finish()

    def lane_pair(first, second):
        lane = lax.broadcasted_iota(jnp.int32, (ROW_TILE, LANES), 1)
        return jnp.where(lane == 0, first, jnp.where(lane == 1, second, 0.0))

    owners = [mp_place * dp_size + owner for owner in range(dp_size)]
    gain = jnp.concatenate(vector_rows(spread_ref, owners, 0, piece), axis=1)
    sums = [jnp.zeros((1, width), jnp.float32) for _ in range(3)]
    for tile in range(tiles):
        here = pl.ds(tile * ROW_TILE, ROW_TILE)
        normalized = (x_ref[here, :].astype(jnp.float32) - stats_ref[here, 0:1]) * stats_ref[here, 1:2]
        grad = from_norm.total(tile, ROW_TILE)
        gained = grad * gain
        gained_ref[here, :] = gained
        terms = lane_pair(
            jnp.sum(gained, axis=1, keepdims=True),
            jnp.sum(gained * normalized, axis=1, keepdims=True),
        )
        terms_ref[:, here] = jnp.transpose(terms)[:8, :]
        upstream = gy_ref[here, :].astype(jnp.float32) * stats_ref[here, 2:3]
        sums[0] += jnp.sum(grad * normalized, axis=0, keepdims=True)
        sums[1] += jnp.sum(grad, axis=0, keepdims=True)
        sums[2] += jnp.sum(upstream, axis=0, keepdims=True)

    store = pltpu.make_async_copy(gained_ref, gained_out, load_sems.at[len(loads)])
    store.start()
    three_width = vector_three.shape[1]
    fields = [vector_three[0:1, pl.ds(0, three_width - head_cols)], vector_four[0:1, :]] + sums
    flat = jnp.concatenate(fields, axis=1)
    per_row = vector_ref.shape[1]
    for row in range(8):
        part = flat[:, row * per_row : (row + 1) * per_row]
        if part.shape[1]:
            vector_ref[row : row + 1, pl.ds(0, part.shape[1])] = part
    def terms_copy(step):
        peer = lax.rem(mp_place + step, mp_size)
        slot = step - 1
        sems = (terms_send.at[slot], terms_recv.at[slot])
        return remote(terms_ref, terms_got.at[slot], *sems, "mp", peer)

    def vector_copy(step):
        peer = lax.rem(dp_place + step, dp_size)
        slot = step - 1
        sems = (vector_send.at[slot], vector_recv.at[slot])
        return remote(vector_ref, vector_got.at[slot], *sems, "dp", peer)

    def vector_begin(step, carry):
        vector_copy(step).start()
        return carry

    for step in range(1, mp_size):
        terms_copy(step).start()
    lax.fori_loop(1, dp_size, vector_begin, 0)
    def vector_end(step, carry):
        vector_copy(step).wait()
        return carry

    by_rows(own_ref.shape[0], 32, lambda here: keep_block(ready_ref, line.spot, own_ref, here))
    line.hand_out(up_send, down_send)
    terms = terms_ref[...]
    for step in range(1, mp_size):
        terms_copy(step).wait()
        terms = terms + terms_got[step - 1]
    terms_out[...] = terms
    lax.fori_loop(1, dp_size, vector_end, 0)
    total = vector_ref[...]
    for slot in range(dp_size - 1):
        total = total + vector_got[slot]
    flat = jnp.concatenate([total[row : row + 1, :] for row in range(8)], axis=1)
    start = 0
    for row, field in enumerate(fields):
        sums_ref[row : row + 1, pl.ds(0, field.shape[1])] = flat[:, start : start + field.shape[1]]
        start += field.shape[1]
    store.wait()


def keep_block(blocks, index, out, here):
    out[here, :] = blocks[index, here, :]


def fifth_step(
    ready,
    grad_hidden,
    grad_projected,
    full_qkvo,
    full_up,
    tokens,
    cotangent,
    stats,
    spread,
    vector_three,
    vector_four,
    earlier,
    piece,
):
    rows, width = tokens.shape
    head_cols = grad_projected.shape[1] // 3
    count, part, columns = ready.shape
    mp_size = lax.axis_size("mp")
    dp_size = lax.axis_size("dp")
    low = jnp.bfloat16
    exact = jnp.float32
    packed = 3 * head_cols + columns + 3 * width
    packed = -(-packed // (8 * LANES)) * LANES
    return carrying(
        functools.partial(fifth_kernel, head_cols, piece),
        7,
        (
            ready,
            grad_hidden,
            grad_projected,
            full_qkvo,
            full_up,
            tokens,
            cotangent,
            stats,
            spread,
            vector_three,
            vector_four,
        )
        + earlier,
        "hhhhhhhhvvvhhh",
        [
            ((rows, width), exact),
            ((8, rows), exact),
            ((part, columns), low),
            ((part, columns), low),
            ((part, columns), low),
            ((8, columns), exact),
        ],
        "hvvvvv",
        sum_scratch(part, columns)
        + scatter_scratch(rows, width)
        + [
            pltpu.VMEM((8, rows), exact),
            pltpu.VMEM((mp_size - 1, 8, rows), exact),
            pltpu.SemaphoreType.DMA((mp_size - 1,)),
            pltpu.SemaphoreType.DMA((mp_size - 1,)),
            pltpu.VMEM((8, packed), exact),
            pltpu.VMEM((dp_size - 1, 8, packed), exact),
            pltpu.SemaphoreType.DMA((dp_size - 1,)),
            pltpu.SemaphoreType.DMA((dp_size - 1,)),
            pltpu.VMEM(ready.shape, low),
            pltpu.VMEM((rows, columns), low),
            pltpu.VMEM((rows, 3 * head_cols), low),
            pltpu.VMEM((rows, width), low),
            pltpu.VMEM((rows, width), low),
            pltpu.VMEM(stats.shape, exact),
            pltpu.VMEM((rows, width), exact),
            pltpu.SemaphoreType.DMA((7,)),
        ],
        4 * rows * width * mp_size * columns,
        "line_beside_norm_grad",
    )


class Averager:
    def __init__(self, grad, stats, stats_out, buffers, sems):
        self.grad, self.stats, self.stats_out = grad, stats, stats_out
        self.stat_in, self.stat_new, self.root_in, self.side_in, self.side_new = buffers
        self.sems = sems
        self.tile_rows = self.stat_in.shape[1]
        self.tiles = grad.shape[1] // self.tile_rows

    def where(self, tile):
        return pl.ds(pl.multiple_of(tile * self.tile_rows, self.tile_rows), self.tile_rows)

    def loads(self, tile, slot):
        pairs = [
            (self.stats.at[0, 0, 0, self.where(tile), :], self.stat_in),
            (self.root_tile(tile), self.root_in),
            (self.side(self.master, tile), self.side_in),
        ]
        return [
            pltpu.make_async_copy(source, target.at[slot], self.sems.at[index, slot])
            for index, (source, target) in enumerate(pairs)
        ]

    def stores(self, tile, slot):
        pairs = [
            (self.stat_new, self.stats_out.at[0, 0, self.where(tile), :]),
            (self.side_new, self.side(self.master_out, tile)),
        ]
        return [
            pltpu.make_async_copy(source.at[slot], target, self.sems.at[3 + index, slot])
            for index, (source, target) in enumerate(pairs)
        ]

    def compute(self, tile, slot):
        product = contract(self.grad[:, self.where(tile)], self.grad[...], 0, 0)
        self.stat_new[slot] = 0.5 * self.stat_in[slot].astype(jnp.float32) + 0.5 * product
        step = self.step(self.root_in[slot].astype(jnp.bfloat16))
        self.side_new[slot] = self.side_in[slot] - matrix_rate * step

    def start(self):
        prime(self.tiles, self.loads)

    def run(self):
        stream(self.tiles, self.loads, self.stores, self.compute, True)


class WideUnit(Averager):
    def __init__(self, grad, stats, stats_out, buffers, sems, first, small, small_out, master, out):
        super().__init__(grad, stats, stats_out, buffers, sems)
        self.first, self.small, self.small_out = first, small, small_out
        self.master, self.master_out = master, out

    def root_tile(self, tile):
        return self.stats.at[1, 0, 0, :, self.where(tile)]

    def side(self, ref, tile):
        if len(ref.shape) == 2:
            return ref.at[:, self.where(tile)]
        per_plane = ref.shape[2] // self.tile_rows
        return ref.at[tile // per_plane, :, self.where(lax.rem(tile, per_plane))]

    def prepare(self):
        root = self.small[1, 0, 0].astype(jnp.bfloat16)
        self.first[...] = contract(root, self.grad[...], 1, 0).astype(jnp.bfloat16)
        average_small(self.small, self.small_out, self.grad)

    def step(self, root):
        return contract(self.first[...], root, 1, 0)


class TallUnit(Averager):
    def __init__(self, grad, stats, stats_out, buffers, sems, small, small_out, master, out):
        super().__init__(grad, stats, stats_out, buffers, sems)
        self.small, self.small_out = small, small_out
        self.master, self.master_out = master, out

    def root_tile(self, tile):
        return self.stats.at[1, 0, 0, self.where(tile), :]

    def side(self, ref, tile):
        return ref.at[self.where(tile), :]

    def prepare(self):
        average_small(self.small, self.small_out, self.grad)

    def step(self, root):
        first = contract(root, self.grad[...], 1, 1).astype(jnp.bfloat16)
        return contract(first, self.small[1, 0, 0].astype(jnp.bfloat16), 1, 0)


def average_small(small, small_out, grad):
    small_out[0, 0] = 0.5 * small[0, 0, 0] + 0.5 * contract(grad[...], grad[...], 1, 1)


def unit_scratch(depth, size, wide, source=jnp.float32):
    tile_rows = min(STREAM, size)
    exact = jnp.float32
    root = (size, tile_rows) if wide else (tile_rows, size)
    side = (depth, tile_rows) if wide else (tile_rows, depth)
    shapes = [(tile_rows, size), (tile_rows, size), root, side, side]
    types = [source, exact, source, exact, exact]
    return [pltpu.VMEM((SLOTS,) + shape, kind) for shape, kind in zip(shapes, types)] + [
        pltpu.SemaphoreType.DMA((5, SLOTS))
    ]


def local_call(kernel, operands, in_places, outs, out_places, scratch, name):
    spaces = {"h": pl.BlockSpec(memory_space=pl.ANY), "v": pl.BlockSpec(memory_space=pltpu.VMEM)}
    return pl.pallas_call(
        kernel,
        in_specs=[spaces[place] for place in in_places],
        out_specs=[spaces[place] for place in out_places],
        out_shape=[jax.ShapeDtypeStruct(shape, dtype) for shape, dtype in outs],
        scratch_shapes=scratch,
        compiler_params=pltpu.CompilerParams(vmem_limit_bytes=VMEM_LIMIT),
        cost_estimate=pl.CostEstimate(flops=1 << 33, bytes_accessed=1 << 26, transcendentals=0),
        name=name,
    )(*operands)


def down_kernel(
    grad, stats, small, master, earlier, stats_out, small_out, master_out, *scratch
):
    *buffers, sems = scratch
    unit = TallUnit(
        grad, stats, stats_out, buffers, sems, small, small_out, master, master_out
    )
    unit.start()
    unit.prepare()
    unit.run()


def down_step(grad, left, right, master, earlier):
    exact = jnp.float32
    return local_call(
        down_kernel,
        (grad, left, right, master, earlier),
        "vhvhh",
        [(left.shape[1:], exact), (right.shape[1:], exact), (master.shape, exact)],
        "hvh",
        unit_scratch(grad.shape[0], grad.shape[1], False),
        "down_weight",
    )


def update_vectors(sums, states, up_state, params_out, stats_out, up_out, up_stat_out):
    columns = sums.shape[1]
    place = lax.axis_index("dp")
    qkv_state, out_state, norm_state = states
    piece = norm_state.shape[2]
    stride = lax.axis_size("dp") * piece
    own = pltpu.roll(sums[...], lax.rem(columns - place * piece, columns), 1)
    picks = [
        (qkv_state[kind, 0:1, :], qkv_state[kind, 1:2, :], own[0:1, kind * stride : kind * stride + piece])
        for kind in range(3)
    ]
    for state, rows in ((out_state, (4, 4)), (norm_state, (2, 3))):
        for kind, row in enumerate(rows):
            param, stat = (state[0, kind : kind + 1, :], state[1, kind : kind + 1, :])
            picks.append((param, stat, own[row : row + 1, :piece]))

    def update(param, stat, grad):
        stat_new = 0.5 * stat + 0.5 * grad * grad
        return (param - vector_rate * grad * lax.rsqrt(stat_new), stat_new)

    for row, (param, stat, grad) in enumerate(picks):
        param, stat = update(param, stat, grad)
        params_out[row : row + 1, :] = param
        stats_out[row : row + 1, :] = stat
    piece = up_state.shape[1]
    own = pltpu.roll(sums[...], lax.rem(columns - place * piece, columns), 1)
    param, stat = update(up_state[0:1, :], up_state[1:2, :], own[1:2, :piece])
    up_out[...] = param
    up_stat_out[...] = stat


def attention_weights_kernel(
    passed,
    own_ref,
    rising_ref,
    falling_ref,
    qkv_left,
    qkv_right,
    w_qkv,
    out_left,
    out_right,
    w_out,
    sums,
    qkv_state,
    out_state,
    norm_state,
    up_state,
    x_ref,
    gy_ref,
    stats_ref,
    gained_ref,
    terms_ref,
    *refs,
):
    sources, refs = (refs[:passed], refs[passed:])
    targets, refs = (refs[:passed], refs[passed:])
    (
        qkv_left_new,
        qkv_right_new,
        w_qkv_new,
        out_left_new,
        out_right_new,
        w_out_new,
        params_out,
        stats_out,
        up_out,
        up_stat_out,
        dx_out,
        low_qkv,
        low_out,
        first,
        dx_ref,
        dx_sem,
    ), refs = (refs[:16], refs[16:])
    held, refs = (refs[:passed], refs[passed:])
    pass_sems, *buffers = refs
    qkv = WideUnit(
        low_qkv,
        qkv_right,
        qkv_right_new,
        buffers[:5],
        buffers[5],
        first,
        qkv_left,
        qkv_left_new,
        w_qkv,
        w_qkv_new,
    )
    out = TallUnit(
        low_out,
        out_left,
        out_left_new,
        buffers[6:11],
        buffers[11],
        out_right,
        out_right_new,
        w_out,
        w_out_new,
    )
    qkv.start()
    out.start()
    into = fetch(zip(sources, held), pass_sems.at[0])
    edge = low_qkv.shape[1]
    owned = summed(own_ref[...], rising_ref[...], falling_ref[...]).astype(jnp.bfloat16)
    low_qkv[...] = owned[:, :edge]
    low_out[...] = owned[:, edge:]
    qkv.prepare()
    out.prepare()
    for copy in into:
        copy.wait()
    onward = fetch(zip(held, targets), pass_sems.at[1])
    rows, width = x_ref.shape
    model_width = width * lax.axis_size("mp")
    for tile in range(rows // ROW_TILE):
        here = pl.ds(tile * ROW_TILE, ROW_TILE)
        zeros = jnp.zeros((LANES - 8, ROW_TILE), jnp.float32)
        terms = jnp.transpose(jnp.concatenate([terms_ref[:, here], zeros], axis=0))
        terms = terms * (1.0 / model_width)
        inv_std = stats_ref[here, 1:2]
        normalized = (x_ref[here, :].astype(jnp.float32) - stats_ref[here, 0:1]) * inv_std
        upstream = gy_ref[here, :].astype(jnp.float32) * stats_ref[here, 2:3]
        change = gained_ref[here, :] - terms[:, 0:1] - normalized * terms[:, 1:2]
        dx_ref[here, :] = upstream + inv_std * change
    onward += fetch([(dx_ref, dx_out)], dx_sem)
    qkv.run()
    out.run()
    update_vectors(
        sums, (qkv_state, out_state, norm_state), up_state, params_out, stats_out, up_out, up_stat_out
    )
    for copy in onward:
        copy.wait()


def attention_weights_step(blocks, qkv, out, sums, states, norm, passed):
    exact = jnp.float32
    low = jnp.bfloat16
    depth = blocks[0].shape[0]
    sizes = (qkv[1].shape[-1], out[0].shape[-1])
    count = len(passed)
    piece = states[2].shape[2]
    up_piece = states[3].shape[1]
    return local_call(
        functools.partial(attention_weights_kernel, count),
        blocks + qkv + out + (sums,) + states + norm + passed,
        "vvv" + "vhh" + "hvh" + "v" + "vvvv" + "vvvvv" + "h" * count,
        [(array.shape, array.dtype) for array in passed]
        + [
            (qkv[0].shape[1:], exact),
            (qkv[1].shape[1:], exact),
            (qkv[2].shape, exact),
            (out[0].shape[1:], exact),
            (out[1].shape[1:], exact),
            (out[2].shape, exact),
            ((7, piece), exact),
            ((7, piece), exact),
            ((1, up_piece), exact),
            ((1, up_piece), exact),
            (norm[0].shape, exact),
        ],
        "h" * count + "vhh" + "hvh" + "vvvv" + "h",
        [
            pltpu.VMEM((depth, sizes[0]), low),
            pltpu.VMEM((depth, sizes[1]), low),
            pltpu.VMEM((depth, sizes[0]), low),
            pltpu.VMEM(norm[0].shape, exact),
            pltpu.SemaphoreType.DMA((1,)),
        ]
        + [pltpu.VMEM(array.shape, array.dtype) for array in passed]
        + [pltpu.SemaphoreType.DMA((2, count))]
        + unit_scratch(depth, sizes[0], True)
        + unit_scratch(depth, sizes[1], False),
        "attention_weights",
    )


def up_kernel(
    own_ref,
    rising_ref,
    falling_ref,
    small,
    stats,
    master,
    earlier,
    small_out,
    stats_out,
    master_out,
    grad,
    first,
    *scratch,
):
    *buffers, sems = scratch
    unit = WideUnit(
        grad, stats, stats_out, buffers, sems, first, small, small_out, master, master_out
    )
    unit.start()
    grad[...] = summed(own_ref[...], rising_ref[...], falling_ref[...]).astype(jnp.bfloat16)
    unit.prepare()
    unit.run()


def up_step(blocks, left, right, master, earlier):
    exact = jnp.float32
    depth, columns = master.shape
    return local_call(
        up_kernel,
        blocks + (left, right, master, earlier),
        "vvvvhhh",
        [(left.shape[1:], exact), (right.shape[1:], exact), (master.shape, exact)],
        "vhh",
        [pltpu.VMEM((depth, columns), jnp.bfloat16) for _ in range(2)]
        + unit_scratch(depth, columns, True, right.dtype),
        "up_weight",
    )


def local(
    tokens,
    cotangent,
    seq_lengths,
    w_qkv,
    qkv_bias_state,
    w_out,
    out_bias_state,
    w_up,
    up_bias_state,
    w_down,
    ln_state,
    qkv_left,
    qkv_right,
    out_left,
    out_right,
    up_left,
    up_right,
    down_left,
    down_right,
):
    row_count, share_width = tokens.shape
    mp_size = lax.axis_size("mp")
    dp_size = lax.axis_size("dp")
    model_width = share_width * mp_size
    own_width = w_qkv.shape[2]
    mp_place = lax.axis_index("mp")

    piece = ln_state.shape[2]
    up_piece = up_bias_state.shape[1]

    planes = w_qkv.transpose(1, 0, 2)
    qkv_states = qkv_bias_state.transpose(1, 0, 2)
    (
        turned_block,
        full_up,
        full_qkvo,
        normed,
        grad_rows,
        spread,
        stats,
        activated,
        slope,
        ready_down,
        up_right_low,
    ) = first_step(
        (w_up, planes, w_out, w_down),
        tokens,
        cotangent,
        (ln_state, qkv_states, out_bias_state, up_bias_state),
        seq_lengths,
        up_right,
    )
    field_row = 1 - (-up_piece // LANES)
    turned_down, grad_projected, attended, ready_qkvo, owned_down, vector_three = third_step(
        turned_block,
        ready_down,
        normed,
        grad_rows,
        full_qkvo,
        spread,
        seq_lengths,
        piece,
        field_row,
    )
    grad_hidden, ready_up, *sends, vector_four, output = fourth_step(
        ready_qkvo,
        normed,
        grad_rows,
        turned_down,
        slope,
        activated,
        attended,
        full_qkvo,
        tokens,
        spread,
        piece,
        field_row,
    )
    steps = range(dp_size - 2)

    def last_hop(up_send, down_send, own):
        rising = lax.ppermute(up_send, "dp", [(place, place + 2) for place in steps])
        falling = lax.ppermute(down_send, "dp", [(place + 2, place) for place in steps])
        return (own, rising, falling)

    blocks_qkvo = last_hop(*sends)
    down_left_new, down_right_new, new_w_down = down_step(
        owned_down, down_left, down_right, w_down, ready_up
    )
    gained, terms, *sends, sums = fifth_step(
        ready_up,
        grad_hidden,
        grad_projected,
        full_qkvo,
        full_up,
        tokens,
        cotangent,
        stats,
        spread,
        vector_three,
        vector_four,
        (down_right_new,) + blocks_qkvo[1:],
        piece,
    )
    blocks_up = last_hop(*sends)
    (
        output,
        qkv_left_new,
        qkv_right_new,
        new_planes,
        out_left_new,
        out_right_new,
        new_w_out,
        new_vector_params,
        new_vector_stats,
        new_up_bias,
        new_up_stat,
        input_grad,
    ) = attention_weights_step(
        blocks_qkvo,
        (qkv_left, qkv_right, planes),
        (out_left, out_right, w_out),
        sums,
        (qkv_states, out_bias_state, ln_state, up_bias_state),
        (tokens, cotangent, stats, gained, terms),
        (output,),
    )
    new_w_qkv = new_planes.transpose(1, 0, 2)
    up_left_new, up_right_new, new_w_up = up_step(
        blocks_up, up_left, up_right_low, w_up, new_vector_params
    )
    new_up_bias = new_up_bias.reshape(-1)
    new_up_stat = new_up_stat.reshape(-1)
    return (
        output,
        input_grad,
        new_w_qkv,
        new_w_out,
        new_w_up,
        new_w_down,
        new_vector_params,
        new_vector_stats,
        new_up_bias,
        new_up_stat,
        qkv_left_new,
        qkv_right_new,
        out_left_new,
        out_right_new,
        up_left_new,
        up_right_new,
        down_left_new,
        down_right_new,
    )


def solution(mesh):
    return jax.shard_map(
        local,
        mesh=mesh,
        in_specs=(
            P("dp", "mp"),
            P("dp", "mp"),
            P("dp", None),
            P("dp", None, "mp"),
            P(None, None, ("mp", "dp")),
            P("mp", "dp"),
            P(None, None, ("mp", "dp")),
            P("dp", "mp"),
            P(None, ("mp", "dp")),
            P("mp", "dp"),
            P(None, None, ("mp", "dp")),
            P(None, "mp", "dp", None, None),
            P(None, "mp", "dp", None, None),
            P(None, "mp", "dp", None, None),
            P(None, "mp", "dp", None, None),
            P(None, "mp", "dp", None, None),
            P(None, "mp", "dp", None, None),
            P(None, "mp", "dp", None, None),
            P(None, "mp", "dp", None, None),
        ),
        out_specs=(
            P("dp", "mp"),
            P("dp", "mp"),
            P("dp", None, "mp"),
            P("mp", "dp"),
            P("dp", "mp"),
            P("mp", "dp"),
            P(None, ("mp", "dp")),
            P(None, ("mp", "dp")),
            P(("mp", "dp")),
            P(("mp", "dp")),
            P("mp", "dp", None, None),
            P("mp", "dp", None, None),
            P("mp", "dp", None, None),
            P("mp", "dp", None, None),
            P("mp", "dp", None, None),
            P("mp", "dp", None, None),
            P("mp", "dp", None, None),
            P("mp", "dp", None, None),
        ),
        check_vma=False,
    )
```

```python
import functools
import math

import jax
import jax.numpy as jnp
from jax import lax
from jax.experimental import pallas as pl
from jax.experimental.pallas import tpu as pltpu
from jax.sharding import PartitionSpec as P

HEAD_DIM = 64
ROT_DIM = 32
LANES = 128
ROW_TILE = 256


norm_eps = 1e-05
matrix_rate = 1.0
vector_rate = 0.4
masked_score = -1e30


def segment_of(ends, positions, axis, slots):
    finished = ends <= positions
    segment = jnp.sum(jnp.where(finished, 1, 0), axis=axis, keepdims=True)
    starting = jnp.max(jnp.where(finished, ends, 0), axis=axis, keepdims=True)
    return (segment, starting, segment < slots)


def ends_of(lengths, padded):
    slots = lengths.shape[1]
    padded[...] = jnp.zeros_like(padded)
    padded[0:1, pl.ds(0, slots)] = lengths[...].astype(jnp.float32)
    shape = (LANES, LANES)
    slot = lax.broadcasted_iota(jnp.int32, shape, 0)
    before = lax.broadcasted_iota(jnp.int32, shape, 1) <= slot
    ends = jnp.sum(jnp.where(before, padded[0:1, :], 0.0), axis=1, keepdims=True)
    ends = jnp.where(slot < slots, ends, 1e9)
    return (jnp.transpose(ends)[0:1, :].astype(jnp.int32), ends[:, 0:1].astype(jnp.int32))


def rope_tables(offsets):
    lane = lax.rem(lax.broadcasted_iota(jnp.int32, (1, LANES), 1), HEAD_DIM)
    half_rot = ROT_DIM // 2
    freq_index = lax.rem(lane, half_rot).astype(jnp.float32)
    inverse = jnp.exp(-(2.0 * freq_index / ROT_DIM) * math.log(10000.0))
    angles = offsets * inverse
    cosine, sine = (jnp.cos(angles), jnp.sin(angles))
    keep = jnp.where(lane < ROT_DIM, cosine, 1.0)
    ahead = jnp.where(lane < half_rot, -sine, 0.0)
    behind = jnp.where((lane >= half_rot) & (lane < ROT_DIM), sine, 0.0)
    return (keep, ahead, behind)


def gelu_pair(values):
    square = values * values
    inner = math.sqrt(2.0 / math.pi) * values * (1.0 + 0.044715 * square)
    bent = jnp.tanh(inner)
    half = 0.5 * (1.0 + bent)
    slope = half + 0.5 * values * (1.0 - bent * bent) * math.sqrt(2.0 / math.pi) * (
        1.0 + 3.0 * 0.044715 * square
    )
    return (values * half, slope)


def take(array, index, axis=0):
    return lax.dynamic_index_in_dim(array, index, axis, keepdims=False)


def summed(*terms):
    total = terms[0].astype(jnp.float32)
    for term in terms[1:]:
        total = total + term.astype(jnp.float32)
    return total


def contract(left, right, left_axis, right_axis):
    return lax.dot_general(
        left, right, (((left_axis,), (right_axis,)), ((), ())), preferred_element_type=jnp.float32
    )


MESH_ID = pl.DeviceIdType.MESH


def remote(source, target, send_sem, recv_sem, axis, peer):
    return pltpu.make_async_remote_copy(
        src_ref=source,
        dst_ref=target,
        send_sem=send_sem,
        recv_sem=recv_sem,
        device_id={axis: peer},
        device_id_type=MESH_ID,
    )


def greet_line():
    size = lax.axis_size("dp")
    place = lax.axis_index("dp")
    barrier = pltpu.get_barrier_semaphore()
    core = lax.rem(place, 2)
    peers = [place + 1 - 2 * core, lax.rem(place + 2, size), lax.rem(place + size - 2, size)]
    for peer in peers:
        pl.semaphore_signal(barrier, inc=1, device_id={"dp": peer}, device_id_type=MESH_ID)
    return (barrier, len(peers))


PIECES = 2
VMEM_LIMIT = 60 * 1024 * 1024


def piecewise(body, first=0, last=PIECES):
    def once(piece, carry):
        body(piece)
        return carry

    lax.fori_loop(first, last, once, 0)


class LineGather:
    def __init__(self, own, full, send, recv):
        self.count = lax.axis_size("dp") // 2
        self.place = lax.axis_index("dp")
        self.spot = self.place // 2
        self.core = lax.rem(self.place, 2)
        self.own, self.full, self.send, self.recv = own, full, send, recv
        self.rows = own.shape[0]
        self.part = self.rows // PIECES

    def copy(self, kind, step, piece, chip, peer, from_own=False):
        offset = piece * self.part
        start = pl.multiple_of((2 * chip + self.core) * self.rows + offset, self.part)
        block = self.full.at[pl.ds(start, self.part), :]
        source = block
        if from_own:
            source = self.own.at[pl.ds(pl.multiple_of(offset, self.part), self.part), :]
        sems = (self.send.at[kind, step, piece], self.recv.at[kind, step, piece])
        return remote(source, block, *sems, "dp", peer)

    def rise(self, step, piece):
        return self.copy(0, step, piece, self.spot - step + 1, self.place + 2, step == 1)

    def fall(self, step, piece):
        return self.copy(1, step, piece, self.spot + step - 1, self.place - 2, step == 1)

    def show(self, kind, step, piece):
        chip = self.spot - step if kind == 2 else self.spot + step
        return self.copy(kind, step, piece, chip, self.place + 1 - 2 * self.core, step == 0)

    def keep(self):
        start = pl.multiple_of(self.place * self.rows, self.rows)
        target = self.full.at[pl.ds(start, self.rows), :]
        return pltpu.make_async_copy(self.own, target, self.send.at[3, 0, 0])

    def start(self):
        def body(piece):
            pl.when(self.spot + 1 < self.count)(lambda: self.rise(1, piece).start())
            pl.when(self.spot > 0)(lambda: self.fall(1, piece).start())
            self.show(2, 0, piece).start()

        piecewise(body)
        self.keep().start()

    def advance(self, step, first=0, last=PIECES):
        def body(piece):
            @pl.when(self.spot >= step)
            def _():
                self.rise(step, piece).wait_recv()
                pl.when(self.spot + 1 < self.count)(lambda: self.rise(step + 1, piece).start())
                self.show(2, step, piece).start()

            @pl.when(self.spot + step < self.count)
            def _():
                self.fall(step, piece).wait_recv()
                pl.when(self.spot > 0)(lambda: self.fall(step + 1, piece).start())
                self.show(3, step, piece).start()

        piecewise(body, first, last)

    def finish(self):
        self.keep().wait()

        def body(piece):
            self.show(2, 0, piece).wait()
            for step in range(1, self.count):
                rises = (self.spot + 1 < self.count) & (self.spot >= step - 1)
                falls = (self.spot > 0) & (self.spot + step - 1 < self.count)
                above = self.spot + step < self.count
                pl.when(rises)(lambda step=step: self.rise(step, piece).wait_send())
                pl.when(falls)(lambda step=step: self.fall(step, piece).wait_send())
                pl.when(self.spot >= step)(lambda step=step: self.show(2, step, piece).wait())
                pl.when(above)(lambda step=step: self.show(3, step, piece).wait())

        piecewise(body)


def gather_sems():
    count = lax.axis_size("dp") // 2
    return [pltpu.SemaphoreType.DMA((4, count + 1, PIECES)) for _ in range(2)]


def by_rows(rows, step, body):
    def once(index, carry):
        body(pl.ds(pl.multiple_of(index * step, step), step))
        return carry

    lax.fori_loop(0, rows // step, once, 0)


class LineSum:
    def __init__(self, blocks, from_below, from_above, send, recv, begun=False):
        self.count = lax.axis_size("dp") // 2
        self.place = lax.axis_index("dp")
        self.spot = self.place // 2
        self.blocks, self.below, self.above = blocks, from_below, from_above
        self.send, self.recv = send, recv
        self.part = blocks.shape[1] // PIECES
        self.begun = begun

    def rows(self, piece):
        return pl.ds(pl.multiple_of(piece * self.part, self.part), self.part)

    def move(self, kind, slots, step, piece, peer, block=None):
        rows = self.rows(piece)
        source = self.blocks.at[block, rows, :] if block is not None else slots.at[step - 2, rows, :]
        sems = (self.send.at[kind, step, piece], self.recv.at[kind, step, piece])
        return remote(source, slots.at[step - 1, rows, :], *sems, "dp", peer)

    def rise(self, step, piece, block=None):
        return self.move(0, self.below, step, piece, self.place + 2, block)

    def fall(self, step, piece, block=None):
        return self.move(1, self.above, step, piece, self.place - 2, block)

    def add(self, slots, step, block, piece):
        def body(rows):
            here = pl.ds(pl.multiple_of(piece * self.part + rows.start, rows.size), rows.size)
            total = slots[step - 2, here, :].astype(jnp.float32)
            total = total + self.blocks[block, here, :].astype(jnp.float32)
            slots[step - 2, here, :] = total.astype(jnp.bfloat16)

        by_rows(self.part, 16, body)

    def advance(self, step, first=0, last=PIECES):
        end = self.count - 1
        mirrored = end - self.spot

        def body(piece):
            pl.when(self.spot == 0)(lambda: self.rise(step, piece, self.count - step).start())
            pl.when(mirrored == 0)(lambda: self.fall(step, piece, step - 1).start())
            if step == 1:
                return

            @pl.when((self.spot > 0) & (self.spot < end) & (self.spot < step))
            def _():
                if step > 2 or not self.begun:
                    self.rise(step - 1, piece, 0).wait_recv()
                self.add(self.below, step, self.count + self.spot - step, piece)
                self.rise(step, piece).start()

            @pl.when((mirrored > 0) & (mirrored < end) & (mirrored < step))
            def _():
                if step > 2 or not self.begun:
                    self.fall(step - 1, piece, 0).wait_recv()
                self.add(self.above, step, self.spot - self.count + step, piece)
                self.fall(step, piece).start()

        piecewise(body, first, last)

    def hand_out(self, up_out, down_out):
        end = self.count - 1
        mirrored = end - self.spot

        def body(piece):
            rows = self.rows(piece)

            def move(out, slots, block):
                def once(small):
                    here = pl.ds(pl.multiple_of(rows.start + small.start, small.size), small.size)
                    total = self.blocks[block, here, :].astype(jnp.float32)
                    if slots is not None:
                        total = total + slots[end - 2, here, :].astype(jnp.float32)
                    out[here, :] = total.astype(jnp.bfloat16)

                by_rows(self.part, 16, once)

            pl.when(self.spot == 0)(lambda: move(up_out, None, 1))
            pl.when(mirrored == 0)(lambda: move(down_out, None, end - 1))

            @pl.when((self.spot > 0) & (self.spot < end))
            def _():
                self.rise(end - 1, piece, 0).wait_recv()
                move(up_out, self.below, self.spot + 1)

            @pl.when((mirrored > 0) & (mirrored < end))
            def _():
                self.fall(end - 1, piece, 0).wait_recv()
                move(down_out, self.above, self.spot - 1)

            pl.when(self.spot == end)(lambda: move(up_out, None, 0))
            pl.when(mirrored == end)(lambda: move(down_out, None, 0))
            for step in range(1, end):
                rises = (self.spot < step) & (self.spot < end)
                falls = (mirrored < step) & (mirrored < end)
                pl.when(rises)(lambda step=step: self.rise(step, piece, 0).wait_send())
                pl.when(falls)(lambda step=step: self.fall(step, piece, 0).wait_send())

        piecewise(body)

    def end_first(self):
        end = self.count - 1

        def body(piece):
            pl.when(self.spot == 0)(lambda: self.rise(1, piece, end).wait_send())
            pl.when(self.spot == end)(lambda: self.fall(1, piece, 0).wait_send())
            pl.when(self.spot == 1)(lambda: self.rise(1, piece, 0).wait_recv())
            pl.when(self.spot == end - 1)(lambda: self.fall(1, piece, 0).wait_recv())

        piecewise(body)

    def finish(self, out, first=0, last=PIECES):
        end = self.count - 1
        mirrored = end - self.spot

        def body(piece):
            start = piece * self.part

            def small(rows):
                return pl.ds(pl.multiple_of(start + rows.start, rows.size), rows.size)

            def begin(rows):
                out[small(rows), :] = self.blocks[self.spot, small(rows), :].astype(out.dtype)

            by_rows(self.part, 16, begin)

            def gain(slots):
                def once(rows):
                    here = small(rows)
                    total = summed(out[here, :], slots[end - 1, here, :])
                    out[here, :] = total.astype(out.dtype)

                by_rows(self.part, 16, once)

            @pl.when(self.spot > 0)
            def _():
                self.rise(end, piece, 0).wait_recv()
                gain(self.below)

            @pl.when(self.spot < end)
            def _():
                self.fall(end, piece, 0).wait_recv()
                gain(self.above)

            for step in range(2 if self.begun else 1, self.count):
                rises = (self.spot < step) & (self.spot < end)
                falls = (mirrored < step) & (mirrored < end)
                pl.when(rises)(lambda step=step: self.rise(step, piece, 0).wait_send())
                pl.when(falls)(lambda step=step: self.fall(step, piece, 0).wait_send())

        piecewise(body, first, last)


def sum_scratch(rows, columns):
    count = lax.axis_size("dp") // 2
    return [
        pltpu.VMEM((count - 1, rows, columns), jnp.bfloat16),
        pltpu.VMEM((count - 1, rows, columns), jnp.bfloat16),
        pltpu.SemaphoreType.DMA((2, count, PIECES)),
        pltpu.SemaphoreType.DMA((2, count, PIECES)),
    ]


class PairProducts:
    def __init__(self, lefts, rights, parcel, sums, send, recv):
        self.count = lax.axis_size("dp") // 2
        self.place = lax.axis_index("dp")
        self.core = lax.rem(self.place, 2)
        self.lefts, self.rights = lefts, rights
        self.parcel, self.sums, self.send, self.recv = parcel, sums, send, recv

    def copy(self, chip):
        return remote(
            self.parcel.at[chip],
            self.sums.at[chip],
            self.send.at[chip],
            self.recv.at[chip],
            "dp",
            self.place + 1 - 2 * self.core,
        )

    def product(self, chip, core, quarter):
        rows = self.sums.shape[1]
        width = self.sums.shape[2] // 4
        start = pl.multiple_of((2 * chip + core) * rows, rows)
        left = self.lefts[quarter][:, pl.ds(start, rows)]
        ref, first = self.rights[quarter]
        return contract(left, ref[:, pl.ds(first, width)], 0, 0)

    def far(self):
        width = self.sums.shape[2] // 4

        def once(chip, carry):
            for quarter in range(4):
                piece = self.product(chip, 1 - self.core, quarter)
                self.parcel[chip, :, pl.ds(quarter * width, width)] = piece.astype(jnp.bfloat16)
            self.copy(chip).start()
            return carry

        lax.fori_loop(0, self.count, once, 0)

    def near(self):
        width = self.sums.shape[2] // 4

        def once(chip, carry):
            self.copy(chip).wait()
            for quarter in range(4):
                columns = pl.ds(quarter * width, width)
                piece = self.product(chip, self.core, quarter)
                total = piece + self.sums[chip, :, columns].astype(jnp.float32)
                self.sums[chip, :, columns] = total.astype(jnp.bfloat16)
            return carry

        lax.fori_loop(0, self.count, once, 0)


def pair_scratch(rows, columns):
    count = lax.axis_size("dp") // 2
    return [
        pltpu.VMEM((count, rows, columns), jnp.bfloat16),
        pltpu.SemaphoreType.DMA((count,)),
        pltpu.SemaphoreType.DMA((count,)),
    ]


class BlockGather:
    def __init__(self, own, full, send, recv):
        self.size = lax.axis_size("mp")
        self.place = lax.axis_index("mp")
        self.own, self.full, self.send, self.recv = own, full, send, recv
        self.rows, self.width = own.shape

    def spread(self, index, rows, owner, peer, first):
        start = pl.multiple_of(owner * self.width, self.width)
        target = self.full.at[rows, pl.ds(start, self.width)]
        source = self.own if first else target
        return remote(source, target, self.send.at[index], self.recv.at[index], "mp", peer)

    def copy(self, index):
        every = pl.ds(0, self.rows)
        if self.size != 4:
            return self.spread(index, every, self.place, lax.rem(self.place + 1 + index, self.size), True)
        beside = self.place + 1 - 2 * lax.rem(self.place, 2)
        above = lax.rem(self.place + 2, 4)
        half = self.rows // 2
        if index < 2:
            return self.spread(index, every, self.place, (beside, above)[index], True)
        if index == 2:
            return self.spread(2, pl.ds(0, half), above, beside, False)
        return self.spread(3, pl.ds(half, half), beside, above, False)

    def keep(self):
        start = pl.multiple_of(self.place * self.width, self.width)
        target = self.full.at[:, pl.ds(start, self.width)]
        return pltpu.make_async_copy(self.own, target, self.send.at[self.size])

    def start(self):
        for index in range(2 if self.size == 4 else self.size - 1):
            self.copy(index).start()
        self.keep().start()

    def forward(self):
        if self.size == 4:
            self.copy(1).wait_recv()
            self.copy(2).start()
            self.copy(0).wait_recv()
            self.copy(3).start()

    def finish(self):
        self.keep().wait()
        for index in range(4 if self.size == 4 else self.size - 1):
            self.copy(index).wait_send()
            if index > 1 or self.size != 4:
                self.copy(index).wait_recv()


def block_sems():
    size = lax.axis_size("mp") + 1
    return [pltpu.SemaphoreType.DMA((size,)), pltpu.SemaphoreType.DMA((size,))]


def field_rows(spread_ref, first_row, index, piece):
    dp_size = lax.axis_size("dp")
    first = lax.axis_index("mp") * dp_size
    devices = [first + owner for owner in range(dp_size)]
    row, lane = divmod(index * piece, LANES)
    return vector_rows(spread_ref, devices, first_row + row, piece, lane)


def vector_rows(spread_ref, devices, row, piece, turn_to=0):
    if piece >= LANES:
        return [
            spread_ref[device, row + part : row + part + 1, :]
            for device in devices
            for part in range(piece // LANES)
        ]
    lane = lax.broadcasted_iota(jnp.int32, (1, LANES), 1)
    fold = LANES // piece
    groups = []
    for first in range(0, len(devices), fold):
        group = jnp.zeros((1, LANES), jnp.float32)
        for part in range(fold):
            values = spread_ref[devices[first + part], row : row + 1, :]
            turn = (part * piece - turn_to) % LANES
            values = pltpu.roll(values, turn, 1) if turn else values
            mine = (lane >= part * piece) & (lane < (part + 1) * piece)
            group = jnp.where(mine, values, group)
        groups.append(group)
    return groups


def round_matrix(source, target):
    size = source.shape[0]
    tile_rows = min(STREAM, size)

    def scope(before, after, sems):
        def where(tile):
            return pl.ds(pl.multiple_of(tile * tile_rows, tile_rows), tile_rows)

        def loads(tile, slot):
            return [
                pltpu.make_async_copy(source.at[where(tile), :], before.at[slot], sems.at[0, slot])
            ]

        def stores(tile, slot):
            return [
                pltpu.make_async_copy(after.at[slot], target.at[where(tile), :], sems.at[1, slot])
            ]

        def compute(tile, slot):
            after[slot] = before[slot].astype(after.dtype)

        stream(size // tile_rows, loads, stores, compute)

    shape = (SLOTS, tile_rows, size)
    pl.run_scoped(
        scope,
        pltpu.VMEM(shape, source.dtype),
        pltpu.VMEM(shape, target.dtype),
        pltpu.SemaphoreType.DMA((2, SLOTS)),
    )


def cast_rows(source, target, here):
    target[here, :] = source[here, :].astype(target.dtype)


def first_kernel(
    w_up_ref,
    w_qkv_hbm,
    w_out_hbm,
    w_down_hbm,
    x_ref,
    gy_ref,
    norm_state,
    qkv_state,
    out_state,
    up_state,
    lengths_ref,
    right_ref,
    left_ref,
    wide_ref,
    turned_out,
    full_ref,
    next_full,
    xn_out,
    gy_out,
    spread_ref,
    stats_ref,
    act_out,
    slope_out,
    sums_out,
    right_low,
    left_low,
    wide_low,
    gather_send,
    gather_recv,
    next_send,
    next_recv,
    x_send,
    x_recv,
    gy_send,
    gy_recv,
    small_send,
    small_recv,
    parcel,
    pair_send,
    pair_recv,
    x_full,
    up_ref,
    act_ref,
    slope_ref,
    local_sems,
    block_ref,
    next_ref,
    valid_ref,
    xn_ref,
    gy_full,
    sums_ref,
    w_qkv_ref,
    w_out_ref,
    w_down_ref,
    small_ref,
    padded_ref,
):
    loads = fetch(
        [(w_qkv_hbm, w_qkv_ref), (w_out_hbm, w_out_ref), (w_down_hbm, w_down_ref)],
        local_sems.at[pl.ds(6, 3)],
    )
    piece = norm_state.shape[2]
    up_piece = up_state.shape[1]
    slots = lengths_ref.shape[1]
    columns = lax.axis_size("dp")
    total = columns * lax.axis_size("mp")
    mp_place = lax.axis_index("mp")
    place = mp_place * columns + lax.axis_index("dp")
    barrier = pltpu.get_barrier_semaphore()

    def device(step):
        peer = lax.rem(place + step, total)
        return {"mp": peer // columns, "dp": lax.rem(peer, columns)}

    def greet(step, carry):
        pl.semaphore_signal(barrier, inc=1, device_id=device(step), device_id_type=MESH_ID)
        return carry

    lax.fori_loop(1, total, greet, 0)
    by_rows(block_ref.shape[0], 64, lambda here: cast_rows(w_up_ref, block_ref, here))
    small_ref[...] = jnp.zeros_like(small_ref)
    up_rows = -(-up_piece // LANES)

    def note(first_row, offset, values):
        values = values.astype(jnp.bfloat16).astype(jnp.float32)
        row, lane = divmod(offset, LANES)
        small_ref[0, first_row + row : first_row + row + 1, pl.ds(lane, values.shape[1])] = values

    for kind in range(2):
        note(0, kind * piece, norm_state[0, kind : kind + 1, :])
        note(1 + up_rows, (3 + kind) * piece, out_state[0, kind : kind + 1, :])
    for kind in range(3):
        note(1 + up_rows, kind * piece, qkv_state[kind, 0:1, :])
    for first in range(0, up_piece, LANES):
        note(1, first, up_state[0:1, first : min(first + LANES, up_piece)])
    pl.semaphore_wait(barrier, total - 1)

    def small_copy(step):
        return pltpu.make_async_remote_copy(
            src_ref=small_ref.at[0],
            dst_ref=spread_ref.at[place],
            send_sem=small_send.at[step],
            recv_sem=small_recv.at[step],
            device_id=device(step),
            device_id_type=MESH_ID,
        )

    def begin(step, carry):
        small_copy(step).start()
        return carry

    def end(step, carry):
        small_copy(step).wait()
        return carry

    weight = LineGather(block_ref, full_ref, gather_send, gather_recv)
    later = LineGather(next_ref, next_full, next_send, next_recv)
    rows_x = BlockGather(x_ref, x_full, x_send, x_recv)
    rows_gy = BlockGather(gy_ref, gy_full, gy_send, gy_recv)
    products = PairProducts(
        [gy_full] * 4, quarters(act_ref), parcel, sums_ref, pair_send, pair_recv
    )
    lax.fori_loop(1, total, begin, 0)
    weight.start()
    rows_x.start()
    rows_gy.start()
    spread_ref[place] = small_ref[0]
    rows, width = xn_ref.shape
    depth = block_ref.shape[0]
    head_cols = w_qkv_ref.shape[2]
    for copy in loads:
        copy.wait()
    for kind in range(3):
        next_ref[:, pl.ds(kind * head_cols, head_cols)] = w_qkv_ref[kind].astype(jnp.bfloat16)
    turned = jnp.transpose(w_out_ref[...]).astype(jnp.bfloat16)
    next_ref[:, pl.ds(3 * head_cols, head_cols)] = turned

    def turn_down(here):
        turned_out[:, here] = jnp.transpose(w_down_ref[here, :]).astype(jnp.bfloat16)

    by_rows(w_down_ref.shape[0], depth, turn_down)

    ends_row, _ = ends_of(lengths_ref, padded_ref)

    def mark(here):
        ids = lax.broadcasted_iota(jnp.int32, (ROW_TILE, 1), 0) + here.start
        valid = segment_of(ends_row, ids, 1, slots)[2]
        valid_ref[here, :] = jnp.where(valid, 1.0, 0.0)

    by_rows(rows, ROW_TILE, mark)
    lax.fori_loop(1, total, end, 0)
    round_matrix(left_ref.at[0, 0, 0], left_low.at[0, 0, 0])
    round_matrix(wide_ref.at[0, 0, 0], wide_low.at[0, 0, 0])
    weight.advance(1)
    round_matrix(right_ref.at[0, 0, 0], right_low.at[0, 0, 0])
    weight.advance(2)
    round_matrix(right_ref.at[1, 0, 0], right_low.at[1, 0, 0])
    rows_x.forward()
    rows_gy.forward()
    weight.advance(3, 0, 1)
    later.start()
    weight.advance(3, 1)
    for step in range(4, weight.count):
        weight.advance(step)
    rows_x.finish()

    gains = vector_rows(spread_ref, range(total), 0, piece)
    shifts = vector_rows(spread_ref, range(total), 0, piece, piece)

    def normalize(here):
        values = x_full[here, :].astype(jnp.float32)
        mean = jnp.sum(values, axis=1, keepdims=True) * (1.0 / width)
        square = jnp.sum(values * values, axis=1, keepdims=True) * (1.0 / width)
        inv_std = lax.rsqrt(square - mean * mean + norm_eps)
        lanes = lax.broadcasted_iota(jnp.int32, (ROW_TILE, LANES), 1)
        stats_ref[here, :] = jnp.where(
            lanes == 0, mean, jnp.where(lanes == 1, inv_std, valid_ref[here, :])
        )
        for group in range(width // LANES):
            part = (x_full[here, pl.ds(group * LANES, LANES)].astype(jnp.float32) - mean) * inv_std
            part = part * gains[group] + shifts[group]
            xn_ref[here, pl.ds(group * LANES, LANES)] = part.astype(jnp.bfloat16)

    by_rows(rows, ROW_TILE, normalize)
    stores = fetch([(xn_ref, xn_out)], local_sems.at[pl.ds(3, 1)])
    weight.finish()
    load = pltpu.make_async_copy(full_ref, up_ref, local_sems.at[0])
    load.start()
    rows_gy.finish()

    def blank(here):
        kept = gy_full[here, :].astype(jnp.float32) * valid_ref[here, :]
        gy_full[here, :] = kept.astype(jnp.bfloat16)

    by_rows(rows, ROW_TILE, blank)
    stores += fetch([(gy_full, gy_out)], local_sems.at[pl.ds(4, 1)])
    bias = vector_rows(
        spread_ref, [mp_place * columns + owner for owner in range(columns)], 1, up_piece
    )
    quarter_width = up_ref.shape[1] // 4
    groups = quarter_width // LANES
    load.wait()

    def tile(here):
        for quarter in range(4):
            part = pl.ds(quarter * quarter_width, quarter_width)
            shift = jnp.concatenate(bias[quarter * groups : (quarter + 1) * groups], axis=1)
            hidden = contract(xn_ref[here, :], up_ref[:, part], 1, 0) + shift
            activated, slope = gelu_pair(hidden)
            act_ref[here, part] = activated.astype(jnp.bfloat16)
            slope_ref[here, part] = slope.astype(jnp.bfloat16)

    by_rows(rows // 2, ROW_TILE, tile)
    later.advance(1)
    by_rows(rows // 2, ROW_TILE, lambda here: tile(pl.ds(rows // 2 + here.start, here.size)))
    stores += fetch([(act_ref, act_out), (slope_ref, slope_out)], local_sems.at[pl.ds(1, 2)])
    later.advance(2, 0, 1)
    products.far()
    later.advance(2, 1)
    products.near()
    stores += fetch([(sums_ref, sums_out)], local_sems.at[pl.ds(5, 1)])
    round_matrix(left_ref.at[1, 0, 0], left_low.at[1, 0, 0])
    round_matrix(wide_ref.at[1, 0, 0], wide_low.at[1, 0, 0])
    for step in range(3, later.count):
        later.advance(step)
    later.finish()
    for store in stores:
        store.wait()


def first_step(weights, tokens, cotangent, states, lengths, right, left, wide_right):
    mp_size, dp_size = (lax.axis_size("mp"), lax.axis_size("dp"))
    count = dp_size // 2
    rows = tokens.shape[0]
    wide = (rows, tokens.shape[1] * mp_size)
    part, columns = weights[0].shape
    total = mp_size * dp_size
    low = jnp.bfloat16
    return carrying(
        first_kernel,
        1,
        weights + (tokens, cotangent) + states + (lengths, right, left, wide_right),
        "vhhhhhvvvvvhhh",
        [
            ((part, columns), low),
            ((part * dp_size, columns), low),
            ((part * dp_size, columns), low),
            (wide, low),
            (wide, low),
            ((total, 8, LANES), jnp.float32),
            ((rows, LANES), jnp.float32),
            ((rows, columns), low),
            ((rows, columns), low),
            ((count, part, columns), low),
            (right.shape, low),
            (left.shape, low),
            (wide_right.shape, low),
        ],
        "vhhhhvvhhhhhh",
        gather_sems()
        + gather_sems()
        + block_sems()
        + block_sems()
        + [pltpu.SemaphoreType.DMA((total,)), pltpu.SemaphoreType.DMA((total,))]
        + pair_scratch(part, columns)
        + [
            pltpu.VMEM(wide, low),
            pltpu.VMEM((part * dp_size, columns), low),
            pltpu.VMEM((rows, columns), low),
            pltpu.VMEM((rows, columns), low),
            pltpu.SemaphoreType.DMA((9,)),
            pltpu.VMEM((part, columns), low),
            pltpu.VMEM((part, columns), low),
            pltpu.VMEM((rows, 1), jnp.float32),
            pltpu.VMEM(wide, low),
            pltpu.VMEM(wide, low),
            pltpu.VMEM((count, part, columns), low),
        ]
        + [pltpu.VMEM(weight.shape, weight.dtype) for weight in weights[1:]]
        + [pltpu.VMEM((1, 8, LANES), jnp.float32), pltpu.VMEM((8, LANES), jnp.float32)],
        4 * rows * wide[1] * columns,
        "gathers_beside_hidden",
    )


def greet_and_wait():
    barrier, count = greet_line()
    pl.semaphore_wait(barrier, count)


def quarters(ref):
    width = ref.shape[1] // 4
    return [(ref, quarter * width) for quarter in range(4)]


def carrying(kernel, collective_id, operands, in_places, outs, out_places, scratch, flops, name):
    spaces = {"h": pl.BlockSpec(memory_space=pl.ANY), "v": pl.BlockSpec(memory_space=pltpu.VMEM)}
    return pl.pallas_call(
        kernel,
        in_specs=[spaces[place] for place in in_places],
        out_specs=[spaces[place] for place in out_places],
        out_shape=[jax.ShapeDtypeStruct(shape, dtype) for shape, dtype in outs],
        scratch_shapes=scratch,
        compiler_params=pltpu.CompilerParams(
            collective_id=collective_id, has_side_effects=True, vmem_limit_bytes=VMEM_LIMIT
        ),
        cost_estimate=pl.CostEstimate(flops=flops, bytes_accessed=1 << 25, transcendentals=0),
        name=name,
    )(*operands)


PLAN = {
    "projected": (),
    0: ((1, 0), (1, 1)),
    1: ((2, 0),),
    "attended": ((2, 1),),
    "far": ((3, 0),),
}


def third_kernel(
    head_cols,
    piece,
    field_row,
    block_ref,
    ready_hbm,
    xn_hbm,
    gy_hbm,
    weight_hbm,
    spread_ref,
    lengths_ref,
    full_ref,
    grad_out,
    or_out,
    sums_out,
    owned_ref,
    vector_ref,
    up_first,
    down_first,
    gather_send,
    gather_recv,
    below,
    above,
    line_send,
    line_recv,
    parcel,
    pair_send,
    pair_recv,
    mask_ref,
    low_ref,
    go_ref,
    dq_acc,
    dk_acc,
    dv_acc,
    ready_ref,
    xn_ref,
    gy_ref,
    weight_ref,
    grad_ref,
    or_ref,
    local_sems,
    keep_ref,
    ahead_ref,
    behind_ref,
    sums_ref,
    padded_ref,
    next_below,
    next_above,
    next_send,
    next_recv,
):
    loads = [
        pltpu.make_async_copy(source, target, local_sems.at[index])
        for index, (source, target) in enumerate(
            [(ready_hbm, ready_ref), (xn_hbm, xn_ref), (weight_hbm, weight_ref), (gy_hbm, gy_ref)]
        )
    ]
    for load in loads:
        load.start()
    weight = LineGather(block_ref, full_ref, gather_send, gather_recv)
    line = LineSum(ready_ref, below, above, line_send, line_recv)
    rights = [(grad_ref, kind * head_cols) for kind in range(3)] + [(or_ref, 0)]
    products = PairProducts(
        [xn_ref] * 3 + [gy_ref], rights, parcel, sums_ref, pair_send, pair_recv
    )
    greet_and_wait()
    weight.start()
    loads[0].wait()
    line.advance(1)

    rows = xn_ref.shape[0]
    tiles = rows // ROW_TILE
    scale = HEAD_DIM ** (-0.5)
    slots = lengths_ref.shape[1]
    ends_row, ends_col = ends_of(lengths_ref, padded_ref)
    row_positions = lax.broadcasted_iota(jnp.int32, (1, rows), 1)
    seg_row, _, row_valid = segment_of(ends_col, row_positions, 0, slots)
    seg_row = jnp.where(row_valid, seg_row, slots + row_positions)
    for tile in range(tiles):
        here = pl.ds(tile * ROW_TILE, ROW_TILE)
        reach = (tile + 1) * ROW_TILE
        shape = (ROW_TILE, reach)
        ids = lax.broadcasted_iota(jnp.int32, (ROW_TILE, 1), 0) + tile * ROW_TILE
        seg_col, starting, valid = segment_of(ends_row, ids, 1, slots)
        seg_col = jnp.where(valid, seg_col, slots + ids)
        tables = rope_tables((ids - starting).astype(jnp.float32))
        for ref, table in zip((keep_ref, ahead_ref, behind_ref), tables):
            ref[here, :] = table
        key_ids = lax.broadcasted_iota(jnp.int32, shape, 1)
        allowed = (seg_col == seg_row[:, :reach]) & (key_ids <= ids)
        mask_ref[here, pl.ds(0, reach)] = jnp.where(allowed, 0.0, masked_score)
    biases = [
        jnp.concatenate(field_rows(spread_ref, field_row, kind, piece), axis=1) for kind in range(3)
    ]

    def turned(values, here, direction):
        ahead = pltpu.roll(values, LANES - ROT_DIM // 2, 1)
        behind = pltpu.roll(values, ROT_DIM // 2, 1)
        return values * keep_ref[here, :] + direction * (
            ahead * ahead_ref[here, :] + behind * behind_ref[here, :]
        )

    def project(here):
        for kind in range(3):
            columns = pl.ds(kind * head_cols, head_cols)
            values = contract(xn_ref[here, :], weight_ref[:, columns], 1, 0) + biases[kind]
            if kind == 2:
                low_ref[here, columns] = values.astype(jnp.bfloat16)
                continue
            for first in range(0, head_cols, LANES):
                part = turned(values[:, first : first + LANES], here, 1.0).astype(jnp.bfloat16)
                if kind == 0:
                    part = part * scale
                low_ref[here, pl.ds(kind * head_cols + first, LANES)] = part
        columns = pl.ds(3 * head_cols, head_cols)
        values = contract(gy_ref[here, :], weight_ref[:, columns], 1, 0)
        go_ref[here, :] = values.astype(jnp.bfloat16)

    for load in loads[1:]:
        load.wait()
    by_rows(rows, ROW_TILE, project)
    vector_ref[...] = jnp.zeros_like(vector_ref)

    done = set()
    pairs = head_cols // LANES

    def events(wanted):
        for step, piece in wanted:
            if (step, piece) not in done and step < weight.count:
                done.add((step, piece))
                weight.advance(step, piece, piece + 1)
                if step + 1 < weight.count:
                    line.advance(step + 1, piece, piece + 1)

    lane = lax.broadcasted_iota(jnp.int32, (ROW_TILE, LANES), 1)
    first_head = lane < HEAD_DIM

    def one_pair(pair, carry):
        column = pl.multiple_of(pair * LANES, LANES)
        q_lanes = pl.ds(column, LANES)
        k_lanes = pl.ds(pl.multiple_of(head_cols + column, LANES), LANES)
        v_lanes = pl.ds(pl.multiple_of(2 * head_cols + column, LANES), LANES)
        dk_acc[...] = jnp.zeros_like(dk_acc)
        dv_acc[...] = jnp.zeros_like(dv_acc)
        for tile in range(tiles):
            here = pl.ds(tile * ROW_TILE, ROW_TILE)
            keys = pl.ds(0, (tile + 1) * ROW_TILE)
            outs = []
            query_grads = []
            for head in range(LANES // HEAD_DIM):
                mine = first_head if head == 0 else jnp.logical_not(first_head)
                none = jnp.zeros((ROW_TILE, LANES), jnp.bfloat16)
                query = jnp.where(mine, low_ref[here, q_lanes], none)
                grad_out = jnp.where(mine, go_ref[here, q_lanes], none)
                scores = contract(query, low_ref[keys, k_lanes], 1, 1) + mask_ref[here, keys]
                peak = jnp.max(scores, axis=1, keepdims=True)
                weights = jnp.exp(scores - peak)
                share = 1.0 / jnp.sum(weights, axis=1, keepdims=True)
                probs = weights * share
                probs_low = probs.astype(jnp.bfloat16)
                outs.append(contract(probs_low, low_ref[keys, v_lanes], 1, 0))
                grad_probs = contract(grad_out, low_ref[keys, v_lanes], 1, 1)
                delta = jnp.sum(probs * grad_probs, axis=1, keepdims=True)
                grad_scores = (probs * (grad_probs - delta)).astype(jnp.bfloat16)
                query_grads.append(contract(grad_scores, low_ref[keys, k_lanes], 1, 0))
                dk_acc[keys, :] += contract(grad_scores, query, 0, 0)
                dv_acc[keys, :] += contract(probs_low, grad_out, 0, 0)
            or_ref[here, q_lanes] = jnp.where(first_head, outs[0], outs[1]).astype(jnp.bfloat16)
            dq_acc[here, :] = jnp.where(first_head, query_grads[0], query_grads[1])
        for tile in range(tiles):
            here = pl.ds(tile * ROW_TILE, ROW_TILE)
            parts = [
                (q_lanes, turned(dq_acc[here, :], here, -1.0) * scale),
                (k_lanes, turned(dk_acc[here, :], here, -1.0)),
                (v_lanes, dv_acc[here, :]),
            ]
            for lanes, part in parts:
                part = part.astype(jnp.bfloat16)
                grad_ref[here, lanes] = part
                vector_ref[0:1, lanes] += jnp.sum(part.astype(jnp.float32), axis=0, keepdims=True)

        for index in range(pairs):
            if index in PLAN:
                pl.when(pair == index)(functools.partial(events, PLAN[index]))
        return carry

    events(PLAN["projected"])
    lax.fori_loop(0, pairs, one_pair, 0)
    stores = [
        pltpu.make_async_copy(grad_ref, grad_out, local_sems.at[4]),
        pltpu.make_async_copy(or_ref, or_out, local_sems.at[5]),
    ]
    for store in stores:
        store.start()
    events(PLAN["attended"])
    products.far()
    events(PLAN["far"])
    products.near()
    stores += fetch([(sums_ref, sums_out)], local_sems.at[pl.ds(6, 1)])
    following = LineSum(sums_ref, next_below, next_above, next_send, next_recv)
    following.advance(1)
    events([(step, piece) for step in range(1, weight.count) for piece in range(PIECES)])
    line.finish(owned_ref)
    weight.finish()
    following.end_first()
    stores += fetch(
        [(next_below.at[0], up_first), (next_above.at[0], down_first)], local_sems.at[pl.ds(7, 2)]
    )
    for store in stores:
        store.wait()


def third_step(
    block, ready, normed, grad_rows, full_qkvo, spread, lengths, piece, field_row
):
    rows, width = normed.shape
    count = lax.axis_size("dp") // 2
    columns = full_qkvo.shape[1]
    head_cols = columns // 4
    part = width // (2 * count)
    low = jnp.bfloat16
    return carrying(
        functools.partial(third_kernel, head_cols, piece, field_row),
        5,
        (
            block,
            ready,
            normed,
            grad_rows,
            full_qkvo,
            spread,
            lengths,
        ),
        "hhhhhvv",
        [
            ((width, block.shape[1]), low),
            ((rows, 3 * head_cols), low),
            ((rows, head_cols), low),
            ((count, part, columns), low),
            ((part, ready.shape[2]), low),
            ((8, columns), jnp.float32),
            ((part, columns), low),
            ((part, columns), low),
        ],
        "hhhhvvhh",
        gather_sems()
        + sum_scratch(part, ready.shape[2])
        + pair_scratch(part, columns)
        + [
            pltpu.VMEM((rows, rows), jnp.float32),
            pltpu.VMEM((rows, 3 * head_cols), low),
            pltpu.VMEM((rows, head_cols), low),
            pltpu.VMEM((rows, LANES), jnp.float32),
            pltpu.VMEM((rows, LANES), jnp.float32),
            pltpu.VMEM((rows, LANES), jnp.float32),
            pltpu.VMEM(ready.shape, low),
            pltpu.VMEM((rows, width), low),
            pltpu.VMEM((rows, width), low),
            pltpu.VMEM((width, columns), low),
            pltpu.VMEM((rows, 3 * head_cols), low),
            pltpu.VMEM((rows, head_cols), low),
            pltpu.SemaphoreType.DMA((9,)),
            pltpu.VMEM((rows, LANES), jnp.float32),
            pltpu.VMEM((rows, LANES), jnp.float32),
            pltpu.VMEM((rows, LANES), jnp.float32),
            pltpu.VMEM((count, part, columns), low),
            pltpu.VMEM((8, LANES), jnp.float32),
            pltpu.VMEM((1, part, columns), low),
            pltpu.VMEM((1, part, columns), low),
            pltpu.SemaphoreType.DMA((2, count, PIECES)),
            pltpu.SemaphoreType.DMA((2, count, PIECES)),
        ],
        4 * rows * width * columns + 12 * rows * rows * head_cols,
        "lines_beside_attention",
    )


def fourth_kernel(
    head_cols,
    piece,
    field_row,
    ready_hbm,
    up_first,
    down_first,
    xn_hbm,
    gy_hbm,
    down_hbm,
    slope_hbm,
    act_hbm,
    or_hbm,
    qkvo_hbm,
    x_ref,
    spread_ref,
    gh_out,
    sums_out,
    own_out,
    vector_ref,
    out_hbm,
    below,
    above,
    line_send,
    line_recv,
    parcel,
    pair_send,
    pair_recv,
    t_parts,
    t_got,
    t_send,
    t_recv,
    ready_ref,
    xn_ref,
    gy_ref,
    down_ref,
    wide_ref,
    or_ref,
    weight_ref,
    gh_ref,
    local_sems,
    sums_ref,
    own_ref,
    out_ref,
):
    branches = BlockScatter(t_parts, t_got, t_send, t_recv)
    share_width = x_ref.shape[1]

    def share_rows(share):
        start = pl.multiple_of(branches.owner(share) * share_width, share_width)
        return pl.ds(start, share_width)

    pairs = [
        (ready_hbm, ready_ref),
        (up_first, below.at[0]),
        (down_first, above.at[0]),
        (act_hbm, wide_ref),
        (or_hbm, or_ref),
        (qkvo_hbm.at[:, pl.ds(3 * head_cols, head_cols)], weight_ref),
    ]
    for share in range(branches.size):
        pairs.append((down_hbm.at[share_rows(share), :], down_ref.at[share_rows(share), :]))
    pairs += [(gy_hbm, gy_ref), (xn_hbm, xn_ref)]
    loads = fetch(pairs, local_sems)
    more_sems = local_sems.at[pl.ds(len(pairs), 5)]
    line = LineSum(ready_ref, below, above, line_send, line_recv, True)
    products = PairProducts(
        [xn_ref] * 4, quarters(gh_ref), parcel, sums_ref, pair_send, pair_recv
    )
    barrier, count = greet_line()
    count += greet_block()
    pl.semaphore_wait(barrier, count)
    for load in loads[:3]:
        load.wait()
    line.advance(2)
    for load in loads[3:6]:
        load.wait()
    rows = x_ref.shape[0]
    width = down_ref.shape[1] // 4
    vector_ref[...] = jnp.zeros_like(vector_ref)

    def tile(here):
        for quarter in range(4):
            columns = pl.ds(quarter * width, width)
            grad_act = contract(gy_ref[here, :], down_ref[:, columns], 1, 0)
            grad_hidden = grad_act * wide_ref[here, columns].astype(jnp.float32)
            grad_hidden = grad_hidden.astype(jnp.bfloat16)
            gh_ref[here, columns] = grad_hidden
            vector_ref[0:1, columns] += jnp.sum(
                grad_hidden.astype(jnp.float32), axis=0, keepdims=True
            )

    def branch(share):
        where = share_rows(share)
        loads[6 + share].wait()

        def once(here):
            part = contract(or_ref[here, :], weight_ref[where, :], 1, 1)
            part = part + contract(wide_ref[here, :], down_ref[where, :], 1, 1)
            t_parts[share, here, :] = part.astype(jnp.bfloat16)

        for bottom in branches.halves(share):
            once(pl.ds(bottom * (rows // 2), rows // 2))
            branches.after_half(share, bottom)

    shares = branches.size
    for share in range(shares):
        branch(share)
        if share == 1:
            line.advance(3, 0, 1)
    late = pltpu.make_async_copy(slope_hbm, wide_ref, more_sems.at[0])
    late.start()
    line.advance(3, 1)
    branches.second()
    for load in loads[6 + shares :]:
        load.wait()
    late.wait()
    by_rows(rows, ROW_TILE, tile)
    stores = fetch([(gh_ref, gh_out)], more_sems.at[pl.ds(1, 1)])
    products.far()
    for step in range(4, line.count):
        line.advance(step)
    branches.finish()
    biases = [
        jnp.concatenate(field_rows(spread_ref, field_row, kind, piece), axis=1) for kind in (3, 4)
    ]
    for tile_index in range(rows // ROW_TILE):
        here = pl.ds(tile_index * ROW_TILE, ROW_TILE)
        total = x_ref[here, :].astype(jnp.float32) + branches.total(tile_index, ROW_TILE)
        total = total + biases[0] + biases[1]
        out_ref[here, :] = total.astype(jnp.bfloat16)
    stores += fetch([(out_ref, out_hbm)], more_sems.at[pl.ds(3, 1)])
    products.near()
    stores += fetch([(sums_ref, sums_out)], more_sems.at[pl.ds(2, 1)])
    line.finish(own_ref)
    stores += fetch([(own_ref, own_out)], more_sems.at[pl.ds(4, 1)])
    for store in stores:
        store.wait()


def fourth_step(
    ready,
    firsts,
    normed,
    grad_rows,
    turned_down,
    slope,
    activated,
    attended,
    full_qkvo,
    tokens,
    spread,
    piece,
    field_row,
):
    rows, width = normed.shape
    head_cols = attended.shape[1]
    count, part, columns = ready.shape
    low = jnp.bfloat16
    return carrying(
        functools.partial(fourth_kernel, head_cols, piece, field_row),
        6,
        (
            ready,
            *firsts,
            normed,
            grad_rows,
            turned_down,
            slope,
            activated,
            attended,
            full_qkvo,
            tokens,
            spread,
        ),
        "hhhhhhhhhhvv",
        [
            ((rows, columns), low),
            ((count, part, columns), low),
            ((part, columns), low),
            ((8, columns), jnp.float32),
            (tokens.shape, low),
        ],
        "hhhvh",
        sum_scratch(part, columns)
        + pair_scratch(part, columns)
        + scatter_scratch(rows, tokens.shape[1])
        + [
            pltpu.VMEM(ready.shape, low),
            pltpu.VMEM((rows, width), low),
            pltpu.VMEM((rows, width), low),
            pltpu.VMEM((width, columns), low),
            pltpu.VMEM((rows, columns), low),
            pltpu.VMEM((rows, head_cols), low),
            pltpu.VMEM((width, head_cols), low),
            pltpu.VMEM((rows, columns), low),
            pltpu.SemaphoreType.DMA((13 + lax.axis_size("mp"),)),
            pltpu.VMEM((count, part, columns), low),
            pltpu.VMEM((part, columns), low),
            pltpu.VMEM(tokens.shape, low),
        ],
        6 * rows * width * columns,
        "line_beside_hidden_grad",
    )


def greet_block():
    size = lax.axis_size("mp")
    place = lax.axis_index("mp")
    barrier = pltpu.get_barrier_semaphore()
    for step in range(1, size):
        peer = lax.rem(place + step, size)
        pl.semaphore_signal(barrier, inc=1, device_id={"mp": peer}, device_id_type=MESH_ID)
    return size - 1


class BlockScatter:
    def __init__(self, parts, got, send, recv):
        self.size = lax.axis_size("mp")
        self.place = lax.axis_index("mp")
        self.parts, self.got, self.send, self.recv = parts, got, send, recv
        self.half = parts.shape[1] // 2
        self.beside = self.place + 1 - 2 * lax.rem(self.place, 2)
        self.above = lax.rem(self.place + 2, 4)

    def owner(self, index):
        if self.size == 4:
            return [lax.rem(self.beside + 2, 4), self.beside, self.above, self.place][index]
        return lax.rem(self.place + 1 + index, self.size)

    def copy(self, index):
        if self.size == 4:
            part, bottom, peer = [
                (0, 0, self.beside),
                (0, 1, self.above),
                (1, 0, self.beside),
                (2, 1, self.above),
                (2, 0, self.above),
                (1, 1, self.beside),
            ][index]
            source = self.parts.at[part, pl.ds(bottom * self.half, self.half), :]
        else:
            source = self.parts.at[index]
            peer = self.owner(index)
        sems = (self.send.at[index], self.recv.at[index])
        return remote(source, self.got.at[index], *sems, "mp", peer)

    def after(self, index):
        if self.size != 4:
            if index < self.size - 1:
                self.copy(index).start()
            return
        for number in ((0, 1), (2,), (3,), ())[index]:
            self.copy(number).start()

    def halves(self, index):
        return (1, 0) if index == 2 and self.size == 4 else (0, 1)

    def after_half(self, index, bottom):
        if self.size != 4:
            if bottom:
                self.after(index)
            return
        number = {(0, 0): 0, (0, 1): 1, (1, 0): 2, (2, 1): 3}.get((index, bottom))
        if number is not None:
            self.copy(number).start()

    def second(self):
        if self.size != 4:
            return
        for number, part, bottom in ((0, 2, 0), (1, 1, 1)):
            self.copy(number).wait_recv()

            def body(rows, number=number, part=part, bottom=bottom):
                here = pl.ds(bottom * self.half + rows.start, rows.size)
                total = summed(self.parts[part, here, :], self.got[number, rows, :])
                self.parts[part, here, :] = total.astype(jnp.bfloat16)

            by_rows(self.half, 64, body)
            self.copy(number + 4).start()

    def finish(self):
        if self.size != 4:
            for index in range(self.size - 1):
                self.copy(index).wait()
            return
        for index in range(6):
            if index > 1:
                self.copy(index).wait_recv()
            self.copy(index).wait_send()

    def total(self, tile, rows):
        here = pl.ds(tile * rows, rows)
        own = self.parts[self.size - 1, here, :]
        if self.size != 4:
            return summed(own, *[self.got[index, here, :] for index in range(self.size - 1)])
        bottom = (tile * rows) // self.half
        there = pl.ds(tile * rows - bottom * self.half, rows)
        return summed(own, self.got[2 + bottom, there, :], self.got[4 + bottom, there, :])


def scatter_scratch(rows, width):
    size = lax.axis_size("mp")
    slots = (6, rows // 2, width) if size == 4 else (size - 1, rows, width)
    return [
        pltpu.VMEM((size, rows, width), jnp.bfloat16),
        pltpu.VMEM(slots, jnp.bfloat16),
        pltpu.SemaphoreType.DMA((slots[0],)),
        pltpu.SemaphoreType.DMA((slots[0],)),
    ]


STREAM = 256
SLOTS = 3


def stream(tiles, loads, stores, compute, primed=False):
    ahead = SLOTS - 1
    if not primed:
        prime(tiles, loads)

    def once(tile, carry):
        slot = lax.rem(tile, SLOTS)

        @pl.when(tile + ahead < tiles)
        def _():
            for copy in loads(tile + ahead, lax.rem(tile + ahead, SLOTS)):
                copy.start()

        for copy in loads(tile, slot):
            copy.wait()

        @pl.when(tile >= SLOTS)
        def _():
            for copy in stores(tile - SLOTS, slot):
                copy.wait()

        compute(tile, slot)
        for copy in stores(tile, slot):
            copy.start()
        return carry

    lax.fori_loop(0, tiles, once, 0)
    for tile in range(max(tiles - SLOTS, 0), tiles):
        for copy in stores(tile, tile % SLOTS):
            copy.wait()


def prime(tiles, loads):
    for tile in range(min(SLOTS - 1, tiles)):
        for copy in loads(tile, tile):
            copy.start()


def fetch(pairs, sems):
    copies = [
        pltpu.make_async_copy(source, target, sems.at[index])
        for index, (source, target) in enumerate(pairs)
    ]
    for copy in copies:
        copy.start()
    return copies


def fifth_kernel(
    head_cols,
    piece,
    ready_hbm,
    gh_hbm,
    grad_hbm,
    qkvo_ref,
    up_ref,
    x_hbm,
    gy_hbm,
    stats_hbm,
    spread_ref,
    vector_three,
    vector_four,
    gained_out,
    terms_out,
    up_send,
    down_send,
    own_ref,
    sums_ref,
    below,
    above,
    line_send,
    line_recv,
    g_parts,
    g_got,
    g_send,
    g_recv,
    terms_ref,
    terms_got,
    terms_send,
    terms_recv,
    vector_ref,
    vector_got,
    vector_send,
    vector_recv,
    ready_ref,
    gh_ref,
    grad_ref,
    x_ref,
    gy_ref,
    stats_ref,
    gained_ref,
    load_sems,
):
    loads = fetch(
        [
            (ready_hbm, ready_ref),
            (grad_hbm, grad_ref),
            (gh_hbm, gh_ref),
            (x_hbm, x_ref),
            (gy_hbm, gy_ref),
            (stats_hbm, stats_ref),
        ],
        load_sems,
    )
    line = LineSum(ready_ref, below, above, line_send, line_recv)
    from_norm = BlockScatter(g_parts, g_got, g_send, g_recv)
    mp_size = from_norm.size
    mp_place = from_norm.place
    dp_size = lax.axis_size("dp")
    dp_place = lax.axis_index("dp")
    rows, width = x_ref.shape
    tiles = rows // ROW_TILE
    barrier = pltpu.get_barrier_semaphore()

    def greet(step, carry):
        peer = lax.rem(dp_place + step, dp_size)
        pl.semaphore_signal(barrier, inc=1, device_id={"dp": peer}, device_id_type=MESH_ID)
        return carry

    lax.fori_loop(1, dp_size, greet, 0)
    pl.semaphore_wait(barrier, dp_size - 1 + greet_block())
    loads[0].wait()
    line.advance(1)
    for load in loads[1:3]:
        load.wait()

    def parts(one_ref, two_ref, sems):
        def load(share):
            start = pl.multiple_of(from_norm.owner(share) * width, width)
            slot = share % 2
            where = pl.ds(start, width)
            narrow = pl.ds(0, 3 * head_cols)
            return [
                pltpu.make_async_copy(qkvo_ref.at[where, narrow], one_ref.at[slot], sems.at[0, slot]),
                pltpu.make_async_copy(up_ref.at[where, :], two_ref.at[slot], sems.at[1, slot]),
            ]

        for copy in load(0):
            copy.start()
        for share in range(mp_size):
            slot = share % 2
            for copy in load(share):
                copy.wait()
            if share + 1 < mp_size:
                for copy in load(share + 1):
                    copy.start()

            def tile(here, share=share, slot=slot):
                part = contract(grad_ref[here, :], one_ref[slot], 1, 1)
                part = part + contract(gh_ref[here, :], two_ref[slot], 1, 1)
                g_parts[share, here, :] = part.astype(jnp.bfloat16)

            for bottom in from_norm.halves(share):
                tile(pl.ds(bottom * (rows // 2), rows // 2))
                from_norm.after_half(share, bottom)

    columns = up_ref.shape[1]
    pl.run_scoped(
        parts,
        pltpu.VMEM((2, width, 3 * head_cols), jnp.bfloat16),
        pltpu.VMEM((2, width, columns), jnp.bfloat16),
        pltpu.SemaphoreType.DMA((2, 2)),
    )
    for step in range(2, line.count - 1):
        line.advance(step)
    from_norm.second()
    for load in loads[3:]:
        load.wait()
    from_norm.finish()

    def lane_pair(first, second):
        lane = lax.broadcasted_iota(jnp.int32, (ROW_TILE, LANES), 1)
        return jnp.where(lane == 0, first, jnp.where(lane == 1, second, 0.0))

    owners = [mp_place * dp_size + owner for owner in range(dp_size)]
    gain = jnp.concatenate(vector_rows(spread_ref, owners, 0, piece), axis=1)
    sums = [jnp.zeros((1, width), jnp.float32) for _ in range(3)]
    for tile in range(tiles):
        here = pl.ds(tile * ROW_TILE, ROW_TILE)
        normalized = (x_ref[here, :].astype(jnp.float32) - stats_ref[here, 0:1]) * stats_ref[here, 1:2]
        grad = from_norm.total(tile, ROW_TILE)
        gained = grad * gain
        gained_ref[here, :] = gained
        terms = lane_pair(
            jnp.sum(gained, axis=1, keepdims=True),
            jnp.sum(gained * normalized, axis=1, keepdims=True),
        )
        terms_ref[:, here] = jnp.transpose(terms)[:8, :]
        upstream = gy_ref[here, :].astype(jnp.float32) * stats_ref[here, 2:3]
        sums[0] += jnp.sum(grad * normalized, axis=0, keepdims=True)
        sums[1] += jnp.sum(grad, axis=0, keepdims=True)
        sums[2] += jnp.sum(upstream, axis=0, keepdims=True)

    store = pltpu.make_async_copy(gained_ref, gained_out, load_sems.at[len(loads)])
    store.start()
    three_width = vector_three.shape[1]
    fields = [vector_three[0:1, pl.ds(0, three_width - head_cols)], vector_four[0:1, :]] + sums
    flat = jnp.concatenate(fields, axis=1)
    per_row = vector_ref.shape[1]
    for row in range(8):
        part = flat[:, row * per_row : (row + 1) * per_row]
        if part.shape[1]:
            vector_ref[row : row + 1, pl.ds(0, part.shape[1])] = part
    def terms_copy(step):
        peer = lax.rem(mp_place + step, mp_size)
        slot = step - 1
        sems = (terms_send.at[slot], terms_recv.at[slot])
        return remote(terms_ref, terms_got.at[slot], *sems, "mp", peer)

    def vector_copy(step):
        peer = lax.rem(dp_place + step, dp_size)
        slot = step - 1
        sems = (vector_send.at[slot], vector_recv.at[slot])
        return remote(vector_ref, vector_got.at[slot], *sems, "dp", peer)

    def vector_begin(step, carry):
        vector_copy(step).start()
        return carry

    for step in range(1, mp_size):
        terms_copy(step).start()
    lax.fori_loop(1, dp_size, vector_begin, 0)
    def vector_end(step, carry):
        vector_copy(step).wait()
        return carry

    by_rows(own_ref.shape[0], 32, lambda here: keep_block(ready_ref, line.spot, own_ref, here))
    line.hand_out(up_send, down_send)
    terms = terms_ref[...]
    for step in range(1, mp_size):
        terms_copy(step).wait()
        terms = terms + terms_got[step - 1]
    terms_out[...] = terms
    lax.fori_loop(1, dp_size, vector_end, 0)
    total = vector_ref[...]
    for slot in range(dp_size - 1):
        total = total + vector_got[slot]
    flat = jnp.concatenate([total[row : row + 1, :] for row in range(8)], axis=1)
    start = 0
    for row, field in enumerate(fields):
        sums_ref[row : row + 1, pl.ds(0, field.shape[1])] = flat[:, start : start + field.shape[1]]
        start += field.shape[1]
    store.wait()


def keep_block(blocks, index, out, here):
    out[here, :] = blocks[index, here, :]


def fifth_step(
    ready,
    grad_hidden,
    grad_projected,
    full_qkvo,
    full_up,
    tokens,
    cotangent,
    stats,
    spread,
    vector_three,
    vector_four,
    piece,
):
    rows, width = tokens.shape
    head_cols = grad_projected.shape[1] // 3
    count, part, columns = ready.shape
    mp_size = lax.axis_size("mp")
    dp_size = lax.axis_size("dp")
    low = jnp.bfloat16
    exact = jnp.float32
    packed = 3 * head_cols + columns + 3 * width
    packed = -(-packed // (8 * LANES)) * LANES
    return carrying(
        functools.partial(fifth_kernel, head_cols, piece),
        7,
        (
            ready,
            grad_hidden,
            grad_projected,
            full_qkvo,
            full_up,
            tokens,
            cotangent,
            stats,
            spread,
            vector_three,
            vector_four,
        ),
        "hhhhhhhhvvv",
        [
            ((rows, width), exact),
            ((8, rows), exact),
            ((part, columns), low),
            ((part, columns), low),
            ((part, columns), low),
            ((8, columns), exact),
        ],
        "hvvvvv",
        sum_scratch(part, columns)
        + scatter_scratch(rows, width)
        + [
            pltpu.VMEM((8, rows), exact),
            pltpu.VMEM((mp_size - 1, 8, rows), exact),
            pltpu.SemaphoreType.DMA((mp_size - 1,)),
            pltpu.SemaphoreType.DMA((mp_size - 1,)),
            pltpu.VMEM((8, packed), exact),
            pltpu.VMEM((dp_size - 1, 8, packed), exact),
            pltpu.SemaphoreType.DMA((dp_size - 1,)),
            pltpu.SemaphoreType.DMA((dp_size - 1,)),
            pltpu.VMEM(ready.shape, low),
            pltpu.VMEM((rows, columns), low),
            pltpu.VMEM((rows, 3 * head_cols), low),
            pltpu.VMEM((rows, width), low),
            pltpu.VMEM((rows, width), low),
            pltpu.VMEM(stats.shape, exact),
            pltpu.VMEM((rows, width), exact),
            pltpu.SemaphoreType.DMA((7,)),
        ],
        4 * rows * width * mp_size * columns,
        "line_beside_norm_grad",
    )


class Averager:
    def __init__(self, grad, stats, stats_out, buffers, sems):
        self.grad, self.stats, self.stats_out = grad, stats, stats_out
        self.stat_in, self.stat_new, self.root_in, self.side_in, self.side_new = buffers
        self.sems = sems
        self.tile_rows = self.stat_in.shape[1]
        self.tiles = grad.shape[1] // self.tile_rows

    def where(self, tile):
        return pl.ds(pl.multiple_of(tile * self.tile_rows, self.tile_rows), self.tile_rows)

    def loads(self, tile, slot):
        pairs = [
            (self.stats.at[0, 0, 0, self.where(tile), :], self.stat_in),
            (self.root_tile(tile), self.root_in),
            (self.side(self.master, tile), self.side_in),
        ]
        return [
            pltpu.make_async_copy(source, target.at[slot], self.sems.at[index, slot])
            for index, (source, target) in enumerate(pairs)
        ]

    def stores(self, tile, slot):
        pairs = [
            (self.stat_new, self.stats_out.at[0, 0, self.where(tile), :]),
            (self.side_new, self.side(self.master_out, tile)),
        ]
        return [
            pltpu.make_async_copy(source.at[slot], target, self.sems.at[3 + index, slot])
            for index, (source, target) in enumerate(pairs)
        ]

    def compute(self, tile, slot):
        product = contract(self.grad[:, self.where(tile)], self.grad[...], 0, 0)
        self.stat_new[slot] = 0.5 * self.stat_in[slot].astype(jnp.float32) + 0.5 * product
        step = self.step(self.root_in[slot].astype(jnp.bfloat16))
        self.side_new[slot] = self.side_in[slot] - matrix_rate * step

    def start(self):
        prime(self.tiles, self.loads)

    def run(self):
        stream(self.tiles, self.loads, self.stores, self.compute, True)


class WideUnit(Averager):
    def __init__(self, grad, stats, stats_out, buffers, sems, first, small, small_out, master, out):
        super().__init__(grad, stats, stats_out, buffers, sems)
        self.first, self.small, self.small_out = first, small, small_out
        self.master, self.master_out = master, out

    def root_tile(self, tile):
        return self.stats.at[1, 0, 0, :, self.where(tile)]

    def side(self, ref, tile):
        if len(ref.shape) == 2:
            return ref.at[:, self.where(tile)]
        per_plane = ref.shape[2] // self.tile_rows
        return ref.at[tile // per_plane, :, self.where(lax.rem(tile, per_plane))]

    def prepare(self):
        root = self.small[1, 0, 0].astype(jnp.bfloat16)
        self.first[...] = contract(root, self.grad[...], 1, 0).astype(jnp.bfloat16)
        average_small(self.small, self.small_out, self.grad)

    def step(self, root):
        return contract(self.first[...], root, 1, 0)


class TallUnit(Averager):
    def __init__(self, grad, stats, stats_out, buffers, sems, small, small_out, master, out):
        super().__init__(grad, stats, stats_out, buffers, sems)
        self.small, self.small_out = small, small_out
        self.master, self.master_out = master, out

    def root_tile(self, tile):
        return self.stats.at[1, 0, 0, self.where(tile), :]

    def side(self, ref, tile):
        return ref.at[self.where(tile), :]

    def prepare(self):
        average_small(self.small, self.small_out, self.grad)

    def step(self, root):
        first = contract(root, self.grad[...], 1, 1).astype(jnp.bfloat16)
        return contract(first, self.small[1, 0, 0].astype(jnp.bfloat16), 1, 0)


def average_small(small, small_out, grad):
    small_out[0, 0] = 0.5 * small[0, 0, 0] + 0.5 * contract(grad[...], grad[...], 1, 1)


def unit_scratch(depth, size, wide, source=jnp.float32):
    tile_rows = min(STREAM, size)
    exact = jnp.float32
    root = (size, tile_rows) if wide else (tile_rows, size)
    side = (depth, tile_rows) if wide else (tile_rows, depth)
    shapes = [(tile_rows, size), (tile_rows, size), root, side, side]
    types = [source, exact, source, exact, exact]
    return [pltpu.VMEM((SLOTS,) + shape, kind) for shape, kind in zip(shapes, types)] + [
        pltpu.SemaphoreType.DMA((5, SLOTS))
    ]


def local_call(kernel, operands, in_places, outs, out_places, scratch, name, limit=VMEM_LIMIT):
    spaces = {"h": pl.BlockSpec(memory_space=pl.ANY), "v": pl.BlockSpec(memory_space=pltpu.VMEM)}
    return pl.pallas_call(
        kernel,
        in_specs=[spaces[place] for place in in_places],
        out_specs=[spaces[place] for place in out_places],
        out_shape=[jax.ShapeDtypeStruct(shape, dtype) for shape, dtype in outs],
        scratch_shapes=scratch,
        compiler_params=pltpu.CompilerParams(vmem_limit_bytes=limit),
        cost_estimate=pl.CostEstimate(flops=1 << 33, bytes_accessed=1 << 26, transcendentals=0),
        name=name,
    )(*operands)


def down_kernel(
    grad, stats, small, master, earlier, stats_out, small_out, master_out, *scratch
):
    *buffers, sems = scratch
    unit = TallUnit(
        grad, stats, stats_out, buffers, sems, small, small_out, master, master_out
    )
    unit.start()
    unit.prepare()
    unit.run()


def down_step(grad, left, right, master, earlier):
    exact = jnp.float32
    return local_call(
        down_kernel,
        (grad, left, right, master, earlier),
        "vhvhh",
        [(left.shape[1:], exact), (right.shape[1:], exact), (master.shape, exact)],
        "hvh",
        unit_scratch(grad.shape[0], grad.shape[1], False, left.dtype),
        "down_weight",
    )


def update_vectors(sums, states, up_state, params_out, stats_out, up_out, up_stat_out):
    columns = sums.shape[1]
    place = lax.axis_index("dp")
    qkv_state, out_state, norm_state = states
    piece = norm_state.shape[2]
    stride = lax.axis_size("dp") * piece
    own = pltpu.roll(sums[...], lax.rem(columns - place * piece, columns), 1)
    picks = [
        (qkv_state[kind, 0:1, :], qkv_state[kind, 1:2, :], own[0:1, kind * stride : kind * stride + piece])
        for kind in range(3)
    ]
    for state, rows in ((out_state, (4, 4)), (norm_state, (2, 3))):
        for kind, row in enumerate(rows):
            param, stat = (state[0, kind : kind + 1, :], state[1, kind : kind + 1, :])
            picks.append((param, stat, own[row : row + 1, :piece]))

    def update(param, stat, grad):
        stat_new = 0.5 * stat + 0.5 * grad * grad
        return (param - vector_rate * grad * lax.rsqrt(stat_new), stat_new)

    for row, (param, stat, grad) in enumerate(picks):
        param, stat = update(param, stat, grad)
        params_out[row : row + 1, :] = param
        stats_out[row : row + 1, :] = stat
    piece = up_state.shape[1]
    own = pltpu.roll(sums[...], lax.rem(columns - place * piece, columns), 1)
    param, stat = update(up_state[0:1, :], up_state[1:2, :], own[1:2, :piece])
    up_out[...] = param
    up_stat_out[...] = stat


def attention_weights_kernel(
    passed,
    owned_ref,
    qkv_left,
    qkv_right,
    w_qkv,
    out_left,
    out_right,
    w_out,
    sums,
    qkv_state,
    out_state,
    norm_state,
    up_state,
    x_ref,
    gy_ref,
    stats_ref,
    gained_ref,
    terms_ref,
    *refs,
):
    sources, refs = (refs[:passed], refs[passed:])
    targets, refs = (refs[:passed], refs[passed:])
    (
        qkv_left_new,
        qkv_right_new,
        w_qkv_new,
        out_left_new,
        out_right_new,
        w_out_new,
        params_out,
        stats_out,
        up_out,
        up_stat_out,
        dx_out,
        low_qkv,
        low_out,
        first,
        dx_ref,
        dx_sem,
    ), refs = (refs[:16], refs[16:])
    held, refs = (refs[:passed], refs[passed:])
    pass_sems, *buffers = refs
    qkv = WideUnit(
        low_qkv,
        qkv_right,
        qkv_right_new,
        buffers[:5],
        buffers[5],
        first,
        qkv_left,
        qkv_left_new,
        w_qkv,
        w_qkv_new,
    )
    out = TallUnit(
        low_out,
        out_left,
        out_left_new,
        buffers[6:11],
        buffers[11],
        out_right,
        out_right_new,
        w_out,
        w_out_new,
    )
    qkv.start()
    out.start()
    into = fetch(zip(sources, held), pass_sems.at[0])
    edge = low_qkv.shape[1]
    low_qkv[...] = owned_ref[:, :edge]
    low_out[...] = owned_ref[:, edge:]
    qkv.prepare()
    out.prepare()
    for copy in into:
        copy.wait()
    onward = fetch(zip(held, targets), pass_sems.at[1])
    rows, width = x_ref.shape
    model_width = width * lax.axis_size("mp")
    for tile in range(rows // ROW_TILE):
        here = pl.ds(tile * ROW_TILE, ROW_TILE)
        zeros = jnp.zeros((LANES - 8, ROW_TILE), jnp.float32)
        terms = jnp.transpose(jnp.concatenate([terms_ref[:, here], zeros], axis=0))
        terms = terms * (1.0 / model_width)
        inv_std = stats_ref[here, 1:2]
        normalized = (x_ref[here, :].astype(jnp.float32) - stats_ref[here, 0:1]) * inv_std
        upstream = gy_ref[here, :].astype(jnp.float32) * stats_ref[here, 2:3]
        change = gained_ref[here, :] - terms[:, 0:1] - normalized * terms[:, 1:2]
        dx_ref[here, :] = upstream + inv_std * change
    onward += fetch([(dx_ref, dx_out)], dx_sem)
    qkv.run()
    out.run()
    update_vectors(
        sums, (qkv_state, out_state, norm_state), up_state, params_out, stats_out, up_out, up_stat_out
    )
    for copy in onward:
        copy.wait()


def attention_weights_step(blocks, qkv, out, sums, states, norm, passed):
    exact = jnp.float32
    low = jnp.bfloat16
    depth = blocks[0].shape[0]
    sizes = (qkv[1].shape[-1], out[0].shape[-1])
    count = len(passed)
    piece = states[2].shape[2]
    up_piece = states[3].shape[1]
    return local_call(
        functools.partial(attention_weights_kernel, count),
        blocks + qkv + out + (sums,) + states + norm + passed,
        "v" + "vhh" + "hvh" + "v" + "vvvv" + "vvvvv" + "h" * count,
        [(array.shape, array.dtype) for array in passed]
        + [
            (qkv[0].shape[1:], exact),
            (qkv[1].shape[1:], exact),
            (qkv[2].shape, exact),
            (out[0].shape[1:], exact),
            (out[1].shape[1:], exact),
            (out[2].shape, exact),
            ((7, piece), exact),
            ((7, piece), exact),
            ((1, up_piece), exact),
            ((1, up_piece), exact),
            (norm[0].shape, exact),
        ],
        "h" * count + "vhh" + "hvh" + "vvvv" + "h",
        [
            pltpu.VMEM((depth, sizes[0]), low),
            pltpu.VMEM((depth, sizes[1]), low),
            pltpu.VMEM((depth, sizes[0]), low),
            pltpu.VMEM(norm[0].shape, exact),
            pltpu.SemaphoreType.DMA((1,)),
        ]
        + [pltpu.VMEM(array.shape, array.dtype) for array in passed]
        + [pltpu.SemaphoreType.DMA((2, count))]
        + unit_scratch(depth, sizes[0], True, qkv[1].dtype)
        + unit_scratch(depth, sizes[1], False),
        "attention_weights",
        VMEM_LIMIT,
    )


def up_kernel(
    own_ref,
    rising_ref,
    falling_ref,
    small,
    stats,
    master,
    earlier_one,
    earlier_two,
    small_out,
    stats_out,
    master_out,
    grad,
    first,
    *scratch,
):
    *buffers, sems = scratch
    unit = WideUnit(
        grad, stats, stats_out, buffers, sems, first, small, small_out, master, master_out
    )
    unit.start()
    grad[...] = summed(own_ref[...], rising_ref[...], falling_ref[...]).astype(jnp.bfloat16)
    unit.prepare()
    unit.run()


def up_step(blocks, left, right, master, *earlier):
    exact = jnp.float32
    depth, columns = master.shape
    return local_call(
        up_kernel,
        blocks + (left, right, master) + earlier,
        "vvvvhhhh",
        [(left.shape[1:], exact), (right.shape[1:], exact), (master.shape, exact)],
        "vhh",
        [pltpu.VMEM((depth, columns), jnp.bfloat16) for _ in range(2)]
        + unit_scratch(depth, columns, True, right.dtype),
        "up_weight",
        VMEM_LIMIT,
    )


def local(
    tokens,
    cotangent,
    seq_lengths,
    w_qkv,
    qkv_bias_state,
    w_out,
    out_bias_state,
    w_up,
    up_bias_state,
    w_down,
    ln_state,
    qkv_left,
    qkv_right,
    out_left,
    out_right,
    up_left,
    up_right,
    down_left,
    down_right,
):
    row_count, share_width = tokens.shape
    mp_size = lax.axis_size("mp")
    dp_size = lax.axis_size("dp")
    model_width = share_width * mp_size
    own_width = w_qkv.shape[2]
    mp_place = lax.axis_index("mp")

    piece = ln_state.shape[2]
    up_piece = up_bias_state.shape[1]

    planes = w_qkv.transpose(1, 0, 2)
    qkv_states = qkv_bias_state.transpose(1, 0, 2)
    (
        turned_block,
        full_up,
        full_qkvo,
        normed,
        grad_rows,
        spread,
        stats,
        activated,
        slope,
        ready_down,
        up_right_low,
        down_left_low,
        qkv_right_low,
    ) = first_step(
        (w_up, planes, w_out, w_down),
        tokens,
        cotangent,
        (ln_state, qkv_states, out_bias_state, up_bias_state),
        seq_lengths,
        up_right,
        down_left,
        qkv_right,
    )
    field_row = 1 - (-up_piece // LANES)
    turned_down, grad_projected, attended, ready_qkvo, owned_down, vector_three, *firsts = third_step(
        turned_block,
        ready_down,
        normed,
        grad_rows,
        full_qkvo,
        spread,
        seq_lengths,
        piece,
        field_row,
    )
    grad_hidden, ready_up, owned_qkvo, vector_four, output = fourth_step(
        ready_qkvo,
        firsts,
        normed,
        grad_rows,
        turned_down,
        slope,
        activated,
        attended,
        full_qkvo,
        tokens,
        spread,
        piece,
        field_row,
    )
    steps = range(dp_size - 2)

    def last_hop(up_send, down_send, own):
        rising = lax.ppermute(up_send, "dp", [(place, place + 2) for place in steps])
        falling = lax.ppermute(down_send, "dp", [(place + 2, place) for place in steps])
        return (own, rising, falling)

    gained, terms, *sends, sums = fifth_step(
        ready_up,
        grad_hidden,
        grad_projected,
        full_qkvo,
        full_up,
        tokens,
        cotangent,
        stats,
        spread,
        vector_three,
        vector_four,
        piece,
    )
    blocks_up = last_hop(*sends)
    down_left_new, down_right_new, new_w_down = down_step(
        owned_down, down_left_low, down_right, w_down, sends[0]
    )
    (
        output,
        qkv_left_new,
        qkv_right_new,
        new_planes,
        out_left_new,
        out_right_new,
        new_w_out,
        new_vector_params,
        new_vector_stats,
        new_up_bias,
        new_up_stat,
        input_grad,
    ) = attention_weights_step(
        (owned_qkvo,),
        (qkv_left, qkv_right_low, planes),
        (out_left, out_right, w_out),
        sums,
        (qkv_states, out_bias_state, ln_state, up_bias_state),
        (tokens, cotangent, stats, gained, terms),
        (output,),
    )
    new_w_qkv = new_planes.transpose(1, 0, 2)
    up_left_new, up_right_new, new_w_up = up_step(
        blocks_up, up_left, up_right_low, w_up, new_vector_params, down_right_new
    )
    new_up_bias = new_up_bias.reshape(-1)
    new_up_stat = new_up_stat.reshape(-1)
    return (
        output,
        input_grad,
        new_w_qkv,
        new_w_out,
        new_w_up,
        new_w_down,
        new_vector_params,
        new_vector_stats,
        new_up_bias,
        new_up_stat,
        qkv_left_new,
        qkv_right_new,
        out_left_new,
        out_right_new,
        up_left_new,
        up_right_new,
        down_left_new,
        down_right_new,
    )


def solution(mesh):
    return jax.shard_map(
        local,
        mesh=mesh,
        in_specs=(
            P("dp", "mp"),
            P("dp", "mp"),
            P("dp", None),
            P("dp", None, "mp"),
            P(None, None, ("mp", "dp")),
            P("mp", "dp"),
            P(None, None, ("mp", "dp")),
            P("dp", "mp"),
            P(None, ("mp", "dp")),
            P("mp", "dp"),
            P(None, None, ("mp", "dp")),
            P(None, "mp", "dp", None, None),
            P(None, "mp", "dp", None, None),
            P(None, "mp", "dp", None, None),
            P(None, "mp", "dp", None, None),
            P(None, "mp", "dp", None, None),
            P(None, "mp", "dp", None, None),
            P(None, "mp", "dp", None, None),
            P(None, "mp", "dp", None, None),
        ),
        out_specs=(
            P("dp", "mp"),
            P("dp", "mp"),
            P("dp", None, "mp"),
            P("mp", "dp"),
            P("dp", "mp"),
            P("mp", "dp"),
            P(None, ("mp", "dp")),
            P(None, ("mp", "dp")),
            P(("mp", "dp")),
            P(("mp", "dp")),
            P("mp", "dp", None, None),
            P("mp", "dp", None, None),
            P("mp", "dp", None, None),
            P("mp", "dp", None, None),
            P("mp", "dp", None, None),
            P("mp", "dp", None, None),
            P("mp", "dp", None, None),
            P("mp", "dp", None, None),
        ),
        check_vma=False,
    )
```
